32 devices in a mesh: dpo: 4 (over z), dpi: 2 (over x), tp: 4 (over y, core).
Axes of the slice: x: 2, y: 2, z: 4, core: 2. Of those that a mesh axis runs over, the one named last changes fastest.
Arguments:
- tokens: bfloat16 [8192, 768], P(('dpo', 'dpi')), may hold values from -6 to 6
- cotangent: bfloat16 [8192, 768], P(('dpo', 'dpi')), may hold values from -6 to 6
- heights: int32 [32], P(('dpo', 'dpi')), may hold values from 1 to 15
- labels: int32 [32], P(('dpo', 'dpi')), may hold values from 0 to 999
- valid: int32 [8192], P(('dpo', 'dpi')), may hold values 0 or 1
- class_table: bfloat16 [1000, 768], replicated, may hold values from -6 to 6
- gains: float32 [2, 2, 768], replicated, may hold values from 0.25 to 1.75
- w_qkv: bfloat16 [2, 768, 3, 768], P(None, None, None, 'tp'), may hold values from -0.21875 to 0.21875
- w_out: bfloat16 [2, 768, 768], P(None, 'tp'), may hold values from -1.75 to 1.75
- w_gate_up: bfloat16 [2, 768, 2, 2048], P(None, None, None, 'tp'), may hold values from -0.21875 to 0.21875
- w_down: bfloat16 [2, 2048, 768], P(None, 'tp'), may hold values from -0.125 to 0.125
Outputs:
- output: float32 [8192, 768], P(('dpo', 'dpi'))
- token_grad: float32 [8192, 768], P(('dpo', 'dpi'))
- table_grad: float32 [1000, 768], P(None, 'dpi')
- gain_grad: float32 [2, 2, 768], replicated
- qkv_grad: float32 [2, 768, 3, 768], P(None, 'dpi', None, 'tp')
- out_grad: float32 [2, 768, 768], P(None, 'tp', 'dpi')
- gate_up_grad: float32 [2, 768, 2, 2048], P(None, 'dpi', None, 'tp')
- down_grad: float32 [2, 2048, 768], P(None, 'tp', 'dpi')
The draws below stay inside these ranges and needn't reach their ends.
All inputs are finite; a program needn't handle non-finite values. No bound on the sum of `valid` on one device may be relied on, other than what follows from the above.
Results may differ from the reference program's by a relative error of at most 0.018.
Values sent between devices are 32-bit elements; how exact they have to be, the bound alone decides.
A program may use at most 128 MiB of HBM per device.

```python
import math
import jax
import jax.numpy as jnp
from jax import lax

D = 768
HEADS = 12
HD = 64
FF = 2048
CLASSES = 1000
LAYERS = 2
COLS = 16
HMAX = 15
SLOT = 256
SEQS = 32
TOKENS = 8192


def plant(result, key, low, top_value):
    longest = result.shape.index(max(result.shape))
    spots = []
    for shift in (0, 1):
        where = [jax.random.randint(jax.random.fold_in(key, axis), (), 0, length) for axis, length in enumerate(result.shape)]
        where[longest] = (where[longest] + shift) % result.shape[longest]
        spots.append(tuple(where))
    return result.at[spots[0]].set(low).at[spots[1]].set(top_value)


def spiked(result, own_key, source, target, parts, factor):
    owner, partner = [(jnp.arange(result.shape[dim]) // (result.shape[dim] // parts)).reshape([-1 if axis == dim else 1 for axis in range(result.ndim)]) for dim in (source, target)]
    chosen = jax.random.permutation(own_key, parts)[partner]
    strong = (owner == chosen) | (owner == (partner + parts // 2) % parts)
    return jnp.where(strong, factor * result, result)


def steps_of(stream_key, dims, split, low, high):
    loudness, own = 1.0, jax.random.fold_in(stream_key, 6)
    for dim, parts in split:
        steps = jnp.exp(jax.random.uniform(jax.random.fold_in(own, dim), (parts,), jnp.float32, low / len(split), high / len(split)))
        loudness = loudness * jnp.repeat(steps, dims[dim] // parts).reshape([-1 if axis == dim else 1 for axis in range(len(dims))])
    return loudness


def scatter_about(rng, shape, deviation, limit, split=(), kind=jnp.bfloat16):
    entries = deviation * jax.random.normal(rng, shape, jnp.float32)
    if split:
        entries = entries * steps_of(rng, shape, split, -0.22, 0.18)
    return jnp.clip(entries, -limit, limit).astype(kind)


def heavy_noise(own_key, shape, spread, most, pieces, heavy, kind=jnp.bfloat16):
    result = spread * jax.random.normal(own_key, shape, jnp.float32)
    if pieces:
        result = result * steps_of(own_key, shape, pieces, -0.22, 0.18)
    return jnp.clip(spiked(result, jax.random.fold_in(own_key, 3), *heavy), -most, most).astype(kind)


def setup_inputs(seed: int = 0) -> dict:
    key_list = jax.random.split(jax.random.key(seed), 12)
    return {
        "tokens": scatter_about(key_list[0], (TOKENS, D), 1.0, 6.0, ((0, 8),)),
        "cotangent": heavy_noise(key_list[1], (TOKENS, D), 1.0, 6.0, ((0, 8),), (0, 1, 8, 2.0)),
        "heights": plant(jax.random.randint(key_list[2], (SEQS,), 1, HMAX + 1), jax.random.fold_in(key_list[2], 1), 1, HMAX).astype(jnp.int32),
        "labels": plant(jax.random.randint(key_list[3], (SEQS,), 0, CLASSES), jax.random.fold_in(key_list[3], 1), 0, CLASSES - 1).astype(jnp.int32),
        "valid": plant((jax.random.randint(key_list[4], (TOKENS,), 0, 8) < 7).astype(jnp.int32), jax.random.fold_in(key_list[4], 1), 0, 1),
        "class_table": scatter_about(key_list[5], (CLASSES, D), 1.0, 6.0),
        "gains": jnp.clip(1.0 + 0.15 * jax.random.normal(key_list[6], (LAYERS, 2, D), jnp.float32), 0.25, 1.75),
        "w_qkv": scatter_about(key_list[7], (LAYERS, D, 3, HEADS * HD), D ** -0.5, 0.21875, ((3, 4),)),
        "w_out": scatter_about(key_list[8], (LAYERS, HEADS * HD, D), (max(HEADS * HD // 64, 1)) ** -0.5, 1.75, ((1, 4),)),
        "w_gate_up": scatter_about(key_list[9], (LAYERS, D, 2, FF), D ** -0.5, 0.21875, ((3, 4),)),
        "w_down": scatter_about(key_list[10], (LAYERS, FF, D), FF ** -0.5, 0.125, ((1, 4),)),
    }


@jax.custom_vjp
def low(v):
    return lax.optimization_barrier(v.astype(jnp.bfloat16)).astype(jnp.float32)

@jax.custom_vjp
def low_back(v):
    return v

def low_keep(v):
    return (low(v), None)

def low_pass(kept, grad):
    return (grad,)

def back_keep(v):
    return (v, None)

def back_low(kept, grad):
    return (low(grad),)
low.defvjp(low_keep, low_pass)
low_back.defvjp(back_keep, back_low)
epsilon = 1e-05

def rope_tables(slot_len):
    quarter = HD // 4
    position = jnp.arange(slot_len)
    raster = jnp.maximum(position - 1, 0)
    row_pos = (raster // COLS).astype(jnp.float32)
    col_pos = (raster % COLS).astype(jnp.float32)
    frequency = 10000.0 ** (-jnp.arange(quarter).astype(jnp.float32) / quarter)
    row_angle = (row_pos[:, None] * frequency[None, :])[:, None, :]
    col_angle = (col_pos[:, None] * frequency[None, :])[:, None, :]
    return (jnp.cos(row_angle), jnp.sin(row_angle), jnp.cos(col_angle), jnp.sin(col_angle))

def rotate_pairs(values_in, tables, direction):
    quarter = values_in.shape[-1] // 4
    cos_row, sin_row, cos_col, sin_col = tables
    sin_row = sin_row * direction
    sin_col = sin_col * direction
    first_part = values_in[..., :quarter]
    second_part = values_in[..., quarter:2 * quarter]
    third_part = values_in[..., 2 * quarter:3 * quarter]
    fourth_part = values_in[..., 3 * quarter:]
    return jnp.concatenate([first_part * cos_row - second_part * sin_row, second_part * cos_row + first_part * sin_row, third_part * cos_col - fourth_part * sin_col, fourth_part * cos_col + third_part * sin_col], axis=-1)

def visible(heights, valid, slot_len):
    position = jnp.arange(slot_len)
    length = 1 + COLS * heights
    open_key = (position[None, :] < length[:, None]) & (valid == 1)
    causal = position[:, None] >= position[None, :]
    diagonal = position[:, None] == position[None, :]
    return causal[None] & (open_key[:, None, :] | diagonal[None])

def normalize(residual, gain):
    scale_inv = lax.rsqrt(lax.optimization_barrier(jnp.mean(residual * residual, axis=-1, keepdims=True)) + epsilon)
    return residual * scale_inv * gain

def attend(operands):
    queries, key_rows, value_rows, allowed = operands
    scores = low_back(jnp.einsum('gihd,gjhd->ghij', queries, key_rows, precision=lax.Precision.HIGHEST) * HD ** (-0.5))
    scores = jnp.where(allowed[:, None], scores, -jnp.inf)
    largest = lax.optimization_barrier(jnp.max(scores, axis=-1, keepdims=True))
    raised = jnp.exp(scores - largest)
    attn_prob = raised / lax.optimization_barrier(jnp.sum(raised, axis=-1, keepdims=True))
    return jnp.einsum('ghij,gjhd->gihd', low(attn_prob), value_rows, precision=lax.Precision.HIGHEST)

def attention_block(residual, gain, w_qkv, w_out, allowed, tables):
    seq_count = allowed.shape[0]
    normed = low(normalize(residual, gain))
    packed = jnp.einsum('nd,dta->nta', normed, w_qkv, precision=lax.Precision.HIGHEST)
    shaped = packed.reshape(seq_count, SLOT, 3, HEADS, HD)
    queries = low(rotate_pairs(low_back(shaped[:, :, 0]), tables, 1.0))
    key_rows = low(rotate_pairs(low_back(shaped[:, :, 1]), tables, 1.0))
    value_rows = low(low_back(shaped[:, :, 2]))
    group_size = math.gcd(seq_count, 16)

    def regroup(values_in):
        return values_in.reshape((seq_count // group_size, group_size) + values_in.shape[1:])
    mixed_heads = lax.map(jax.checkpoint(attend), (regroup(queries), regroup(key_rows), regroup(value_rows), regroup(allowed)))
    mixed_heads = low(low_back(mixed_heads.reshape(seq_count * SLOT, HEADS * HD)))
    branch = low_back(jnp.dot(mixed_heads, w_out, precision=lax.Precision.HIGHEST))
    return residual + branch

def feed_forward(residual, gain, w_gate_up, w_down):
    normed = low(normalize(residual, gain))
    packed = jnp.einsum('nd,dtf->ntf', normed, w_gate_up, precision=lax.Precision.HIGHEST)
    gate_value = low_back(packed[:, 0])
    up_value = low_back(packed[:, 1])
    hidden = low(jax.nn.silu(gate_value) * up_value)
    return residual + low_back(jnp.dot(hidden, w_down, precision=lax.Precision.HIGHEST))

def reference(tokens, cotangent, heights, labels, valid, class_table, gains, w_qkv, w_out, w_gate_up, w_down):
    seq_count = heights.shape[0]
    allowed = visible(heights, valid.reshape(seq_count, SLOT), SLOT)
    tables = rope_tables(SLOT)
    floats = tuple((operand.astype(jnp.float32) for operand in (tokens, class_table, gains, w_qkv, w_out, w_gate_up, w_down)))

    def whole_model(inputs, table, gain_all, qkv_all, out_all, gate_up_all, down_all):
        token_grid = inputs.reshape(seq_count, SLOT, D)
        first_rows = table[labels]
        residual = jnp.concatenate([first_rows[:, None, :], token_grid[:, 1:, :]], axis=1).reshape(seq_count * SLOT, D)
        for layer_index in range(LAYERS):
            residual = attention_block(residual, gain_all[layer_index, 0], qkv_all[layer_index], out_all[layer_index], allowed, tables)
            residual = feed_forward(residual, gain_all[layer_index, 1], gate_up_all[layer_index], down_all[layer_index])
        return residual
    output, pullback = jax.vjp(whole_model, *floats)
    token_grad, table_grad, gain_grad, qkv_grad, out_grad, gate_up_grad, down_grad = pullback(cotangent.astype(jnp.float32))
    return (output, token_grad, table_grad, gain_grad, qkv_grad, out_grad, gate_up_grad, down_grad)
```

```python
import functools

import jax
import jax.numpy as jnp
import numpy as np
from jax import lax
from jax.experimental import pallas as pl
from jax.experimental.pallas import tpu as pltpu
from jax.sharding import PartitionSpec as P

HD = 64
COLS = 16
EPS = 1e-05
F32 = jnp.float32
BF16 = jnp.bfloat16
LOW = -1e30

NN = (((1,), (0,)), ((), ()))
NT = (((1,), (1,)), ((), ()))
TN = (((0,), (0,)), ((), ()))


def mm(a, b, dims=NN):
    return lax.dot_general(a, b, dims, preferred_element_type=F32)


def rope_constants(slot_len):
    quarter = HD // 4
    raster = np.maximum(np.arange(slot_len) - 1, 0)
    row_pos = (raster // COLS).astype(np.float32)
    col_pos = (raster % COLS).astype(np.float32)
    frequency = (10000.0 ** (-np.arange(quarter).astype(np.float32) / quarter)).astype(np.float32)
    row_angle = row_pos[:, None] * frequency[None, :]
    col_angle = col_pos[:, None] * frequency[None, :]
    zero = np.zeros_like(row_angle)
    cos = np.concatenate([np.cos(row_angle)] * 2 + [np.cos(col_angle)] * 2, axis=1)
    first = np.concatenate([-np.sin(row_angle), zero, -np.sin(col_angle), zero], axis=1)
    second = np.concatenate([zero, np.sin(row_angle), zero, np.sin(col_angle)], axis=1)
    return np.stack([np.tile(t, (1, 2)) for t in (cos, first, second)]).astype(np.float32)


def rotate(x, table_ref, sign):
    quarter = HD // 4
    ahead = pltpu.roll(x, 2 * HD - quarter, 1) * table_ref[1]
    behind = pltpu.roll(x, quarter, 1) * table_ref[2]
    turned = ahead + behind
    return x * table_ref[0] + (turned if sign > 0 else -turned)


def merge(axis, mine_ref, other_ref, out_ref):
    size = mine_ref.shape[axis]
    if axis == 1:
        out_ref[:, :size, :] = mine_ref[...].astype(BF16)
        out_ref[:, size:, :] = other_ref[...].astype(BF16)
    else:
        out_ref[:, :, :size] = mine_ref[...].astype(BF16)
        out_ref[:, :, size:] = other_ref[...].astype(BF16)


def inv_rms(h):
    return lax.rsqrt(jnp.mean(h * h, axis=-1, keepdims=True) + EPS)


def norm_back(grad, normed, scale, gain):
    scaled = grad * gain
    return scale * (scaled - normed * jnp.mean(scaled * normed, axis=-1, keepdims=True))


def key_mask(open_ref, n):
    key = lax.broadcasted_iota(jnp.int32, (n, n), 0)
    query = lax.broadcasted_iota(jnp.int32, (n, n), 1)
    return ((key < query) & (open_ref[...] > 0.5)) | (key == query)


def attn_fwd(first, *refs):
    if first:
        h_ref, gain_ref, wqkv_ref, wout_ref, table_ref, open_ref = refs[:6]
        refs = refs[6:]
        h = h_ref[...]
    else:
        h_ref, p_ref, r_ref, gain_ref, wqkv_ref, wout_ref, table_ref, open_ref = refs[:8]
        refs = refs[8:]
        h = h_ref[...] + (p_ref[...] + r_ref[...])
        refs[0][...] = h
        refs = refs[1:]
    a_ref, qkv_ref, lse_ref, o_ref, part_ref = refs
    n = h.shape[0]
    width = wout_ref.shape[0]
    a = (h * inv_rms(h) * gain_ref[...]).astype(BF16)
    a_ref[...] = a
    lane = lax.broadcasted_iota(jnp.int32, (n, 2 * HD), 1)
    low_half = lane < HD
    zero = jnp.zeros((n, 2 * HD), BF16)
    mask = key_mask(open_ref, n)
    for t in range(width // (2 * HD)):
        spots = [slice(s * width + t * 2 * HD, s * width + (t + 1) * 2 * HD) for s in range(3)]
        q = rotate(mm(a, wqkv_ref[spots[0], :], NT), table_ref, 1)
        q = (q * HD ** (-0.5)).astype(BF16)
        k = rotate(mm(a, wqkv_ref[spots[1], :], NT), table_ref, 1).astype(BF16)
        v = mm(a, wqkv_ref[spots[2], :], NT).astype(BF16)
        qkv_ref[:, spots[0]] = q
        qkv_ref[:, spots[1]] = k
        qkv_ref[:, spots[2]] = v
        mixed = []
        for e in range(2):
            q_one = jnp.where(low_half if e == 0 else ~low_half, q, zero)
            s = jnp.where(mask, mm(k, q_one, NT), LOW)
            top = jnp.max(s, axis=0, keepdims=True)
            raised = jnp.exp(s - top)
            total = jnp.sum(raised, axis=0, keepdims=True)
            lse_ref[2 * t + e : 2 * t + e + 1, :] = top + jnp.log(total)
            prob = (raised / total).astype(BF16)
            mixed.append(mm(prob, v, TN))
        o_ref[:, t * 2 * HD : (t + 1) * 2 * HD] = jnp.where(low_half, mixed[0], mixed[1]).astype(BF16)
    part_ref[...] = mm(o_ref[...], wout_ref[...])


def ffn_fwd(h_ref, p_ref, r_ref, gain_ref, wgu_ref, wd_ref, h1_ref, b_ref, gu_ref, hid_ref, part_ref):
    h = h_ref[...] + (p_ref[...] + r_ref[...])
    h1_ref[...] = h
    b = (h * inv_rms(h) * gain_ref[...]).astype(BF16)
    b_ref[...] = b
    width = wd_ref.shape[0]
    step = min(width, 256)
    total = None
    for f in range(0, width, step):
        gate = mm(b, wgu_ref[0, :, f : f + step])
        up = mm(b, wgu_ref[1, :, f : f + step])
        gu_ref[:, f : f + step] = gate
        gu_ref[:, width + f : width + f + step] = up
        hid = (gate * jax.nn.sigmoid(gate) * up).astype(BF16)
        hid_ref[:, f : f + step] = hid
    part_ref[...] = mm(hid_ref[...], wd_ref[...])


def ffn_bwd(first, *refs):
    if first:
        g_ref, gu_ref, wgu_ref, wd_ref = refs[:4]
        refs = refs[4:]
        gm = g_ref[...]
    else:
        g1_ref, p_ref, r_ref, hin_ref, gain_ref, gu_ref, wgu_ref, wd_ref = refs[:8]
        refs = refs[8:]
        grad, gain_grad = close_norm(g1_ref[...], p_ref, r_ref, hin_ref, gain_ref)
        refs[0][...] = grad
        refs[1][...] = gain_grad
        gm = grad.astype(BF16)
        refs[2][...] = gm
        refs = refs[3:]
    dgu_ref, part_ref = refs
    width = wd_ref.shape[0]
    step = min(width, 256)
    for f in range(0, width, step):
        dhid = mm(gm, wd_ref[f : f + step, :], NT)
        gate = gu_ref[:, f : f + step]
        up = gu_ref[:, width + f : width + f + step]
        sig = jax.nn.sigmoid(gate)
        dgu_ref[:, f : f + step] = (dhid * up * (sig * (1.0 + gate * (1.0 - sig)))).astype(BF16)
        dgu_ref[:, width + f : width + f + step] = (dhid * (gate * sig)).astype(BF16)
    part_ref[...] = mm(dgu_ref[:, :width], wgu_ref[0], NT) + mm(dgu_ref[:, width:], wgu_ref[1], NT)


def close_norm(g, p_ref, r_ref, h_ref, gain_ref):
    grad = p_ref[...] + r_ref[...]
    h = h_ref[...]
    scale = inv_rms(h)
    normed = h * scale
    gain_grad = jnp.sum(grad * normed, axis=0, keepdims=True)
    return g + norm_back(grad, normed, scale, gain_ref[...]), gain_grad


def attn_bwd(
    g_ref, p_ref, r_ref, h1_ref, gain_ref, wqkv_ref, wout_ref, table_ref, open_ref, qkv_ref, lse_ref,
    g1_ref, gain_grad_ref, ga_ref, dqkv_ref, part_ref,
):
    g1, gain_grad = close_norm(g_ref[...].astype(F32), p_ref, r_ref, h1_ref, gain_ref)
    g1_ref[...] = g1
    gain_grad_ref[...] = gain_grad
    ga = g1.astype(BF16)
    ga_ref[...] = ga
    n = ga.shape[0]
    width = wout_ref.shape[0]
    lane = lax.broadcasted_iota(jnp.int32, (n, 2 * HD), 1)
    low_half = lane < HD
    zero = jnp.zeros((n, 2 * HD), BF16)
    mask = key_mask(open_ref, n)
    for t in range(width // (2 * HD)):
        spots = [slice(s * width + t * 2 * HD, s * width + (t + 1) * 2 * HD) for s in range(3)]
        q = qkv_ref[:, spots[0]]
        k = qkv_ref[:, spots[1]]
        v = qkv_ref[:, spots[2]]
        dout = mm(ga, wout_ref[t * 2 * HD : (t + 1) * 2 * HD, :], NT).astype(BF16)
        dq, dk, dv = [], [], []
        for e in range(2):
            mine = low_half if e == 0 else ~low_half
            q_one = jnp.where(mine, q, zero)
            d_one = jnp.where(mine, dout, zero)
            s = jnp.where(mask, mm(k, q_one, NT), LOW)
            prob = jnp.exp(s - lse_ref[2 * t + e : 2 * t + e + 1, :])
            dprob = mm(v, d_one, NT)
            delta = jnp.sum(prob * dprob, axis=0, keepdims=True)
            ds = (prob * (dprob - delta)).astype(BF16)
            dv.append(mm(prob.astype(BF16), dout))
            dk.append(mm(ds, q))
            dq.append(mm(ds, k, TN))
        dq = jnp.where(low_half, dq[0], dq[1]) * HD ** (-0.5)
        dk = jnp.where(low_half, dk[0], dk[1])
        dv = jnp.where(low_half, dv[0], dv[1])
        dqkv_ref[:, spots[0]] = rotate(dq, table_ref, -1).astype(BF16)
        dqkv_ref[:, spots[1]] = rotate(dk, table_ref, -1).astype(BF16)
        dqkv_ref[:, spots[2]] = dv.astype(BF16)
    part_ref[...] = mm(dqkv_ref[...], wqkv_ref[...])


def close_layer(g1_ref, p_ref, r_ref, h_ref, gain_ref, out_ref, gain_grad_ref):
    grad, gain_grad = close_norm(g1_ref[...], p_ref, r_ref, h_ref, gain_ref)
    out_ref[...] = grad
    gain_grad_ref[...] = gain_grad


def halves_of(half_ref, dim):
    one = dim // 2
    return [pl.ds(pl.multiple_of(half_ref[s] * one, one), one) for s in range(2)]


def grad_rows(spans, half_ref, *refs):
    chunks = (len(refs) - 2) // 2
    lefts, rights = refs[:chunks], refs[chunks : 2 * chunks]
    outs = refs[2 * chunks :]
    for s, spot in enumerate(halves_of(half_ref, rights[0].shape[1])):
        for out, picks in zip(outs, spans):
            at = 0
            for lo, hi in picks:
                total = None
                for left, right in zip(lefts, rights):
                    term = mm(left[:, lo:hi], right[:, spot], TN)
                    total = term if total is None else total + term
                out[s, at : at + hi - lo, :] = total
                at += hi - lo


def grad_columns(spans, half_ref, *refs):
    chunks = (len(refs) - 2) // 2
    lefts, rights = refs[:chunks], refs[chunks : 2 * chunks]
    outs = refs[2 * chunks :]
    for s, spot in enumerate(halves_of(half_ref, lefts[0].shape[1])):
        for out, picks in zip(outs, spans):
            at = 0
            for lo, hi in picks:
                total = None
                for left, right in zip(lefts, rights):
                    term = mm(left[:, spot], right[:, lo:hi], TN)
                    total = term if total is None else total + term
                out[s, :, at : at + hi - lo] = total
                at += hi - lo


def call(body, outs, args, flops, limit=40, smem=0):
    moved = sum(x.size * x.dtype.itemsize for x in args) + sum(
        int(np.prod(s)) * np.dtype(d).itemsize for s, d in outs
    )
    spec = pl.BlockSpec(memory_space=pltpu.VMEM)
    got = pl.pallas_call(
        body,
        out_shape=[jax.ShapeDtypeStruct(s, d) for s, d in outs],
        in_specs=[pl.BlockSpec(memory_space=pltpu.SMEM)] * smem + [spec] * (len(args) - smem),
        out_specs=[spec] * len(outs),
        compiler_params=pltpu.CompilerParams(vmem_limit_bytes=limit * 2**20),
        cost_estimate=pl.CostEstimate(flops=int(flops), bytes_accessed=int(moved), transcendentals=0),
    )(*args)
    return list(got)


def on_device(sizes, tokens, cotangent, heights, labels, valid, class_table, gains, w_qkv, w_out, w_gate_up, w_down):
    seq_count = heights.shape[0]
    row_count, dim = tokens.shape
    n = row_count // seq_count
    layers = gains.shape[0]
    classes = class_table.shape[0]
    la = w_out.shape[1]
    lf = w_down.shape[1]
    wa, wf = 2 * la, 2 * lf
    tp, dpo, dpi = sizes["tp"], sizes["dpo"], sizes["dpi"]
    mine = seq_count // 2
    core = lax.rem(lax.axis_index("tp"), 2)
    z = lax.axis_index("dpo")
    swap_core = [(i, i ^ 1) for i in range(tp)]

    def core_swap(x):
        return lax.ppermute(x, "tp", swap_core)

    def sum_chips(part):
        total = None
        for step in range(2, tp, 2):
            got = lax.ppermute(part, "tp", [(i, i ^ step) for i in range(tp)])
            total = got if total is None else total + got
        return total

    wqkv, wout, wgu, wd = [], [], [], []
    for l in range(layers):
        for into, w in (
            (wqkv, jnp.transpose(w_qkv[l], (1, 2, 0))),
            (wout, w_out[l][None]),
            (wgu, jnp.transpose(w_gate_up[l], (1, 0, 2))),
            (wd, w_down[l][None]),
        ):
            wide = w.astype(F32)
            axis = 2 if into is wgu else 1
            shape = list(w.shape)
            shape[axis] *= 2
            into.append(call(functools.partial(merge, axis), [(tuple(shape), BF16)], (wide, core_swap(wide)), 1000)[0])
        wqkv[l] = wqkv[l].reshape(3 * wa, dim)
        wout[l] = wout[l][0]
        wd[l] = wd[l][0]

    tables = jnp.asarray(rope_constants(n))
    position = jnp.arange(n)
    own = lambda x: lax.dynamic_slice_in_dim(x, core * mine, mine, 0)
    open_key = (position[None, :] < 1 + COLS * own(heights)[:, None]) & (own(valid.reshape(seq_count, n)) == 1)
    open_key = open_key.astype(F32)[:, :, None]
    own_labels = own(labels)
    token_own = own(tokens.reshape(seq_count, n, dim))
    cot_own = own(cotangent.reshape(seq_count, n, dim))
    chunks = range(mine)
    hs = []
    for c in chunks:
        row = lax.dynamic_slice_in_dim(class_table, own_labels[c], 1, 0)
        hs.append(jnp.where((position == 0)[:, None], row, token_own[c]).astype(F32))

    shape_d = ((n, dim), F32)
    shape_b = ((n, dim), BF16)
    flops_a = 2 * n * dim * 4 * wa + 8 * n * n * wa
    flops_f = 2 * n * dim * 3 * wf

    kept = []
    state = [(hs[c],) for c in chunks]
    parts = None
    for l in range(layers):
        keep = [dict() for _ in chunks]
        for c in chunks:
            args = state[c] + (gains[l, 0][None], wqkv[l], wout[l], tables, open_key[c])
            outs = [shape_b, ((n, 3 * wa), BF16), ((max(8, wa // HD), n), F32), ((n, wa), BF16), shape_d]
            if l > 0:
                outs = [shape_d] + outs
            got = call(functools.partial(attn_fwd, l == 0), outs, args, flops_a)
            h = state[c][0] if l == 0 else got.pop(0)
            a, qkv, lse, o, part = got
            keep[c].update(h=h, a=a, qkv=qkv, lse=lse, o=o)
            state[c] = (h, part, sum_chips(part))
        for c in chunks:
            args = state[c] + (gains[l, 1][None], wgu[l], wd[l])
            outs = [shape_d, shape_b, ((n, 2 * wf), F32), ((n, wf), BF16), shape_d]
            h1, b, gu, hid, part = call(ffn_fwd, outs, args, flops_f)
            keep[c].update(h1=h1, b=b, gu=gu, hid=hid)
            state[c] = (h1, part, sum_chips(part))
        kept.append(keep)

    output = jnp.concatenate([s[0] + (s[1] + s[2]) for s in state], axis=0)

    half = lax.axis_index("dpi") if dpi == 2 else 1
    order = jnp.stack([jnp.int32(1) - half, jnp.int32(half)])

    def dp_sum(both, other, axis):
        got = core_swap(other)
        if dpi == 2:
            sent = lax.ppermute(both[0] + got[0], "dpi", [(0, 1), (1, 0)])
            total = (both[1] + got[1]) + sent
        else:
            both = both + got
            whole = jnp.concatenate([both[0], both[1]], axis=axis)
            total = lax.psum_scatter(whole, "dpi", scatter_dimension=axis, tiled=True)
        return line_sum(total)

    def line_sum(x):
        if dpo != 4:
            return lax.psum(x, "dpo")
        got = lax.ppermute(x, "dpo", [(0, 1), (3, 2)])
        x = x + got
        got = lax.ppermute(x, "dpo", [(1, 2), (2, 1)])
        x = x + got
        got = lax.ppermute(x, "dpo", [(1, 0), (2, 3)])
        return jnp.where((z == 0) | (z == dpo - 1), got, x)

    gain_rows = [[None, None] for _ in range(layers)]
    grads = [None] * layers
    state = [None] * mine
    for l in reversed(range(layers)):
        top = l == layers - 1
        keep = kept[l]
        gms = []
        for c in chunks:
            outs = [((n, 2 * wf), BF16), shape_d]
            args = (keep[c]["gu"], wgu[l], wd[l])
            if top:
                g = cot_own[c]
                dgu, part = call(functools.partial(ffn_bwd, True), outs, (g,) + args, flops_f)
                gms.append(g)
            else:
                outs = [shape_d, ((1, dim), F32), shape_b] + outs
                args = state[c] + args
                g, gain_c, gm, dgu, part = call(functools.partial(ffn_bwd, False), outs, args, flops_f)
                gain_rows[l + 1][0] = gain_c if c == 0 else gain_rows[l + 1][0] + gain_c
                gms.append(gm)
            keep[c]["dgu"] = dgu
            state[c] = (g, part, sum_chips(part), keep[c]["h1"], gains[l, 1][None])
        flops_w = 2 * n * mine * dim * wf
        outs = [((2, lf, dim // 2), F32)] * 2
        args = [order] + [keep[c]["hid"] for c in chunks] + gms
        spans = (((0, lf),), ((lf, wf),))
        down = call(functools.partial(grad_rows, spans), outs, args, flops_w, smem=1)
        outs = [((2, dim // 2, 2 * lf), F32)] * 2
        args = [order] + [keep[c]["b"] for c in chunks] + [keep[c]["dgu"] for c in chunks]
        spans = (((0, lf), (wf, wf + lf)), ((lf, wf), (wf + lf, 2 * wf)))
        gate_up = call(functools.partial(grad_columns, spans), outs, args, 2 * flops_w, smem=1)
        down = dp_sum(*down, 1)
        gate_up = dp_sum(*gate_up, 0)
        gas = []
        for c in chunks:
            outs = [shape_d, ((1, dim), F32), shape_b, ((n, 3 * wa), BF16), shape_d]
            args = state[c] + (wqkv[l], wout[l], tables, open_key[c], keep[c]["qkv"], keep[c]["lse"])
            g1, gain_c, ga, dqkv, part = call(attn_bwd, outs, args, flops_a + 12 * n * n * wa)
            gain_rows[l][1] = gain_c if c == 0 else gain_rows[l][1] + gain_c
            gas.append(ga)
            keep[c]["dqkv"] = dqkv
            state[c] = (g1, part, sum_chips(part), keep[c]["h"], gains[l, 0][None])
        flops_w = 2 * n * mine * dim * wa
        outs = [((2, la, dim // 2), F32)] * 2
        args = [order] + [keep[c]["o"] for c in chunks] + gas
        spans = (((0, la),), ((la, wa),))
        out = call(functools.partial(grad_rows, spans), outs, args, flops_w, smem=1)
        outs = [((2, 3 * la, dim // 2), F32)] * 2
        args = [order] + [keep[c]["dqkv"] for c in chunks] + [keep[c]["a"] for c in chunks]
        spans = tuple(tuple((t * wa + s * la, t * wa + (s + 1) * la) for t in range(3)) for s in range(2))
        qkv = call(functools.partial(grad_rows, spans), outs, args, 3 * flops_w, smem=1)
        out = dp_sum(*out, 1)
        qkv = dp_sum(*qkv, 1)
        grads[l] = (qkv, out, gate_up, down)

    finals = []
    for c in chunks:
        g, gain_c = call(close_layer, [shape_d, ((1, dim), F32)], state[c], 1000)
        gain_rows[0][0] = gain_c if c == 0 else gain_rows[0][0] + gain_c
        finals.append(g)

    slot0 = lax.axis_index("dpo") * dpi + lax.axis_index("dpi")
    seqs = seq_count * dpo * dpi
    firsts = jnp.concatenate([g[0:1] for g in finals], axis=0)
    small = jnp.zeros((seqs + 2 * layers + 1, dim), F32)
    small = lax.dynamic_update_slice(small, firsts, (slot0 * seq_count + core * mine, 0))
    terms = jnp.concatenate([gain_rows[l][i] for l in range(layers) for i in range(2)], axis=0)
    small = lax.dynamic_update_slice(small, terms, (seqs, 0))
    label_row = lax.dynamic_update_slice(
        jnp.zeros((1, dim), F32), own_labels.astype(F32)[None], (0, slot0 * seq_count + core * mine)
    )
    small = lax.dynamic_update_slice(small, label_row, (seqs + 2 * layers, 0))
    small = jnp.where(lax.axis_index("tp") < 2, small, 0.0)
    small = lax.psum(small, ("dpo", "dpi", "tp"))
    all_labels = jnp.round(small[seqs + 2 * layers, :seqs]).astype(jnp.int32)
    gain_total = small[seqs : seqs + 2 * layers].reshape(layers, 2, dim)
    onehot = (all_labels[None, :] == jnp.arange(classes)[:, None]).astype(F32)
    share = dim // dpi
    rows = lax.dynamic_slice(small, (0, lax.axis_index("dpi") * share), (seqs, share))
    table_part = jnp.dot(onehot, rows, precision=lax.Precision.HIGHEST)

    token_own = jnp.concatenate([jnp.where((position == 0)[:, None], 0.0, g) for g in finals], axis=0)

    def both_cores(x):
        other = core_swap(x)
        return jnp.where(core == 0, jnp.concatenate([x, other], 0), jnp.concatenate([other, x], 0))

    qkv_part = jnp.stack([g[0].reshape(3, la, share) for g in grads]).transpose(0, 3, 1, 2)
    out_part = jnp.stack([g[1] for g in grads])
    gate_up_part = jnp.stack([g[2].reshape(share, 2, lf) for g in grads])
    down_part = jnp.stack([g[3] for g in grads])
    return (
        both_cores(output),
        both_cores(token_own),
        table_part,
        gain_total,
        qkv_part,
        out_part,
        gate_up_part,
        down_part,
    )


def solution(mesh):
    sizes = dict(mesh.shape)
    placed = (
        P(("dpo", "dpi"), None),
        P(("dpo", "dpi"), None),
        P(("dpo", "dpi")),
        P(("dpo", "dpi")),
        P(("dpo", "dpi")),
        P(),
        P(),
        P(None, None, None, "tp"),
        P(None, "tp", None),
        P(None, None, None, "tp"),
        P(None, "tp", None),
    )
    return jax.shard_map(
        functools.partial(on_device, sizes),
        mesh=mesh,
        in_specs=placed,
        out_specs=(
            P(("dpo", "dpi"), None),
            P(("dpo", "dpi"), None),
            P(None, "dpi"),
            P(),
            P(None, "dpi", None, "tp"),
            P(None, "tp", "dpi"),
            P(None, "dpi", None, "tp"),
            P(None, "tp", "dpi"),
        ),
        check_vma=False,
    )
```

```python
import functools

import jax
import jax.numpy as jnp
import numpy as np
from jax import lax
from jax.experimental import pallas as pl
from jax.experimental.pallas import tpu as pltpu
from jax.sharding import PartitionSpec as P

HD = 64
COLS = 16
EPS = 1e-05
F32 = jnp.float32
BF16 = jnp.bfloat16
LOW = -1e30
MESH = pl.DeviceIdType.MESH

NN = (((1,), (0,)), ((), ()))
NT = (((1,), (1,)), ((), ()))
TN = (((0,), (0,)), ((), ()))


def mm(a, b, dims=NN):
    return lax.dot_general(a, b, dims, preferred_element_type=F32)


def rope_constants(slot_len):
    quarter = HD // 4
    raster = np.maximum(np.arange(slot_len) - 1, 0)
    row_pos = (raster // COLS).astype(np.float32)
    col_pos = (raster % COLS).astype(np.float32)
    frequency = (10000.0 ** (-np.arange(quarter).astype(np.float32) / quarter)).astype(np.float32)
    row_angle = row_pos[:, None] * frequency[None, :]
    col_angle = col_pos[:, None] * frequency[None, :]
    zero = np.zeros_like(row_angle)
    cos = np.concatenate([np.cos(row_angle)] * 2 + [np.cos(col_angle)] * 2, axis=1)
    first = np.concatenate([-np.sin(row_angle), zero, -np.sin(col_angle), zero], axis=1)
    second = np.concatenate([zero, np.sin(row_angle), zero, np.sin(col_angle)], axis=1)
    return np.stack([np.tile(t, (1, 2)) for t in (cos, first, second)]).astype(np.float32)


def rotate(x, table_ref, sign):
    quarter = HD // 4
    ahead = pltpu.roll(x, 2 * HD - quarter, 1) * table_ref[1]
    behind = pltpu.roll(x, quarter, 1) * table_ref[2]
    turned = ahead + behind
    return x * table_ref[0] + (turned if sign > 0 else -turned)


def merge(axis, mine_ref, other_ref, out_ref):
    size = mine_ref.shape[axis]
    if axis == 1:
        out_ref[:, :size, :] = mine_ref[...].astype(BF16)
        out_ref[:, size:, :] = other_ref[...].astype(BF16)
    else:
        out_ref[:, :, :size] = mine_ref[...].astype(BF16)
        out_ref[:, :, size:] = other_ref[...].astype(BF16)


def inv_rms(h):
    return lax.rsqrt(jnp.mean(h * h, axis=-1, keepdims=True) + EPS)


def norm_back(grad, normed, scale, gain):
    scaled = grad * gain
    return scale * (scaled - normed * jnp.mean(scaled * normed, axis=-1, keepdims=True))


def key_mask(open_ref, n):
    key = lax.broadcasted_iota(jnp.int32, (n, n), 0)
    query = lax.broadcasted_iota(jnp.int32, (n, n), 1)
    return ((key < query) & (open_ref[...] > 0.5)) | (key == query)


def attn_fwd(first, lean, *refs):
    if first:
        h_ref, gain_ref, wqkv_ref, wout_ref, table_ref, open_ref = refs[:6]
        refs = refs[6:]
        h = h_ref[...]
    else:
        h_ref, p_ref, r_ref, gain_ref, wqkv_ref, wout_ref, table_ref, open_ref = refs[:8]
        refs = refs[8:]
        h = h_ref[...] + (p_ref[...] + r_ref[...])
        refs[0][...] = h
        refs = refs[1:]
    if not lean:
        refs[0][...] = (h * inv_rms(h) * gain_ref[...]).astype(BF16)
        refs = refs[1:]
    qkv_ref, lse_ref, o_ref, part_ref = refs
    n = h.shape[0]
    width = wout_ref.shape[0]
    a = (h * inv_rms(h) * gain_ref[...]).astype(BF16)
    lane = lax.broadcasted_iota(jnp.int32, (n, 2 * HD), 1)
    low_half = lane < HD
    zero = jnp.zeros((n, 2 * HD), BF16)
    mask = key_mask(open_ref, n)
    for t in range(width // (2 * HD)):
        spots = [slice(s * width + t * 2 * HD, s * width + (t + 1) * 2 * HD) for s in range(3)]
        q = rotate(mm(a, wqkv_ref[spots[0], :], NT), table_ref, 1)
        q = (q * HD ** (-0.5)).astype(BF16)
        k = rotate(mm(a, wqkv_ref[spots[1], :], NT), table_ref, 1).astype(BF16)
        v = mm(a, wqkv_ref[spots[2], :], NT).astype(BF16)
        qkv_ref[:, spots[0]] = q
        qkv_ref[:, spots[1]] = k
        qkv_ref[:, spots[2]] = v
        mixed = []
        for e in range(2):
            q_one = jnp.where(low_half if e == 0 else ~low_half, q, zero)
            s = jnp.where(mask, mm(k, q_one, NT), LOW)
            top = jnp.max(s, axis=0, keepdims=True)
            raised = jnp.exp(s - top)
            total = jnp.sum(raised, axis=0, keepdims=True)
            lse_ref[2 * t + e : 2 * t + e + 1, :] = top + jnp.log(total)
            prob = (raised / total).astype(BF16)
            mixed.append(mm(prob, v, TN))
        o_ref[:, t * 2 * HD : (t + 1) * 2 * HD] = jnp.where(low_half, mixed[0], mixed[1]).astype(BF16)
    part_ref[...] = mm(o_ref[...], wout_ref[...])


def ffn_fwd(lean, h_ref, p_ref, r_ref, gain_ref, wgu_ref, wd_ref, h1_ref, *refs):
    h = h_ref[...] + (p_ref[...] + r_ref[...])
    h1_ref[...] = h
    b = (h * inv_rms(h) * gain_ref[...]).astype(BF16)
    if lean:
        part_ref, hid_ref = refs
    else:
        b_ref, gu_ref, hid_ref, part_ref = refs
        b_ref[...] = b
    width = wd_ref.shape[0]
    step = min(width, 256)
    for f in range(0, width, step):
        gate = mm(b, wgu_ref[0, :, f : f + step])
        up = mm(b, wgu_ref[1, :, f : f + step])
        if not lean:
            gu_ref[:, f : f + step] = gate
            gu_ref[:, width + f : width + f + step] = up
        hid_ref[:, f : f + step] = (gate * jax.nn.sigmoid(gate) * up).astype(BF16)
    part_ref[...] = mm(hid_ref[...], wd_ref[...])


def ffn_bwd(first, *refs):
    if first:
        g_ref, gu_ref, wgu_ref, wd_ref = refs[:4]
        refs = refs[4:]
        gm = g_ref[...]
    else:
        g1_ref, p_ref, r_ref, hin_ref, gain_ref, gu_ref, wgu_ref, wd_ref = refs[:8]
        refs = refs[8:]
        grad, gain_grad = close_norm(g1_ref[...], p_ref, r_ref, hin_ref, gain_ref)
        refs[0][...] = grad
        refs[1][...] = gain_grad
        gm = grad.astype(BF16)
        refs[2][...] = gm
        refs = refs[3:]
    dgu_ref, part_ref = refs
    width = wd_ref.shape[0]
    step = min(width, 256)
    for f in range(0, width, step):
        dhid = mm(gm, wd_ref[f : f + step, :], NT)
        gate = gu_ref[:, f : f + step]
        up = gu_ref[:, width + f : width + f + step]
        sig = jax.nn.sigmoid(gate)
        dgu_ref[:, f : f + step] = (dhid * up * (sig * (1.0 + gate * (1.0 - sig)))).astype(BF16)
        dgu_ref[:, width + f : width + f + step] = (dhid * (gate * sig)).astype(BF16)
    part_ref[...] = mm(dgu_ref[:, :width], wgu_ref[0], NT) + mm(dgu_ref[:, width:], wgu_ref[1], NT)


def close_norm(g, p_ref, r_ref, h_ref, gain_ref):
    grad = p_ref[...] + r_ref[...]
    h = h_ref[...]
    scale = inv_rms(h)
    normed = h * scale
    gain_grad = jnp.sum(grad * normed, axis=0, keepdims=True)
    return g + norm_back(grad, normed, scale, gain_ref[...]), gain_grad


def attn_bwd(
    g_ref, p_ref, r_ref, h1_ref, gain_ref, wqkv_ref, wout_ref, table_ref, open_ref, qkv_ref, lse_ref,
    g1_ref, gain_grad_ref, ga_ref, dqkv_ref, part_ref,
):
    g1, gain_grad = close_norm(g_ref[...].astype(F32), p_ref, r_ref, h1_ref, gain_ref)
    g1_ref[...] = g1
    gain_grad_ref[...] = gain_grad
    ga = g1.astype(BF16)
    ga_ref[...] = ga
    n = ga.shape[0]
    width = wout_ref.shape[0]
    lane = lax.broadcasted_iota(jnp.int32, (n, 2 * HD), 1)
    low_half = lane < HD
    zero = jnp.zeros((n, 2 * HD), BF16)
    mask = key_mask(open_ref, n)
    for t in range(width // (2 * HD)):
        spots = [slice(s * width + t * 2 * HD, s * width + (t + 1) * 2 * HD) for s in range(3)]
        q = qkv_ref[:, spots[0]]
        k = qkv_ref[:, spots[1]]
        v = qkv_ref[:, spots[2]]
        dout = mm(ga, wout_ref[t * 2 * HD : (t + 1) * 2 * HD, :], NT).astype(BF16)
        dq, dk, dv = [], [], []
        for e in range(2):
            mine = low_half if e == 0 else ~low_half
            q_one = jnp.where(mine, q, zero)
            d_one = jnp.where(mine, dout, zero)
            s = jnp.where(mask, mm(k, q_one, NT), LOW)
            prob = jnp.exp(s - lse_ref[2 * t + e : 2 * t + e + 1, :])
            dprob = mm(v, d_one, NT)
            delta = jnp.sum(prob * dprob, axis=0, keepdims=True)
            ds = (prob * (dprob - delta)).astype(BF16)
            dv.append(mm(prob.astype(BF16), dout))
            dk.append(mm(ds, q))
            dq.append(mm(ds, k, TN))
        dq = jnp.where(low_half, dq[0], dq[1]) * HD ** (-0.5)
        dk = jnp.where(low_half, dk[0], dk[1])
        dv = jnp.where(low_half, dv[0], dv[1])
        dqkv_ref[:, spots[0]] = rotate(dq, table_ref, -1).astype(BF16)
        dqkv_ref[:, spots[1]] = rotate(dk, table_ref, -1).astype(BF16)
        dqkv_ref[:, spots[2]] = dv.astype(BF16)
    part_ref[...] = mm(dqkv_ref[...], wqkv_ref[...])


def close_layer(g1_ref, p_ref, r_ref, h_ref, gain_ref, out_ref, gain_grad_ref):
    grad, gain_grad = close_norm(g1_ref[...], p_ref, r_ref, h_ref, gain_ref)
    out_ref[...] = grad
    gain_grad_ref[...] = gain_grad


def halves_of(half_ref, dim):
    one = dim // 2
    return [pl.ds(pl.multiple_of(half_ref[s] * one, one), one) for s in range(2)]


def grad_rows(spans, half_ref, *refs):
    chunks = (len(refs) - 2) // 2
    lefts, rights = refs[:chunks], refs[chunks : 2 * chunks]
    outs = refs[2 * chunks :]
    for s, spot in enumerate(halves_of(half_ref, rights[0].shape[1])):
        for out, picks in zip(outs, spans):
            at = 0
            for lo, hi in picks:
                total = None
                for left, right in zip(lefts, rights):
                    term = mm(left[:, lo:hi], right[:, spot], TN)
                    total = term if total is None else total + term
                out[s, at : at + hi - lo, :] = total
                at += hi - lo


def grad_columns(spans, half_ref, *refs):
    chunks = (len(refs) - 2) // 2
    lefts, rights = refs[:chunks], refs[chunks : 2 * chunks]
    outs = refs[2 * chunks :]
    for s, spot in enumerate(halves_of(half_ref, lefts[0].shape[1])):
        for out, picks in zip(outs, spans):
            at = 0
            for lo, hi in picks:
                total = None
                for left, right in zip(lefts, rights):
                    term = mm(left[:, spot], right[:, lo:hi], TN)
                    total = term if total is None else total + term
                out[s, :, at : at + hi - lo] = total
                at += hi - lo


def backward(sizes, dims, *refs):
    n, dim, wa, wf, layers, chunks = dims
    la, lf, half = wa // 2, wf // 2, dim // 2
    refs = list(refs)

    def take(count):
        got = refs[:count]
        del refs[:count]
        return got

    def grid(rows):
        return [take(chunks) for _ in range(rows)]

    gains_ref, tables, open_ref, block_ref = take(4)
    cot_in, pout_in = take(chunks), take(chunks)
    h_in, h1_in, qkv_in, lse_in, o_in = [grid(layers) for _ in range(5)]
    wgu_in, wd_in, wqkv_in, wout_in = [take(layers) for _ in range(4)]
    output, token_grad, small_out, down_out, gate_up_out, attn_out = take(6)
    wgu, wd, wqkv, wout = take(4)
    hs, h1s, qkvs, os, lses = take(5)
    ysend, yrecv, gs, gm, ab, hid, dgu = take(7)
    oth_g, oth_s, cr_d, cr_g, cr_a = take(5)
    os_d, os_g, os_a, ok_d, ok_g, ok_a = take(6)
    xr_d, xr_g, xr_a, z1_d, z1_g, z1_a, z2_d, z2_g, z2_a, small = take(10)
    load_sem, ys_sem, yr_sem, cs_sem, cr_sem, xs_sem, xr_sem = take(7)
    z1s, z1r, z2s, z2r, z3s, z3r, store_sem, row_sem, rows_s, rows_r, small_s, small_r = take(12)
    x_free, z1_free, z2_free = take(3)

    tp = lax.axis_index("tp")
    x = lax.axis_index("dpi")
    z = lax.axis_index("dpo")
    core = lax.rem(tp, 2)
    to_core = {"tp": tp + 1 - 2 * core}
    to_chip = {"tp": lax.rem(tp + 2, 4)}
    to_x = {"dpi": 1 - x}
    to_mate = {"dpo": z + 1 - 2 * lax.rem(z, 2)}
    to_inner = {"dpo": 3 - z}
    outer = (z == 0) | (z == 3)
    inner = (z == 1) | (z == 2)
    far = [{"dpo": lax.rem(z + k, 4)} for k in (1, 2, 3)]

    barrier = pltpu.get_barrier_semaphore()
    for peer in [to_core, to_chip, to_x] + far:
        pl.semaphore_signal(barrier, inc=1, device_id=peer, device_id_type=MESH)
    loads = {}

    def load(key, src, dst, slot):
        copy = pltpu.make_async_copy(src, dst, load_sem.at[slot])
        copy.start()
        loads[key] = copy

    def need(*keys):
        for key in keys:
            if key in loads:
                loads.pop(key).wait()

    def rows(c):
        return pl.ds(c * n, n)

    def load_ffn_weights(l):
        load("wgu", wgu_in[l], wgu, 0)
        load("wd", wd_in[l], wd, 1)

    def load_attn_weights(l):
        load("wqkv", wqkv_in[l], wqkv, 2)
        load("wout", wout_in[l], wout, 3)

    def load_h1(l, c):
        load(("h1", c), h1_in[l][c], h1s.at[c], 4 + c)

    def load_qkv(l, c):
        load(("qkv", c), qkv_in[l][c], qkvs.at[c], 6 + c)
        load(("lse", c), lse_in[l][c], lses.at[c], 8 + c)

    def load_o(l, c):
        load(("o", c), o_in[l][c], os.at[rows(c)], 10 + c)

    def load_h(l, c):
        load(("h", c), h_in[l][c], hs.at[c], 12 + c)

    top = layers - 1
    for c in range(chunks):
        load_h1(top, c)
        load(("cot", c), cot_in[c], gm.at[rows(c)], 14 + c)
    load_ffn_weights(top)
    load_attn_weights(top)
    for c in range(chunks):
        load_qkv(top, c)
        load_h(top, c)
        load_o(top, c)
    pl.semaphore_wait(barrier, 6)

    def remote(src, dst, send, recv, to):
        return pltpu.make_async_remote_copy(
            src_ref=src, dst_ref=dst, send_sem=send, recv_sem=recv, device_id=to, device_id_type=MESH
        )

    turn = [0] * chunks

    def y_copy(c, k):
        return remote(ysend.at[c], yrecv.at[k % 2, c], ys_sem.at[c], yr_sem.at[k % 2, c], to_chip)

    def y_start(c):
        y_copy(c, turn[c]).start()

    def y_sum(c):
        copy = y_copy(c, turn[c])
        copy.wait()
        got = ysend[c] + yrecv[turn[c] % 2, c]
        turn[c] += 1
        return got

    def gain_of(l, i):
        k = 2 * l + i
        return gains_ref[k : k + 1, :]

    def add_gain(l, i, c, term):
        k = 2 + 2 * l + i
        spot = (z, x, core, slice(k, k + 1), slice(None))
        small[spot] = term if c == 0 else small[spot] + term

    def close(l, i, c, g, h):
        grad = y_sum(c)
        scale = inv_rms(h)
        normed = h * scale
        add_gain(l, i, c, jnp.sum(grad * normed, axis=0, keepdims=True))
        return g + norm_back(grad, normed, scale, gain_of(l, i))

    small[z, x, core] = block_ref[...]

    def ffn(l, c):
        spot = rows(c)
        if l == top:
            need(("cot", c))
            gs[c] = gm[spot, :].astype(F32)
        else:
            need(("h", c))
            g = close(l + 1, 0, c, gs[c], hs[c])
            gs[c] = g
            gm[spot, :] = g.astype(BF16)
            load_h(l, c)
        need(("h1", c), "wgu", "wd")
        h1 = h1s[c]
        b = (h1 * inv_rms(h1) * gain_of(l, 1)).astype(BF16)
        ab[spot, :] = b
        step = min(wf, 256)
        for f in range(0, wf, step):
            gate = mm(b, wgu[0, :, f : f + step])
            up = mm(b, wgu[1, :, f : f + step])
            dhid = mm(gm[spot, :], wd[f : f + step, :], NT)
            sig = jax.nn.sigmoid(gate)
            silu = gate * sig
            hid[spot, f : f + step] = (silu * up).astype(BF16)
            dgu[spot, f : f + step] = (dhid * up * (sig * (1.0 + gate * (1.0 - sig)))).astype(BF16)
            dgu[spot, wf + f : wf + f + step] = (dhid * silu).astype(BF16)
        ysend[c] = mm(dgu[spot, :wf], wgu[0], NT) + mm(dgu[spot, wf:], wgu[1], NT)
        y_start(c)

    def attn(l, c):
        spot = rows(c)
        g1 = close(l, 1, c, gs[c], h1s[c])
        gs[c] = g1
        if l > 0:
            load_h1(l - 1, c)
        gm[spot, :] = g1.astype(BF16)
        need("wqkv", "wout", ("qkv", c), ("lse", c))
        lane = lax.broadcasted_iota(jnp.int32, (n, 2 * HD), 1)
        low_half = lane < HD
        zero = jnp.zeros((n, 2 * HD), BF16)
        mask = key_mask(open_ref.at[c], n)
        ga = gm[spot, :]
        for t in range(wa // (2 * HD)):
            spots = [slice(s * wa + t * 2 * HD, s * wa + (t + 1) * 2 * HD) for s in range(3)]
            q, k, v = [qkvs[c, :, s] for s in spots]
            dout = mm(ga, wout[t * 2 * HD : (t + 1) * 2 * HD, :], NT).astype(BF16)
            dq, dk, dv = [], [], []
            for e in range(2):
                mine = low_half if e == 0 else ~low_half
                s = jnp.where(mask, mm(k, jnp.where(mine, q, zero), NT), LOW)
                prob = jnp.exp(s - lses[c, 2 * t + e : 2 * t + e + 1, :])
                dprob = mm(v, jnp.where(mine, dout, zero), NT)
                delta = jnp.sum(prob * dprob, axis=0, keepdims=True)
                ds = (prob * (dprob - delta)).astype(BF16)
                dv.append(mm(prob.astype(BF16), dout))
                dk.append(mm(ds, q))
                dq.append(mm(ds, k, TN))
            dq = jnp.where(low_half, dq[0], dq[1]) * HD ** (-0.5)
            dk = jnp.where(low_half, dk[0], dk[1])
            dv = jnp.where(low_half, dv[0], dv[1])
            dgu[spot, spots[0]] = rotate(dq, tables, -1).astype(BF16)
            dgu[spot, spots[1]] = rotate(dk, tables, -1).astype(BF16)
            dgu[spot, spots[2]] = dv.astype(BF16)
        ysend[c] = mm(dgu[spot, : 3 * wa], wqkv[...])
        y_start(c)
        if l > 0:
            load_qkv(l - 1, c)
        need(("h", c))
        h = hs[c]
        ab[spot, :] = (h * inv_rms(h) * gain_of(l, 0)).astype(BF16)

    spans = [pl.ds(pl.multiple_of((1 - x) * half, half), half), pl.ds(pl.multiple_of(x * half, half), half)]
    kinds = {
        "d": (oth_s.at[:, pl.ds(0, lf)], cr_d, os_d, ok_d, xr_d, z1_d, z2_d, down_out, [(0, lf)]),
        "g": (oth_g, cr_g, os_g, ok_g, xr_g, z1_g, z2_g, gate_up_out, [(0, half // 2), (half // 2, half // 2)]),
        "a": (oth_s, cr_a, os_a, ok_a, xr_a, z1_a, z2_a, attn_out, [(i * la, la) for i in range(4)]),
    }
    first_unit = {"d": 0, "g": 1, "a": 3}
    index = {"d": 0, "g": 1, "a": 2}

    def c_copy(kind):
        at = index[kind]
        return remote(kinds[kind][0], kinds[kind][1], cs_sem.at[at], cr_sem.at[at], to_core)

    def piece(kind, s, shard, put):
        if kind == "d":
            put(slice(None), slice(None), mm(hid[:, shard * lf : (shard + 1) * lf], gm[:, spans[s]], TN))
        elif kind == "g":
            for t in range(2):
                cols = slice(t * wf + shard * lf, t * wf + (shard + 1) * lf)
                put(slice(None), slice(t * lf, (t + 1) * lf), mm(ab[:, spans[s]], dgu[:, cols], TN))
        else:
            put(slice(0, la), slice(None), mm(os[:, shard * la : (shard + 1) * la], gm[:, spans[s]], TN))
            for t in range(3):
                cols = slice(t * wa + shard * la, t * wa + (shard + 1) * la)
                put(slice((t + 1) * la, (t + 2) * la), slice(None), mm(dgu[:, cols], ab[:, spans[s]], TN))

    def put_in(ref, *lead):
        def put(r, c, value):
            ref[lead + (r, c)] = value

        return put

    def grad_other(kind):
        for s in range(2):
            piece(kind, s, 1, put_in(kinds[kind][0], s))
        c_copy(kind).start()

    def grad_own(l, kind):
        piece(kind, 0, 0, put_in(kinds[kind][2]))
        piece(kind, 1, 0, put_in(kinds[kind][3], l))

    def units(kind):
        for i, (at, size) in enumerate(kinds[kind][8]):
            yield first_unit[kind] + i, pl.ds(at, size)

    def x_copy(l, kind, u, spot):
        return remote(kinds[kind][2].at[spot], kinds[kind][4].at[spot], xs_sem.at[l, u], xr_sem.at[l, u], to_x)

    def core_sum(l, kind):
        _, cr, own_s, own_k, *_ = kinds[kind]
        c_copy(kind).wait()
        for u, spot in units(kind):
            own_s[spot, :] = own_s[spot, :] + cr[0, spot, :]
            if l < top:
                pl.semaphore_wait(x_free.at[u], 1)
            x_copy(l, kind, u, spot).start()
        own_k[l] = own_k[l] + cr[1]

    def unit(u):
        for kind in kinds:
            for v, spot in units(kind):
                if v == u:
                    return kind, spot

    def z1_copy(l, u):
        kind, spot = unit(u)
        return remote(kinds[kind][3].at[l, spot], kinds[kind][5].at[spot], z1s.at[l, u], z1r.at[l, u], to_mate)

    def z2_copy(l, u):
        kind, spot = unit(u)
        return remote(kinds[kind][3].at[l, spot], kinds[kind][6].at[spot], z2s.at[l, u], z2r.at[l, u], to_inner)

    def z3_copy(l, u):
        kind, spot = unit(u)
        return remote(kinds[kind][6].at[spot], kinds[kind][7].at[l, spot], z3s.at[l, u], z3r.at[l, u], to_mate)

    def store_copy(l, u):
        kind, spot = unit(u)
        return pltpu.make_async_copy(kinds[kind][6].at[spot], kinds[kind][7].at[l, spot], store_sem.at[l, u])

    def x_sum(l, u):
        kind, spot = unit(u)
        keep, got = kinds[kind][3], kinds[kind][4]
        x_copy(l, kind, u, spot).wait()
        keep[l, spot, :] = keep[l, spot, :] + got[spot, :]
        if l > 0:
            pl.semaphore_signal(x_free.at[u], inc=1, device_id=to_x, device_id_type=MESH)

        @pl.when(outer)
        def _():
            if l < top:
                pl.semaphore_wait(z1_free.at[u], 1)
            z1_copy(l, u).start()

    def z_one(l, u):
        kind, spot = unit(u)
        keep, got = kinds[kind][3], kinds[kind][5]

        @pl.when(inner)
        def _():
            z1_copy(l, u).wait_recv()
            keep[l, spot, :] = keep[l, spot, :] + got[spot, :]
            if l > 0:
                pl.semaphore_signal(z1_free.at[u], inc=1, device_id=to_mate, device_id_type=MESH)
            if l < top:
                pl.semaphore_wait(z2_free.at[u], 1)
            z2_copy(l, u).start()

    def z_two(l, u):
        kind, spot = unit(u)
        keep, got = kinds[kind][3], kinds[kind][6]

        @pl.when(inner)
        def _():
            z2_copy(l, u).wait()
            got[spot, :] = got[spot, :] + keep[l, spot, :]
            z3_copy(l, u).start()
            store_copy(l, u).start()

    def z_end(l, u):
        @pl.when(inner)
        def _():
            z3_copy(l, u).wait_send()
            store_copy(l, u).wait()
            if l > 0:
                pl.semaphore_signal(z2_free.at[u], inc=1, device_id=to_inner, device_id_type=MESH)

        @pl.when(outer)
        def _():
            z1_copy(l, u).wait_send()
            z3_copy(l, u).wait_recv()

    def row_copies(src, dst, i, c):
        spot = pl.ds(pl.multiple_of((core * chunks + c) * n, n), n)
        return (
            pltpu.make_async_copy(src, dst.at[spot], row_sem.at[i, c]),
            remote(src, dst.at[spot], rows_s.at[i, c], rows_r.at[i, c], to_core),
        )

    def share_rows(src, dst, i, c):
        for copy in row_copies(src, dst, i, c):
            copy.start()

    def end_rows(src, dst, i, c):
        for copy in row_copies(src, dst, i, c):
            copy.wait()

    def token(c):
        need(("h", c))
        g = close(0, 0, c, gs[c], hs[c])
        small[z, x, core, c : c + 1, :] = g[0:1, :]
        row = lax.broadcasted_iota(jnp.int32, (n, dim), 0)
        gs[c] = jnp.where(row == 0, 0.0, g)
        share_rows(gs.at[c], token_grad, 0, c)

    def pout_copy(c):
        k = turn[c] % 2
        return remote(pout_in[c], yrecv.at[k, c], ys_sem.at[c], yr_sem.at[k, c], to_chip)

    def start_output(c):
        pout_copy(c).start()
        load(("pout", c), pout_in[c], ysend.at[c], 4 + c)
        load(("out", c), h1_in[top][c], hs.at[c], 12 + c)

    def end_output(c):
        need(("pout", c), ("out", c))
        pout_copy(c).wait()
        hs[c] = hs[c] + (ysend[c] + yrecv[turn[c] % 2, c])
        share_rows(hs.at[c], output, 1, c)

    def small_core():
        return remote(small.at[z, x, core], small.at[z, x, core], small_s.at[0], small_r.at[0], to_core)

    def small_x():
        return remote(small.at[z, x], small.at[z, x], small_s.at[1], small_r.at[1], to_x)

    def small_z(k):
        return remote(small.at[z], small.at[z], small_s.at[2 + k], small_r.at[2 + k], far[k])

    def small_got(k):
        back = lax.rem(z + 3 - k, 4)
        return remote(small.at[back], small.at[back], small_s.at[2 + k], small_r.at[2 + k], far[k])

    ffn(1, 0)
    ffn(1, 1)
    load_ffn_weights(0)
    grad_other("d")
    grad_own(1, "d")
    grad_other("g")
    core_sum(1, "d")
    grad_own(1, "g")
    core_sum(1, "g")
    attn(1, 0)
    attn(1, 1)
    load_attn_weights(0)
    need(("o", 0), ("o", 1))
    grad_other("a")
    grad_own(1, "a")
    for c in range(chunks):
        load_o(0, c)
    x_sum(1, 0)
    core_sum(1, "a")
    ffn(0, 0)
    x_sum(1, 1)
    z_one(1, 0)
    ffn(0, 1)
    grad_other("d")
    grad_own(0, "d")
    x_sum(1, 2)
    grad_other("g")
    z_two(1, 0)
    core_sum(0, "d")
    grad_own(0, "g")
    core_sum(0, "g")
    attn(0, 0)
    z_one(1, 1)
    for u in (3, 4, 5, 6):
        x_sum(1, u)
    z_end(1, 0)
    attn(0, 1)
    need(("o", 0), ("o", 1))
    grad_other("a")
    grad_own(0, "a")
    z_one(1, 2)
    z_two(1, 1)
    core_sum(0, "a")
    x_sum(0, 0)
    token(0)
    start_output(0)
    for u in (3, 4, 5, 6):
        z_one(1, u)
    z_two(1, 2)
    z_end(1, 1)
    z_one(0, 0)
    x_sum(0, 1)
    token(1)
    start_output(1)
    small_core().start()
    for u in (3, 4, 5, 6):
        z_two(1, u)
    z_end(1, 2)
    small_core().wait_send()
    remote(
        small.at[z, x, 1 - core], small.at[z, x, 1 - core], small_s.at[0], small_r.at[0], to_core
    ).wait_recv()
    small_x().start()
    z_two(0, 0)
    z_one(0, 1)
    x_sum(0, 2)
    for u in (3, 4, 5, 6):
        z_end(1, u)
    end_rows(gs.at[0], token_grad, 0, 0)
    end_rows(gs.at[1], token_grad, 0, 1)
    end_output(0)
    z_end(0, 0)
    z_two(0, 1)
    x_sum(0, 3)
    z_one(0, 2)
    x_sum(0, 4)
    x_sum(0, 5)
    z_one(0, 3)
    x_sum(0, 6)
    z_two(0, 2)
    z_one(0, 4)
    end_output(1)
    small_x().wait_send()
    remote(small.at[z, 1 - x], small.at[z, 1 - x], small_s.at[1], small_r.at[1], to_x).wait_recv()
    for k in range(3):
        small_z(k).start()
    z_two(0, 3)
    z_one(0, 5)
    z_two(0, 4)
    z_one(0, 6)
    z_two(0, 5)
    z_two(0, 6)
    for k in range(3):
        small_z(k).wait_send()
        small_got(k).wait_recv()
    store = pltpu.make_async_copy(small, small_out, load_sem.at[16])
    store.start()
    end_rows(hs.at[0], output, 1, 0)
    end_rows(hs.at[1], output, 1, 1)
    for u in range(1, 7):
        z_end(0, u)
    store.wait()


def call(body, outs, args, flops, limit=40, smem=0, scratch=()):
    moved = sum(x.size * x.dtype.itemsize for x in args) + sum(
        int(np.prod(s)) * np.dtype(d).itemsize for s, d in outs
    )
    spec = pl.BlockSpec(memory_space=pltpu.VMEM)
    got = pl.pallas_call(
        body,
        out_shape=[jax.ShapeDtypeStruct(s, d) for s, d in outs],
        in_specs=[pl.BlockSpec(memory_space=pltpu.SMEM)] * smem + [spec] * (len(args) - smem),
        out_specs=[spec] * len(outs),
        scratch_shapes=list(scratch),
        compiler_params=pltpu.CompilerParams(vmem_limit_bytes=limit * 2**20),
        cost_estimate=pl.CostEstimate(flops=int(flops), bytes_accessed=int(moved), transcendentals=0),
    )(*args)
    return list(got)


def call_backward(sizes, n, dim, wa, wf, layers, chunks, fixed, lists):
    la, lf, half = wa // 2, wf // 2, dim // 2
    groups = sizes["dpo"], sizes["dpi"]
    outs = [
        (2 * chunks * n, dim),
        (2 * chunks * n, dim),
        groups + (2, 8, dim),
        (layers, lf, half),
        (layers, half, 2 * lf),
        (layers, 4 * la, half),
    ]
    d, g, a = (lf, half), (half, 2 * lf), (4 * la, half)
    f, h = lambda *s: pltpu.VMEM(s, F32), lambda *s: pltpu.VMEM(s, BF16)
    dma, count = pltpu.SemaphoreType.DMA, pltpu.SemaphoreType.REGULAR
    scratch = [h(2, dim, wf), h(wf, dim), h(3 * wa, dim), h(wa, dim)]
    scratch += [f(chunks, n, dim), f(chunks, n, dim), h(chunks, n, 3 * wa), h(chunks * n, wa), f(chunks, 8, n)]
    scratch += [f(chunks, n, dim), f(2, chunks, n, dim), f(chunks, n, dim)]
    scratch += [h(chunks * n, dim), h(chunks * n, dim), h(chunks * n, wf), h(chunks * n, 2 * wf)]
    scratch += [f(2, *g), f(2, *a)] + [f(2, *k) for k in (d, g, a)]
    scratch += [f(*k) for k in (d, g, a)] + [f(layers, *k) for k in (d, g, a)]
    scratch += [f(*k) for _ in range(3) for k in (d, g, a)] + [f(*groups, 2, 8, dim)]
    scratch += [dma((17,)), dma((chunks,)), dma((2, chunks)), dma((3,)), dma((3,))]
    scratch += [dma((layers, 7))] * 9 + [dma((2, chunks))] * 3 + [dma((5,))] * 2 + [count((7,))] * 3
    args = list(fixed) + [x for group in lists for x in group]
    flops = layers * chunks * n * (2 * dim * (10 * wa + 9 * wf) + 24 * n * wa)
    vmem, anywhere = pl.BlockSpec(memory_space=pltpu.VMEM), pl.BlockSpec(memory_space=pl.ANY)
    return pl.pallas_call(
        functools.partial(backward, sizes, (n, dim, wa, wf, layers, chunks)),
        out_shape=[jax.ShapeDtypeStruct(s, F32) for s in outs],
        in_specs=[vmem] * len(fixed) + [anywhere] * (len(args) - len(fixed)),
        out_specs=[anywhere] * len(outs),
        scratch_shapes=scratch,
        compiler_params=pltpu.CompilerParams(
            vmem_limit_bytes=62 * 2**20, collective_id=0, has_side_effects=True
        ),
        cost_estimate=pl.CostEstimate(flops=flops, bytes_accessed=60 * 10**6, transcendentals=0),
    )(*args)


def on_device(sizes, tokens, cotangent, heights, labels, valid, class_table, gains, w_qkv, w_out, w_gate_up, w_down):
    seq_count = heights.shape[0]
    row_count, dim = tokens.shape
    n = row_count // seq_count
    layers = gains.shape[0]
    classes = class_table.shape[0]
    la = w_out.shape[1]
    lf = w_down.shape[1]
    wa, wf = 2 * la, 2 * lf
    tp, dpo, dpi = sizes["tp"], sizes["dpo"], sizes["dpi"]
    mine = seq_count // 2
    lean = (tp, dpo, dpi) == (4, 4, 2) and (mine, layers) == (2, 2)
    core = lax.rem(lax.axis_index("tp"), 2)
    z = lax.axis_index("dpo")
    swap_core = [(i, i ^ 1) for i in range(tp)]

    def core_swap(x):
        return lax.ppermute(x, "tp", swap_core)

    def sum_chips(part):
        total = None
        for step in range(2, tp, 2):
            got = lax.ppermute(part, "tp", [(i, i ^ step) for i in range(tp)])
            total = got if total is None else total + got
        return total

    wqkv, wout, wgu, wd = [], [], [], []
    for l in range(layers):
        for into, w in (
            (wqkv, jnp.transpose(w_qkv[l], (1, 2, 0))),
            (wout, w_out[l][None]),
            (wgu, jnp.transpose(w_gate_up[l], (1, 0, 2))),
            (wd, w_down[l][None]),
        ):
            wide = w.astype(F32)
            axis = 2 if into is wgu else 1
            shape = list(w.shape)
            shape[axis] *= 2
            into.append(call(functools.partial(merge, axis), [(tuple(shape), BF16)], (wide, core_swap(wide)), 1000)[0])
        wqkv[l] = wqkv[l].reshape(3 * wa, dim)
        wout[l] = wout[l][0]
        wd[l] = wd[l][0]

    tables = jnp.asarray(rope_constants(n))
    position = jnp.arange(n)
    own = lambda x: lax.dynamic_slice_in_dim(x, core * mine, mine, 0)
    open_key = (position[None, :] < 1 + COLS * own(heights)[:, None]) & (own(valid.reshape(seq_count, n)) == 1)
    open_key = open_key.astype(F32)[:, :, None]
    own_labels = own(labels)
    token_own = own(tokens.reshape(seq_count, n, dim))
    cot_own = own(cotangent.reshape(seq_count, n, dim))
    chunks = range(mine)
    hs = []
    for c in chunks:
        row = lax.dynamic_slice_in_dim(class_table, own_labels[c], 1, 0)
        hs.append(jnp.where((position == 0)[:, None], row, token_own[c]).astype(F32))

    shape_d = ((n, dim), F32)
    shape_b = ((n, dim), BF16)
    flops_a = 2 * n * dim * 4 * wa + 8 * n * n * wa
    flops_f = 2 * n * dim * 3 * wf

    kept = []
    state = [(hs[c],) for c in chunks]
    parts = None
    for l in range(layers):
        keep = [dict() for _ in chunks]
        for c in chunks:
            args = state[c] + (gains[l, 0][None], wqkv[l], wout[l], tables, open_key[c])
            outs = [((n, 3 * wa), BF16), ((max(8, wa // HD), n), F32), ((n, wa), BF16), shape_d]
            outs = ([shape_d] if l > 0 else []) + ([] if lean else [shape_b]) + outs
            got = call(functools.partial(attn_fwd, l == 0, lean), outs, args, flops_a)
            h = state[c][0] if l == 0 else got.pop(0)
            if not lean:
                keep[c]["a"] = got.pop(0)
            qkv, lse, o, part = got
            keep[c].update(h=h, qkv=qkv, lse=lse, o=o)
            state[c] = (h, part, sum_chips(part))
        for c in chunks:
            args = state[c] + (gains[l, 1][None], wgu[l], wd[l])
            hid_shape = ((n, wf), BF16)
            if lean:
                h1, part = call(
                    functools.partial(ffn_fwd, True), [shape_d] * 2, args, flops_f, scratch=[pltpu.VMEM(*hid_shape)]
                )
                keep[c].update(h1=h1, part=part)
            else:
                outs = [shape_d, shape_b, ((n, 2 * wf), F32), hid_shape, shape_d]
                h1, b, gu, hid, part = call(functools.partial(ffn_fwd, False), outs, args, flops_f)
                keep[c].update(h1=h1, b=b, gu=gu, hid=hid)
            if not (lean and l == layers - 1):
                state[c] = (h1, part, sum_chips(part))
        kept.append(keep)

    if lean:
        block = jnp.zeros((8, dim), F32)
        block = lax.dynamic_update_slice(block, own_labels.astype(F32)[None], (6, 0))
        lists = [[cot_own[c] for c in chunks], [kept[-1][c]["part"] for c in chunks]]
        for name in ("h", "h1", "qkv", "lse", "o"):
            lists += [[kept[l][c][name] for c in chunks] for l in range(layers)]
        lists += [wgu, wd, wqkv, wout]
        fixed = (gains.reshape(2 * layers, dim), tables, open_key, block)
        got = call_backward(sizes, n, dim, wa, wf, layers, mine, fixed, lists)
        output, token_grad, small, down_part, gate_up_part, attn_part = got
        gain_total = jnp.sum(small[..., 2 : 2 + 2 * layers, :], axis=(0, 1, 2)).reshape(layers, 2, dim)
        rows = small[..., :mine, :].reshape(-1, dim)
        all_labels = jnp.round(small[..., 6, :mine]).astype(jnp.int32).reshape(-1)
        half = dim // dpi
        rows = lax.dynamic_slice(rows, (0, lax.axis_index("dpi") * half), (rows.shape[0], half))
        onehot = (all_labels[None, :] == jnp.arange(classes)[:, None]).astype(F32)
        return (
            output,
            token_grad,
            jnp.dot(onehot, rows, precision=lax.Precision.HIGHEST),
            gain_total,
            attn_part[:, la:].reshape(layers, 3, la, half).transpose(0, 3, 1, 2),
            attn_part[:, :la],
            gate_up_part.reshape(layers, half, 2, lf),
            down_part,
        )

    output = jnp.concatenate([s[0] + (s[1] + s[2]) for s in state], axis=0)

    half = lax.axis_index("dpi") if dpi == 2 else 1
    order = jnp.stack([jnp.int32(1) - half, jnp.int32(half)])

    def dp_sum(both, other, axis):
        got = core_swap(other)
        if dpi == 2:
            sent = lax.ppermute(both[0] + got[0], "dpi", [(0, 1), (1, 0)])
            total = (both[1] + got[1]) + sent
        else:
            both = both + got
            whole = jnp.concatenate([both[0], both[1]], axis=axis)
            total = lax.psum_scatter(whole, "dpi", scatter_dimension=axis, tiled=True)
        return line_sum(total)

    def line_sum(x):
        if dpo != 4:
            return lax.psum(x, "dpo")
        got = lax.ppermute(x, "dpo", [(0, 1), (3, 2)])
        x = x + got
        got = lax.ppermute(x, "dpo", [(1, 2), (2, 1)])
        x = x + got
        got = lax.ppermute(x, "dpo", [(1, 0), (2, 3)])
        return jnp.where((z == 0) | (z == dpo - 1), got, x)

    gain_rows = [[None, None] for _ in range(layers)]
    grads = [None] * layers
    state = [None] * mine
    for l in reversed(range(layers)):
        top = l == layers - 1
        keep = kept[l]
        gms = []
        for c in chunks:
            outs = [((n, 2 * wf), BF16), shape_d]
            args = (keep[c]["gu"], wgu[l], wd[l])
            if top:
                g = cot_own[c]
                dgu, part = call(functools.partial(ffn_bwd, True), outs, (g,) + args, flops_f)
                gms.append(g)
            else:
                outs = [shape_d, ((1, dim), F32), shape_b] + outs
                args = state[c] + args
                g, gain_c, gm, dgu, part = call(functools.partial(ffn_bwd, False), outs, args, flops_f)
                gain_rows[l + 1][0] = gain_c if c == 0 else gain_rows[l + 1][0] + gain_c
                gms.append(gm)
            keep[c]["dgu"] = dgu
            state[c] = (g, part, sum_chips(part), keep[c]["h1"], gains[l, 1][None])
        flops_w = 2 * n * mine * dim * wf
        outs = [((2, lf, dim // 2), F32)] * 2
        args = [order] + [keep[c]["hid"] for c in chunks] + gms
        spans = (((0, lf),), ((lf, wf),))
        down = call(functools.partial(grad_rows, spans), outs, args, flops_w, smem=1)
        outs = [((2, dim // 2, 2 * lf), F32)] * 2
        args = [order] + [keep[c]["b"] for c in chunks] + [keep[c]["dgu"] for c in chunks]
        spans = (((0, lf), (wf, wf + lf)), ((lf, wf), (wf + lf, 2 * wf)))
        gate_up = call(functools.partial(grad_columns, spans), outs, args, 2 * flops_w, smem=1)
        down = dp_sum(*down, 1)
        gate_up = dp_sum(*gate_up, 0)
        gas = []
        for c in chunks:
            outs = [shape_d, ((1, dim), F32), shape_b, ((n, 3 * wa), BF16), shape_d]
            args = state[c] + (wqkv[l], wout[l], tables, open_key[c], keep[c]["qkv"], keep[c]["lse"])
            g1, gain_c, ga, dqkv, part = call(attn_bwd, outs, args, flops_a + 12 * n * n * wa)
            gain_rows[l][1] = gain_c if c == 0 else gain_rows[l][1] + gain_c
            gas.append(ga)
            keep[c]["dqkv"] = dqkv
            state[c] = (g1, part, sum_chips(part), keep[c]["h"], gains[l, 0][None])
        flops_w = 2 * n * mine * dim * wa
        outs = [((2, la, dim // 2), F32)] * 2
        args = [order] + [keep[c]["o"] for c in chunks] + gas
        spans = (((0, la),), ((la, wa),))
        out = call(functools.partial(grad_rows, spans), outs, args, flops_w, smem=1)
        outs = [((2, 3 * la, dim // 2), F32)] * 2
        args = [order] + [keep[c]["dqkv"] for c in chunks] + [keep[c]["a"] for c in chunks]
        spans = tuple(tuple((t * wa + s * la, t * wa + (s + 1) * la) for t in range(3)) for s in range(2))
        qkv = call(functools.partial(grad_rows, spans), outs, args, 3 * flops_w, smem=1)
        out = dp_sum(*out, 1)
        qkv = dp_sum(*qkv, 1)
        grads[l] = (qkv, out, gate_up, down)

    finals = []
    for c in chunks:
        g, gain_c = call(close_layer, [shape_d, ((1, dim), F32)], state[c], 1000)
        gain_rows[0][0] = gain_c if c == 0 else gain_rows[0][0] + gain_c
        finals.append(g)

    slot0 = lax.axis_index("dpo") * dpi + lax.axis_index("dpi")
    seqs = seq_count * dpo * dpi
    firsts = jnp.concatenate([g[0:1] for g in finals], axis=0)
    small = jnp.zeros((seqs + 2 * layers + 1, dim), F32)
    small = lax.dynamic_update_slice(small, firsts, (slot0 * seq_count + core * mine, 0))
    terms = jnp.concatenate([gain_rows[l][i] for l in range(layers) for i in range(2)], axis=0)
    small = lax.dynamic_update_slice(small, terms, (seqs, 0))
    label_row = lax.dynamic_update_slice(
        jnp.zeros((1, dim), F32), own_labels.astype(F32)[None], (0, slot0 * seq_count + core * mine)
    )
    small = lax.dynamic_update_slice(small, label_row, (seqs + 2 * layers, 0))
    small = jnp.where(lax.axis_index("tp") < 2, small, 0.0)
    small = lax.psum(small, ("dpo", "dpi", "tp"))
    all_labels = jnp.round(small[seqs + 2 * layers, :seqs]).astype(jnp.int32)
    gain_total = small[seqs : seqs + 2 * layers].reshape(layers, 2, dim)
    onehot = (all_labels[None, :] == jnp.arange(classes)[:, None]).astype(F32)
    share = dim // dpi
    rows = lax.dynamic_slice(small, (0, lax.axis_index("dpi") * share), (seqs, share))
    table_part = jnp.dot(onehot, rows, precision=lax.Precision.HIGHEST)

    token_own = jnp.concatenate([jnp.where((position == 0)[:, None], 0.0, g) for g in finals], axis=0)

    def both_cores(x):
        other = core_swap(x)
        return jnp.where(core == 0, jnp.concatenate([x, other], 0), jnp.concatenate([other, x], 0))

    qkv_part = jnp.stack([g[0].reshape(3, la, share) for g in grads]).transpose(0, 3, 1, 2)
    out_part = jnp.stack([g[1] for g in grads])
    gate_up_part = jnp.stack([g[2].reshape(share, 2, lf) for g in grads])
    down_part = jnp.stack([g[3] for g in grads])
    return (
        both_cores(output),
        both_cores(token_own),
        table_part,
        gain_total,
        qkv_part,
        out_part,
        gate_up_part,
        down_part,
    )


def solution(mesh):
    sizes = dict(mesh.shape)
    placed = (
        P(("dpo", "dpi"), None),
        P(("dpo", "dpi"), None),
        P(("dpo", "dpi")),
        P(("dpo", "dpi")),
        P(("dpo", "dpi")),
        P(),
        P(),
        P(None, None, None, "tp"),
        P(None, "tp", None),
        P(None, None, None, "tp"),
        P(None, "tp", None),
    )
    return jax.shard_map(
        functools.partial(on_device, sizes),
        mesh=mesh,
        in_specs=placed,
        out_specs=(
            P(("dpo", "dpi"), None),
            P(("dpo", "dpi"), None),
            P(None, "dpi"),
            P(),
            P(None, "dpi", None, "tp"),
            P(None, "tp", "dpi"),
            P(None, "dpi", None, "tp"),
            P(None, "tp", "dpi"),
        ),
        check_vma=False,
    )
```

```python
import functools

import jax
import jax.numpy as jnp
import numpy as np
from jax import lax
from jax.experimental import pallas as pl
from jax.experimental.pallas import tpu as pltpu
from jax.sharding import PartitionSpec as P

HD = 64
COLS = 16
EPS = 1e-05
F32 = jnp.float32
BF16 = jnp.bfloat16
LOW = -1e30
MESH = pl.DeviceIdType.MESH

PIECES = {"d": (128,) * 4, "g": (48,) * 8, "a": (192, 144, 144, 144, 144)}
ORDER = (
    ("ffn", 1, 0), ("ffn", 1, 1), ("go", 1, "d"), ("gw", 1, "g"), ("gw", 1, "d"), ("cu", 1, 1),
    ("go", 1, "g"), ("cu", 1, 0), ("cu", 1, 3), ("xs", 1, 1), ("attn", 1, 0), ("xs", 1, 0), ("cu", 1, 5),
    ("cu", 1, 4), ("z1", 1, 1), ("cu", 1, 2), ("cu", 1, 9), ("cu", 1, 6), ("z1", 1, 0), ("xs", 1, 3),
    ("z2", 1, 1), ("xs", 1, 5), ("cu", 1, 7), ("z1", 1, 3), ("z2", 1, 0), ("xs", 1, 4), ("z1", 1, 5),
    ("attn", 1, 1), ("z2", 1, 3), ("z2", 1, 5), ("cu", 1, 11), ("cu", 1, 8), ("ze", 1, 1), ("xs", 1, 2),
    ("cu", 1, 10), ("z1", 1, 4), ("go", 1, "a"), ("xs", 1, 9), ("z1", 1, 2), ("gw", 1, "a"), ("ze", 1, 0),
    ("xs", 1, 6), ("z2", 1, 4), ("ze", 1, 3), ("z1", 1, 9), ("xs", 1, 7), ("cu", 1, 12), ("cu", 1, 13),
    ("cu", 1, 14), ("xs", 1, 11), ("z2", 1, 2), ("z1", 1, 6), ("z2", 1, 9), ("z1", 1, 7), ("cu", 1, 16),
    ("cu", 1, 15), ("ffn", 0, 0), ("z2", 1, 6), ("xs", 1, 8), ("z1", 1, 11), ("xs", 1, 10), ("ze", 1, 2),
    ("z1", 1, 8), ("z2", 1, 7), ("z1", 1, 10), ("z2", 1, 11), ("xs", 1, 12), ("ffn", 0, 1), ("xs", 1, 13),
    ("z2", 1, 8), ("z1", 1, 12), ("gw", 0, "d"), ("z2", 1, 10), ("go", 0, "d"), ("xs", 1, 14), ("go", 0, "g"),
    ("z1", 1, 13), ("cu", 0, 1), ("ze", 1, 5), ("z2", 1, 12), ("cu", 0, 2), ("z1", 1, 14), ("ze", 1, 9),
    ("xs", 1, 16), ("ze", 1, 8), ("cu", 0, 0), ("gw", 0, "g"), ("z2", 1, 13), ("xs", 1, 15), ("cu", 0, 6),
    ("ze", 1, 6), ("cu", 0, 3), ("ze", 1, 10), ("cu", 0, 5), ("z1", 1, 16), ("xs", 0, 1), ("z2", 1, 14),
    ("z1", 1, 15), ("attn", 0, 0), ("z2", 1, 16), ("cu", 0, 4), ("xs", 0, 2), ("cu", 0, 7), ("ze", 1, 12),
    ("ze", 1, 7), ("z1", 0, 1), ("cu", 0, 9), ("cu", 0, 10), ("ze", 1, 4), ("xs", 0, 0), ("z2", 1, 15),
    ("cu", 0, 8), ("ze", 1, 14), ("xs", 0, 6), ("z1", 0, 2), ("z1", 0, 0), ("z2", 0, 1), ("attn", 0, 1),
    ("z1", 0, 6), ("z2", 0, 2), ("z2", 0, 0), ("ze", 1, 11), ("xs", 0, 3), ("cu", 0, 11), ("go", 0, "a"),
    ("xs", 0, 5), ("z1", 0, 3), ("z2", 0, 6), ("xs", 0, 4), ("ze", 0, 2), ("tok", 0), ("ze", 1, 13),
    ("xs", 0, 7), ("z1", 0, 5), ("so", 0), ("z1", 0, 4), ("ze", 0, 1), ("xs", 0, 9), ("z2", 0, 3),
    ("gw", 0, "a"), ("z1", 0, 7), ("z2", 0, 5), ("ze", 0, 6), ("z2", 0, 4), ("cu", 0, 12), ("cu", 0, 14),
    ("ze", 1, 15), ("xs", 0, 10), ("cu", 0, 16), ("z1", 0, 9), ("tok", 1), ("so", 1), ("z2", 0, 7),
    ("xs", 0, 8), ("xs", 0, 11), ("z1", 0, 10), ("z2", 0, 9), ("sc",), ("z1", 0, 8), ("z2", 0, 10),
    ("z1", 0, 11), ("ze", 0, 3), ("cu", 0, 13), ("ze", 0, 5), ("cu", 0, 15), ("xs", 0, 12), ("ze", 0, 7),
    ("xs", 0, 14), ("z2", 0, 8), ("z1", 0, 12), ("ze", 1, 16), ("ze", 0, 0), ("eo", 0), ("ze", 0, 4),
    ("z2", 0, 11), ("z1", 0, 14), ("xs", 0, 16), ("ze", 0, 9), ("sx",), ("z2", 0, 12), ("z1", 0, 16),
    ("ze", 0, 10), ("z2", 0, 14), ("xs", 0, 13), ("z1", 0, 13), ("z2", 0, 16), ("xs", 0, 15), ("z1", 0, 15),
    ("eo", 1), ("ze", 0, 8), ("ze", 0, 12), ("z2", 0, 13), ("ze", 0, 11), ("z2", 0, 15), ("sz",),
    ("ze", 0, 14), ("ze", 0, 15), ("ze", 0, 16), ("ze", 0, 13), ("sw",),
)

NN = (((1,), (0,)), ((), ()))
NT = (((1,), (1,)), ((), ()))
TN = (((0,), (0,)), ((), ()))


def mm(a, b, dims=NN):
    return lax.dot_general(a, b, dims, preferred_element_type=F32)


def rope_constants(slot_len):
    quarter = HD // 4
    raster = np.maximum(np.arange(slot_len) - 1, 0)
    row_pos = (raster // COLS).astype(np.float32)
    col_pos = (raster % COLS).astype(np.float32)
    frequency = (10000.0 ** (-np.arange(quarter).astype(np.float32) / quarter)).astype(np.float32)
    row_angle = row_pos[:, None] * frequency[None, :]
    col_angle = col_pos[:, None] * frequency[None, :]
    zero = np.zeros_like(row_angle)
    cos = np.concatenate([np.cos(row_angle)] * 2 + [np.cos(col_angle)] * 2, axis=1)
    first = np.concatenate([-np.sin(row_angle), zero, -np.sin(col_angle), zero], axis=1)
    second = np.concatenate([zero, np.sin(row_angle), zero, np.sin(col_angle)], axis=1)
    return np.stack([np.tile(t, (1, 2)) for t in (cos, first, second)]).astype(np.float32)


def rotate(x, table_ref, sign):
    quarter = HD // 4
    ahead = pltpu.roll(x, 2 * HD - quarter, 1) * table_ref[1]
    behind = pltpu.roll(x, quarter, 1) * table_ref[2]
    turned = ahead + behind
    return x * table_ref[0] + (turned if sign > 0 else -turned)


def merge(axis, mine_ref, other_ref, out_ref):
    size = mine_ref.shape[axis]
    if axis == 1:
        out_ref[:, :size, :] = mine_ref[...].astype(BF16)
        out_ref[:, size:, :] = other_ref[...].astype(BF16)
    else:
        out_ref[:, :, :size] = mine_ref[...].astype(BF16)
        out_ref[:, :, size:] = other_ref[...].astype(BF16)


def inv_rms(h):
    return lax.rsqrt(jnp.mean(h * h, axis=-1, keepdims=True) + EPS)


def norm_back(grad, normed, scale, gain):
    scaled = grad * gain
    return scale * (scaled - normed * jnp.mean(scaled * normed, axis=-1, keepdims=True))


def key_mask(open_ref, n):
    key = lax.broadcasted_iota(jnp.int32, (n, n), 0)
    query = lax.broadcasted_iota(jnp.int32, (n, n), 1)
    return ((key < query) & (open_ref[...] > 0.5)) | (key == query)


def attn_fwd(first, *refs):
    if first:
        h_ref, gain_ref, wqkv_ref, wout_ref, table_ref, open_ref = refs[:6]
        refs = refs[6:]
        h = h_ref[...]
    else:
        h_ref, p_ref, r_ref, gain_ref, wqkv_ref, wout_ref, table_ref, open_ref = refs[:8]
        refs = refs[8:]
        h = h_ref[...] + (p_ref[...] + r_ref[...])
        refs[0][...] = h
        refs = refs[1:]
    a_ref, qkv_ref, lse_ref, o_ref, part_ref = refs
    n = h.shape[0]
    width = wout_ref.shape[0]
    a = (h * inv_rms(h) * gain_ref[...]).astype(BF16)
    a_ref[...] = a
    lane = lax.broadcasted_iota(jnp.int32, (n, 2 * HD), 1)
    low_half = lane < HD
    zero = jnp.zeros((n, 2 * HD), BF16)
    mask = key_mask(open_ref, n)
    for t in range(width // (2 * HD)):
        spots = [slice(s * width + t * 2 * HD, s * width + (t + 1) * 2 * HD) for s in range(3)]
        q = rotate(mm(a, wqkv_ref[spots[0], :], NT), table_ref, 1)
        q = (q * HD ** (-0.5)).astype(BF16)
        k = rotate(mm(a, wqkv_ref[spots[1], :], NT), table_ref, 1).astype(BF16)
        v = mm(a, wqkv_ref[spots[2], :], NT).astype(BF16)
        qkv_ref[:, spots[0]] = q
        qkv_ref[:, spots[1]] = k
        qkv_ref[:, spots[2]] = v
        mixed = []
        for e in range(2):
            q_one = jnp.where(low_half if e == 0 else ~low_half, q, zero)
            s = jnp.where(mask, mm(k, q_one, NT), LOW)
            top = jnp.max(s, axis=0, keepdims=True)
            raised = jnp.exp(s - top)
            total = jnp.sum(raised, axis=0, keepdims=True)
            lse_ref[2 * t + e : 2 * t + e + 1, :] = top + jnp.log(total)
            prob = (raised / total).astype(BF16)
            mixed.append(mm(prob, v, TN))
        o_ref[:, t * 2 * HD : (t + 1) * 2 * HD] = jnp.where(low_half, mixed[0], mixed[1]).astype(BF16)
    part_ref[...] = mm(o_ref[...], wout_ref[...])


def ffn_fwd(h_ref, p_ref, r_ref, gain_ref, wgu_ref, wd_ref, h1_ref, *refs):
    h = h_ref[...] + (p_ref[...] + r_ref[...])
    h1_ref[...] = h
    b = (h * inv_rms(h) * gain_ref[...]).astype(BF16)
    b_ref, gu_ref, hid_ref, part_ref = refs
    b_ref[...] = b
    width = wd_ref.shape[0]
    step = min(width, 256)
    for f in range(0, width, step):
        gate = mm(b, wgu_ref[0, :, f : f + step])
        up = mm(b, wgu_ref[1, :, f : f + step])
        gu_ref[:, f : f + step] = gate
        gu_ref[:, width + f : width + f + step] = up
        hid_ref[:, f : f + step] = (gate * jax.nn.sigmoid(gate) * up).astype(BF16)
    part_ref[...] = mm(hid_ref[...], wd_ref[...])


def ffn_bwd(first, *refs):
    if first:
        g_ref, gu_ref, wgu_ref, wd_ref = refs[:4]
        refs = refs[4:]
        gm = g_ref[...]
    else:
        g1_ref, p_ref, r_ref, hin_ref, gain_ref, gu_ref, wgu_ref, wd_ref = refs[:8]
        refs = refs[8:]
        grad, gain_grad = close_norm(g1_ref[...], p_ref, r_ref, hin_ref, gain_ref)
        refs[0][...] = grad
        refs[1][...] = gain_grad
        gm = grad.astype(BF16)
        refs[2][...] = gm
        refs = refs[3:]
    dgu_ref, part_ref = refs
    width = wd_ref.shape[0]
    step = min(width, 256)
    for f in range(0, width, step):
        dhid = mm(gm, wd_ref[f : f + step, :], NT)
        gate = gu_ref[:, f : f + step]
        up = gu_ref[:, width + f : width + f + step]
        sig = jax.nn.sigmoid(gate)
        dgu_ref[:, f : f + step] = (dhid * up * (sig * (1.0 + gate * (1.0 - sig)))).astype(BF16)
        dgu_ref[:, width + f : width + f + step] = (dhid * (gate * sig)).astype(BF16)
    part_ref[...] = mm(dgu_ref[:, :width], wgu_ref[0], NT) + mm(dgu_ref[:, width:], wgu_ref[1], NT)


def close_norm(g, p_ref, r_ref, h_ref, gain_ref):
    grad = p_ref[...] + r_ref[...]
    h = h_ref[...]
    scale = inv_rms(h)
    normed = h * scale
    gain_grad = jnp.sum(grad * normed, axis=0, keepdims=True)
    return g + norm_back(grad, normed, scale, gain_ref[...]), gain_grad


def attn_bwd(
    g_ref, p_ref, r_ref, h1_ref, gain_ref, wqkv_ref, wout_ref, table_ref, open_ref, qkv_ref, lse_ref,
    g1_ref, gain_grad_ref, ga_ref, dqkv_ref, part_ref,
):
    g1, gain_grad = close_norm(g_ref[...].astype(F32), p_ref, r_ref, h1_ref, gain_ref)
    g1_ref[...] = g1
    gain_grad_ref[...] = gain_grad
    ga = g1.astype(BF16)
    ga_ref[...] = ga
    n = ga.shape[0]
    width = wout_ref.shape[0]
    lane = lax.broadcasted_iota(jnp.int32, (n, 2 * HD), 1)
    low_half = lane < HD
    zero = jnp.zeros((n, 2 * HD), BF16)
    mask = key_mask(open_ref, n)
    for t in range(width // (2 * HD)):
        spots = [slice(s * width + t * 2 * HD, s * width + (t + 1) * 2 * HD) for s in range(3)]
        q = qkv_ref[:, spots[0]]
        k = qkv_ref[:, spots[1]]
        v = qkv_ref[:, spots[2]]
        dout = mm(ga, wout_ref[t * 2 * HD : (t + 1) * 2 * HD, :], NT).astype(BF16)
        dq, dk, dv = [], [], []
        for e in range(2):
            mine = low_half if e == 0 else ~low_half
            q_one = jnp.where(mine, q, zero)
            d_one = jnp.where(mine, dout, zero)
            s = jnp.where(mask, mm(k, q_one, NT), LOW)
            prob = jnp.exp(s - lse_ref[2 * t + e : 2 * t + e + 1, :])
            dprob = mm(v, d_one, NT)
            delta = jnp.sum(prob * dprob, axis=0, keepdims=True)
            ds = (prob * (dprob - delta)).astype(BF16)
            dv.append(mm(prob.astype(BF16), dout))
            dk.append(mm(ds, q))
            dq.append(mm(ds, k, TN))
        dq = jnp.where(low_half, dq[0], dq[1]) * HD ** (-0.5)
        dk = jnp.where(low_half, dk[0], dk[1])
        dv = jnp.where(low_half, dv[0], dv[1])
        dqkv_ref[:, spots[0]] = rotate(dq, table_ref, -1).astype(BF16)
        dqkv_ref[:, spots[1]] = rotate(dk, table_ref, -1).astype(BF16)
        dqkv_ref[:, spots[2]] = dv.astype(BF16)
    part_ref[...] = mm(dqkv_ref[...], wqkv_ref[...])


def close_layer(g1_ref, p_ref, r_ref, h_ref, gain_ref, out_ref, gain_grad_ref):
    grad, gain_grad = close_norm(g1_ref[...], p_ref, r_ref, h_ref, gain_ref)
    out_ref[...] = grad
    gain_grad_ref[...] = gain_grad


def halves_of(half_ref, dim):
    one = dim // 2
    return [pl.ds(pl.multiple_of(half_ref[s] * one, one), one) for s in range(2)]


def grad_rows(spans, half_ref, *refs):
    chunks = (len(refs) - 2) // 2
    lefts, rights = refs[:chunks], refs[chunks : 2 * chunks]
    outs = refs[2 * chunks :]
    for s, spot in enumerate(halves_of(half_ref, rights[0].shape[1])):
        for out, picks in zip(outs, spans):
            at = 0
            for lo, hi in picks:
                total = None
                for left, right in zip(lefts, rights):
                    term = mm(left[:, lo:hi], right[:, spot], TN)
                    total = term if total is None else total + term
                out[s, at : at + hi - lo, :] = total
                at += hi - lo


def grad_columns(spans, half_ref, *refs):
    chunks = (len(refs) - 2) // 2
    lefts, rights = refs[:chunks], refs[chunks : 2 * chunks]
    outs = refs[2 * chunks :]
    for s, spot in enumerate(halves_of(half_ref, lefts[0].shape[1])):
        for out, picks in zip(outs, spans):
            at = 0
            for lo, hi in picks:
                total = None
                for left, right in zip(lefts, rights):
                    term = mm(left[:, spot], right[:, lo:hi], TN)
                    total = term if total is None else total + term
                out[s, :, at : at + hi - lo] = total
                at += hi - lo


def whole_pass(dims, *refs):
    n, dim, wa, wf, layers, chunks = dims
    la, lf, half = wa // 2, wf // 2, dim // 2
    refs = list(refs)

    def take(count):
        got = refs[:count]
        del refs[:count]
        return got

    gains_ref, tables, open_ref, block_ref, first_ref = take(5)
    tokens, cotangent, w_qkv, w_out, w_gate_up, w_down = take(6)
    output, token_grad, small_out, down_out, gate_up_out, out_out, qkv_out = take(7)
    wgu_st, wd_st, wqkv_st, wout_st, h_st, h1_st, qkv_st, lse_st, o_st, last_st = take(10)
    wgu, wd, wqkv, wout = take(4)
    hs, h1s, qkvs, os, lses = take(5)
    ysend, yrecv, gs, gm, ab, hid, dgu = take(7)
    oth_g, oth_s, cr_d, cr_g, cr_a = take(5)
    os_d, os_g, os_a, ok_d, ok_g, ok_a = take(6)
    xr_d, xr_g, xr_a, z1_d, z1_g, z1_a, z2_d, z2_g, z2_a, small = take(10)
    load_sem, ys_sem, yr_sem, cs_sem, cr_sem, xs_sem, xr_sem = take(7)
    z1s, z1r, z2s, z2r, z3s, z3r, store_sem, row_sem, rows_s, rows_r, small_s, small_r = take(12)
    x_free, z1_free, z2_free, c_free = take(4)

    tp = lax.axis_index("tp")
    x = lax.axis_index("dpi")
    z = lax.axis_index("dpo")
    core = lax.rem(tp, 2)
    to_core = {"tp": tp + 1 - 2 * core}
    to_chip = {"tp": lax.rem(tp + 2, 4)}
    to_x = {"dpi": 1 - x}
    to_mate = {"dpo": z + 1 - 2 * lax.rem(z, 2)}
    to_inner = {"dpo": 3 - z}
    outer = (z == 0) | (z == 3)
    inner = (z == 1) | (z == 2)
    far = [{"dpo": lax.rem(z + k, 4)} for k in (1, 2, 3)]

    barrier = pltpu.get_barrier_semaphore()
    for peer in [to_core, to_chip, to_x] + far:
        pl.semaphore_signal(barrier, inc=1, device_id=peer, device_id_type=MESH)
    loads = {}

    def load(key, src, dst, slot):
        copy = pltpu.make_async_copy(src, dst, load_sem.at[slot])
        copy.start()
        loads[key] = copy

    def need(*keys):
        for key in keys:
            if key in loads:
                loads.pop(key).wait()

    def rows(c):
        return pl.ds(c * n, n)

    def load_ffn_weights():
        load("wgu", wgu_st, wgu, 0)
        load("wd", wd_st, wd, 1)

    def load_attn_weights():
        load("wqkv", wqkv_st, wqkv, 2)
        load("wout", wout_st, wout, 3)

    def load_h1(c):
        load(("h1", c), h1_st.at[0, c], h1s.at[c], 4 + c)

    def load_qkv(c):
        load(("qkv", c), qkv_st.at[c], qkvs.at[c], 6 + c)
        load(("lse", c), lse_st.at[c], lses.at[c], 8 + c)

    def load_o(c):
        load(("o", c), o_st.at[rows(c)], os.at[rows(c)], 10 + c)

    def load_h(c):
        load(("h", c), h_st.at[c], hs.at[c], 12 + c)

    top = layers - 1

    def own_rows(ref, c):
        return ref.at[pl.ds(pl.multiple_of((core * chunks + c) * n, n), n)]

    def own_attn(l):
        for t in range(3):
            load(("own", "a", t), w_qkv.at[l, t], wqkv.at[pl.ds(t * wa, la)], 17 + t)
        load(("own", "a", 3), w_out.at[l], wout.at[pl.ds(0, la)], 20)

    def own_ffn(l):
        for t in range(2):
            load(("own", "g", t), w_gate_up.at[l, t], wgu.at[t, :, pl.ds(0, lf)], 21 + t)
        load(("own", "d", 0), w_down.at[l], wd.at[pl.ds(0, lf)], 23)

    own_attn(0)
    for c in range(chunks):
        load(("token", c), own_rows(tokens, c), gm.at[rows(c)], 14 + c)
    own_ffn(0)
    pl.semaphore_wait(barrier, 6)

    def remote(src, dst, send, recv, to):
        return pltpu.make_async_remote_copy(
            src_ref=src, dst_ref=dst, send_sem=send, recv_sem=recv, device_id=to, device_id_type=MESH
        )

    turn = [0] * chunks

    def y_copy(c, k):
        return remote(ysend.at[c], yrecv.at[k % 2, c], ys_sem.at[c], yr_sem.at[k % 2, c], to_chip)

    def y_start(c):
        y_copy(c, turn[c]).start()

    def y_sum(c):
        copy = y_copy(c, turn[c])
        copy.wait()
        got = ysend[c] + yrecv[turn[c] % 2, c]
        turn[c] += 1
        return got

    def gain_of(l, i):
        k = 2 * l + i
        return gains_ref[k : k + 1, :]

    def add_gain(l, i, c, term):
        k = 2 + 2 * l + i
        spot = (z, x, core, slice(k, k + 1), slice(None))
        small[spot] = term if c == 0 else small[spot] + term

    def close(l, i, c, g, h):
        grad = y_sum(c)
        scale = inv_rms(h)
        normed = h * scale
        add_gain(l, i, c, jnp.sum(grad * normed, axis=0, keepdims=True))
        return g + norm_back(grad, normed, scale, gain_of(l, i))

    small[z, x, core] = block_ref[...]

    def ffn(l, c):
        spot = rows(c)
        if l == top:
            need(("cot", c))
            gs[c] = gm[spot, :].astype(F32)
            h = hs_next(c)
            h1s[c] = h
            load(("stash", c), h1s.at[c], h1_st.at[top, c], 28 + c)
        else:
            need(("h", c))
            g = close(l + 1, 0, c, gs[c], hs[c])
            gs[c] = g
            gm[spot, :] = g.astype(BF16)
            load_h(c)
        need(("h1", c), "wgu", "wd")
        h1 = h1s[c]
        b = (h1 * inv_rms(h1) * gain_of(l, 1)).astype(BF16)
        ab[spot, :] = b
        step = min(wf, 256)
        for f in range(0, wf, step):
            gate = mm(b, wgu[0, :, f : f + step])
            up = mm(b, wgu[1, :, f : f + step])
            dhid = mm(gm[spot, :], wd[f : f + step, :], NT)
            sig = jax.nn.sigmoid(gate)
            silu = gate * sig
            hid[spot, f : f + step] = (silu * up).astype(BF16)
            dgu[spot, f : f + step] = (dhid * up * (sig * (1.0 + gate * (1.0 - sig)))).astype(BF16)
            dgu[spot, wf + f : wf + f + step] = (dhid * silu).astype(BF16)
        ysend[c] = mm(dgu[spot, :wf], wgu[0], NT) + mm(dgu[spot, wf:], wgu[1], NT)
        y_start(c)
        if l == top:
            spare = oth_g.at[c, pl.ds(0, n), pl.ds(0, dim)]
            spare[...] = mm(hid[spot, :], wd[...])
            load(("last", c), spare, last_st.at[c], 30 + c)

    def attn(l, c):
        spot = rows(c)
        g1 = close(l, 1, c, gs[c], h1s[c])
        gs[c] = g1
        if l > 0:
            need(("stash", c))
            load_h1(c)
        gm[spot, :] = g1.astype(BF16)
        need("wqkv", "wout", ("qkv", c), ("lse", c))
        lane = lax.broadcasted_iota(jnp.int32, (n, 2 * HD), 1)
        low_half = lane < HD
        zero = jnp.zeros((n, 2 * HD), BF16)
        mask = key_mask(open_ref.at[c], n)
        ga = gm[spot, :]
        for t in range(wa // (2 * HD)):
            spots = [slice(s * wa + t * 2 * HD, s * wa + (t + 1) * 2 * HD) for s in range(3)]
            q, k, v = [qkvs[c, :, s] for s in spots]
            dout = mm(ga, wout[t * 2 * HD : (t + 1) * 2 * HD, :], NT).astype(BF16)
            dq, dk, dv = [], [], []
            for e in range(2):
                mine = low_half if e == 0 else ~low_half
                s = jnp.where(mask, mm(k, jnp.where(mine, q, zero), NT), LOW)
                prob = jnp.exp(s - lses[c, 2 * t + e : 2 * t + e + 1, :])
                dprob = mm(v, jnp.where(mine, dout, zero), NT)
                delta = jnp.sum(prob * dprob, axis=0, keepdims=True)
                ds = (prob * (dprob - delta)).astype(BF16)
                dv.append(mm(prob.astype(BF16), dout))
                dk.append(mm(ds, q))
                dq.append(mm(ds, k, TN))
            dq = jnp.where(low_half, dq[0], dq[1]) * HD ** (-0.5)
            dk = jnp.where(low_half, dk[0], dk[1])
            dv = jnp.where(low_half, dv[0], dv[1])
            dgu[spot, spots[0]] = rotate(dq, tables, -1).astype(BF16)
            dgu[spot, spots[1]] = rotate(dk, tables, -1).astype(BF16)
            dgu[spot, spots[2]] = dv.astype(BF16)
        ysend[c] = mm(dgu[spot, : 3 * wa], wqkv[...])
        y_start(c)
        if l > 0:
            load_qkv(c)
        need(("h", c))
        h = hs[c]
        ab[spot, :] = (h * inv_rms(h) * gain_of(l, 0)).astype(BF16)

    spans = [pl.ds(pl.multiple_of((1 - x) * half, half), half), pl.ds(pl.multiple_of(x * half, half), half)]
    kinds = {
        "d": (oth_s.at[:, pl.ds(0, lf)], cr_d, os_d, ok_d, xr_d, z1_d, z2_d),
        "g": (oth_g, cr_g, os_g, ok_g, xr_g, z1_g, z2_g),
        "a": (oth_s, cr_a, os_a, ok_a, xr_a, z1_a, z2_a),
    }
    index = {"d": 0, "g": 1, "a": 2}
    units = []
    for kind in kinds:
        at = 0
        for size in PIECES[kind]:
            target = {"d": down_out, "g": gate_up_out, "a": out_out if at < la else qkv_out}[kind]
            base = la if kind == "a" and at >= la else 0
            units.append((kind, pl.ds(at, size), target, pl.ds(at - base, size)))
            at += size

    def c_copy(kind):
        at = index[kind]
        return remote(kinds[kind][0], kinds[kind][1], cs_sem.at[at], cr_sem.at[at], to_core)

    def piece(kind, s, shard, put):
        if kind == "d":
            put(slice(None), slice(None), mm(hid[:, shard * lf : (shard + 1) * lf], gm[:, spans[s]], TN))
        elif kind == "g":
            for t in range(2):
                cols = slice(t * wf + shard * lf, t * wf + (shard + 1) * lf)
                put(slice(None), slice(t * lf, (t + 1) * lf), mm(ab[:, spans[s]], dgu[:, cols], TN))
        else:
            put(slice(0, la), slice(None), mm(os[:, shard * la : (shard + 1) * la], gm[:, spans[s]], TN))
            for t in range(3):
                cols = slice(t * wa + shard * la, t * wa + (shard + 1) * la)
                put(slice((t + 1) * la, (t + 2) * la), slice(None), mm(dgu[:, cols], ab[:, spans[s]], TN))

    def put_in(ref, *lead):
        def put(r, c, value):
            ref[lead + (r, c)] = value

        return put

    arrived = set()

    def grad_other(l, kind):
        if l == top and kind == "g":
            need(("last", 0), ("last", 1))
        if kind == "a":
            need(("o", 0), ("o", 1))
        if "c" not in arrived:
            pl.semaphore_wait(c_free, 1)
            arrived.add("c")
        for s in range(2):
            piece(kind, s, 1, put_in(kinds[kind][0], s))
        c_copy(kind).start()

    def grad_own(l, kind):
        if kind == "a":
            need(("o", 0), ("o", 1))
        piece(kind, 0, 0, put_in(kinds[kind][2]))
        piece(kind, 1, 0, put_in(kinds[kind][3], l))

    def x_copy(l, u):
        kind, spot = units[u][:2]
        return remote(kinds[kind][2].at[spot], kinds[kind][4].at[spot], xs_sem.at[l, u], xr_sem.at[l, u], to_x)

    def core_sum(l, u):
        kind, spot = units[u][:2]
        _, cr, own_s, own_k, *_ = kinds[kind]
        if (l, kind) not in arrived:
            c_copy(kind).wait()
            arrived.add((l, kind))
        own_s[spot, :] = own_s[spot, :] + cr[0, spot, :]
        if l < top:
            pl.semaphore_wait(x_free.at[u], 1)
        x_copy(l, u).start()
        own_k[l, spot, :] = own_k[l, spot, :] + cr[1, spot, :]

    def z1_copy(l, u):
        kind, spot = units[u][:2]
        return remote(kinds[kind][3].at[l, spot], kinds[kind][5].at[spot], z1s.at[l, u], z1r.at[l, u], to_mate)

    def z2_copy(l, u):
        kind, spot = units[u][:2]
        return remote(kinds[kind][3].at[l, spot], kinds[kind][6].at[spot], z2s.at[l, u], z2r.at[l, u], to_inner)

    def z3_copy(l, u):
        kind, spot, target, place = units[u]
        return remote(kinds[kind][6].at[spot], target.at[l, place], z3s.at[l, u], z3r.at[l, u], to_mate)

    def store_copy(l, u):
        kind, spot, target, place = units[u]
        return pltpu.make_async_copy(kinds[kind][6].at[spot], target.at[l, place], store_sem.at[l, u])

    def x_sum(l, u):
        kind, spot = units[u][:2]
        keep, got = kinds[kind][3], kinds[kind][4]
        x_copy(l, u).wait()
        keep[l, spot, :] = keep[l, spot, :] + got[spot, :]
        if l > 0:
            pl.semaphore_signal(x_free.at[u], inc=1, device_id=to_x, device_id_type=MESH)

        @pl.when(outer)
        def _():
            if l < top:
                pl.semaphore_wait(z1_free.at[u], 1)
            z1_copy(l, u).start()

    def z_one(l, u):
        kind, spot = units[u][:2]
        keep, got = kinds[kind][3], kinds[kind][5]

        @pl.when(inner)
        def _():
            z1_copy(l, u).wait_recv()
            keep[l, spot, :] = keep[l, spot, :] + got[spot, :]
            if l > 0:
                pl.semaphore_signal(z1_free.at[u], inc=1, device_id=to_mate, device_id_type=MESH)
            if l < top:
                pl.semaphore_wait(z2_free.at[u], 1)
            z2_copy(l, u).start()

    def z_two(l, u):
        kind, spot = units[u][:2]
        keep, got = kinds[kind][3], kinds[kind][6]

        @pl.when(inner)
        def _():
            z2_copy(l, u).wait()
            got[spot, :] = got[spot, :] + keep[l, spot, :]
            z3_copy(l, u).start()
            store_copy(l, u).start()

    def z_end(l, u):
        @pl.when(inner)
        def _():
            z3_copy(l, u).wait_send()
            store_copy(l, u).wait()
            if l > 0:
                pl.semaphore_signal(z2_free.at[u], inc=1, device_id=to_inner, device_id_type=MESH)

        @pl.when(outer)
        def _():
            z1_copy(l, u).wait_send()
            z3_copy(l, u).wait_recv()

    def row_copies(src, dst, i, c):
        spot = pl.ds(pl.multiple_of((core * chunks + c) * n, n), n)
        return (
            pltpu.make_async_copy(src, dst.at[spot], row_sem.at[i, c]),
            remote(src, dst.at[spot], rows_s.at[i, c], rows_r.at[i, c], to_core),
        )

    def share_rows(src, dst, i, c):
        for copy in row_copies(src, dst, i, c):
            copy.start()

    def end_rows(src, dst, i, c):
        for copy in row_copies(src, dst, i, c):
            copy.wait()

    def token(c):
        need(("h", c))
        g = close(0, 0, c, gs[c], hs[c])
        small[z, x, core, c : c + 1, :] = g[0:1, :]
        row = lax.broadcasted_iota(jnp.int32, (n, dim), 0)
        gs[c] = jnp.where(row == 0, 0.0, g)
        share_rows(gs.at[c], token_grad, 0, c)

    def pout_copy(c):
        k = turn[c] % 2
        return remote(last_st.at[c], yrecv.at[k, c], ys_sem.at[c], yr_sem.at[k, c], to_chip)

    def start_output(c):
        pout_copy(c).start()
        load(("pout", c), last_st.at[c], ysend.at[c], 4 + c)
        load(("out", c), h1_st.at[top, c], hs.at[c], 12 + c)

    def end_output(c):
        need(("pout", c), ("out", c))
        pout_copy(c).wait()
        hs[c] = hs[c] + (ysend[c] + yrecv[turn[c] % 2, c])
        share_rows(hs.at[c], output, 1, c)

    def small_core():
        return remote(small.at[z, x, core], small.at[z, x, core], small_s.at[0], small_r.at[0], to_core)

    def small_x():
        return remote(small.at[z, x], small.at[z, x], small_s.at[1], small_r.at[1], to_x)

    def small_z(k):
        return remote(small.at[z], small.at[z], small_s.at[2 + k], small_r.at[2 + k], far[k])

    def small_got(k):
        back = lax.rem(z + 3 - k, 4)
        return remote(small.at[back], small.at[back], small_s.at[2 + k], small_r.at[2 + k], far[k])

    def weight_send(l, kind):
        if kind == "a":
            need(*[("own", "a", t) for t in range(4)])
            for s in range(2):
                lanes = slice(s * half, (s + 1) * half)
                for t in range(3):
                    oth_s[s, t * la : (t + 1) * la, :] = wqkv[t * wa : t * wa + la, lanes].astype(F32)
                oth_s[s, 3 * la :, :] = wout[:la, lanes].astype(F32)
        elif kind == "g":
            need(("own", "g", 0), ("own", "g", 1))
            for s in range(2):
                for t in range(2):
                    oth_g[s, :, t * lf : (t + 1) * lf] = wgu[t, s * half : (s + 1) * half, :lf].astype(F32)
        else:
            need(("own", "d", 0))
            for s in range(2):
                oth_s[s, :lf, :] = wd[:lf, s * half : (s + 1) * half].astype(F32)
        c_copy(kind).start()

    def weight_take(l, kind):
        c_copy(kind).wait()
        for s in range(2):
            lanes = slice(s * half, (s + 1) * half)
            if kind == "a":
                for t in range(3):
                    wqkv[t * wa + la : (t + 1) * wa, lanes] = cr_a[s, t * la : (t + 1) * la, :].astype(BF16)
                wout[la:, lanes] = cr_a[s, 3 * la :, :].astype(BF16)
            elif kind == "g":
                for t in range(2):
                    wgu[t, lanes, lf:] = cr_g[s, :, t * lf : (t + 1) * lf].astype(BF16)
            else:
                wd[lf:, lanes] = cr_d[s].astype(BF16)

    def hs_next(c):
        return base_of(c) + y_sum(c)

    def base_of(c):
        return hs[c] if turn[c] % 2 == 0 else h1s[c]

    def attn_up(l, c):
        spot = rows(c)
        if l == 0:
            need(("token", c))
            h = gm[spot, :].astype(F32)
            row = lax.broadcasted_iota(jnp.int32, (n, dim), 0)
            h = jnp.where(row == 0, first_ref[c : c + 1, :], h)
        else:
            h = hs_next(c)
            need(("st_h", c), ("st_qkv", c), ("st_lse", c), ("st_o", c))
        hs[c] = h
        a = (h * inv_rms(h) * gain_of(l, 0)).astype(BF16)
        lane = lax.broadcasted_iota(jnp.int32, (n, 2 * HD), 1)
        low_half = lane < HD
        zero = jnp.zeros((n, 2 * HD), BF16)
        mask = key_mask(open_ref.at[c], n)
        for t in range(wa // (2 * HD)):
            spots = [slice(s * wa + t * 2 * HD, s * wa + (t + 1) * 2 * HD) for s in range(3)]
            q = rotate(mm(a, wqkv[spots[0], :], NT), tables, 1)
            q = (q * HD ** (-0.5)).astype(BF16)
            k = rotate(mm(a, wqkv[spots[1], :], NT), tables, 1).astype(BF16)
            v = mm(a, wqkv[spots[2], :], NT).astype(BF16)
            for part, value in zip(spots, (q, k, v)):
                qkvs[c, :, part] = value
            mixed = []
            for e in range(2):
                q_one = jnp.where(low_half if e == 0 else ~low_half, q, zero)
                s = jnp.where(mask, mm(k, q_one, NT), LOW)
                peak = jnp.max(s, axis=0, keepdims=True)
                raised = jnp.exp(s - peak)
                total = jnp.sum(raised, axis=0, keepdims=True)
                lses[c, 2 * t + e : 2 * t + e + 1, :] = peak + jnp.log(total)
                mixed.append(mm((raised / total).astype(BF16), v, TN))
            os[spot, t * 2 * HD : (t + 1) * 2 * HD] = jnp.where(low_half, mixed[0], mixed[1]).astype(BF16)
        ysend[c] = mm(os[spot, :], wout[...])
        y_start(c)
        if l == 0:
            load(("st_h", c), hs.at[c], h_st.at[c], 12 + c)
            load(("st_qkv", c), qkvs.at[c], qkv_st.at[c], 6 + c)
            load(("st_lse", c), lses.at[c], lse_st.at[c], 8 + c)
            load(("st_o", c), os.at[rows(c)], o_st.at[rows(c)], 10 + c)

    def ffn_up(c):
        spot = rows(c)
        h1 = hs_next(c)
        h1s[c] = h1
        b = (h1 * inv_rms(h1) * gain_of(0, 1)).astype(BF16)
        step = min(wf, 256)
        for f in range(0, wf, step):
            gate = mm(b, wgu[0, :, f : f + step])
            up = mm(b, wgu[1, :, f : f + step])
            hid[spot, f : f + step] = (gate * jax.nn.sigmoid(gate) * up).astype(BF16)
        ysend[c] = mm(hid[spot, :], wd[...])
        y_start(c)
        load(("stash", c), h1s.at[c], h1_st.at[0, c], 28 + c)

    weight_send(0, "a")
    weight_send(0, "g")
    weight_take(0, "a")
    attn_up(0, 0)
    weight_send(0, "d")
    attn_up(0, 1)
    for c in range(chunks):
        load(("cot", c), own_rows(cotangent, c), gm.at[rows(c)], 14 + c)
    load("st_wqkv", wqkv, wqkv_st, 2)
    load("st_wout", wout, wout_st, 3)
    weight_take(0, "g")
    weight_take(0, "d")
    need("st_wqkv", "st_wout")
    own_attn(1)
    ffn_up(0)
    weight_send(1, "a")
    ffn_up(1)
    load("st_wgu", wgu, wgu_st, 0)
    load("st_wd", wd, wd_st, 1)
    weight_take(1, "a")
    need("st_wgu", "st_wd")
    own_ffn(1)
    attn_up(1, 0)
    need(("stash", 0))
    weight_send(1, "d")
    weight_send(1, "g")
    attn_up(1, 1)
    need(("stash", 1))
    weight_take(1, "d")
    weight_take(1, "g")
    pl.semaphore_signal(c_free, inc=1, device_id=to_core, device_id_type=MESH)

    def start_small():
        small_core().start()

    def move_small():
        small_core().wait_send()
        spot = small.at[z, x, 1 - core]
        remote(spot, spot, small_s.at[0], small_r.at[0], to_core).wait_recv()
        small_x().start()

    def spread_small():
        small_x().wait_send()
        spot = small.at[z, 1 - x]
        remote(spot, spot, small_s.at[1], small_r.at[1], to_x).wait_recv()
        for k in range(3):
            small_z(k).start()

    def end_small():
        for k in range(3):
            small_z(k).wait_send()
            small_got(k).wait_recv()
        load("small", small, small_out, 16)

    def ffn_down(l, c):
        ffn(l, c)
        if (l, c) == (1, chunks - 1):
            load_ffn_weights()

    def attn_down(l, c):
        attn(l, c)
        if (l, c) == (1, chunks - 1):
            load_attn_weights()

    acts = {
        "ffn": ffn_down, "attn": attn_down, "go": grad_other, "gw": grad_own, "cu": core_sum, "xs": x_sum,
        "z1": z_one, "z2": z_two, "ze": z_end, "tok": token, "so": start_output, "eo": end_output,
        "sc": start_small, "sx": move_small, "sz": spread_small, "sw": end_small,
    }
    left = {("go", 1, "a"), ("gw", 1, "a")}
    for name, *at in ORDER:
        acts[name](*at)
        if left:
            left.discard((name, *at))
            if not left:
                for c in range(chunks):
                    load_o(c)
    need("small")
    for c in range(chunks):
        end_rows(gs.at[c], token_grad, 0, c)
        end_rows(hs.at[c], output, 1, c)


def call(body, outs, args, flops, limit=40, smem=0, scratch=()):
    moved = sum(x.size * x.dtype.itemsize for x in args) + sum(
        int(np.prod(s)) * np.dtype(d).itemsize for s, d in outs
    )
    spec = pl.BlockSpec(memory_space=pltpu.VMEM)
    got = pl.pallas_call(
        body,
        out_shape=[jax.ShapeDtypeStruct(s, d) for s, d in outs],
        in_specs=[pl.BlockSpec(memory_space=pltpu.SMEM)] * smem + [spec] * (len(args) - smem),
        out_specs=[spec] * len(outs),
        scratch_shapes=list(scratch),
        compiler_params=pltpu.CompilerParams(vmem_limit_bytes=limit * 2**20),
        cost_estimate=pl.CostEstimate(flops=int(flops), bytes_accessed=int(moved), transcendentals=0),
    )(*args)
    return list(got)


def call_whole(sizes, n, dim, wa, wf, layers, chunks, fixed, moved):
    la, lf, half = wa // 2, wf // 2, dim // 2
    groups = sizes["dpo"], sizes["dpi"]
    outs = [
        ((2 * chunks * n, dim), F32),
        ((2 * chunks * n, dim), F32),
        (groups + (2, 8, dim), F32),
        ((layers, lf, half), F32),
        ((layers, half, 2 * lf), F32),
        ((layers, la, half), F32),
        ((layers, 3 * la, half), F32),
        ((2, dim, wf), BF16),
        ((wf, dim), BF16),
        ((3 * wa, dim), BF16),
        ((wa, dim), BF16),
        ((chunks, n, dim), F32),
        ((layers, chunks, n, dim), F32),
        ((chunks, n, 3 * wa), BF16),
        ((chunks, 8, n), F32),
        ((chunks * n, wa), BF16),
        ((chunks, n, dim), F32),
    ]
    d, g, a = (lf, half), (half, 2 * lf), (4 * la, half)
    f, h = lambda *s: pltpu.VMEM(s, F32), lambda *s: pltpu.VMEM(s, BF16)
    dma, count = pltpu.SemaphoreType.DMA, pltpu.SemaphoreType.REGULAR
    units = sum(len(k) for k in PIECES.values())
    scratch = [h(2, dim, wf), h(wf, dim), h(3 * wa, dim), h(wa, dim)]
    scratch += [f(chunks, n, dim), f(chunks, n, dim), h(chunks, n, 3 * wa), h(chunks * n, wa), f(chunks, 8, n)]
    scratch += [f(chunks, n, dim), f(2, chunks, n, dim), f(chunks, n, dim)]
    scratch += [h(chunks * n, dim), h(chunks * n, dim), h(chunks * n, wf), h(chunks * n, 2 * wf)]
    scratch += [f(2, *g), f(2, *a)] + [f(2, *k) for k in (d, g, a)]
    scratch += [f(*k) for k in (d, g, a)] + [f(layers, *k) for k in (d, g, a)]
    scratch += [f(*k) for _ in range(3) for k in (d, g, a)] + [f(*groups, 2, 8, dim)]
    scratch += [dma((32,)), dma((chunks,)), dma((2, chunks)), dma((3,)), dma((3,))]
    scratch += [dma((layers, units))] * 9 + [dma((2, chunks))] * 3 + [dma((5,))] * 2
    scratch += [count((units,))] * 3 + [count]
    args = list(fixed) + list(moved)
    flops = layers * chunks * n * (2 * dim * (14 * wa + 12 * wf) + 32 * n * wa)
    vmem, anywhere = pl.BlockSpec(memory_space=pltpu.VMEM), pl.BlockSpec(memory_space=pl.ANY)
    return pl.pallas_call(
        functools.partial(whole_pass, (n, dim, wa, wf, layers, chunks)),
        out_shape=[jax.ShapeDtypeStruct(s, t) for s, t in outs],
        in_specs=[vmem] * len(fixed) + [anywhere] * len(moved),
        out_specs=[anywhere] * len(outs),
        scratch_shapes=scratch,
        compiler_params=pltpu.CompilerParams(
            vmem_limit_bytes=62 * 2**20, collective_id=0, has_side_effects=True
        ),
        cost_estimate=pl.CostEstimate(flops=flops, bytes_accessed=90 * 10**6, transcendentals=0),
        name="whole_pass",
    )(*args)[:7]


def on_device(sizes, tokens, cotangent, heights, labels, valid, class_table, gains, w_qkv, w_out, w_gate_up, w_down):
    seq_count = heights.shape[0]
    row_count, dim = tokens.shape
    n = row_count // seq_count
    layers = gains.shape[0]
    classes = class_table.shape[0]
    la = w_out.shape[1]
    lf = w_down.shape[1]
    wa, wf = 2 * la, 2 * lf
    tp, dpo, dpi = sizes["tp"], sizes["dpo"], sizes["dpi"]
    mine = seq_count // 2
    lean = (tp, dpo, dpi) == (4, 4, 2) and (mine, layers) == (2, 2)
    core = lax.rem(lax.axis_index("tp"), 2)
    z = lax.axis_index("dpo")
    swap_core = [(i, i ^ 1) for i in range(tp)]

    def core_swap(x):
        return lax.ppermute(x, "tp", swap_core)

    def sum_chips(part):
        total = None
        for step in range(2, tp, 2):
            got = lax.ppermute(part, "tp", [(i, i ^ step) for i in range(tp)])
            total = got if total is None else total + got
        return total

    tables = jnp.asarray(rope_constants(n))
    position = jnp.arange(n)
    own = lambda x: lax.dynamic_slice_in_dim(x, core * mine, mine, 0)
    open_key = (position[None, :] < 1 + COLS * own(heights)[:, None]) & (own(valid.reshape(seq_count, n)) == 1)
    open_key = open_key.astype(F32)[:, :, None]
    own_labels = own(labels)
    if lean:
        block = jnp.zeros((8, dim), F32)
        block = lax.dynamic_update_slice(block, own_labels.astype(F32)[None], (6, 0))
        firsts = [lax.dynamic_slice_in_dim(class_table, own_labels[c], 1, 0) for c in range(mine)]
        firsts = jnp.concatenate(firsts, axis=0).astype(F32)
        fixed = (gains.reshape(2 * layers, dim), tables, open_key, block, firsts)
        moved = (
            tokens, cotangent, jnp.transpose(w_qkv, (0, 2, 3, 1)), w_out, jnp.transpose(w_gate_up, (0, 2, 1, 3)), w_down
        )
        got = call_whole(sizes, n, dim, wa, wf, layers, mine, fixed, moved)
        output, token_grad, small, down_part, gate_up_part, out_part, qkv_part = got
        gain_total = jnp.sum(small[..., 2 : 2 + 2 * layers, :], axis=(0, 1, 2)).reshape(layers, 2, dim)
        rows = small[..., :mine, :].reshape(-1, dim)
        all_labels = jnp.round(small[..., 6, :mine]).astype(jnp.int32).reshape(-1)
        half = dim // dpi
        rows = lax.dynamic_slice(rows, (0, lax.axis_index("dpi") * half), (rows.shape[0], half))
        onehot = (all_labels[None, :] == jnp.arange(classes)[:, None]).astype(F32)
        return (
            output,
            token_grad,
            jnp.dot(onehot, rows, precision=lax.Precision.HIGHEST),
            gain_total,
            qkv_part.reshape(layers, 3, la, half).transpose(0, 3, 1, 2),
            out_part,
            gate_up_part.reshape(layers, half, 2, lf),
            down_part,
        )

    wqkv, wout, wgu, wd = [], [], [], []
    for l in range(layers):
        for into, w in (
            (wqkv, jnp.transpose(w_qkv[l], (1, 2, 0))),
            (wout, w_out[l][None]),
            (wgu, jnp.transpose(w_gate_up[l], (1, 0, 2))),
            (wd, w_down[l][None]),
        ):
            wide = w.astype(F32)
            axis = 2 if into is wgu else 1
            shape = list(w.shape)
            shape[axis] *= 2
            into.append(call(functools.partial(merge, axis), [(tuple(shape), BF16)], (wide, core_swap(wide)), 1000)[0])
        wqkv[l] = wqkv[l].reshape(3 * wa, dim)
        wout[l] = wout[l][0]
        wd[l] = wd[l][0]

    token_own = own(tokens.reshape(seq_count, n, dim))
    cot_own = own(cotangent.reshape(seq_count, n, dim))
    chunks = range(mine)
    hs = []
    for c in chunks:
        row = lax.dynamic_slice_in_dim(class_table, own_labels[c], 1, 0)
        hs.append(jnp.where((position == 0)[:, None], row, token_own[c]).astype(F32))

    shape_d = ((n, dim), F32)
    shape_b = ((n, dim), BF16)
    flops_a = 2 * n * dim * 4 * wa + 8 * n * n * wa
    flops_f = 2 * n * dim * 3 * wf

    kept = []
    state = [(hs[c],) for c in chunks]
    parts = None
    for l in range(layers):
        keep = [dict() for _ in chunks]
        for c in chunks:
            args = state[c] + (gains[l, 0][None], wqkv[l], wout[l], tables, open_key[c])
            outs = [((n, 3 * wa), BF16), ((max(8, wa // HD), n), F32), ((n, wa), BF16), shape_d]
            outs = ([shape_d] if l > 0 else []) + [shape_b] + outs
            got = call(functools.partial(attn_fwd, l == 0), outs, args, flops_a)
            h = state[c][0] if l == 0 else got.pop(0)
            a, qkv, lse, o, part = got
            keep[c].update(h=h, a=a, qkv=qkv, lse=lse, o=o)
            state[c] = (h, part, sum_chips(part))
        for c in chunks:
            args = state[c] + (gains[l, 1][None], wgu[l], wd[l])
            outs = [shape_d, shape_b, ((n, 2 * wf), F32), ((n, wf), BF16), shape_d]
            h1, b, gu, hid, part = call(ffn_fwd, outs, args, flops_f)
            keep[c].update(h1=h1, b=b, gu=gu, hid=hid)
            state[c] = (h1, part, sum_chips(part))
        kept.append(keep)

    output = jnp.concatenate([s[0] + (s[1] + s[2]) for s in state], axis=0)

    half = lax.axis_index("dpi") if dpi == 2 else 1
    order = jnp.stack([jnp.int32(1) - half, jnp.int32(half)])

    def dp_sum(both, other, axis):
        got = core_swap(other)
        if dpi == 2:
            sent = lax.ppermute(both[0] + got[0], "dpi", [(0, 1), (1, 0)])
            total = (both[1] + got[1]) + sent
        else:
            both = both + got
            whole = jnp.concatenate([both[0], both[1]], axis=axis)
            total = lax.psum_scatter(whole, "dpi", scatter_dimension=axis, tiled=True)
        return line_sum(total)

    def line_sum(x):
        if dpo != 4:
            return lax.psum(x, "dpo")
        got = lax.ppermute(x, "dpo", [(0, 1), (3, 2)])
        x = x + got
        got = lax.ppermute(x, "dpo", [(1, 2), (2, 1)])
        x = x + got
        got = lax.ppermute(x, "dpo", [(1, 0), (2, 3)])
        return jnp.where((z == 0) | (z == dpo - 1), got, x)

    gain_rows = [[None, None] for _ in range(layers)]
    grads = [None] * layers
    state = [None] * mine
    for l in reversed(range(layers)):
        top = l == layers - 1
        keep = kept[l]
        gms = []
        for c in chunks:
            outs = [((n, 2 * wf), BF16), shape_d]
            args = (keep[c]["gu"], wgu[l], wd[l])
            if top:
                g = cot_own[c]
                dgu, part = call(functools.partial(ffn_bwd, True), outs, (g,) + args, flops_f)
                gms.append(g)
            else:
                outs = [shape_d, ((1, dim), F32), shape_b] + outs
                args = state[c] + args
                g, gain_c, gm, dgu, part = call(functools.partial(ffn_bwd, False), outs, args, flops_f)
                gain_rows[l + 1][0] = gain_c if c == 0 else gain_rows[l + 1][0] + gain_c
                gms.append(gm)
            keep[c]["dgu"] = dgu
            state[c] = (g, part, sum_chips(part), keep[c]["h1"], gains[l, 1][None])
        flops_w = 2 * n * mine * dim * wf
        outs = [((2, lf, dim // 2), F32)] * 2
        args = [order] + [keep[c]["hid"] for c in chunks] + gms
        spans = (((0, lf),), ((lf, wf),))
        down = call(functools.partial(grad_rows, spans), outs, args, flops_w, smem=1)
        outs = [((2, dim // 2, 2 * lf), F32)] * 2
        args = [order] + [keep[c]["b"] for c in chunks] + [keep[c]["dgu"] for c in chunks]
        spans = (((0, lf), (wf, wf + lf)), ((lf, wf), (wf + lf, 2 * wf)))
        gate_up = call(functools.partial(grad_columns, spans), outs, args, 2 * flops_w, smem=1)
        down = dp_sum(*down, 1)
        gate_up = dp_sum(*gate_up, 0)
        gas = []
        for c in chunks:
            outs = [shape_d, ((1, dim), F32), shape_b, ((n, 3 * wa), BF16), shape_d]
            args = state[c] + (wqkv[l], wout[l], tables, open_key[c], keep[c]["qkv"], keep[c]["lse"])
            g1, gain_c, ga, dqkv, part = call(attn_bwd, outs, args, flops_a + 12 * n * n * wa)
            gain_rows[l][1] = gain_c if c == 0 else gain_rows[l][1] + gain_c
            gas.append(ga)
            keep[c]["dqkv"] = dqkv
            state[c] = (g1, part, sum_chips(part), keep[c]["h"], gains[l, 0][None])
        flops_w = 2 * n * mine * dim * wa
        outs = [((2, la, dim // 2), F32)] * 2
        args = [order] + [keep[c]["o"] for c in chunks] + gas
        spans = (((0, la),), ((la, wa),))
        out = call(functools.partial(grad_rows, spans), outs, args, flops_w, smem=1)
        outs = [((2, 3 * la, dim // 2), F32)] * 2
        args = [order] + [keep[c]["dqkv"] for c in chunks] + [keep[c]["a"] for c in chunks]
        spans = tuple(tuple((t * wa + s * la, t * wa + (s + 1) * la) for t in range(3)) for s in range(2))
        qkv = call(functools.partial(grad_rows, spans), outs, args, 3 * flops_w, smem=1)
        out = dp_sum(*out, 1)
        qkv = dp_sum(*qkv, 1)
        grads[l] = (qkv, out, gate_up, down)

    finals = []
    for c in chunks:
        g, gain_c = call(close_layer, [shape_d, ((1, dim), F32)], state[c], 1000)
        gain_rows[0][0] = gain_c if c == 0 else gain_rows[0][0] + gain_c
        finals.append(g)

    slot0 = lax.axis_index("dpo") * dpi + lax.axis_index("dpi")
    seqs = seq_count * dpo * dpi
    firsts = jnp.concatenate([g[0:1] for g in finals], axis=0)
    small = jnp.zeros((seqs + 2 * layers + 1, dim), F32)
    small = lax.dynamic_update_slice(small, firsts, (slot0 * seq_count + core * mine, 0))
    terms = jnp.concatenate([gain_rows[l][i] for l in range(layers) for i in range(2)], axis=0)
    small = lax.dynamic_update_slice(small, terms, (seqs, 0))
    label_row = lax.dynamic_update_slice(
        jnp.zeros((1, dim), F32), own_labels.astype(F32)[None], (0, slot0 * seq_count + core * mine)
    )
    small = lax.dynamic_update_slice(small, label_row, (seqs + 2 * layers, 0))
    small = jnp.where(lax.axis_index("tp") < 2, small, 0.0)
    small = lax.psum(small, ("dpo", "dpi", "tp"))
    all_labels = jnp.round(small[seqs + 2 * layers, :seqs]).astype(jnp.int32)
    gain_total = small[seqs : seqs + 2 * layers].reshape(layers, 2, dim)
    onehot = (all_labels[None, :] == jnp.arange(classes)[:, None]).astype(F32)
    share = dim // dpi
    rows = lax.dynamic_slice(small, (0, lax.axis_index("dpi") * share), (seqs, share))
    table_part = jnp.dot(onehot, rows, precision=lax.Precision.HIGHEST)

    token_own = jnp.concatenate([jnp.where((position == 0)[:, None], 0.0, g) for g in finals], axis=0)

    def both_cores(x):
        other = core_swap(x)
        return jnp.where(core == 0, jnp.concatenate([x, other], 0), jnp.concatenate([other, x], 0))

    qkv_part = jnp.stack([g[0].reshape(3, la, share) for g in grads]).transpose(0, 3, 1, 2)
    out_part = jnp.stack([g[1] for g in grads])
    gate_up_part = jnp.stack([g[2].reshape(share, 2, lf) for g in grads])
    down_part = jnp.stack([g[3] for g in grads])
    return (
        both_cores(output),
        both_cores(token_own),
        table_part,
        gain_total,
        qkv_part,
        out_part,
        gate_up_part,
        down_part,
    )


def solution(mesh):
    sizes = dict(mesh.shape)
    placed = (
        P(("dpo", "dpi"), None),
        P(("dpo", "dpi"), None),
        P(("dpo", "dpi")),
        P(("dpo", "dpi")),
        P(("dpo", "dpi")),
        P(),
        P(),
        P(None, None, None, "tp"),
        P(None, "tp", None),
        P(None, None, None, "tp"),
        P(None, "tp", None),
    )
    return jax.shard_map(
        functools.partial(on_device, sizes),
        mesh=mesh,
        in_specs=placed,
        out_specs=(
            P(("dpo", "dpi"), None),
            P(("dpo", "dpi"), None),
            P(None, "dpi"),
            P(),
            P(None, "dpi", None, "tp"),
            P(None, "tp", "dpi"),
            P(None, "dpi", None, "tp"),
            P(None, "tp", "dpi"),
        ),
        check_vma=False,
    )
```

```python
import functools

import jax
import jax.numpy as jnp
import numpy as np
from jax import lax
from jax.experimental import pallas as pl
from jax.experimental.pallas import tpu as pltpu
from jax.sharding import PartitionSpec as P

HD = 64
COLS = 16
EPS = 1e-05
F32 = jnp.float32
BF16 = jnp.bfloat16
LOW = -1e30
MESH = pl.DeviceIdType.MESH

PIECES = {"d": (128,) * 4, "g": (48,) * 8, "a": (96,) * 8}
ORDER = (
    ("fa", 1, 0), ("po", 0), ("fb", 1, 0), ("fa", 1, 1), ("go", 1, "d"), ("gw", 1, "d"), ("go", 1, "g"),
    ("cu", 1, 0), ("po", 1), ("fb", 1, 1), ("cu", 1, 1), ("gw", 1, "g"), ("xs", 1, 0), ("cu", 1, 3),
    ("cu", 1, 2), ("cu", 1, 4), ("cu", 1, 6), ("cu", 1, 7), ("z1", 1, 0), ("xs", 1, 1), ("cu", 1, 5),
    ("z1", 1, 1), ("xs", 1, 3), ("attn", 1, 0), ("xs", 1, 2), ("z2", 1, 0), ("z1", 1, 3), ("cu", 1, 8),
    ("cu", 1, 9), ("xs", 1, 4), ("z2", 1, 1), ("z1", 1, 2), ("cu", 1, 11), ("xs", 1, 6), ("z2", 1, 3),
    ("z1", 1, 4), ("attn", 1, 1), ("z2", 1, 2), ("xs", 1, 7), ("z1", 1, 6), ("xs", 1, 5), ("z2", 1, 4),
    ("ze", 1, 0), ("cu", 1, 10), ("go", 1, "a"), ("z1", 1, 7), ("ze", 1, 3), ("ze", 1, 1), ("z2", 1, 6),
    ("xs", 1, 8), ("z1", 1, 5), ("gw", 1, "a"), ("cu", 1, 18), ("cu", 1, 12), ("cu", 1, 15), ("z2", 1, 7),
    ("xs", 1, 9), ("z1", 1, 8), ("ze", 1, 4), ("cu", 1, 14), ("cu", 1, 19), ("fa", 0, 0), ("z2", 1, 5),
    ("z1", 1, 9), ("ze", 1, 2), ("xs", 1, 11), ("z2", 1, 8), ("cu", 1, 13), ("fb", 0, 0), ("xs", 1, 10),
    ("cu", 1, 17), ("z1", 1, 11), ("z2", 1, 9), ("cu", 1, 16), ("xs", 1, 18), ("z1", 1, 10), ("ze", 1, 5),
    ("xs", 1, 12), ("fa", 0, 1), ("z2", 1, 11), ("xs", 1, 15), ("z1", 1, 18), ("go", 0, "d"), ("xs", 1, 14),
    ("z1", 1, 12), ("z2", 1, 10), ("gw", 0, "d"), ("z2", 1, 18), ("z1", 1, 15), ("fb", 0, 1), ("xs", 1, 19),
    ("ze", 1, 9), ("z1", 1, 14), ("ze", 1, 6), ("go", 0, "g"), ("ze", 1, 11), ("cu", 0, 2), ("z2", 1, 12),
    ("xs", 1, 13), ("z2", 1, 15), ("cu", 0, 0), ("cu", 0, 1), ("cu", 0, 3), ("ze", 1, 10), ("xs", 1, 17),
    ("z1", 1, 13), ("xs", 1, 16), ("gw", 0, "g"), ("z1", 1, 19), ("z2", 1, 14), ("z1", 1, 17), ("xs", 0, 2),
    ("ze", 1, 8), ("z2", 1, 13), ("z1", 1, 16), ("z2", 1, 19), ("cu", 0, 4), ("z1", 0, 2), ("z2", 1, 17),
    ("xs", 0, 0), ("attn", 0, 0), ("xs", 0, 1), ("z2", 1, 16), ("z1", 0, 0), ("ze", 1, 12), ("cu", 0, 5),
    ("cu", 0, 8), ("cu", 0, 7), ("z1", 0, 1), ("cu", 0, 11), ("z2", 0, 2), ("ze", 1, 13), ("cu", 0, 9),
    ("ze", 1, 15), ("cu", 0, 6), ("xs", 0, 3), ("xs", 0, 4), ("ze", 1, 7), ("z2", 0, 0), ("ze", 1, 19),
    ("ze", 1, 16), ("z1", 0, 3), ("attn", 0, 1), ("z2", 0, 1), ("ze", 1, 17), ("cu", 0, 10), ("z1", 0, 4),
    ("xs", 0, 5), ("xs", 0, 8), ("z2", 0, 3), ("ze", 0, 0), ("go", 0, "a"), ("z1", 0, 5), ("gw", 0, "a"),
    ("z2", 0, 4), ("ze", 0, 2), ("tok", 0), ("z1", 0, 8), ("xs", 0, 7), ("cu", 0, 19), ("z2", 0, 5),
    ("cu", 0, 18), ("z1", 0, 7), ("cu", 0, 12), ("cu", 0, 15), ("ze", 1, 14), ("so", 0), ("xs", 0, 11),
    ("xs", 0, 9), ("z2", 0, 8), ("z1", 0, 11), ("ze", 0, 3), ("cu", 0, 14), ("z2", 0, 7), ("cu", 0, 17),
    ("z1", 0, 9), ("xs", 0, 6), ("xs", 0, 10), ("z2", 0, 11), ("z1", 0, 6), ("z2", 0, 9), ("xs", 0, 19),
    ("ze", 0, 7), ("z1", 0, 10), ("ze", 0, 8), ("xs", 0, 18), ("z2", 0, 6), ("tok", 1), ("cu", 0, 13),
    ("z1", 0, 19), ("ze", 0, 1), ("so", 1), ("sc",), ("z2", 0, 10), ("xs", 0, 12), ("ze", 1, 18),
    ("z1", 0, 12), ("xs", 0, 15), ("z2", 0, 19), ("z1", 0, 15), ("z2", 0, 12), ("z1", 0, 18), ("xs", 0, 14),
    ("ze", 0, 10), ("xs", 0, 17), ("ze", 0, 5), ("ze", 0, 11), ("z1", 0, 14), ("z2", 0, 15), ("sx",),
    ("cu", 0, 16), ("z2", 0, 18), ("ze", 0, 9), ("ze", 0, 4), ("z1", 0, 17), ("ze", 0, 6), ("sz",),
    ("z2", 0, 14), ("z2", 0, 17), ("xs", 0, 13), ("eo", 0), ("ze", 0, 12), ("z1", 0, 13), ("ze", 0, 15),
    ("xs", 0, 16), ("ze", 0, 19), ("z1", 0, 16), ("ze", 0, 18), ("eo", 1), ("z2", 0, 13), ("sw",),
    ("z2", 0, 16), ("ze", 0, 17), ("ze", 0, 13), ("ze", 0, 14), ("ze", 0, 16),
)

NN = (((1,), (0,)), ((), ()))
NT = (((1,), (1,)), ((), ()))
TN = (((0,), (0,)), ((), ()))


def mm(a, b, dims=NN):
    return lax.dot_general(a, b, dims, preferred_element_type=F32)


def rope_constants(slot_len):
    quarter = HD // 4
    raster = np.maximum(np.arange(slot_len) - 1, 0)
    row_pos = (raster // COLS).astype(np.float32)
    col_pos = (raster % COLS).astype(np.float32)
    frequency = (10000.0 ** (-np.arange(quarter).astype(np.float32) / quarter)).astype(np.float32)
    row_angle = row_pos[:, None] * frequency[None, :]
    col_angle = col_pos[:, None] * frequency[None, :]
    zero = np.zeros_like(row_angle)
    cos = np.concatenate([np.cos(row_angle)] * 2 + [np.cos(col_angle)] * 2, axis=1)
    first = np.concatenate([-np.sin(row_angle), zero, -np.sin(col_angle), zero], axis=1)
    second = np.concatenate([zero, np.sin(row_angle), zero, np.sin(col_angle)], axis=1)
    return np.stack([np.tile(t, (1, 2)) for t in (cos, first, second)]).astype(np.float32)


def rotate(x, table_ref, sign):
    quarter = HD // 4
    ahead = pltpu.roll(x, 2 * HD - quarter, 1) * table_ref[1]
    behind = pltpu.roll(x, quarter, 1) * table_ref[2]
    turned = ahead + behind
    return x * table_ref[0] + (turned if sign > 0 else -turned)


def merge(axis, mine_ref, other_ref, out_ref):
    size = mine_ref.shape[axis]
    if axis == 1:
        out_ref[:, :size, :] = mine_ref[...].astype(BF16)
        out_ref[:, size:, :] = other_ref[...].astype(BF16)
    else:
        out_ref[:, :, :size] = mine_ref[...].astype(BF16)
        out_ref[:, :, size:] = other_ref[...].astype(BF16)


def inv_rms(h):
    return lax.rsqrt(jnp.mean(h * h, axis=-1, keepdims=True) + EPS)


def norm_back(grad, normed, scale, gain):
    scaled = grad * gain
    return scale * (scaled - normed * jnp.mean(scaled * normed, axis=-1, keepdims=True))


def key_mask(open_ref, n):
    key = lax.broadcasted_iota(jnp.int32, (n, n), 0)
    query = lax.broadcasted_iota(jnp.int32, (n, n), 1)
    return ((key < query) & (open_ref[...] > 0.5)) | (key == query)


def attn_fwd(first, *refs):
    if first:
        h_ref, gain_ref, wqkv_ref, wout_ref, table_ref, open_ref = refs[:6]
        refs = refs[6:]
        h = h_ref[...]
    else:
        h_ref, p_ref, r_ref, gain_ref, wqkv_ref, wout_ref, table_ref, open_ref = refs[:8]
        refs = refs[8:]
        h = h_ref[...] + (p_ref[...] + r_ref[...])
        refs[0][...] = h
        refs = refs[1:]
    a_ref, qkv_ref, lse_ref, o_ref, part_ref = refs
    n = h.shape[0]
    width = wout_ref.shape[0]
    a = (h * inv_rms(h) * gain_ref[...]).astype(BF16)
    a_ref[...] = a
    lane = lax.broadcasted_iota(jnp.int32, (n, 2 * HD), 1)
    low_half = lane < HD
    zero = jnp.zeros((n, 2 * HD), BF16)
    mask = key_mask(open_ref, n)
    for t in range(width // (2 * HD)):
        spots = [slice(s * width + t * 2 * HD, s * width + (t + 1) * 2 * HD) for s in range(3)]
        q = rotate(mm(a, wqkv_ref[spots[0], :], NT), table_ref, 1)
        q = (q * HD ** (-0.5)).astype(BF16)
        k = rotate(mm(a, wqkv_ref[spots[1], :], NT), table_ref, 1).astype(BF16)
        v = mm(a, wqkv_ref[spots[2], :], NT).astype(BF16)
        qkv_ref[:, spots[0]] = q
        qkv_ref[:, spots[1]] = k
        qkv_ref[:, spots[2]] = v
        mixed = []
        for e in range(2):
            q_one = jnp.where(low_half if e == 0 else ~low_half, q, zero)
            s = jnp.where(mask, mm(k, q_one, NT), LOW)
            top = jnp.max(s, axis=0, keepdims=True)
            raised = jnp.exp(s - top)
            total = jnp.sum(raised, axis=0, keepdims=True)
            lse_ref[2 * t + e : 2 * t + e + 1, :] = top + jnp.log(total)
            prob = (raised / total).astype(BF16)
            mixed.append(mm(prob, v, TN))
        o_ref[:, t * 2 * HD : (t + 1) * 2 * HD] = jnp.where(low_half, mixed[0], mixed[1]).astype(BF16)
    part_ref[...] = mm(o_ref[...], wout_ref[...])


def ffn_fwd(h_ref, p_ref, r_ref, gain_ref, wgu_ref, wd_ref, h1_ref, *refs):
    h = h_ref[...] + (p_ref[...] + r_ref[...])
    h1_ref[...] = h
    b = (h * inv_rms(h) * gain_ref[...]).astype(BF16)
    b_ref, gu_ref, hid_ref, part_ref = refs
    b_ref[...] = b
    width = wd_ref.shape[0]
    step = min(width, 256)
    for f in range(0, width, step):
        gate = mm(b, wgu_ref[0, :, f : f + step])
        up = mm(b, wgu_ref[1, :, f : f + step])
        gu_ref[:, f : f + step] = gate
        gu_ref[:, width + f : width + f + step] = up
        hid_ref[:, f : f + step] = (gate * jax.nn.sigmoid(gate) * up).astype(BF16)
    part_ref[...] = mm(hid_ref[...], wd_ref[...])


def ffn_bwd(first, *refs):
    if first:
        g_ref, gu_ref, wgu_ref, wd_ref = refs[:4]
        refs = refs[4:]
        gm = g_ref[...]
    else:
        g1_ref, p_ref, r_ref, hin_ref, gain_ref, gu_ref, wgu_ref, wd_ref = refs[:8]
        refs = refs[8:]
        grad, gain_grad = close_norm(g1_ref[...], p_ref, r_ref, hin_ref, gain_ref)
        refs[0][...] = grad
        refs[1][...] = gain_grad
        gm = grad.astype(BF16)
        refs[2][...] = gm
        refs = refs[3:]
    dgu_ref, part_ref = refs
    width = wd_ref.shape[0]
    step = min(width, 256)
    for f in range(0, width, step):
        dhid = mm(gm, wd_ref[f : f + step, :], NT)
        gate = gu_ref[:, f : f + step]
        up = gu_ref[:, width + f : width + f + step]
        sig = jax.nn.sigmoid(gate)
        dgu_ref[:, f : f + step] = (dhid * up * (sig * (1.0 + gate * (1.0 - sig)))).astype(BF16)
        dgu_ref[:, width + f : width + f + step] = (dhid * (gate * sig)).astype(BF16)
    part_ref[...] = mm(dgu_ref[:, :width], wgu_ref[0], NT) + mm(dgu_ref[:, width:], wgu_ref[1], NT)


def close_norm(g, p_ref, r_ref, h_ref, gain_ref):
    grad = p_ref[...] + r_ref[...]
    h = h_ref[...]
    scale = inv_rms(h)
    normed = h * scale
    gain_grad = jnp.sum(grad * normed, axis=0, keepdims=True)
    return g + norm_back(grad, normed, scale, gain_ref[...]), gain_grad


def attn_bwd(
    g_ref, p_ref, r_ref, h1_ref, gain_ref, wqkv_ref, wout_ref, table_ref, open_ref, qkv_ref, lse_ref,
    g1_ref, gain_grad_ref, ga_ref, dqkv_ref, part_ref,
):
    g1, gain_grad = close_norm(g_ref[...].astype(F32), p_ref, r_ref, h1_ref, gain_ref)
    g1_ref[...] = g1
    gain_grad_ref[...] = gain_grad
    ga = g1.astype(BF16)
    ga_ref[...] = ga
    n = ga.shape[0]
    width = wout_ref.shape[0]
    lane = lax.broadcasted_iota(jnp.int32, (n, 2 * HD), 1)
    low_half = lane < HD
    zero = jnp.zeros((n, 2 * HD), BF16)
    mask = key_mask(open_ref, n)
    for t in range(width // (2 * HD)):
        spots = [slice(s * width + t * 2 * HD, s * width + (t + 1) * 2 * HD) for s in range(3)]
        q = qkv_ref[:, spots[0]]
        k = qkv_ref[:, spots[1]]
        v = qkv_ref[:, spots[2]]
        dout = mm(ga, wout_ref[t * 2 * HD : (t + 1) * 2 * HD, :], NT).astype(BF16)
        dq, dk, dv = [], [], []
        for e in range(2):
            mine = low_half if e == 0 else ~low_half
            q_one = jnp.where(mine, q, zero)
            d_one = jnp.where(mine, dout, zero)
            s = jnp.where(mask, mm(k, q_one, NT), LOW)
            prob = jnp.exp(s - lse_ref[2 * t + e : 2 * t + e + 1, :])
            dprob = mm(v, d_one, NT)
            delta = jnp.sum(prob * dprob, axis=0, keepdims=True)
            ds = (prob * (dprob - delta)).astype(BF16)
            dv.append(mm(prob.astype(BF16), dout))
            dk.append(mm(ds, q))
            dq.append(mm(ds, k, TN))
        dq = jnp.where(low_half, dq[0], dq[1]) * HD ** (-0.5)
        dk = jnp.where(low_half, dk[0], dk[1])
        dv = jnp.where(low_half, dv[0], dv[1])
        dqkv_ref[:, spots[0]] = rotate(dq, table_ref, -1).astype(BF16)
        dqkv_ref[:, spots[1]] = rotate(dk, table_ref, -1).astype(BF16)
        dqkv_ref[:, spots[2]] = dv.astype(BF16)
    part_ref[...] = mm(dqkv_ref[...], wqkv_ref[...])


def close_layer(g1_ref, p_ref, r_ref, h_ref, gain_ref, out_ref, gain_grad_ref):
    grad, gain_grad = close_norm(g1_ref[...], p_ref, r_ref, h_ref, gain_ref)
    out_ref[...] = grad
    gain_grad_ref[...] = gain_grad


def halves_of(half_ref, dim):
    one = dim // 2
    return [pl.ds(pl.multiple_of(half_ref[s] * one, one), one) for s in range(2)]


def grad_rows(spans, half_ref, *refs):
    chunks = (len(refs) - 2) // 2
    lefts, rights = refs[:chunks], refs[chunks : 2 * chunks]
    outs = refs[2 * chunks :]
    for s, spot in enumerate(halves_of(half_ref, rights[0].shape[1])):
        for out, picks in zip(outs, spans):
            at = 0
            for lo, hi in picks:
                total = None
                for left, right in zip(lefts, rights):
                    term = mm(left[:, lo:hi], right[:, spot], TN)
                    total = term if total is None else total + term
                out[s, at : at + hi - lo, :] = total
                at += hi - lo


def grad_columns(spans, half_ref, *refs):
    chunks = (len(refs) - 2) // 2
    lefts, rights = refs[:chunks], refs[chunks : 2 * chunks]
    outs = refs[2 * chunks :]
    for s, spot in enumerate(halves_of(half_ref, lefts[0].shape[1])):
        for out, picks in zip(outs, spans):
            at = 0
            for lo, hi in picks:
                total = None
                for left, right in zip(lefts, rights):
                    term = mm(left[:, spot], right[:, lo:hi], TN)
                    total = term if total is None else total + term
                out[s, :, at : at + hi - lo] = total
                at += hi - lo


def whole_pass(dims, *refs):
    n, dim, wa, wf, layers, chunks = dims
    la, lf, half = wa // 2, wf // 2, dim // 2
    refs = list(refs)

    def take(count):
        got = refs[:count]
        del refs[:count]
        return got

    gains_ref, tables, valid_ref, first_ref, heights_ref, labels_ref = take(6)
    tokens, cotangent, w_qkv, w_out, w_gate_up, w_down = take(6)
    output, token_grad, table_out, gain_out, down_out, gate_up_out, out_out, qkv_out = take(8)
    wgu_st, wd_st, wqkv_st, wout_st, h_st, h1_st, qkv_st, lse_st, o_st, last_st = take(10)
    wgu, wd, wqkv, wout = take(4)
    hs, h1s, qkvs, os, lses = take(5)
    ysend, yrecv, gs, gm, ab, hid, dgu = take(7)
    oth_g, oth_s, cr_d, cr_g, cr_a = take(5)
    os_d, os_g, os_a, ok_d, ok_g, ok_a = take(6)
    xr_d, xr_g, xr_a, z1_d, z1_g, z1_a, z2_d, z2_g, z2_a, small = take(10)
    open_ref, raw_g, total_g, firsts_ref = take(4)
    load_sem, ys_sem, yr_sem, cs_sem, cr_sem, xs_sem, xr_sem = take(7)
    z1s, z1r, z2s, z2r, z3s, z3r, store_sem, row_sem, rows_s, rows_r, small_s, small_r = take(12)
    x_free, z1_free, z2_free, c_free = take(4)

    tp = lax.axis_index("tp")
    x = lax.axis_index("dpi")
    z = lax.axis_index("dpo")
    core = lax.rem(tp, 2)
    to_core = {"tp": tp + 1 - 2 * core}
    to_chip = {"tp": lax.rem(tp + 2, 4)}
    to_x = {"dpi": 1 - x}
    to_mate = {"dpo": z + 1 - 2 * lax.rem(z, 2)}
    to_inner = {"dpo": 3 - z}
    outer = (z == 0) | (z == 3)
    inner = (z == 1) | (z == 2)
    far = [{"dpo": lax.rem(z + k, 4)} for k in (1, 2, 3)]

    barrier = pltpu.get_barrier_semaphore()
    for peer in [to_core, to_chip, to_x] + far:
        pl.semaphore_signal(barrier, inc=1, device_id=peer, device_id_type=MESH)
    loads = {}

    def load(key, src, dst, slot):
        copy = pltpu.make_async_copy(src, dst, load_sem.at[slot])
        copy.start()
        loads[key] = copy

    def need(*keys):
        for key in keys:
            if key in loads:
                loads.pop(key).wait()

    def rows(c):
        return pl.ds(c * n, n)

    def load_ffn_weights():
        load("wgu", wgu_st, wgu, 0)
        load("wd", wd_st, wd, 1)

    def load_attn_weights():
        load("wqkv", wqkv_st, wqkv, 2)
        load("wout", wout_st, wout, 3)

    def load_h1(c):
        load(("h1", c), h1_st.at[0, c], h1s.at[c], 4 + c)

    def load_qkv(c):
        load(("qkv", c), qkv_st.at[c], qkvs.at[c], 6 + c)
        load(("lse", c), lse_st.at[c], lses.at[c], 8 + c)

    def load_o(c):
        load(("o", c), o_st.at[rows(c)], os.at[rows(c)], 10 + c)

    def load_h(c):
        load(("h", c), h_st.at[c], hs.at[c], 12 + c)

    top = layers - 1

    def own_rows(ref, c):
        return ref.at[pl.ds(pl.multiple_of((core * chunks + c) * n, n), n)]

    def own_attn(l):
        for t in range(3):
            load(("own", "a", t), w_qkv.at[l, t], wqkv.at[pl.ds(t * wa, la)], 17 + t)
        load(("own", "a", 3), w_out.at[l], wout.at[pl.ds(0, la)], 20)

    def own_ffn(l):
        load(("own", "g", 0), w_gate_up.at[l], raw_g, 21)
        load(("own", "d", 0), w_down.at[l], wd.at[pl.ds(0, lf)], 23)

    own_attn(0)
    for c in range(chunks):
        load(("token", c), own_rows(tokens, c), gm.at[rows(c)], 14 + c)
    own_ffn(0)

    def remote(src, dst, send, recv, to):
        return pltpu.make_async_remote_copy(
            src_ref=src, dst_ref=dst, send_sem=send, recv_sem=recv, device_id=to, device_id_type=MESH
        )

    turn = [0] * chunks

    def y_copy(c, k):
        return remote(ysend.at[c], yrecv.at[k % 2, c], ys_sem.at[c], yr_sem.at[k % 2, c], to_chip)

    def y_start(c):
        y_copy(c, turn[c]).start()

    def y_sum(c):
        copy = y_copy(c, turn[c])
        copy.wait()
        got = ysend[c] + yrecv[turn[c] % 2, c]
        turn[c] += 1
        return got

    def gain_of(l, i):
        return gains_ref[l, i : i + 1, :]

    def add_gain(l, i, c, term):
        k = 2 + 2 * l + i
        spot = (z, x, core, slice(k, k + 1), slice(None))
        small[spot] = term if c == 0 else small[spot] + term

    def close(l, i, c, g, h):
        grad = y_sum(c)
        scale = inv_rms(h)
        normed = h * scale
        add_gain(l, i, c, jnp.sum(grad * normed, axis=0, keepdims=True))
        return g + norm_back(grad, normed, scale, gain_of(l, i))

    def prepare(c):
        at = core * chunks + c
        lane = lax.broadcasted_iota(jnp.int32, (1, n), 1)
        is_open = (lane < 1 + COLS * heights_ref[at]) & (valid_ref[pl.ds(at, 1), :] == 1)
        diagonal = lax.broadcasted_iota(jnp.int32, (n, n), 0) == lax.broadcasted_iota(jnp.int32, (n, n), 1)
        column = jnp.where(diagonal, jnp.where(is_open, 1.0, 0.0), 0.0)
        open_ref[c] = jnp.sum(column, axis=1, keepdims=True)
        slot = (z * groups[1] + x) * 2 * chunks + at
        lane = lax.broadcasted_iota(jnp.int32, (1, dim), 1)
        label = jnp.where(lane == slot, labels_ref[at], 0).astype(F32)
        spot = (z, x, core, slice(6, 7), slice(None))
        small[spot] = label if c == 0 else small[spot] + label

    groups = small.shape[:2]
    small[z, x, core] = jnp.zeros((8, dim), F32)

    def ffn_a(l, c):
        spot = rows(c)
        if l == top:
            need(("cot", c))
            gs[c] = gm[spot, :].astype(F32)
            h = hs_next(c)
            h1s[c] = h
            load(("stash", c), h1s.at[c], h1_st.at[top, c], 28 + c)
        else:
            need(("h", c))
            g = close(l + 1, 0, c, gs[c], hs[c])
            gs[c] = g
            gm[spot, :] = g.astype(BF16)
            load_h(c)
        need(("h1", c), "wgu", "wd")
        h1 = h1s[c]
        b = (h1 * inv_rms(h1) * gain_of(l, 1)).astype(BF16)
        ab[spot, :] = b
        step = min(wf, 256)
        for f in range(0, wf, step):
            gate = mm(b, wgu[0, :, f : f + step])
            up = mm(b, wgu[1, :, f : f + step])
            dhid = mm(gm[spot, :], wd[f : f + step, :], NT)
            sig = jax.nn.sigmoid(gate)
            silu = gate * sig
            hid[spot, f : f + step] = (silu * up).astype(BF16)
            dgu[spot, f : f + step] = (dhid * up * (sig * (1.0 + gate * (1.0 - sig)))).astype(BF16)
            dgu[spot, wf + f : wf + f + step] = (dhid * silu).astype(BF16)

    later = {("fb", 1, 0), ("fb", 1, 1), ("po", 0), ("po", 1)}

    def ffn_done(*what):
        if what in later:
            later.discard(what)
            if not later:
                load_ffn_weights()

    def ffn_b(l, c):
        spot = rows(c)
        ysend[c] = mm(dgu[spot, :wf], wgu[0], NT) + mm(dgu[spot, wf:], wgu[1], NT)
        y_start(c)
        ffn_done("fb", l, c)

    def last_sum(c):
        need(("last", c - 1))
        spare = ok_g.at[0, pl.ds(0, n), pl.ds(0, dim)]
        spare[...] = mm(hid[rows(c), :], wd[...])
        load(("last", c), spare, last_st.at[c], 30)
        ffn_done("po", c)

    def attn(l, c):
        spot = rows(c)
        g1 = close(l, 1, c, gs[c], h1s[c])
        gs[c] = g1
        if l > 0:
            need(("stash", c))
            load_h1(c)
        gm[spot, :] = g1.astype(BF16)
        need("wqkv", "wout", ("qkv", c), ("lse", c))
        lane = lax.broadcasted_iota(jnp.int32, (n, 2 * HD), 1)
        low_half = lane < HD
        zero = jnp.zeros((n, 2 * HD), BF16)
        mask = key_mask(open_ref.at[c], n)
        ga = gm[spot, :]
        for t in range(wa // (2 * HD)):
            spots = [slice(s * wa + t * 2 * HD, s * wa + (t + 1) * 2 * HD) for s in range(3)]
            q, k, v = [qkvs[c, :, s] for s in spots]
            dout = mm(ga, wout[t * 2 * HD : (t + 1) * 2 * HD, :], NT).astype(BF16)
            dq, dk, dv = [], [], []
            for e in range(2):
                mine = low_half if e == 0 else ~low_half
                s = jnp.where(mask, mm(k, jnp.where(mine, q, zero), NT), LOW)
                prob = jnp.exp(s - lses[c, 2 * t + e : 2 * t + e + 1, :])
                dprob = mm(v, jnp.where(mine, dout, zero), NT)
                delta = jnp.sum(prob * dprob, axis=0, keepdims=True)
                ds = (prob * (dprob - delta)).astype(BF16)
                dv.append(mm(prob.astype(BF16), dout))
                dk.append(mm(ds, q))
                dq.append(mm(ds, k, TN))
            dq = jnp.where(low_half, dq[0], dq[1]) * HD ** (-0.5)
            dk = jnp.where(low_half, dk[0], dk[1])
            dv = jnp.where(low_half, dv[0], dv[1])
            dgu[spot, spots[0]] = rotate(dq, tables, -1).astype(BF16)
            dgu[spot, spots[1]] = rotate(dk, tables, -1).astype(BF16)
            dgu[spot, spots[2]] = dv.astype(BF16)
        ysend[c] = mm(dgu[spot, : 3 * wa], wqkv[...])
        y_start(c)
        if l > 0:
            load_qkv(c)
        need(("h", c))
        h = hs[c]
        ab[spot, :] = (h * inv_rms(h) * gain_of(l, 0)).astype(BF16)

    spans = [pl.ds(pl.multiple_of((1 - x) * half, half), half), pl.ds(pl.multiple_of(x * half, half), half)]
    kinds = {
        "d": (oth_s.at[:, pl.ds(0, lf)], cr_d, os_d, ok_d, xr_d, z1_d, z2_d),
        "g": (oth_g, cr_g, os_g, ok_g, xr_g, z1_g, z2_g),
        "a": (oth_s, cr_a, os_a, ok_a, xr_a, z1_a, z2_a),
    }
    index = {"d": 0, "g": 1, "a": 2}
    units = []
    for kind in kinds:
        at = 0
        for size in PIECES[kind]:
            target = {"d": down_out, "g": gate_up_out, "a": out_out if at < la else qkv_out}[kind]
            base = la if kind == "a" and at >= la else 0
            units.append((kind, pl.ds(at, size), target, pl.ds(at - base, size)))
            at += size

    def c_copy(kind):
        at = index[kind]
        return remote(kinds[kind][0], kinds[kind][1], cs_sem.at[at], cr_sem.at[at], to_core)

    def piece(kind, s, shard, put):
        if kind == "d":
            put(slice(None), slice(None), mm(hid[:, shard * lf : (shard + 1) * lf], gm[:, spans[s]], TN))
        elif kind == "g":
            for t in range(2):
                cols = slice(t * wf + shard * lf, t * wf + (shard + 1) * lf)
                put(slice(None), slice(t * lf, (t + 1) * lf), mm(ab[:, spans[s]], dgu[:, cols], TN))
        else:
            put(slice(0, la), slice(None), mm(os[:, shard * la : (shard + 1) * la], gm[:, spans[s]], TN))
            for t in range(3):
                cols = slice(t * wa + shard * la, t * wa + (shard + 1) * la)
                put(slice((t + 1) * la, (t + 2) * la), slice(None), mm(dgu[:, cols], ab[:, spans[s]], TN))

    def put_in(ref, *lead):
        def put(r, c, value):
            ref[lead + (r, c)] = value

        return put

    arrived = set()

    def grad_other(l, kind):
        if kind == "a":
            need(("o", 0), ("o", 1))
        if "c" not in arrived:
            pl.semaphore_wait(c_free, 1)
            arrived.add("c")
        for s in range(2):
            piece(kind, s, 1, put_in(kinds[kind][0], s))
        c_copy(kind).start()

    def grad_own(l, kind):
        if kind == "a":
            need(("o", 0), ("o", 1))
        if l < top and kind == "g":
            need(("last", chunks - 1))
        piece(kind, 0, 0, put_in(kinds[kind][2]))
        piece(kind, 1, 0, put_in(kinds[kind][3], l))

    def x_copy(l, u):
        kind, spot = units[u][:2]
        return remote(kinds[kind][2].at[spot], kinds[kind][4].at[spot], xs_sem.at[l, u], xr_sem.at[l, u], to_x)

    def core_sum(l, u):
        kind, spot = units[u][:2]
        _, cr, own_s, own_k, *_ = kinds[kind]
        if (l, kind) not in arrived:
            c_copy(kind).wait()
            arrived.add((l, kind))
        own_s[spot, :] = own_s[spot, :] + cr[0, spot, :]
        if l < top:
            pl.semaphore_wait(x_free.at[u], 1)
        x_copy(l, u).start()
        own_k[l, spot, :] = own_k[l, spot, :] + cr[1, spot, :]

    def z1_copy(l, u):
        kind, spot = units[u][:2]
        return remote(kinds[kind][3].at[l, spot], kinds[kind][5].at[spot], z1s.at[l, u], z1r.at[l, u], to_mate)

    def z2_copy(l, u):
        kind, spot = units[u][:2]
        return remote(kinds[kind][3].at[l, spot], kinds[kind][6].at[spot], z2s.at[l, u], z2r.at[l, u], to_inner)

    def total_of(l, u):
        kind, spot, target, place = units[u]
        source = total_g if kind == "g" else kinds[kind][6]
        return source.at[spot], target.at[l, place]

    def z3_copy(l, u):
        source, target = total_of(l, u)
        return remote(source, target, z3s.at[l, u], z3r.at[l, u], to_mate)

    def store_copy(l, u):
        source, target = total_of(l, u)
        return pltpu.make_async_copy(source, target, store_sem.at[l, u])

    def x_sum(l, u):
        kind, spot = units[u][:2]
        keep, got = kinds[kind][3], kinds[kind][4]
        x_copy(l, u).wait()
        keep[l, spot, :] = keep[l, spot, :] + got[spot, :]
        if l > 0:
            pl.semaphore_signal(x_free.at[u], inc=1, device_id=to_x, device_id_type=MESH)

        @pl.when(outer)
        def _():
            if l < top:
                pl.semaphore_wait(z1_free.at[u], 1)
            z1_copy(l, u).start()

    def z_one(l, u):
        kind, spot = units[u][:2]
        keep, got = kinds[kind][3], kinds[kind][5]

        @pl.when(inner)
        def _():
            z1_copy(l, u).wait_recv()
            keep[l, spot, :] = keep[l, spot, :] + got[spot, :]
            if l > 0:
                pl.semaphore_signal(z1_free.at[u], inc=1, device_id=to_mate, device_id_type=MESH)
            if l < top:
                pl.semaphore_wait(z2_free.at[u], 1)
            z2_copy(l, u).start()

    def z_two(l, u):
        kind, spot = units[u][:2]
        keep, got = kinds[kind][3], kinds[kind][6]

        @pl.when(inner)
        def _():
            z2_copy(l, u).wait()
            total = got[spot, :] + keep[l, spot, :]
            if kind == "g":
                for t in range(2):
                    total_g[spot, t, :] = total[:, t * lf : (t + 1) * lf]
            else:
                got[spot, :] = total
            z3_copy(l, u).start()
            store_copy(l, u).start()

    def z_end(l, u):
        @pl.when(inner)
        def _():
            z3_copy(l, u).wait_send()
            store_copy(l, u).wait()
            if l > 0:
                pl.semaphore_signal(z2_free.at[u], inc=1, device_id=to_inner, device_id_type=MESH)

        @pl.when(outer)
        def _():
            z1_copy(l, u).wait_send()
            z3_copy(l, u).wait_recv()

    def row_copies(src, dst, i, c):
        spot = pl.ds(pl.multiple_of((core * chunks + c) * n, n), n)
        return (
            pltpu.make_async_copy(src, dst.at[spot], row_sem.at[i, c]),
            remote(src, dst.at[spot], rows_s.at[i, c], rows_r.at[i, c], to_core),
        )

    def share_rows(src, dst, i, c):
        for copy in row_copies(src, dst, i, c):
            copy.start()

    def end_rows(src, dst, i, c):
        for copy in row_copies(src, dst, i, c):
            copy.wait()

    def token(c):
        need(("h", c))
        g = close(0, 0, c, gs[c], hs[c])
        small[z, x, core, c : c + 1, :] = g[0:1, :]
        row = lax.broadcasted_iota(jnp.int32, (n, dim), 0)
        gs[c] = jnp.where(row == 0, 0.0, g)
        share_rows(gs.at[c], token_grad, 0, c)

    def pout_copy(c):
        k = turn[c] % 2
        return remote(last_st.at[c], yrecv.at[k, c], ys_sem.at[c], yr_sem.at[k, c], to_chip)

    def start_output(c):
        pout_copy(c).start()
        load(("pout", c), last_st.at[c], ysend.at[c], 4 + c)
        load(("out", c), h1_st.at[top, c], hs.at[c], 12 + c)

    def end_output(c):
        need(("pout", c), ("out", c))
        pout_copy(c).wait()
        hs[c] = hs[c] + (ysend[c] + yrecv[turn[c] % 2, c])
        share_rows(hs.at[c], output, 1, c)

    def small_core():
        return remote(small.at[z, x, core], small.at[z, x, core], small_s.at[0], small_r.at[0], to_core)

    def small_x():
        return remote(small.at[z, x], small.at[z, x], small_s.at[1], small_r.at[1], to_x)

    def small_z(k):
        return remote(small.at[z], small.at[z], small_s.at[2 + k], small_r.at[2 + k], far[k])

    def small_got(k):
        back = lax.rem(z + 3 - k, 4)
        return remote(small.at[back], small.at[back], small_s.at[2 + k], small_r.at[2 + k], far[k])

    def attn_copy(part):
        rows_of = [pl.ds(0, 3 * la), pl.ds(3 * la, la)][part]
        return remote(
            oth_s.at[:, rows_of], cr_a.at[:, rows_of], cs_sem.at[2 + part], cr_sem.at[2 + part], to_core
        )

    def weight_stage(l, kind):
        if kind == "a":
            need(*[("own", "a", t) for t in range(4)])
            for s in range(2):
                lanes = slice(s * half, (s + 1) * half)
                for t in range(3):
                    oth_s[s, t * la : (t + 1) * la, :] = wqkv[t * wa : t * wa + la, lanes].astype(F32)
                oth_s[s, 3 * la :, :] = wout[:la, lanes].astype(F32)
        elif kind == "g":
            need(("own", "g", 0))
            step = half // 3
            for s in range(2):
                for r in range(0, half, step):
                    for t in range(2):
                        shard = raw_g[s * half + r : s * half + r + step, t, :]
                        wgu[t, s * half + r : s * half + r + step, :lf] = shard
                        oth_g[s, r : r + step, t * lf : (t + 1) * lf] = shard.astype(F32)
        else:
            need(("own", "d", 0))
            for s in range(2):
                oth_s[s, :lf, :] = wd[:lf, s * half : (s + 1) * half].astype(F32)

    def weight_send(l, kind):
        weight_stage(l, kind)
        if kind == "a":
            attn_copy(0).start()
            attn_copy(1).start()
        else:
            c_copy(kind).start()

    def weight_take(l, kind, part=0):
        if kind == "a":
            attn_copy(part).wait()
        else:
            c_copy(kind).wait()
        for s in range(2):
            lanes = slice(s * half, (s + 1) * half)
            if kind == "a" and part == 0:
                for t in range(3):
                    wqkv[t * wa + la : (t + 1) * wa, lanes] = cr_a[s, t * la : (t + 1) * la, :].astype(BF16)
            elif kind == "a":
                wout[la:, lanes] = cr_a[s, 3 * la :, :].astype(BF16)
            elif kind == "g":
                for t in range(2):
                    wgu[t, lanes, lf:] = cr_g[s, :, t * lf : (t + 1) * lf].astype(BF16)
            else:
                wd[lf:, lanes] = cr_d[s].astype(BF16)

    def hs_next(c):
        return base_of(c) + y_sum(c)

    def base_of(c):
        return hs[c] if turn[c] % 2 == 0 else h1s[c]

    def attn_up_start(l, c):
        spot = rows(c)
        if l == 0:
            need(("token", c))
            h = gm[spot, :].astype(F32)
            row = lax.broadcasted_iota(jnp.int32, (n, dim), 0)
            h = jnp.where(row == 0, first_ref[pl.ds(core * chunks + c, 1), :], h)
        else:
            h = hs_next(c)
            need(("st_h", c), ("st_qkv", c), ("st_lse", c), ("st_o", c))
        hs[c] = h
        ab[spot, :] = (h * inv_rms(h) * gain_of(l, 0)).astype(BF16)

    def attn_up_heads(c, pairs):
        spot = rows(c)
        a = ab[spot, :]
        lane = lax.broadcasted_iota(jnp.int32, (n, 2 * HD), 1)
        low_half = lane < HD
        zero = jnp.zeros((n, 2 * HD), BF16)
        mask = key_mask(open_ref.at[c], n)
        for t in pairs:
            spots = [slice(s * wa + t * 2 * HD, s * wa + (t + 1) * 2 * HD) for s in range(3)]
            q = rotate(mm(a, wqkv[spots[0], :], NT), tables, 1)
            q = (q * HD ** (-0.5)).astype(BF16)
            k = rotate(mm(a, wqkv[spots[1], :], NT), tables, 1).astype(BF16)
            v = mm(a, wqkv[spots[2], :], NT).astype(BF16)
            for part, value in zip(spots, (q, k, v)):
                qkvs[c, :, part] = value
            mixed = []
            for e in range(2):
                q_one = jnp.where(low_half if e == 0 else ~low_half, q, zero)
                s = jnp.where(mask, mm(k, q_one, NT), LOW)
                peak = jnp.max(s, axis=0, keepdims=True)
                raised = jnp.exp(s - peak)
                total = jnp.sum(raised, axis=0, keepdims=True)
                lses[c, 2 * t + e : 2 * t + e + 1, :] = peak + jnp.log(total)
                mixed.append(mm((raised / total).astype(BF16), v, TN))
            os[spot, t * 2 * HD : (t + 1) * 2 * HD] = jnp.where(low_half, mixed[0], mixed[1]).astype(BF16)

    def attn_up_end(l, c):
        spot = rows(c)
        ysend[c] = mm(os[spot, :], wout[...])
        y_start(c)
        if l == 0:
            load(("st_h", c), hs.at[c], h_st.at[c], 12 + c)
            load(("st_qkv", c), qkvs.at[c], qkv_st.at[c], 6 + c)
            load(("st_lse", c), lses.at[c], lse_st.at[c], 8 + c)
            load(("st_o", c), os.at[rows(c)], o_st.at[rows(c)], 10 + c)

    def ffn_up(c):
        spot = rows(c)
        h1 = hs_next(c)
        h1s[c] = h1
        b = (h1 * inv_rms(h1) * gain_of(0, 1)).astype(BF16)
        step = min(wf, 256)
        for f in range(0, wf, step):
            gate = mm(b, wgu[0, :, f : f + step])
            up = mm(b, wgu[1, :, f : f + step])
            hid[spot, f : f + step] = (gate * jax.nn.sigmoid(gate) * up).astype(BF16)
        ysend[c] = mm(hid[spot, :], wd[...])
        y_start(c)
        load(("stash", c), h1s.at[c], h1_st.at[0, c], 28 + c)

    pairs = wa // (2 * HD)
    alone = la // (2 * HD)
    weight_stage(0, "a")
    pl.semaphore_wait(barrier, 6)
    attn_copy(0).start()
    attn_copy(1).start()
    for c in range(chunks):
        prepare(c)
        attn_up_start(0, c)
        attn_up_heads(c, range(alone))
    weight_take(0, "a", 0)
    attn_up_heads(0, range(alone, pairs))
    weight_take(0, "a", 1)
    attn_up_end(0, 0)
    weight_send(0, "g")
    attn_up_heads(1, range(alone, pairs))
    attn_up_end(0, 1)
    weight_send(0, "d")
    for c in range(chunks):
        load(("cot", c), own_rows(cotangent, c), gm.at[rows(c)], 14 + c)
    load("st_wqkv", wqkv, wqkv_st, 2)
    load("st_wout", wout, wout_st, 3)
    weight_take(0, "d")
    weight_take(0, "g")
    need("st_wqkv", "st_wout")
    own_attn(1)
    ffn_up(0)
    weight_send(1, "a")
    ffn_up(1)
    load("st_wgu", wgu, wgu_st, 0)
    load("st_wd", wd, wd_st, 1)
    weight_take(1, "a", 0)
    weight_take(1, "a", 1)
    need("st_wgu", "st_wd")
    own_ffn(1)
    for c in range(chunks):
        attn_up_start(1, c)
        attn_up_heads(c, range(pairs))
        attn_up_end(1, c)
        need(("stash", c))
        if c == 0:
            weight_send(1, "d")
            weight_send(1, "g")
    weight_take(1, "d")
    weight_take(1, "g")
    pl.semaphore_signal(c_free, inc=1, device_id=to_core, device_id_type=MESH)

    def start_small():
        small_core().start()

    def move_small():
        small_core().wait_send()
        spot = small.at[z, x, 1 - core]
        remote(spot, spot, small_s.at[0], small_r.at[0], to_core).wait_recv()
        small_x().start()

    def spread_small():
        small_x().wait_send()
        spot = small.at[z, 1 - x]
        remote(spot, spot, small_s.at[1], small_r.at[1], to_x).wait_recv()
        for k in range(3):
            small_z(k).start()

    def end_small():
        for k in range(3):
            small_z(k).wait_send()
            small_got(k).wait_recv()
        everyone = [(i, j, k) for i in range(groups[0]) for j in range(groups[1]) for k in range(2)]
        total = None
        for at, place in enumerate(everyone):
            block = small[place]
            total = block if total is None else total + block
            firsts_ref[at * chunks : (at + 1) * chunks, :] = small[place + (slice(0, chunks), spans[1])]
        for l in range(layers):
            gain_out[l] = total[2 + 2 * l : 4 + 2 * l, :]
        slots = firsts_ref.shape[0]
        label = total[6:7, :slots].astype(jnp.int32)
        classes, step = table_out.shape[0], 256
        for at in range(0, classes, step):
            size = min(step, classes - at)
            same = lax.broadcasted_iota(jnp.int32, (size, slots), 0) + at == label
            spare = oth_s.at[at // (4 * la), pl.ds(at % (4 * la), size)]
            spare[...] = lax.dot_general(
                jnp.where(same, 1.0, 0.0), firsts_ref[...], NN,
                precision=lax.Precision.HIGHEST, preferred_element_type=F32,
            )
            load(("table", at), spare, table_out.at[pl.ds(at, size)], 24 + at // step)

    def attn_down(l, c):
        attn(l, c)
        if (l, c) == (1, chunks - 1):
            load_attn_weights()

    acts = {
        "fa": ffn_a, "fb": ffn_b, "po": last_sum, "attn": attn_down, "go": grad_other, "gw": grad_own, "cu": core_sum, "xs": x_sum,
        "z1": z_one, "z2": z_two, "ze": z_end, "tok": token, "so": start_output, "eo": end_output,
        "sc": start_small, "sx": move_small, "sz": spread_small, "sw": end_small,
    }
    left = {("go", 1, "a"), ("gw", 1, "a")}
    for name, *at in ORDER:
        acts[name](*at)
        if left:
            left.discard((name, *at))
            if not left:
                for c in range(chunks):
                    load_o(c)
    need(*list(loads))
    for c in range(chunks):
        end_rows(gs.at[c], token_grad, 0, c)
        end_rows(hs.at[c], output, 1, c)


def call(body, outs, args, flops, limit=40, smem=0, scratch=()):
    moved = sum(x.size * x.dtype.itemsize for x in args) + sum(
        int(np.prod(s)) * np.dtype(d).itemsize for s, d in outs
    )
    spec = pl.BlockSpec(memory_space=pltpu.VMEM)
    got = pl.pallas_call(
        body,
        out_shape=[jax.ShapeDtypeStruct(s, d) for s, d in outs],
        in_specs=[pl.BlockSpec(memory_space=pltpu.SMEM)] * smem + [spec] * (len(args) - smem),
        out_specs=[spec] * len(outs),
        scratch_shapes=list(scratch),
        compiler_params=pltpu.CompilerParams(vmem_limit_bytes=limit * 2**20),
        cost_estimate=pl.CostEstimate(flops=int(flops), bytes_accessed=int(moved), transcendentals=0),
    )(*args)
    return list(got)


def call_whole(sizes, n, dim, wa, wf, layers, chunks, classes, fixed, numbers, moved):
    la, lf, half = wa // 2, wf // 2, dim // 2
    groups = sizes["dpo"], sizes["dpi"]
    outs = [
        ((2 * chunks * n, dim), F32),
        ((2 * chunks * n, dim), F32),
        ((classes, half), F32),
        ((layers, 2, dim), F32),
        ((layers, lf, half), F32),
        ((layers, half, 2, lf), F32),
        ((layers, la, half), F32),
        ((layers, 3 * la, half), F32),
        ((2, dim, wf), BF16),
        ((wf, dim), BF16),
        ((3 * wa, dim), BF16),
        ((wa, dim), BF16),
        ((chunks, n, dim), F32),
        ((layers, chunks, n, dim), F32),
        ((chunks, n, 3 * wa), BF16),
        ((chunks, 8, n), F32),
        ((chunks * n, wa), BF16),
        ((chunks, n, dim), F32),
    ]
    d, g, a = (lf, half), (half, 2 * lf), (4 * la, half)
    f, h = lambda *s: pltpu.VMEM(s, F32), lambda *s: pltpu.VMEM(s, BF16)
    dma, count = pltpu.SemaphoreType.DMA, pltpu.SemaphoreType.REGULAR
    units = sum(len(k) for k in PIECES.values())
    scratch = [h(2, dim, wf), h(wf, dim), h(3 * wa, dim), h(wa, dim)]
    scratch += [f(chunks, n, dim), f(chunks, n, dim), h(chunks, n, 3 * wa), h(chunks * n, wa), f(chunks, 8, n)]
    scratch += [f(chunks, n, dim), f(2, chunks, n, dim), f(chunks, n, dim)]
    scratch += [h(chunks * n, dim), h(chunks * n, dim), h(chunks * n, wf), h(chunks * n, 2 * wf)]
    scratch += [f(2, *g), f(2, *a)] + [f(2, *k) for k in (d, g, a)]
    scratch += [f(*k) for k in (d, g, a)] + [f(layers, *k) for k in (d, g, a)]
    scratch += [f(*k) for _ in range(3) for k in (d, g, a)] + [f(*groups, 2, 8, dim)]
    scratch += [f(chunks, n, 1), h(dim, 2, lf), f(half, 2, lf), f(groups[0] * groups[1] * 2 * chunks, half)]
    scratch += [dma((32,)), dma((chunks,)), dma((2, chunks)), dma((4,)), dma((4,))]
    scratch += [dma((layers, units))] * 9 + [dma((2, chunks))] * 3 + [dma((5,))] * 2
    scratch += [count((units,))] * 3 + [count]
    args = list(fixed) + list(numbers) + list(moved)
    flops = layers * chunks * n * (2 * dim * (14 * wa + 12 * wf) + 32 * n * wa)
    vmem, smem = pl.BlockSpec(memory_space=pltpu.VMEM), pl.BlockSpec(memory_space=pltpu.SMEM)
    anywhere = pl.BlockSpec(memory_space=pl.ANY)
    return pl.pallas_call(
        functools.partial(whole_pass, (n, dim, wa, wf, layers, chunks)),
        out_shape=[jax.ShapeDtypeStruct(s, t) for s, t in outs],
        in_specs=[vmem] * len(fixed) + [smem] * len(numbers) + [anywhere] * len(moved),
        out_specs=[vmem if i == 3 else anywhere for i in range(len(outs))],
        scratch_shapes=scratch,
        compiler_params=pltpu.CompilerParams(
            vmem_limit_bytes=62 * 2**20, collective_id=0, has_side_effects=True
        ),
        cost_estimate=pl.CostEstimate(flops=flops, bytes_accessed=90 * 10**6, transcendentals=0),
        name="whole_pass",
    )(*args)[:8]


def on_device(sizes, tokens, cotangent, heights, labels, valid, class_table, gains, w_qkv, w_out, w_gate_up, w_down):
    seq_count = heights.shape[0]
    row_count, dim = tokens.shape
    n = row_count // seq_count
    layers = gains.shape[0]
    classes = class_table.shape[0]
    la = w_out.shape[1]
    lf = w_down.shape[1]
    wa, wf = 2 * la, 2 * lf
    tp, dpo, dpi = sizes["tp"], sizes["dpo"], sizes["dpi"]
    mine = seq_count // 2
    lean = (tp, dpo, dpi) == (4, 4, 2) and (mine, layers) == (2, 2)
    core = lax.rem(lax.axis_index("tp"), 2)
    z = lax.axis_index("dpo")
    swap_core = [(i, i ^ 1) for i in range(tp)]

    def core_swap(x):
        return lax.ppermute(x, "tp", swap_core)

    def sum_chips(part):
        total = None
        for step in range(2, tp, 2):
            got = lax.ppermute(part, "tp", [(i, i ^ step) for i in range(tp)])
            total = got if total is None else total + got
        return total

    tables = jnp.asarray(rope_constants(n))
    if lean:
        onehot = (labels[:, None] == jnp.arange(classes)[None, :]).astype(BF16)
        firsts = jnp.dot(onehot, class_table, preferred_element_type=F32)
        fixed = (gains, tables, valid.reshape(seq_count, n), firsts)
        moved = (tokens, cotangent, jnp.transpose(w_qkv, (0, 2, 3, 1)), w_out, w_gate_up, w_down)
        got = call_whole(sizes, n, dim, wa, wf, layers, mine, classes, fixed, (heights, labels), moved)
        output, token_grad, table_part, gain_total, down_part, gate_up_part, out_part, qkv_part = got
        half = dim // dpi
        return (
            output,
            token_grad,
            table_part,
            gain_total,
            qkv_part.reshape(layers, 3, la, half).transpose(0, 3, 1, 2),
            out_part,
            gate_up_part,
            down_part,
        )

    position = jnp.arange(n)
    own = lambda x: lax.dynamic_slice_in_dim(x, core * mine, mine, 0)
    open_key = (position[None, :] < 1 + COLS * own(heights)[:, None]) & (own(valid.reshape(seq_count, n)) == 1)
    open_key = open_key.astype(F32)[:, :, None]
    own_labels = own(labels)
    wqkv, wout, wgu, wd = [], [], [], []
    for l in range(layers):
        for into, w in (
            (wqkv, jnp.transpose(w_qkv[l], (1, 2, 0))),
            (wout, w_out[l][None]),
            (wgu, jnp.transpose(w_gate_up[l], (1, 0, 2))),
            (wd, w_down[l][None]),
        ):
            wide = w.astype(F32)
            axis = 2 if into is wgu else 1
            shape = list(w.shape)
            shape[axis] *= 2
            into.append(call(functools.partial(merge, axis), [(tuple(shape), BF16)], (wide, core_swap(wide)), 1000)[0])
        wqkv[l] = wqkv[l].reshape(3 * wa, dim)
        wout[l] = wout[l][0]
        wd[l] = wd[l][0]

    token_own = own(tokens.reshape(seq_count, n, dim))
    cot_own = own(cotangent.reshape(seq_count, n, dim))
    chunks = range(mine)
    hs = []
    for c in chunks:
        row = lax.dynamic_slice_in_dim(class_table, own_labels[c], 1, 0)
        hs.append(jnp.where((position == 0)[:, None], row, token_own[c]).astype(F32))

    shape_d = ((n, dim), F32)
    shape_b = ((n, dim), BF16)
    flops_a = 2 * n * dim * 4 * wa + 8 * n * n * wa
    flops_f = 2 * n * dim * 3 * wf

    kept = []
    state = [(hs[c],) for c in chunks]
    parts = None
    for l in range(layers):
        keep = [dict() for _ in chunks]
        for c in chunks:
            args = state[c] + (gains[l, 0][None], wqkv[l], wout[l], tables, open_key[c])
            outs = [((n, 3 * wa), BF16), ((max(8, wa // HD), n), F32), ((n, wa), BF16), shape_d]
            outs = ([shape_d] if l > 0 else []) + [shape_b] + outs
            got = call(functools.partial(attn_fwd, l == 0), outs, args, flops_a)
            h = state[c][0] if l == 0 else got.pop(0)
            a, qkv, lse, o, part = got
            keep[c].update(h=h, a=a, qkv=qkv, lse=lse, o=o)
            state[c] = (h, part, sum_chips(part))
        for c in chunks:
            args = state[c] + (gains[l, 1][None], wgu[l], wd[l])
            outs = [shape_d, shape_b, ((n, 2 * wf), F32), ((n, wf), BF16), shape_d]
            h1, b, gu, hid, part = call(ffn_fwd, outs, args, flops_f)
            keep[c].update(h1=h1, b=b, gu=gu, hid=hid)
            state[c] = (h1, part, sum_chips(part))
        kept.append(keep)

    output = jnp.concatenate([s[0] + (s[1] + s[2]) for s in state], axis=0)

    half = lax.axis_index("dpi") if dpi == 2 else 1
    order = jnp.stack([jnp.int32(1) - half, jnp.int32(half)])

    def dp_sum(both, other, axis):
        got = core_swap(other)
        if dpi == 2:
            sent = lax.ppermute(both[0] + got[0], "dpi", [(0, 1), (1, 0)])
            total = (both[1] + got[1]) + sent
        else:
            both = both + got
            whole = jnp.concatenate([both[0], both[1]], axis=axis)
            total = lax.psum_scatter(whole, "dpi", scatter_dimension=axis, tiled=True)
        return line_sum(total)

    def line_sum(x):
        if dpo != 4:
            return lax.psum(x, "dpo")
        got = lax.ppermute(x, "dpo", [(0, 1), (3, 2)])
        x = x + got
        got = lax.ppermute(x, "dpo", [(1, 2), (2, 1)])
        x = x + got
        got = lax.ppermute(x, "dpo", [(1, 0), (2, 3)])
        return jnp.where((z == 0) | (z == dpo - 1), got, x)

    gain_rows = [[None, None] for _ in range(layers)]
    grads = [None] * layers
    state = [None] * mine
    for l in reversed(range(layers)):
        top = l == layers - 1
        keep = kept[l]
        gms = []
        for c in chunks:
            outs = [((n, 2 * wf), BF16), shape_d]
            args = (keep[c]["gu"], wgu[l], wd[l])
            if top:
                g = cot_own[c]
                dgu, part = call(functools.partial(ffn_bwd, True), outs, (g,) + args, flops_f)
                gms.append(g)
            else:
                outs = [shape_d, ((1, dim), F32), shape_b] + outs
                args = state[c] + args
                g, gain_c, gm, dgu, part = call(functools.partial(ffn_bwd, False), outs, args, flops_f)
                gain_rows[l + 1][0] = gain_c if c == 0 else gain_rows[l + 1][0] + gain_c
                gms.append(gm)
            keep[c]["dgu"] = dgu
            state[c] = (g, part, sum_chips(part), keep[c]["h1"], gains[l, 1][None])
        flops_w = 2 * n * mine * dim * wf
        outs = [((2, lf, dim // 2), F32)] * 2
        args = [order] + [keep[c]["hid"] for c in chunks] + gms
        spans = (((0, lf),), ((lf, wf),))
        down = call(functools.partial(grad_rows, spans), outs, args, flops_w, smem=1)
        outs = [((2, dim // 2, 2 * lf), F32)] * 2
        args = [order] + [keep[c]["b"] for c in chunks] + [keep[c]["dgu"] for c in chunks]
        spans = (((0, lf), (wf, wf + lf)), ((lf, wf), (wf + lf, 2 * wf)))
        gate_up = call(functools.partial(grad_columns, spans), outs, args, 2 * flops_w, smem=1)
        down = dp_sum(*down, 1)
        gate_up = dp_sum(*gate_up, 0)
        gas = []
        for c in chunks:
            outs = [shape_d, ((1, dim), F32), shape_b, ((n, 3 * wa), BF16), shape_d]
            args = state[c] + (wqkv[l], wout[l], tables, open_key[c], keep[c]["qkv"], keep[c]["lse"])
            g1, gain_c, ga, dqkv, part = call(attn_bwd, outs, args, flops_a + 12 * n * n * wa)
            gain_rows[l][1] = gain_c if c == 0 else gain_rows[l][1] + gain_c
            gas.append(ga)
            keep[c]["dqkv"] = dqkv
            state[c] = (g1, part, sum_chips(part), keep[c]["h"], gains[l, 0][None])
        flops_w = 2 * n * mine * dim * wa
        outs = [((2, la, dim // 2), F32)] * 2
        args = [order] + [keep[c]["o"] for c in chunks] + gas
        spans = (((0, la),), ((la, wa),))
        out = call(functools.partial(grad_rows, spans), outs, args, flops_w, smem=1)
        outs = [((2, 3 * la, dim // 2), F32)] * 2
        args = [order] + [keep[c]["dqkv"] for c in chunks] + [keep[c]["a"] for c in chunks]
        spans = tuple(tuple((t * wa + s * la, t * wa + (s + 1) * la) for t in range(3)) for s in range(2))
        qkv = call(functools.partial(grad_rows, spans), outs, args, 3 * flops_w, smem=1)
        out = dp_sum(*out, 1)
        qkv = dp_sum(*qkv, 1)
        grads[l] = (qkv, out, gate_up, down)

    finals = []
    for c in chunks:
        g, gain_c = call(close_layer, [shape_d, ((1, dim), F32)], state[c], 1000)
        gain_rows[0][0] = gain_c if c == 0 else gain_rows[0][0] + gain_c
        finals.append(g)

    slot0 = lax.axis_index("dpo") * dpi + lax.axis_index("dpi")
    seqs = seq_count * dpo * dpi
    firsts = jnp.concatenate([g[0:1] for g in finals], axis=0)
    small = jnp.zeros((seqs + 2 * layers + 1, dim), F32)
    small = lax.dynamic_update_slice(small, firsts, (slot0 * seq_count + core * mine, 0))
    terms = jnp.concatenate([gain_rows[l][i] for l in range(layers) for i in range(2)], axis=0)
    small = lax.dynamic_update_slice(small, terms, (seqs, 0))
    label_row = lax.dynamic_update_slice(
        jnp.zeros((1, dim), F32), own_labels.astype(F32)[None], (0, slot0 * seq_count + core * mine)
    )
    small = lax.dynamic_update_slice(small, label_row, (seqs + 2 * layers, 0))
    small = jnp.where(lax.axis_index("tp") < 2, small, 0.0)
    small = lax.psum(small, ("dpo", "dpi", "tp"))
    all_labels = jnp.round(small[seqs + 2 * layers, :seqs]).astype(jnp.int32)
    gain_total = small[seqs : seqs + 2 * layers].reshape(layers, 2, dim)
    onehot = (all_labels[None, :] == jnp.arange(classes)[:, None]).astype(F32)
    share = dim // dpi
    rows = lax.dynamic_slice(small, (0, lax.axis_index("dpi") * share), (seqs, share))
    table_part = jnp.dot(onehot, rows, precision=lax.Precision.HIGHEST)

    token_own = jnp.concatenate([jnp.where((position == 0)[:, None], 0.0, g) for g in finals], axis=0)

    def both_cores(x):
        other = core_swap(x)
        return jnp.where(core == 0, jnp.concatenate([x, other], 0), jnp.concatenate([other, x], 0))

    qkv_part = jnp.stack([g[0].reshape(3, la, share) for g in grads]).transpose(0, 3, 1, 2)
    out_part = jnp.stack([g[1] for g in grads])
    gate_up_part = jnp.stack([g[2].reshape(share, 2, lf) for g in grads])
    down_part = jnp.stack([g[3] for g in grads])
    return (
        both_cores(output),
        both_cores(token_own),
        table_part,
        gain_total,
        qkv_part,
        out_part,
        gate_up_part,
        down_part,
    )


def solution(mesh):
    sizes = dict(mesh.shape)
    placed = (
        P(("dpo", "dpi"), None),
        P(("dpo", "dpi"), None),
        P(("dpo", "dpi")),
        P(("dpo", "dpi")),
        P(("dpo", "dpi")),
        P(),
        P(),
        P(None, None, None, "tp"),
        P(None, "tp", None),
        P(None, None, None, "tp"),
        P(None, "tp", None),
    )
    return jax.shard_map(
        functools.partial(on_device, sizes),
        mesh=mesh,
        in_specs=placed,
        out_specs=(
            P(("dpo", "dpi"), None),
            P(("dpo", "dpi"), None),
            P(None, "dpi"),
            P(),
            P(None, "dpi", None, "tp"),
            P(None, "tp", "dpi"),
            P(None, "dpi", None, "tp"),
            P(None, "tp", "dpi"),
        ),
        check_vma=False,
    )
```

```python
import functools

import jax
import jax.numpy as jnp
import numpy as np
from jax import lax
from jax.experimental import pallas as pl
from jax.experimental.pallas import tpu as pltpu
from jax.sharding import PartitionSpec as P

HD = 64
COLS = 16
EPS = 1e-05
F32 = jnp.float32
BF16 = jnp.bfloat16
LOW = -1e30
MESH = pl.DeviceIdType.MESH

E, D, G, A = "edga"
PIECES = {E: (64,) * 2, D: (96,) * 4, G: (48,) * 8, A: (96,) * 8}
FX, FA, FB, PO, AT, TK, GO, GW, CU, XS, ZA, ZB, ZC, SO, EO, SC, SX, SZ, SW = range(19)
ORDER = (
    (FA, 1, 0), (PO, 0), (FB, 1, 0), (FX,), (FA, 1, 1), (GO, 1, E), (GO, 1, D), (GW, 1, E), (CU, 1, 1),
    (CU, 1, 0), (PO, 1), (GW, 1, D), (CU, 1, 2), (XS, 1, 1), (GO, 1, G), (CU, 1, 4), (CU, 1, 5), (ZA, 1, 1),
    (XS, 1, 0), (FB, 1, 1), (XS, 1, 2), (ZA, 1, 0), (CU, 1, 3), (GW, 1, G), (ZA, 1, 2), (ZB, 1, 0), (ZB, 1, 1),
    (XS, 1, 4), (CU, 1, 10), (ZA, 1, 4), (CU, 1, 9), (CU, 1, 7), (XS, 1, 5), (ZA, 1, 5), (ZB, 1, 2),
    (CU, 1, 11), (XS, 1, 3), (CU, 1, 13), (CU, 1, 6), (CU, 1, 12), (CU, 1, 8), (ZB, 1, 4), (XS, 1, 10),
    (ZA, 1, 3), (AT, 1, 0), (ZA, 1, 10), (ZB, 1, 5), (XS, 1, 9), (ZC, 1, 1), (XS, 1, 7), (ZB, 1, 3), (ZA, 1, 9),
    (ZB, 1, 10), (AT, 1, 1), (ZA, 1, 7), (XS, 1, 11), (ZB, 1, 9), (XS, 1, 13), (GO, 1, A), (ZA, 1, 11),
    (ZB, 1, 7), (GW, 1, A), (XS, 1, 6), (ZA, 1, 13), (ZC, 1, 10), (XS, 1, 12), (ZB, 1, 11), (CU, 1, 17),
    (CU, 1, 14), (ZA, 1, 6), (ZC, 1, 7), (CU, 1, 15), (ZC, 1, 4), (CU, 1, 19), (XS, 1, 8), (CU, 1, 20),
    (CU, 1, 16), (ZB, 1, 13), (ZA, 1, 12), (FA, 0, 0), (ZB, 1, 6), (ZA, 1, 8), (XS, 1, 17), (CU, 1, 18),
    (ZA, 1, 17), (XS, 1, 14), (ZB, 1, 12), (FB, 0, 0), (ZC, 1, 9), (CU, 1, 21), (XS, 1, 15), (ZB, 1, 8),
    (XS, 1, 19), (ZA, 1, 14), (ZC, 1, 3), (FA, 0, 1), (ZA, 1, 15), (ZB, 1, 17), (GO, 0, D), (ZB, 1, 14),
    (ZA, 1, 19), (ZC, 1, 2), (XS, 1, 20), (GW, 0, D), (ZA, 1, 20), (ZB, 1, 15), (GO, 0, E), (CU, 0, 2),
    (XS, 1, 16), (CU, 0, 4), (GO, 0, G), (ZB, 1, 19), (XS, 1, 18), (ZA, 1, 16), (GW, 0, E), (XS, 1, 21),
    (ZC, 1, 5), (CU, 0, 1), (ZC, 1, 12), (ZA, 1, 18), (ZC, 1, 8), (CU, 0, 5), (ZB, 1, 20), (GW, 0, G),
    (ZB, 1, 16), (FB, 0, 1), (ZA, 1, 21), (XS, 0, 2), (CU, 0, 9), (CU, 0, 0), (ZC, 1, 17), (ZA, 0, 2),
    (XS, 0, 4), (ZC, 1, 11), (XS, 0, 1), (ZB, 1, 18), (XS, 0, 5), (CU, 0, 10), (CU, 0, 7), (ZA, 0, 4),
    (ZB, 1, 21), (AT, 0, 0), (ZA, 0, 5), (ZC, 1, 6), (ZB, 0, 2), (XS, 0, 9), (ZB, 0, 4), (CU, 0, 11),
    (ZA, 0, 1), (CU, 0, 13), (XS, 0, 0), (CU, 0, 3), (ZB, 0, 5), (ZC, 1, 21), (ZA, 0, 9), (ZC, 1, 15),
    (ZC, 1, 0), (ZC, 1, 18), (XS, 0, 10), (ZC, 1, 16), (CU, 0, 12), (ZC, 1, 20), (XS, 0, 7), (CU, 0, 6),
    (ZA, 0, 0), (CU, 0, 8), (ZB, 0, 1), (ZC, 1, 13), (ZB, 0, 9), (ZA, 0, 10), (AT, 0, 1), (ZB, 0, 0),
    (ZA, 0, 7), (ZB, 0, 10), (XS, 0, 11), (GW, 0, A), (ZC, 0, 4), (ZA, 0, 11), (GO, 0, A), (XS, 0, 13),
    (ZB, 0, 7), (ZA, 0, 13), (ZB, 0, 11), (XS, 0, 12), (CU, 0, 21), (XS, 0, 3), (ZC, 0, 5), (TK, 0),
    (ZA, 0, 12), (XS, 0, 6), (ZB, 0, 13), (ZA, 0, 3), (ZC, 1, 19), (ZB, 0, 12), (CU, 0, 20), (CU, 0, 19),
    (ZA, 0, 6), (SO, 0), (XS, 0, 8), (ZB, 0, 3), (ZC, 0, 0), (ZA, 0, 8), (CU, 0, 15), (ZC, 1, 14), (CU, 0, 14),
    (ZB, 0, 6), (XS, 0, 21), (TK, 1), (XS, 0, 20), (ZA, 0, 21), (ZB, 0, 8), (ZC, 0, 9), (SC,), (XS, 0, 19),
    (ZA, 0, 20), (CU, 0, 16), (SX,), (ZA, 0, 19), (ZC, 0, 1), (ZC, 0, 2), (CU, 0, 18), (ZB, 0, 21), (ZC, 0, 6),
    (XS, 0, 14), (SO, 1), (XS, 0, 16), (XS, 0, 15), (ZB, 0, 20), (ZC, 0, 8), (ZC, 0, 11), (SZ,), (XS, 0, 18),
    (CU, 0, 17), (ZA, 0, 14), (ZC, 0, 10), (ZA, 0, 16), (ZA, 0, 15), (EO, 0), (ZB, 0, 19), (ZC, 0, 7),
    (ZC, 0, 3), (XS, 0, 17), (ZC, 0, 12), (ZB, 0, 14), (ZB, 0, 16), (ZA, 0, 18), (ZA, 0, 17), (ZB, 0, 15),
    (ZC, 0, 20), (SW,), (ZC, 0, 13), (ZB, 0, 18), (ZC, 0, 16), (ZC, 0, 14), (ZC, 0, 15), (EO, 1), (ZC, 0, 19),
    (ZB, 0, 17), (ZC, 0, 18), (ZC, 0, 21), (ZC, 0, 17),
)

NN = (((1,), (0,)), ((), ()))
NT = (((1,), (1,)), ((), ()))
TN = (((0,), (0,)), ((), ()))


def mm(a, b, dims=NN):
    return lax.dot_general(a, b, dims, preferred_element_type=F32)


def rope_constants(slot_len):
    quarter = HD // 4
    raster = np.maximum(np.arange(slot_len) - 1, 0)
    row_pos = (raster // COLS).astype(np.float32)
    col_pos = (raster % COLS).astype(np.float32)
    frequency = (10000.0 ** (-np.arange(quarter).astype(np.float32) / quarter)).astype(np.float32)
    row_angle = row_pos[:, None] * frequency[None, :]
    col_angle = col_pos[:, None] * frequency[None, :]
    zero = np.zeros_like(row_angle)
    cos = np.concatenate([np.cos(row_angle)] * 2 + [np.cos(col_angle)] * 2, axis=1)
    first = np.concatenate([-np.sin(row_angle), zero, -np.sin(col_angle), zero], axis=1)
    second = np.concatenate([zero, np.sin(row_angle), zero, np.sin(col_angle)], axis=1)
    return np.stack([np.tile(t, (1, 2)) for t in (cos, first, second)]).astype(np.float32)


def rotate(x, table_ref, sign):
    quarter = HD // 4
    ahead = pltpu.roll(x, 2 * HD - quarter, 1) * table_ref[1]
    behind = pltpu.roll(x, quarter, 1) * table_ref[2]
    turned = ahead + behind
    return x * table_ref[0] + (turned if sign > 0 else -turned)


def merge(axis, mine_ref, other_ref, out_ref):
    size = mine_ref.shape[axis]
    if axis == 1:
        out_ref[:, :size, :] = mine_ref[...].astype(BF16)
        out_ref[:, size:, :] = other_ref[...].astype(BF16)
    else:
        out_ref[:, :, :size] = mine_ref[...].astype(BF16)
        out_ref[:, :, size:] = other_ref[...].astype(BF16)


def inv_rms(h):
    return lax.rsqrt(jnp.mean(h * h, axis=-1, keepdims=True) + EPS)


def norm_back(grad, normed, scale, gain):
    scaled = grad * gain
    return scale * (scaled - normed * jnp.mean(scaled * normed, axis=-1, keepdims=True))


def key_mask(open_ref, n):
    key = lax.broadcasted_iota(jnp.int32, (n, n), 0)
    query = lax.broadcasted_iota(jnp.int32, (n, n), 1)
    return ((key < query) & (open_ref[...] > 0.5)) | (key == query)


def attn_fwd(first, *refs):
    if first:
        h_ref, gain_ref, wqkv_ref, wout_ref, table_ref, open_ref = refs[:6]
        refs = refs[6:]
        h = h_ref[...]
    else:
        h_ref, p_ref, r_ref, gain_ref, wqkv_ref, wout_ref, table_ref, open_ref = refs[:8]
        refs = refs[8:]
        h = h_ref[...] + (p_ref[...] + r_ref[...])
        refs[0][...] = h
        refs = refs[1:]
    a_ref, qkv_ref, lse_ref, o_ref, part_ref = refs
    n = h.shape[0]
    width = wout_ref.shape[0]
    a = (h * inv_rms(h) * gain_ref[...]).astype(BF16)
    a_ref[...] = a
    lane = lax.broadcasted_iota(jnp.int32, (n, 2 * HD), 1)
    low_half = lane < HD
    zero = jnp.zeros((n, 2 * HD), BF16)
    mask = key_mask(open_ref, n)
    for t in range(width // (2 * HD)):
        spots = [slice(s * width + t * 2 * HD, s * width + (t + 1) * 2 * HD) for s in range(3)]
        q = rotate(mm(a, wqkv_ref[spots[0], :], NT), table_ref, 1)
        q = (q * HD ** (-0.5)).astype(BF16)
        k = rotate(mm(a, wqkv_ref[spots[1], :], NT), table_ref, 1).astype(BF16)
        v = mm(a, wqkv_ref[spots[2], :], NT).astype(BF16)
        qkv_ref[:, spots[0]] = q
        qkv_ref[:, spots[1]] = k
        qkv_ref[:, spots[2]] = v
        mixed = []
        for e in range(2):
            q_one = jnp.where(low_half if e == 0 else ~low_half, q, zero)
            s = jnp.where(mask, mm(k, q_one, NT), LOW)
            top = jnp.max(s, axis=0, keepdims=True)
            raised = jnp.exp(s - top)
            total = jnp.sum(raised, axis=0, keepdims=True)
            lse_ref[2 * t + e : 2 * t + e + 1, :] = top + jnp.log(total)
            prob = (raised / total).astype(BF16)
            mixed.append(mm(prob, v, TN))
        o_ref[:, t * 2 * HD : (t + 1) * 2 * HD] = jnp.where(low_half, mixed[0], mixed[1]).astype(BF16)
    part_ref[...] = mm(o_ref[...], wout_ref[...])


def ffn_fwd(h_ref, p_ref, r_ref, gain_ref, wgu_ref, wd_ref, h1_ref, *refs):
    h = h_ref[...] + (p_ref[...] + r_ref[...])
    h1_ref[...] = h
    b = (h * inv_rms(h) * gain_ref[...]).astype(BF16)
    b_ref, gu_ref, hid_ref, part_ref = refs
    b_ref[...] = b
    width = wd_ref.shape[0]
    step = min(width, 256)
    for f in range(0, width, step):
        gate = mm(b, wgu_ref[0, :, f : f + step])
        up = mm(b, wgu_ref[1, :, f : f + step])
        gu_ref[:, f : f + step] = gate
        gu_ref[:, width + f : width + f + step] = up
        hid_ref[:, f : f + step] = (gate * jax.nn.sigmoid(gate) * up).astype(BF16)
    part_ref[...] = mm(hid_ref[...], wd_ref[...])


def ffn_bwd(first, *refs):
    if first:
        g_ref, gu_ref, wgu_ref, wd_ref = refs[:4]
        refs = refs[4:]
        gm = g_ref[...]
    else:
        g1_ref, p_ref, r_ref, hin_ref, gain_ref, gu_ref, wgu_ref, wd_ref = refs[:8]
        refs = refs[8:]
        grad, gain_grad = close_norm(g1_ref[...], p_ref, r_ref, hin_ref, gain_ref)
        refs[0][...] = grad
        refs[1][...] = gain_grad
        gm = grad.astype(BF16)
        refs[2][...] = gm
        refs = refs[3:]
    dgu_ref, part_ref = refs
    width = wd_ref.shape[0]
    step = min(width, 256)
    for f in range(0, width, step):
        dhid = mm(gm, wd_ref[f : f + step, :], NT)
        gate = gu_ref[:, f : f + step]
        up = gu_ref[:, width + f : width + f + step]
        sig = jax.nn.sigmoid(gate)
        dgu_ref[:, f : f + step] = (dhid * up * (sig * (1.0 + gate * (1.0 - sig)))).astype(BF16)
        dgu_ref[:, width + f : width + f + step] = (dhid * (gate * sig)).astype(BF16)
    part_ref[...] = mm(dgu_ref[:, :width], wgu_ref[0], NT) + mm(dgu_ref[:, width:], wgu_ref[1], NT)


def close_norm(g, p_ref, r_ref, h_ref, gain_ref):
    grad = p_ref[...] + r_ref[...]
    h = h_ref[...]
    scale = inv_rms(h)
    normed = h * scale
    gain_grad = jnp.sum(grad * normed, axis=0, keepdims=True)
    return g + norm_back(grad, normed, scale, gain_ref[...]), gain_grad


def attn_bwd(
    g_ref, p_ref, r_ref, h1_ref, gain_ref, wqkv_ref, wout_ref, table_ref, open_ref, qkv_ref, lse_ref,
    g1_ref, gain_grad_ref, ga_ref, dqkv_ref, part_ref,
):
    g1, gain_grad = close_norm(g_ref[...].astype(F32), p_ref, r_ref, h1_ref, gain_ref)
    g1_ref[...] = g1
    gain_grad_ref[...] = gain_grad
    ga = g1.astype(BF16)
    ga_ref[...] = ga
    n = ga.shape[0]
    width = wout_ref.shape[0]
    lane = lax.broadcasted_iota(jnp.int32, (n, 2 * HD), 1)
    low_half = lane < HD
    zero = jnp.zeros((n, 2 * HD), BF16)
    mask = key_mask(open_ref, n)
    for t in range(width // (2 * HD)):
        spots = [slice(s * width + t * 2 * HD, s * width + (t + 1) * 2 * HD) for s in range(3)]
        q = qkv_ref[:, spots[0]]
        k = qkv_ref[:, spots[1]]
        v = qkv_ref[:, spots[2]]
        dout = mm(ga, wout_ref[t * 2 * HD : (t + 1) * 2 * HD, :], NT).astype(BF16)
        dq, dk, dv = [], [], []
        for e in range(2):
            mine = low_half if e == 0 else ~low_half
            q_one = jnp.where(mine, q, zero)
            d_one = jnp.where(mine, dout, zero)
            s = jnp.where(mask, mm(k, q_one, NT), LOW)
            prob = jnp.exp(s - lse_ref[2 * t + e : 2 * t + e + 1, :])
            dprob = mm(v, d_one, NT)
            delta = jnp.sum(prob * dprob, axis=0, keepdims=True)
            ds = (prob * (dprob - delta)).astype(BF16)
            dv.append(mm(prob.astype(BF16), dout))
            dk.append(mm(ds, q))
            dq.append(mm(ds, k, TN))
        dq = jnp.where(low_half, dq[0], dq[1]) * HD ** (-0.5)
        dk = jnp.where(low_half, dk[0], dk[1])
        dv = jnp.where(low_half, dv[0], dv[1])
        dqkv_ref[:, spots[0]] = rotate(dq, table_ref, -1).astype(BF16)
        dqkv_ref[:, spots[1]] = rotate(dk, table_ref, -1).astype(BF16)
        dqkv_ref[:, spots[2]] = dv.astype(BF16)
    part_ref[...] = mm(dqkv_ref[...], wqkv_ref[...])


def close_layer(g1_ref, p_ref, r_ref, h_ref, gain_ref, out_ref, gain_grad_ref):
    grad, gain_grad = close_norm(g1_ref[...], p_ref, r_ref, h_ref, gain_ref)
    out_ref[...] = grad
    gain_grad_ref[...] = gain_grad


def halves_of(half_ref, dim):
    one = dim // 2
    return [pl.ds(pl.multiple_of(half_ref[s] * one, one), one) for s in range(2)]


def grad_rows(spans, half_ref, *refs):
    chunks = (len(refs) - 2) // 2
    lefts, rights = refs[:chunks], refs[chunks : 2 * chunks]
    outs = refs[2 * chunks :]
    for s, spot in enumerate(halves_of(half_ref, rights[0].shape[1])):
        for out, picks in zip(outs, spans):
            at = 0
            for lo, hi in picks:
                total = None
                for left, right in zip(lefts, rights):
                    term = mm(left[:, lo:hi], right[:, spot], TN)
                    total = term if total is None else total + term
                out[s, at : at + hi - lo, :] = total
                at += hi - lo


def grad_columns(spans, half_ref, *refs):
    chunks = (len(refs) - 2) // 2
    lefts, rights = refs[:chunks], refs[chunks : 2 * chunks]
    outs = refs[2 * chunks :]
    for s, spot in enumerate(halves_of(half_ref, lefts[0].shape[1])):
        for out, picks in zip(outs, spans):
            at = 0
            for lo, hi in picks:
                total = None
                for left, right in zip(lefts, rights):
                    term = mm(left[:, spot], right[:, lo:hi], TN)
                    total = term if total is None else total + term
                out[s, :, at : at + hi - lo] = total
                at += hi - lo


def whole_pass(dims, *refs):
    n, dim, wa, wf, layers, chunks = dims
    la, lf, half = wa // 2, wf // 2, dim // 2
    refs = list(refs)

    def take(count):
        got = refs[:count]
        del refs[:count]
        return got

    gains_ref, tables, valid_ref, first_ref, heights_ref, labels_ref = take(6)
    tokens, cotangent, w_qkv, w_out, w_gate_up, w_down = take(6)
    output, token_grad, table_out, gain_out, down_out, gate_up_out, out_out, qkv_out = take(8)
    wgu_st, wd_st, wqkv_st, wout_st, h_st, h1_st, qkv_st, lse_st, o_st, last_st = take(10)
    wgu, wd, wqkv, wout = take(4)
    hs, h1s, qkvs, os, lses = take(5)
    ysend, yrecv, gs, gm, ab, hid, dgu = take(7)
    oth_g, oth_s, cr_d, cr_g, cr_a = take(5)
    os_d, os_g, os_a, ok_d, ok_g, ok_a = take(6)
    xr_d, xr_g, xr_a, z1_d, z1_g, z1_a, z2_d, z2_g, z2_a, small = take(10)
    open_ref, raw_g, total_g, firsts_ref = take(4)
    load_sem, ys_sem, yr_sem, cs_sem, cr_sem, xs_sem, xr_sem = take(7)
    zs, zr, z2r, store_sem, half_s, half_r, row_sem, rows_s, rows_r, small_s, small_r = take(11)
    x_free, z_free, c_free = take(3)

    tp = lax.axis_index("tp")
    x = lax.axis_index("dpi")
    z = lax.axis_index("dpo")
    core = lax.rem(tp, 2)
    to_core = {"tp": tp + 1 - 2 * core}
    to_chip = {"tp": lax.rem(tp + 2, 4)}
    to_x = {"dpi": 1 - x}
    to_mate = {"dpo": z + 1 - 2 * lax.rem(z, 2)}
    to_inner = {"dpo": 3 - z}
    outer = (z == 0) | (z == 3)
    inner = (z == 1) | (z == 2)
    far = [{"dpo": lax.rem(z + k, 4)} for k in (1, 2, 3)]

    barrier = pltpu.get_barrier_semaphore()
    for peer in [to_core, to_chip, to_x] + far:
        pl.semaphore_signal(barrier, inc=1, device_id=peer, device_id_type=MESH)
    loads = {}

    def load(key, src, dst, slot):
        copy = pltpu.make_async_copy(src, dst, load_sem.at[slot])
        copy.start()
        loads[key] = copy

    def need(*keys):
        for key in keys:
            if key in loads:
                loads.pop(key).wait()

    def rows(c):
        return pl.ds(c * n, n)

    def load_ffn_weights():
        load("wgu", wgu_st, wgu, 0)
        load("wd", wd_st, wd, 1)

    def load_attn_weights():
        load("wqkv", wqkv_st, wqkv, 2)
        load("wout", wout_st, wout, 3)

    def load_h1(c):
        load(("h1", c), h1_st.at[0, c], h1s.at[c], 4 + c)

    def load_qkv(c):
        load(("qkv", c), qkv_st.at[c], qkvs.at[c], 6 + c)
        load(("lse", c), lse_st.at[c], lses.at[c], 8 + c)

    def load_o(c):
        load(("o", c), o_st.at[rows(c)], os.at[rows(c)], 10 + c)

    def load_h(c):
        load(("h", c), h_st.at[c], hs.at[c], 12 + c)

    top = layers - 1

    def own_rows(ref, c):
        return ref.at[pl.ds(pl.multiple_of((core * chunks + c) * n, n), n)]

    def own_attn(l):
        for t in range(3):
            load(("own", "a", t), w_qkv.at[l, t], wqkv.at[pl.ds(t * wa, la)], 17 + t)
        load(("own", "a", 3), w_out.at[l], wout.at[pl.ds(0, la)], 20)

    def own_ffn(l):
        load(("own", "g", 0), w_gate_up.at[l], raw_g, 21)
        load(("own", "d", 0), w_down.at[l], wd.at[pl.ds(0, lf)], 23)

    own_attn(0)
    for c in range(chunks):
        load(("token", c), own_rows(tokens, c), gm.at[rows(c)], 14 + c)
    own_ffn(0)

    def remote(src, dst, send, recv, to):
        return pltpu.make_async_remote_copy(
            src_ref=src, dst_ref=dst, send_sem=send, recv_sem=recv, device_id=to, device_id_type=MESH
        )

    turn = [0] * chunks

    def y_copy(c, k):
        return remote(ysend.at[c], yrecv.at[k % 2, c], ys_sem.at[c], yr_sem.at[k % 2, c], to_chip)

    def y_start(c):
        y_copy(c, turn[c]).start()

    def y_sum(c):
        copy = y_copy(c, turn[c])
        copy.wait()
        got = ysend[c] + yrecv[turn[c] % 2, c]
        turn[c] += 1
        return got

    def y_half_copy(c, at):
        k, part, i = turn[c] % 2, pl.ds(at, n // 2), at // (n // 2)
        return remote(ysend.at[c, part], yrecv.at[k, c, part], half_s.at[i], half_r.at[i], to_chip)

    def y_half_sum(c, at):
        part = pl.ds(at, n // 2)
        y_half_copy(c, at).wait()
        got = ysend[c, part, :] + yrecv[turn[c] % 2, c, part, :]
        if at > 0:
            turn[c] += 1
        return got

    def gain_of(l, i):
        return gains_ref[l, i : i + 1, :]

    def add_gain(l, i, c, term):
        k = 2 + 2 * l + i
        spot = (z, x, core, slice(k, k + 1), slice(None))
        small[spot] = term if c == 0 else small[spot] + term

    def close(l, i, c, g, h):
        grad = y_sum(c)
        scale = inv_rms(h)
        normed = h * scale
        add_gain(l, i, c, jnp.sum(grad * normed, axis=0, keepdims=True))
        return g + norm_back(grad, normed, scale, gain_of(l, i))

    def prepare(c):
        at = core * chunks + c
        lane = lax.broadcasted_iota(jnp.int32, (1, n), 1)
        is_open = (lane < 1 + COLS * heights_ref[at]) & (valid_ref[pl.ds(at, 1), :] == 1)
        diagonal = lax.broadcasted_iota(jnp.int32, (n, n), 0) == lax.broadcasted_iota(jnp.int32, (n, n), 1)
        column = jnp.where(diagonal, jnp.where(is_open, 1.0, 0.0), 0.0)
        open_ref[c] = jnp.sum(column, axis=1, keepdims=True)
        slot = (z * groups[1] + x) * 2 * chunks + at
        lane = lax.broadcasted_iota(jnp.int32, (1, dim), 1)
        label = jnp.where(lane == slot, labels_ref[at], 0).astype(F32)
        spot = (z, x, core, slice(6, 7), slice(None))
        small[spot] = label if c == 0 else small[spot] + label

    groups = small.shape[:2]
    small[z, x, core] = jnp.zeros((8, dim), F32)

    def ffn_a(l, c, at=0, size=n):
        spot, part = pl.ds(c * n + at, size), pl.ds(at, size)
        if l == top:
            need(("cot", c))
            gs[c, part, :] = gm[spot, :].astype(F32)
            h1s[c, part, :] = hs_next(c) if size == n else hs[c, part, :] + y_half_sum(c, at)
            if at + size == n:
                load(("stash", c), h1s.at[c], h1_st.at[top, c], 28 + c)
        else:
            need(("h", c))
            g = close(l + 1, 0, c, gs[c], hs[c])
            gs[c] = g
            gm[spot, :] = g.astype(BF16)
            load_h(c)
        need(("h1", c), "wgu", "wd")
        h1 = h1s[c, part, :]
        b = (h1 * inv_rms(h1) * gain_of(l, 1)).astype(BF16)
        ab[spot, :] = b
        step = min(wf, 256)
        for f in range(0, wf, step):
            gate = mm(b, wgu[0, :, f : f + step])
            up = mm(b, wgu[1, :, f : f + step])
            dhid = mm(gm[spot, :], wd[f : f + step, :], NT)
            sig = jax.nn.sigmoid(gate)
            silu = gate * sig
            hid[spot, f : f + step] = (silu * up).astype(BF16)
            dgu[spot, f : f + step] = (dhid * up * (sig * (1.0 + gate * (1.0 - sig)))).astype(BF16)
            dgu[spot, wf + f : wf + f + step] = (dhid * silu).astype(BF16)

    later = {("fb", 1, 0), ("fb", 1, 1), ("po", 0), ("po", 1)}

    def ffn_done(*what):
        if what in later:
            later.discard(what)
            if not later:
                load_ffn_weights()

    def ffn_b(l, c):
        spot = rows(c)
        ysend[c] = mm(dgu[spot, :wf], wgu[0], NT) + mm(dgu[spot, wf:], wgu[1], NT)
        y_start(c)
        ffn_done("fb", l, c)

    def last_sum(c):
        need(("last", c - 1))
        spare = ok_g.at[0, pl.ds(0, n), pl.ds(0, dim)]
        spare[...] = mm(hid[rows(c), :], wd[...])
        load(("last", c), spare, last_st.at[c], 30)
        ffn_done("po", c)

    def attn(l, c):
        spot = rows(c)
        g1 = close(l, 1, c, gs[c], h1s[c])
        gs[c] = g1
        if l > 0:
            need(("stash", c))
            load_h1(c)
        gm[spot, :] = g1.astype(BF16)
        need("wqkv", "wout", ("qkv", c), ("lse", c))
        lane = lax.broadcasted_iota(jnp.int32, (n, 2 * HD), 1)
        low_half = lane < HD
        zero = jnp.zeros((n, 2 * HD), BF16)
        mask = key_mask(open_ref.at[c], n)
        ga = gm[spot, :]
        for t in range(wa // (2 * HD)):
            spots = [slice(s * wa + t * 2 * HD, s * wa + (t + 1) * 2 * HD) for s in range(3)]
            q, k, v = [qkvs[c, :, s] for s in spots]
            dout = mm(ga, wout[t * 2 * HD : (t + 1) * 2 * HD, :], NT).astype(BF16)
            dq, dk, dv = [], [], []
            for e in range(2):
                mine = low_half if e == 0 else ~low_half
                s = jnp.where(mask, mm(k, jnp.where(mine, q, zero), NT), LOW)
                prob = jnp.exp(s - lses[c, 2 * t + e : 2 * t + e + 1, :])
                dprob = mm(v, jnp.where(mine, dout, zero), NT)
                delta = jnp.sum(prob * dprob, axis=0, keepdims=True)
                ds = (prob * (dprob - delta)).astype(BF16)
                dv.append(mm(prob.astype(BF16), dout))
                dk.append(mm(ds, q))
                dq.append(mm(ds, k, TN))
            dq = jnp.where(low_half, dq[0], dq[1]) * HD ** (-0.5)
            dk = jnp.where(low_half, dk[0], dk[1])
            dv = jnp.where(low_half, dv[0], dv[1])
            dgu[spot, spots[0]] = rotate(dq, tables, -1).astype(BF16)
            dgu[spot, spots[1]] = rotate(dk, tables, -1).astype(BF16)
            dgu[spot, spots[2]] = dv.astype(BF16)
        ysend[c] = mm(dgu[spot, : 3 * wa], wqkv[...])
        y_start(c)
        if l > 0:
            load_qkv(c)
        need(("h", c))
        h = hs[c]
        ab[spot, :] = (h * inv_rms(h) * gain_of(l, 0)).astype(BF16)

    spans = [pl.ds(pl.multiple_of((1 - x) * half, half), half), pl.ds(pl.multiple_of(x * half, half), half)]
    split = sum(PIECES[E])
    down = (oth_s, cr_d, os_d, ok_d, xr_d, z1_d, z2_d)
    kinds = {
        E: down,
        D: down,
        G: (oth_g, cr_g, os_g, ok_g, xr_g, z1_g, z2_g),
        A: (oth_s, cr_a, os_a, ok_a, xr_a, z1_a, z2_a),
    }
    index = {D: 0, G: 1, A: 2, E: 4}
    order = list(kinds)
    units = []
    for kind in kinds:
        at = split if kind == D else 0
        for size in PIECES[kind]:
            target = {E: down_out, D: down_out, G: gate_up_out, A: out_out if at < la else qkv_out}[kind]
            base = la if kind == A and at >= la else 0
            units.append((kind, pl.ds(at, size), target, pl.ds(at - base, size)))
            at += size

    def c_copy(kind, lo=None, size=None):
        at = index[kind]
        source, target = kinds[kind][:2]
        if kind == E:
            lo, size = 0, split
        elif kind == D and lo is None:
            lo, size = split, lf - split
        if kind in (E, D):
            source, target = source.at[:, pl.ds(lo, size)], target.at[:, pl.ds(lo, size)]
        return remote(source, target, cs_sem.at[at], cr_sem.at[at], to_core)

    def weight_copy(kind):
        return c_copy(kind, 0, lf)

    def piece(kind, s, shard, put):
        if kind in (E, D):
            lo, hi = (0, split) if kind == E else (split, lf)
            put(slice(lo, hi), slice(None), mm(hid[:, shard * lf + lo : shard * lf + hi], gm[:, spans[s]], TN))
        elif kind == G:
            for t in range(2):
                cols = slice(t * wf + shard * lf, t * wf + (shard + 1) * lf)
                put(slice(None), slice(t * lf, (t + 1) * lf), mm(ab[:, spans[s]], dgu[:, cols], TN))
        else:
            put(slice(0, la), slice(None), mm(os[:, shard * la : (shard + 1) * la], gm[:, spans[s]], TN))
            for t in range(3):
                cols = slice(t * wa + shard * la, t * wa + (shard + 1) * la)
                put(slice((t + 1) * la, (t + 2) * la), slice(None), mm(dgu[:, cols], ab[:, spans[s]], TN))

    def put_in(ref, *lead):
        def put(r, c, value):
            ref[lead + (r, c)] = value

        return put

    arrived = set()

    def grad_other(l, kind):
        if kind == A:
            need(("o", 0), ("o", 1))
        if "c" not in arrived:
            pl.semaphore_wait(c_free, 1)
            arrived.add("c")
        for s in range(2):
            piece(kind, s, 1, put_in(kinds[kind][0], s))
        c_copy(kind).start()

    def grad_own(l, kind):
        if kind == A:
            need(("o", 0), ("o", 1))
        if l < top and kind == G:
            need(("last", chunks - 1))
        piece(kind, 0, 0, put_in(kinds[kind][2]))
        piece(kind, 1, 0, put_in(kinds[kind][3], l))

    def x_copy(l, u):
        kind, spot = units[u][:2]
        return remote(kinds[kind][2].at[spot], kinds[kind][4].at[spot], xs_sem.at[u], xr_sem.at[u], to_x)

    def core_sum(l, u):
        kind, spot = units[u][:2]
        _, cr, own_s, own_k, *_ = kinds[kind]
        if (l, kind) not in arrived:
            c_copy(kind).wait()
            if l < top:
                pl.semaphore_wait(x_free.at[order.index(kind)], len(PIECES[kind]))
            arrived.add((l, kind))
        own_s[spot, :] = own_s[spot, :] + cr[0, spot, :]
        x_copy(l, u).start()
        own_k[l, spot, :] = own_k[l, spot, :] + cr[1, spot, :]

    def z1_copy(l, u):
        kind, spot = units[u][:2]
        return remote(kinds[kind][3].at[l, spot], kinds[kind][5].at[spot], zs.at[l, u], zr.at[l, u], to_mate)

    def z2_copy(l, u):
        kind, spot = units[u][:2]
        return remote(kinds[kind][3].at[l, spot], kinds[kind][6].at[spot], zs.at[l, u], z2r.at[u], to_inner)

    def total_of(l, u):
        kind, spot, target, place = units[u]
        source = total_g if kind == G else kinds[kind][6]
        return source.at[spot], target.at[l, place]

    def z3_copy(l, u):
        source, target = total_of(l, u)
        return remote(source, target, zs.at[l, u], zr.at[l, u], to_mate)

    def store_copy(l, u):
        source, target = total_of(l, u)
        return pltpu.make_async_copy(source, target, store_sem.at[u])

    def x_sum(l, u):
        kind, spot = units[u][:2]
        keep, got = kinds[kind][3], kinds[kind][4]
        x_copy(l, u).wait()
        keep[l, spot, :] = keep[l, spot, :] + got[spot, :]
        if l > 0:
            pl.semaphore_signal(x_free.at[order.index(kind)], inc=1, device_id=to_x, device_id_type=MESH)

        @pl.when(outer)
        def _():
            if l < top:
                pl.semaphore_wait(z_free.at[u], 1)
            z1_copy(l, u).start()

    def z_one(l, u):
        kind, spot = units[u][:2]
        keep, got = kinds[kind][3], kinds[kind][5]

        @pl.when(inner)
        def _():
            z1_copy(l, u).wait_recv()
            keep[l, spot, :] = keep[l, spot, :] + got[spot, :]
            if l > 0:
                pl.semaphore_signal(z_free.at[u], inc=1, device_id=to_mate, device_id_type=MESH)
            if l < top:
                pl.semaphore_wait(z_free.at[u], 1)
            z2_copy(l, u).start()

    def z_two(l, u):
        kind, spot = units[u][:2]
        keep, got = kinds[kind][3], kinds[kind][6]

        @pl.when(inner)
        def _():
            z2_copy(l, u).wait()
            total = got[spot, :] + keep[l, spot, :]
            if kind == G:
                for t in range(2):
                    total_g[spot, t, :] = total[:, t * lf : (t + 1) * lf]
            else:
                got[spot, :] = total
            z3_copy(l, u).start()
            store_copy(l, u).start()

    def z_end(l, u):
        @pl.when(inner)
        def _():
            z3_copy(l, u).wait_send()
            store_copy(l, u).wait()
            if l > 0:
                pl.semaphore_signal(z_free.at[u], inc=1, device_id=to_inner, device_id_type=MESH)

        @pl.when(outer)
        def _():
            z1_copy(l, u).wait_send()
            z3_copy(l, u).wait_recv()

    def row_copies(src, dst, i, c):
        spot = pl.ds(pl.multiple_of((core * chunks + c) * n, n), n)
        return (
            pltpu.make_async_copy(src, dst.at[spot], row_sem.at[i, c]),
            remote(src, dst.at[spot], rows_s.at[i, c], rows_r.at[i, c], to_core),
        )

    def share_rows(src, dst, i, c):
        for copy in row_copies(src, dst, i, c):
            copy.start()

    def end_rows(src, dst, i, c):
        for copy in row_copies(src, dst, i, c):
            copy.wait()

    def token(c):
        need(("h", c))
        g = close(0, 0, c, gs[c], hs[c])
        small[z, x, core, c : c + 1, :] = g[0:1, :]
        row = lax.broadcasted_iota(jnp.int32, (n, dim), 0)
        gs[c] = jnp.where(row == 0, 0.0, g)
        share_rows(gs.at[c], token_grad, 0, c)

    def pout_copy(c):
        k = turn[c] % 2
        return remote(last_st.at[c], yrecv.at[k, c], ys_sem.at[c], yr_sem.at[k, c], to_chip)

    def start_output(c):
        pout_copy(c).start()
        load(("pout", c), last_st.at[c], ysend.at[c], 4 + c)
        load(("out", c), h1_st.at[top, c], hs.at[c], 12 + c)

    def end_output(c):
        need(("pout", c), ("out", c))
        pout_copy(c).wait()
        hs[c] = hs[c] + (ysend[c] + yrecv[turn[c] % 2, c])
        share_rows(hs.at[c], output, 1, c)

    def small_core():
        return remote(small.at[z, x, core], small.at[z, x, core], small_s.at[0], small_r.at[0], to_core)

    def small_x():
        return remote(small.at[z, x], small.at[z, x], small_s.at[1], small_r.at[1], to_x)

    def small_z(k):
        return remote(small.at[z], small.at[z], small_s.at[2 + k], small_r.at[2 + k], far[k])

    def small_got(k):
        back = lax.rem(z + 3 - k, 4)
        return remote(small.at[back], small.at[back], small_s.at[2 + k], small_r.at[2 + k], far[k])

    def attn_copy(part):
        rows_of = [pl.ds(0, 3 * la), pl.ds(3 * la, la)][part]
        return remote(
            oth_s.at[:, rows_of], cr_a.at[:, rows_of], cs_sem.at[2 + part], cr_sem.at[2 + part], to_core
        )

    def weight_stage(l, kind):
        if kind == A:
            need(*[("own", "a", t) for t in range(4)])
            for s in range(2):
                lanes = slice(s * half, (s + 1) * half)
                for t in range(3):
                    oth_s[s, t * la : (t + 1) * la, :] = wqkv[t * wa : t * wa + la, lanes].astype(F32)
                oth_s[s, 3 * la :, :] = wout[:la, lanes].astype(F32)
        elif kind == G:
            need(("own", "g", 0))
            step = half // 3
            for s in range(2):
                for r in range(0, half, step):
                    for t in range(2):
                        shard = raw_g[s * half + r : s * half + r + step, t, :]
                        wgu[t, s * half + r : s * half + r + step, :lf] = shard
                        oth_g[s, r : r + step, t * lf : (t + 1) * lf] = shard.astype(F32)
        else:
            need(("own", "d", 0))
            for s in range(2):
                oth_s[s, :lf, :] = wd[:lf, s * half : (s + 1) * half].astype(F32)

    def weight_send(l, kind):
        weight_stage(l, kind)
        if kind == A:
            attn_copy(0).start()
            attn_copy(1).start()
        else:
            weight_copy(kind).start()

    def weight_take(l, kind, part=0):
        if kind == A:
            attn_copy(part).wait()
        else:
            weight_copy(kind).wait()
        for s in range(2):
            lanes = slice(s * half, (s + 1) * half)
            if kind == A and part == 0:
                for t in range(3):
                    wqkv[t * wa + la : (t + 1) * wa, lanes] = cr_a[s, t * la : (t + 1) * la, :].astype(BF16)
            elif kind == A:
                wout[la:, lanes] = cr_a[s, 3 * la :, :].astype(BF16)
            elif kind == G:
                for t in range(2):
                    wgu[t, lanes, lf:] = cr_g[s, :, t * lf : (t + 1) * lf].astype(BF16)
            else:
                wd[lf:, lanes] = cr_d[s].astype(BF16)

    def hs_next(c):
        return base_of(c) + y_sum(c)

    def base_of(c):
        return hs[c] if turn[c] % 2 == 0 else h1s[c]

    def attn_up_start(l, c):
        spot = rows(c)
        if l == 0:
            need(("token", c))
            h = gm[spot, :].astype(F32)
            row = lax.broadcasted_iota(jnp.int32, (n, dim), 0)
            h = jnp.where(row == 0, first_ref[pl.ds(core * chunks + c, 1), :], h)
        else:
            h = hs_next(c)
            need(("st_h", c), ("st_qkv", c), ("st_lse", c), ("st_o", c))
        hs[c] = h
        ab[spot, :] = (h * inv_rms(h) * gain_of(l, 0)).astype(BF16)

    def attn_up_heads(c, pairs):
        spot = rows(c)
        a = ab[spot, :]
        lane = lax.broadcasted_iota(jnp.int32, (n, 2 * HD), 1)
        low_half = lane < HD
        zero = jnp.zeros((n, 2 * HD), BF16)
        mask = key_mask(open_ref.at[c], n)
        for t in pairs:
            spots = [slice(s * wa + t * 2 * HD, s * wa + (t + 1) * 2 * HD) for s in range(3)]
            q = rotate(mm(a, wqkv[spots[0], :], NT), tables, 1)
            q = (q * HD ** (-0.5)).astype(BF16)
            k = rotate(mm(a, wqkv[spots[1], :], NT), tables, 1).astype(BF16)
            v = mm(a, wqkv[spots[2], :], NT).astype(BF16)
            for part, value in zip(spots, (q, k, v)):
                qkvs[c, :, part] = value
            mixed = []
            for e in range(2):
                q_one = jnp.where(low_half if e == 0 else ~low_half, q, zero)
                s = jnp.where(mask, mm(k, q_one, NT), LOW)
                peak = jnp.max(s, axis=0, keepdims=True)
                raised = jnp.exp(s - peak)
                total = jnp.sum(raised, axis=0, keepdims=True)
                lses[c, 2 * t + e : 2 * t + e + 1, :] = peak + jnp.log(total)
                mixed.append(mm((raised / total).astype(BF16), v, TN))
            os[spot, t * 2 * HD : (t + 1) * 2 * HD] = jnp.where(low_half, mixed[0], mixed[1]).astype(BF16)

    def attn_up_end(l, c):
        if (l, c) == (top, chunks - 1):
            for at in (0, n // 2):
                ysend[c, pl.ds(at, n // 2), :] = mm(os[pl.ds(c * n + at, n // 2), :], wout[...])
                y_half_copy(c, at).start()
            return
        ysend[c] = mm(os[rows(c), :], wout[...])
        y_start(c)
        if l == 0:
            load(("st_h", c), hs.at[c], h_st.at[c], 12 + c)
            load(("st_qkv", c), qkvs.at[c], qkv_st.at[c], 6 + c)
            load(("st_lse", c), lses.at[c], lse_st.at[c], 8 + c)
            load(("st_o", c), os.at[rows(c)], o_st.at[rows(c)], 10 + c)

    def ffn_up(c):
        spot = rows(c)
        h1 = hs_next(c)
        h1s[c] = h1
        b = (h1 * inv_rms(h1) * gain_of(0, 1)).astype(BF16)
        step = min(wf, 256)
        for f in range(0, wf, step):
            gate = mm(b, wgu[0, :, f : f + step])
            up = mm(b, wgu[1, :, f : f + step])
            hid[spot, f : f + step] = (gate * jax.nn.sigmoid(gate) * up).astype(BF16)
        ysend[c] = mm(hid[spot, :], wd[...])
        y_start(c)
        load(("stash", c), h1s.at[c], h1_st.at[0, c], 28 + c)

    pairs = wa // (2 * HD)
    alone = la // (2 * HD)
    weight_stage(0, A)
    pl.semaphore_wait(barrier, 6)
    attn_copy(0).start()
    attn_copy(1).start()
    for c in range(chunks):
        prepare(c)
        attn_up_start(0, c)
        attn_up_heads(c, range(alone))
    weight_take(0, A, 0)
    attn_up_heads(0, range(alone, pairs))
    weight_take(0, A, 1)
    attn_up_end(0, 0)
    weight_send(0, G)
    attn_up_heads(1, range(alone, pairs))
    attn_up_end(0, 1)
    weight_send(0, D)
    for c in range(chunks):
        load(("cot", c), own_rows(cotangent, c), gm.at[rows(c)], 14 + c)
    load("st_wqkv", wqkv, wqkv_st, 2)
    load("st_wout", wout, wout_st, 3)
    weight_take(0, D)
    weight_take(0, G)
    need("st_wqkv", "st_wout")
    own_attn(1)
    ffn_up(0)
    weight_send(1, A)
    ffn_up(1)
    load("st_wgu", wgu, wgu_st, 0)
    load("st_wd", wd, wd_st, 1)
    weight_take(1, A, 0)
    weight_take(1, A, 1)
    need("st_wgu", "st_wd")
    own_ffn(1)
    for c in range(chunks):
        attn_up_start(1, c)
        attn_up_heads(c, range(pairs))
        attn_up_end(1, c)
        need(("stash", c))
        if c == 0:
            weight_send(1, D)
            weight_send(1, G)
    weight_take(1, D)
    weight_take(1, G)
    pl.semaphore_signal(c_free, inc=1, device_id=to_core, device_id_type=MESH)

    def start_small():
        small_core().start()

    def move_small():
        small_core().wait_send()
        spot = small.at[z, x, 1 - core]
        remote(spot, spot, small_s.at[0], small_r.at[0], to_core).wait_recv()
        small_x().start()

    def spread_small():
        small_x().wait_send()
        spot = small.at[z, 1 - x]
        remote(spot, spot, small_s.at[1], small_r.at[1], to_x).wait_recv()
        for k in range(3):
            small_z(k).start()

    def end_small():
        for k in range(3):
            small_z(k).wait_send()
            small_got(k).wait_recv()
        everyone = [(i, j, k) for i in range(groups[0]) for j in range(groups[1]) for k in range(2)]
        total = None
        for at, place in enumerate(everyone):
            block = small[place]
            total = block if total is None else total + block
            firsts_ref[at * chunks : (at + 1) * chunks, :] = small[place + (slice(0, chunks), spans[1])]
        for l in range(layers):
            gain_out[l] = total[2 + 2 * l : 4 + 2 * l, :]
        slots = firsts_ref.shape[0]
        label = total[6:7, :slots].astype(jnp.int32)
        classes, step = table_out.shape[0], 256
        for at in range(0, classes, step):
            size = min(step, classes - at)
            same = lax.broadcasted_iota(jnp.int32, (size, slots), 0) + at == label
            spare = oth_s.at[at // (4 * la), pl.ds(at % (4 * la), size)]
            spare[...] = lax.dot_general(
                jnp.where(same, 1.0, 0.0), firsts_ref[...], NN,
                precision=lax.Precision.HIGHEST, preferred_element_type=F32,
            )
            load(("table", at), spare, table_out.at[pl.ds(at, size)], 24 + at // step)

    def attn_down(l, c):
        attn(l, c)
        if (l, c) == (1, chunks - 1):
            load_attn_weights()

    def ffn_first(l, c):
        ffn_a(l, c, *((n // 2, n // 2) if (l, c) == (top, chunks - 1) else ()))

    acts = {
        FX: lambda: ffn_a(top, chunks - 1, 0, n // 2),
        FA: ffn_first, FB: ffn_b, PO: last_sum, AT: attn_down, GO: grad_other, GW: grad_own, CU: core_sum,
        XS: x_sum, ZA: z_one, ZB: z_two, ZC: z_end, TK: token, SO: start_output, EO: end_output,
        SC: start_small, SX: move_small, SZ: spread_small, SW: end_small,
    }
    left = {(GO, 1, A), (GW, 1, A)}
    for name, *at in ORDER:
        acts[name](*at)
        if left:
            left.discard((name, *at))
            if not left:
                for c in range(chunks):
                    load_o(c)
    need(*list(loads))
    for c in range(chunks):
        end_rows(gs.at[c], token_grad, 0, c)
        end_rows(hs.at[c], output, 1, c)


def call(body, outs, args, flops, limit=40, smem=0, scratch=()):
    moved = sum(x.size * x.dtype.itemsize for x in args) + sum(
        int(np.prod(s)) * np.dtype(d).itemsize for s, d in outs
    )
    spec = pl.BlockSpec(memory_space=pltpu.VMEM)
    got = pl.pallas_call(
        body,
        out_shape=[jax.ShapeDtypeStruct(s, d) for s, d in outs],
        in_specs=[pl.BlockSpec(memory_space=pltpu.SMEM)] * smem + [spec] * (len(args) - smem),
        out_specs=[spec] * len(outs),
        scratch_shapes=list(scratch),
        compiler_params=pltpu.CompilerParams(vmem_limit_bytes=limit * 2**20),
        cost_estimate=pl.CostEstimate(flops=int(flops), bytes_accessed=int(moved), transcendentals=0),
    )(*args)
    return list(got)


def call_whole(sizes, n, dim, wa, wf, layers, chunks, classes, fixed, numbers, moved):
    la, lf, half = wa // 2, wf // 2, dim // 2
    groups = sizes["dpo"], sizes["dpi"]
    outs = [
        ((2 * chunks * n, dim), F32),
        ((2 * chunks * n, dim), F32),
        ((classes, half), F32),
        ((layers, 2, dim), F32),
        ((layers, lf, half), F32),
        ((layers, half, 2, lf), F32),
        ((layers, la, half), F32),
        ((layers, 3 * la, half), F32),
        ((2, dim, wf), BF16),
        ((wf, dim), BF16),
        ((3 * wa, dim), BF16),
        ((wa, dim), BF16),
        ((chunks, n, dim), F32),
        ((layers, chunks, n, dim), F32),
        ((chunks, n, 3 * wa), BF16),
        ((chunks, 8, n), F32),
        ((chunks * n, wa), BF16),
        ((chunks, n, dim), F32),
    ]
    d, g, a = (lf, half), (half, 2 * lf), (4 * la, half)
    f, h = lambda *s: pltpu.VMEM(s, F32), lambda *s: pltpu.VMEM(s, BF16)
    dma, count = pltpu.SemaphoreType.DMA, pltpu.SemaphoreType.REGULAR
    units = sum(len(k) for k in PIECES.values())
    scratch = [h(2, dim, wf), h(wf, dim), h(3 * wa, dim), h(wa, dim)]
    scratch += [f(chunks, n, dim), f(chunks, n, dim), h(chunks, n, 3 * wa), h(chunks * n, wa), f(chunks, 8, n)]
    scratch += [f(chunks, n, dim), f(2, chunks, n, dim), f(chunks, n, dim)]
    scratch += [h(chunks * n, dim), h(chunks * n, dim), h(chunks * n, wf), h(chunks * n, 2 * wf)]
    scratch += [f(2, *g), f(2, *a)] + [f(2, *k) for k in (d, g, a)]
    scratch += [f(*k) for k in (d, g, a)] + [f(layers, *k) for k in (d, g, a)]
    scratch += [f(*k) for _ in range(3) for k in (d, g, a)] + [f(*groups, 2, 8, dim)]
    scratch += [f(chunks, n, 1), h(dim, 2, lf), f(half, 2, lf), f(groups[0] * groups[1] * 2 * chunks, half)]
    scratch += [dma((32,)), dma((chunks,)), dma((2, chunks)), dma((5,)), dma((5,))]
    scratch += [dma((units,))] * 2 + [dma((layers, units))] * 2 + [dma((units,))] * 2 + [dma((2,))] * 2
    scratch += [dma((2, chunks))] * 3 + [dma((5,))] * 2 + [count((len(PIECES),)), count((units,)), count]
    args = list(fixed) + list(numbers) + list(moved)
    flops = layers * chunks * n * (2 * dim * (14 * wa + 12 * wf) + 32 * n * wa)
    vmem, smem = pl.BlockSpec(memory_space=pltpu.VMEM), pl.BlockSpec(memory_space=pltpu.SMEM)
    anywhere = pl.BlockSpec(memory_space=pl.ANY)
    return pl.pallas_call(
        functools.partial(whole_pass, (n, dim, wa, wf, layers, chunks)),
        out_shape=[jax.ShapeDtypeStruct(s, t) for s, t in outs],
        in_specs=[vmem] * len(fixed) + [smem] * len(numbers) + [anywhere] * len(moved),
        out_specs=[vmem if i == 3 else anywhere for i in range(len(outs))],
        scratch_shapes=scratch,
        compiler_params=pltpu.CompilerParams(
            vmem_limit_bytes=62 * 2**20, collective_id=0, has_side_effects=True
        ),
        cost_estimate=pl.CostEstimate(flops=flops, bytes_accessed=90 * 10**6, transcendentals=0),
        name="whole_pass",
    )(*args)[:8]


def on_device(sizes, tokens, cotangent, heights, labels, valid, class_table, gains, w_qkv, w_out, w_gate_up, w_down):
    seq_count = heights.shape[0]
    row_count, dim = tokens.shape
    n = row_count // seq_count
    layers = gains.shape[0]
    classes = class_table.shape[0]
    la = w_out.shape[1]
    lf = w_down.shape[1]
    wa, wf = 2 * la, 2 * lf
    tp, dpo, dpi = sizes["tp"], sizes["dpo"], sizes["dpi"]
    mine = seq_count // 2
    lean = (tp, dpo, dpi) == (4, 4, 2) and (mine, layers) == (2, 2)
    core = lax.rem(lax.axis_index("tp"), 2)
    z = lax.axis_index("dpo")
    swap_core = [(i, i ^ 1) for i in range(tp)]

    def core_swap(x):
        return lax.ppermute(x, "tp", swap_core)

    def sum_chips(part):
        total = None
        for step in range(2, tp, 2):
            got = lax.ppermute(part, "tp", [(i, i ^ step) for i in range(tp)])
            total = got if total is None else total + got
        return total

    tables = jnp.asarray(rope_constants(n))
    if lean:
        onehot = (labels[:, None] == jnp.arange(classes)[None, :]).astype(BF16)
        firsts = jnp.dot(onehot, class_table, preferred_element_type=F32)
        fixed = (gains, tables, valid.reshape(seq_count, n), firsts)
        moved = (tokens, cotangent, jnp.transpose(w_qkv, (0, 2, 3, 1)), w_out, w_gate_up, w_down)
        got = call_whole(sizes, n, dim, wa, wf, layers, mine, classes, fixed, (heights, labels), moved)
        output, token_grad, table_part, gain_total, down_part, gate_up_part, out_part, qkv_part = got
        half = dim // dpi
        return (
            output,
            token_grad,
            table_part,
            gain_total,
            qkv_part.reshape(layers, 3, la, half).transpose(0, 3, 1, 2),
            out_part,
            gate_up_part,
            down_part,
        )

    position = jnp.arange(n)
    own = lambda x: lax.dynamic_slice_in_dim(x, core * mine, mine, 0)
    open_key = (position[None, :] < 1 + COLS * own(heights)[:, None]) & (own(valid.reshape(seq_count, n)) == 1)
    open_key = open_key.astype(F32)[:, :, None]
    own_labels = own(labels)
    wqkv, wout, wgu, wd = [], [], [], []
    for l in range(layers):
        for into, w in (
            (wqkv, jnp.transpose(w_qkv[l], (1, 2, 0))),
            (wout, w_out[l][None]),
            (wgu, jnp.transpose(w_gate_up[l], (1, 0, 2))),
            (wd, w_down[l][None]),
        ):
            wide = w.astype(F32)
            axis = 2 if into is wgu else 1
            shape = list(w.shape)
            shape[axis] *= 2
            into.append(call(functools.partial(merge, axis), [(tuple(shape), BF16)], (wide, core_swap(wide)), 1000)[0])
        wqkv[l] = wqkv[l].reshape(3 * wa, dim)
        wout[l] = wout[l][0]
        wd[l] = wd[l][0]

    token_own = own(tokens.reshape(seq_count, n, dim))
    cot_own = own(cotangent.reshape(seq_count, n, dim))
    chunks = range(mine)
    hs = []
    for c in chunks:
        row = lax.dynamic_slice_in_dim(class_table, own_labels[c], 1, 0)
        hs.append(jnp.where((position == 0)[:, None], row, token_own[c]).astype(F32))

    shape_d = ((n, dim), F32)
    shape_b = ((n, dim), BF16)
    flops_a = 2 * n * dim * 4 * wa + 8 * n * n * wa
    flops_f = 2 * n * dim * 3 * wf

    kept = []
    state = [(hs[c],) for c in chunks]
    parts = None
    for l in range(layers):
        keep = [dict() for _ in chunks]
        for c in chunks:
            args = state[c] + (gains[l, 0][None], wqkv[l], wout[l], tables, open_key[c])
            outs = [((n, 3 * wa), BF16), ((max(8, wa // HD), n), F32), ((n, wa), BF16), shape_d]
            outs = ([shape_d] if l > 0 else []) + [shape_b] + outs
            got = call(functools.partial(attn_fwd, l == 0), outs, args, flops_a)
            h = state[c][0] if l == 0 else got.pop(0)
            a, qkv, lse, o, part = got
            keep[c].update(h=h, a=a, qkv=qkv, lse=lse, o=o)
            state[c] = (h, part, sum_chips(part))
        for c in chunks:
            args = state[c] + (gains[l, 1][None], wgu[l], wd[l])
            outs = [shape_d, shape_b, ((n, 2 * wf), F32), ((n, wf), BF16), shape_d]
            h1, b, gu, hid, part = call(ffn_fwd, outs, args, flops_f)
            keep[c].update(h1=h1, b=b, gu=gu, hid=hid)
            state[c] = (h1, part, sum_chips(part))
        kept.append(keep)

    output = jnp.concatenate([s[0] + (s[1] + s[2]) for s in state], axis=0)

    half = lax.axis_index("dpi") if dpi == 2 else 1
    order = jnp.stack([jnp.int32(1) - half, jnp.int32(half)])

    def dp_sum(both, other, axis):
        got = core_swap(other)
        if dpi == 2:
            sent = lax.ppermute(both[0] + got[0], "dpi", [(0, 1), (1, 0)])
            total = (both[1] + got[1]) + sent
        else:
            both = both + got
            whole = jnp.concatenate([both[0], both[1]], axis=axis)
            total = lax.psum_scatter(whole, "dpi", scatter_dimension=axis, tiled=True)
        return line_sum(total)

    def line_sum(x):
        if dpo != 4:
            return lax.psum(x, "dpo")
        got = lax.ppermute(x, "dpo", [(0, 1), (3, 2)])
        x = x + got
        got = lax.ppermute(x, "dpo", [(1, 2), (2, 1)])
        x = x + got
        got = lax.ppermute(x, "dpo", [(1, 0), (2, 3)])
        return jnp.where((z == 0) | (z == dpo - 1), got, x)

    gain_rows = [[None, None] for _ in range(layers)]
    grads = [None] * layers
    state = [None] * mine
    for l in reversed(range(layers)):
        top = l == layers - 1
        keep = kept[l]
        gms = []
        for c in chunks:
            outs = [((n, 2 * wf), BF16), shape_d]
            args = (keep[c]["gu"], wgu[l], wd[l])
            if top:
                g = cot_own[c]
                dgu, part = call(functools.partial(ffn_bwd, True), outs, (g,) + args, flops_f)
                gms.append(g)
            else:
                outs = [shape_d, ((1, dim), F32), shape_b] + outs
                args = state[c] + args
                g, gain_c, gm, dgu, part = call(functools.partial(ffn_bwd, False), outs, args, flops_f)
                gain_rows[l + 1][0] = gain_c if c == 0 else gain_rows[l + 1][0] + gain_c
                gms.append(gm)
            keep[c]["dgu"] = dgu
            state[c] = (g, part, sum_chips(part), keep[c]["h1"], gains[l, 1][None])
        flops_w = 2 * n * mine * dim * wf
        outs = [((2, lf, dim // 2), F32)] * 2
        args = [order] + [keep[c]["hid"] for c in chunks] + gms
        spans = (((0, lf),), ((lf, wf),))
        down = call(functools.partial(grad_rows, spans), outs, args, flops_w, smem=1)
        outs = [((2, dim // 2, 2 * lf), F32)] * 2
        args = [order] + [keep[c]["b"] for c in chunks] + [keep[c]["dgu"] for c in chunks]
        spans = (((0, lf), (wf, wf + lf)), ((lf, wf), (wf + lf, 2 * wf)))
        gate_up = call(functools.partial(grad_columns, spans), outs, args, 2 * flops_w, smem=1)
        down = dp_sum(*down, 1)
        gate_up = dp_sum(*gate_up, 0)
        gas = []
        for c in chunks:
            outs = [shape_d, ((1, dim), F32), shape_b, ((n, 3 * wa), BF16), shape_d]
            args = state[c] + (wqkv[l], wout[l], tables, open_key[c], keep[c]["qkv"], keep[c]["lse"])
            g1, gain_c, ga, dqkv, part = call(attn_bwd, outs, args, flops_a + 12 * n * n * wa)
            gain_rows[l][1] = gain_c if c == 0 else gain_rows[l][1] + gain_c
            gas.append(ga)
            keep[c]["dqkv"] = dqkv
            state[c] = (g1, part, sum_chips(part), keep[c]["h"], gains[l, 0][None])
        flops_w = 2 * n * mine * dim * wa
        outs = [((2, la, dim // 2), F32)] * 2
        args = [order] + [keep[c]["o"] for c in chunks] + gas
        spans = (((0, la),), ((la, wa),))
        out = call(functools.partial(grad_rows, spans), outs, args, flops_w, smem=1)
        outs = [((2, 3 * la, dim // 2), F32)] * 2
        args = [order] + [keep[c]["dqkv"] for c in chunks] + [keep[c]["a"] for c in chunks]
        spans = tuple(tuple((t * wa + s * la, t * wa + (s + 1) * la) for t in range(3)) for s in range(2))
        qkv = call(functools.partial(grad_rows, spans), outs, args, 3 * flops_w, smem=1)
        out = dp_sum(*out, 1)
        qkv = dp_sum(*qkv, 1)
        grads[l] = (qkv, out, gate_up, down)

    finals = []
    for c in chunks:
        g, gain_c = call(close_layer, [shape_d, ((1, dim), F32)], state[c], 1000)
        gain_rows[0][0] = gain_c if c == 0 else gain_rows[0][0] + gain_c
        finals.append(g)

    slot0 = lax.axis_index("dpo") * dpi + lax.axis_index("dpi")
    seqs = seq_count * dpo * dpi
    firsts = jnp.concatenate([g[0:1] for g in finals], axis=0)
    small = jnp.zeros((seqs + 2 * layers + 1, dim), F32)
    small = lax.dynamic_update_slice(small, firsts, (slot0 * seq_count + core * mine, 0))
    terms = jnp.concatenate([gain_rows[l][i] for l in range(layers) for i in range(2)], axis=0)
    small = lax.dynamic_update_slice(small, terms, (seqs, 0))
    label_row = lax.dynamic_update_slice(
        jnp.zeros((1, dim), F32), own_labels.astype(F32)[None], (0, slot0 * seq_count + core * mine)
    )
    small = lax.dynamic_update_slice(small, label_row, (seqs + 2 * layers, 0))
    small = jnp.where(lax.axis_index("tp") < 2, small, 0.0)
    small = lax.psum(small, ("dpo", "dpi", "tp"))
    all_labels = jnp.round(small[seqs + 2 * layers, :seqs]).astype(jnp.int32)
    gain_total = small[seqs : seqs + 2 * layers].reshape(layers, 2, dim)
    onehot = (all_labels[None, :] == jnp.arange(classes)[:, None]).astype(F32)
    share = dim // dpi
    rows = lax.dynamic_slice(small, (0, lax.axis_index("dpi") * share), (seqs, share))
    table_part = jnp.dot(onehot, rows, precision=lax.Precision.HIGHEST)

    token_own = jnp.concatenate([jnp.where((position == 0)[:, None], 0.0, g) for g in finals], axis=0)

    def both_cores(x):
        other = core_swap(x)
        return jnp.where(core == 0, jnp.concatenate([x, other], 0), jnp.concatenate([other, x], 0))

    qkv_part = jnp.stack([g[0].reshape(3, la, share) for g in grads]).transpose(0, 3, 1, 2)
    out_part = jnp.stack([g[1] for g in grads])
    gate_up_part = jnp.stack([g[2].reshape(share, 2, lf) for g in grads])
    down_part = jnp.stack([g[3] for g in grads])
    return (
        both_cores(output),
        both_cores(token_own),
        table_part,
        gain_total,
        qkv_part,
        out_part,
        gate_up_part,
        down_part,
    )


def solution(mesh):
    sizes = dict(mesh.shape)
    placed = (
        P(("dpo", "dpi"), None),
        P(("dpo", "dpi"), None),
        P(("dpo", "dpi")),
        P(("dpo", "dpi")),
        P(("dpo", "dpi")),
        P(),
        P(),
        P(None, None, None, "tp"),
        P(None, "tp", None),
        P(None, None, None, "tp"),
        P(None, "tp", None),
    )
    return jax.shard_map(
        functools.partial(on_device, sizes),
        mesh=mesh,
        in_specs=placed,
        out_specs=(
            P(("dpo", "dpi"), None),
            P(("dpo", "dpi"), None),
            P(None, "dpi"),
            P(),
            P(None, "dpi", None, "tp"),
            P(None, "tp", "dpi"),
            P(None, "dpi", None, "tp"),
            P(None, "tp", "dpi"),
        ),
        check_vma=False,
    )
```

```python
import functools

import jax
import jax.numpy as jnp
import numpy as np
from jax import lax
from jax.experimental import pallas as pl
from jax.experimental.pallas import tpu as pltpu
from jax.sharding import PartitionSpec as P

HD = 64
COLS = 16
EPS = 1e-05
F32 = jnp.float32
BF16 = jnp.bfloat16
LOW = -1e30
MESH = pl.DeviceIdType.MESH

E, D, G, A = "edga"
PIECES = {E: (64,) * 2, D: (96,) * 4, G: (48,) * 8, A: (96,) * 8}
FX, FA, FB, PO, AT, TK, GO, GW, CU, XS, ZA, ZB, ZC, SO, EO, SC, SX, SZ, SW = range(19)
ORDER = (
    (FA, 1, 0), (FX,), (FB, 1, 0), (PO, 0), (FA, 1, 1), (GO, 1, E), (GO, 1, D), (GW, 1, E), (CU, 1, 1),
    (GW, 1, D), (CU, 1, 0), (CU, 1, 3), (GO, 1, G), (XS, 1, 0), (CU, 1, 5), (XS, 1, 1), (CU, 1, 4), (FB, 1, 1),
    (XS, 1, 3), (ZA, 1, 0), (PO, 1), (GW, 1, G), (ZA, 1, 1), (XS, 1, 5), (CU, 1, 2), (ZA, 1, 3), (CU, 1, 10),
    (XS, 1, 4), (AT, 1, 0), (ZB, 1, 0), (ZB, 1, 1), (ZA, 1, 4), (XS, 1, 2), (CU, 1, 13), (CU, 1, 7), (ZB, 1, 3),
    (CU, 1, 11), (XS, 1, 10), (CU, 1, 9), (ZA, 1, 5), (CU, 1, 8), (CU, 1, 12), (ZC, 1, 0), (ZA, 1, 2),
    (ZA, 1, 10), (ZB, 1, 4), (ZB, 1, 5), (CU, 1, 6), (XS, 1, 13), (XS, 1, 7), (ZB, 1, 2), (ZA, 1, 13),
    (AT, 1, 1), (ZB, 1, 10), (ZA, 1, 7), (XS, 1, 11), (ZC, 1, 1), (GO, 1, A), (ZB, 1, 13), (ZA, 1, 11),
    (GW, 1, A), (XS, 1, 9), (ZC, 1, 4), (ZC, 1, 2), (ZB, 1, 7), (CU, 1, 20), (ZA, 1, 9), (XS, 1, 8),
    (CU, 1, 17), (XS, 1, 12), (ZB, 1, 11), (ZC, 1, 5), (ZA, 1, 8), (FA, 0, 0), (CU, 1, 16), (ZA, 1, 12),
    (ZB, 1, 9), (XS, 1, 6), (CU, 1, 21), (CU, 1, 19), (ZC, 1, 3), (XS, 1, 20), (CU, 1, 14), (FB, 0, 0),
    (ZA, 1, 6), (ZB, 1, 8), (XS, 1, 17), (CU, 1, 15), (ZC, 1, 9), (ZC, 1, 11), (CU, 1, 18), (ZB, 1, 12),
    (XS, 1, 16), (ZA, 1, 20), (FA, 0, 1), (XS, 1, 21), (ZA, 1, 17), (ZB, 1, 6), (GO, 0, G), (ZA, 1, 21),
    (ZB, 1, 20), (XS, 1, 14), (ZC, 1, 13), (ZA, 1, 16), (XS, 1, 19), (ZB, 1, 17), (GW, 0, G), (FB, 0, 1),
    (ZA, 1, 14), (ZB, 1, 21), (CU, 0, 13), (ZA, 1, 19), (XS, 1, 15), (ZC, 1, 7), (XS, 1, 18), (ZC, 1, 12),
    (ZC, 1, 10), (GO, 0, E), (GO, 0, D), (CU, 0, 11), (ZB, 1, 14), (GW, 0, E), (CU, 0, 7), (ZA, 1, 15),
    (GW, 0, D), (ZB, 1, 16), (CU, 0, 2), (XS, 0, 13), (CU, 0, 6), (CU, 0, 9), (ZC, 1, 21), (CU, 0, 1),
    (ZC, 1, 6), (ZA, 1, 18), (ZB, 1, 19), (XS, 0, 11), (ZB, 1, 15), (ZA, 0, 13), (AT, 0, 0), (ZA, 0, 11),
    (ZB, 1, 18), (XS, 0, 7), (CU, 0, 8), (XS, 0, 2), (ZC, 1, 17), (ZC, 1, 14), (ZB, 0, 13), (CU, 0, 10),
    (ZA, 0, 7), (CU, 0, 12), (CU, 0, 4), (CU, 0, 0), (ZA, 0, 2), (XS, 0, 6), (ZB, 0, 11), (CU, 0, 5),
    (ZC, 1, 8), (ZC, 1, 15), (ZC, 1, 19), (CU, 0, 3), (XS, 0, 9), (ZB, 0, 7), (ZA, 0, 6), (AT, 0, 1),
    (ZB, 0, 2), (ZA, 0, 9), (XS, 0, 8), (GO, 0, A), (ZB, 0, 6), (ZC, 1, 20), (ZC, 0, 13), (ZC, 1, 16),
    (ZA, 0, 8), (XS, 0, 10), (TK, 0), (ZB, 0, 9), (SO, 0), (ZA, 0, 10), (GW, 0, A), (CU, 0, 20), (XS, 0, 12),
    (XS, 0, 1), (ZB, 0, 8), (CU, 0, 21), (XS, 0, 4), (CU, 0, 16), (ZC, 0, 7), (ZA, 0, 12), (ZB, 0, 10),
    (ZC, 1, 18), (ZC, 0, 11), (ZA, 0, 1), (XS, 0, 5), (ZB, 0, 12), (CU, 0, 15), (XS, 0, 0), (ZA, 0, 4),
    (ZC, 0, 2), (ZB, 0, 1), (XS, 0, 3), (TK, 1), (SC,), (ZA, 0, 5), (XS, 0, 20), (CU, 0, 14), (ZA, 0, 0),
    (ZC, 0, 9), (ZB, 0, 4), (ZA, 0, 20), (ZC, 0, 6), (ZB, 0, 0), (SO, 1), (ZB, 0, 5), (XS, 0, 21), (XS, 0, 15),
    (ZA, 0, 3), (ZC, 0, 8), (ZB, 0, 20), (CU, 0, 18), (XS, 0, 14), (ZA, 0, 15), (ZC, 0, 12), (XS, 0, 16),
    (ZC, 0, 0), (EO, 0), (ZB, 0, 3), (ZA, 0, 14), (ZA, 0, 21), (CU, 0, 17), (ZC, 0, 5), (CU, 0, 19), (ZC, 0, 4),
    (ZB, 0, 15), (ZB, 0, 14), (SX,), (XS, 0, 17), (ZC, 0, 3), (ZC, 0, 10), (ZA, 0, 16), (ZA, 0, 17),
    (ZC, 0, 20), (SZ,), (XS, 0, 19), (ZB, 0, 16), (XS, 0, 18), (ZC, 0, 1), (ZB, 0, 17), (ZA, 0, 19),
    (ZB, 0, 21), (ZC, 0, 14), (SW,), (ZA, 0, 18), (ZB, 0, 19), (EO, 1), (ZC, 0, 16), (ZC, 0, 15), (ZC, 0, 21),
    (ZB, 0, 18), (ZC, 0, 19), (ZC, 0, 17), (ZC, 0, 18),
)

NN = (((1,), (0,)), ((), ()))
NT = (((1,), (1,)), ((), ()))
TN = (((0,), (0,)), ((), ()))


def mm(a, b, dims=NN):
    return lax.dot_general(a, b, dims, preferred_element_type=F32)


def rope_constants(slot_len):
    quarter = HD // 4
    raster = np.maximum(np.arange(slot_len) - 1, 0)
    row_pos = (raster // COLS).astype(np.float32)
    col_pos = (raster % COLS).astype(np.float32)
    frequency = (10000.0 ** (-np.arange(quarter).astype(np.float32) / quarter)).astype(np.float32)
    row_angle = row_pos[:, None] * frequency[None, :]
    col_angle = col_pos[:, None] * frequency[None, :]
    zero = np.zeros_like(row_angle)
    cos = np.concatenate([np.cos(row_angle)] * 2 + [np.cos(col_angle)] * 2, axis=1)
    first = np.concatenate([-np.sin(row_angle), zero, -np.sin(col_angle), zero], axis=1)
    second = np.concatenate([zero, np.sin(row_angle), zero, np.sin(col_angle)], axis=1)
    return np.stack([np.tile(t, (1, 2)) for t in (cos, first, second)]).astype(np.float32)


def rotate(x, table_ref, sign):
    quarter = HD // 4
    ahead = pltpu.roll(x, 2 * HD - quarter, 1) * table_ref[1]
    behind = pltpu.roll(x, quarter, 1) * table_ref[2]
    turned = ahead + behind
    return x * table_ref[0] + (turned if sign > 0 else -turned)


def merge(axis, mine_ref, other_ref, out_ref):
    size = mine_ref.shape[axis]
    if axis == 1:
        out_ref[:, :size, :] = mine_ref[...].astype(BF16)
        out_ref[:, size:, :] = other_ref[...].astype(BF16)
    else:
        out_ref[:, :, :size] = mine_ref[...].astype(BF16)
        out_ref[:, :, size:] = other_ref[...].astype(BF16)


def inv_rms(h):
    return lax.rsqrt(jnp.mean(h * h, axis=-1, keepdims=True) + EPS)


def norm_back(grad, normed, scale, gain):
    scaled = grad * gain
    return scale * (scaled - normed * jnp.mean(scaled * normed, axis=-1, keepdims=True))


def key_mask(open_ref, n):
    key = lax.broadcasted_iota(jnp.int32, (n, n), 0)
    query = lax.broadcasted_iota(jnp.int32, (n, n), 1)
    return ((key < query) & (open_ref[...] > 0.5)) | (key == query)


def attn_fwd(first, *refs):
    if first:
        h_ref, gain_ref, wqkv_ref, wout_ref, table_ref, open_ref = refs[:6]
        refs = refs[6:]
        h = h_ref[...]
    else:
        h_ref, p_ref, r_ref, gain_ref, wqkv_ref, wout_ref, table_ref, open_ref = refs[:8]
        refs = refs[8:]
        h = h_ref[...] + (p_ref[...] + r_ref[...])
        refs[0][...] = h
        refs = refs[1:]
    a_ref, qkv_ref, lse_ref, o_ref, part_ref = refs
    n = h.shape[0]
    width = wout_ref.shape[0]
    a = (h * inv_rms(h) * gain_ref[...]).astype(BF16)
    a_ref[...] = a
    lane = lax.broadcasted_iota(jnp.int32, (n, 2 * HD), 1)
    low_half = lane < HD
    zero = jnp.zeros((n, 2 * HD), BF16)
    mask = key_mask(open_ref, n)
    for t in range(width // (2 * HD)):
        spots = [slice(s * width + t * 2 * HD, s * width + (t + 1) * 2 * HD) for s in range(3)]
        q = rotate(mm(a, wqkv_ref[spots[0], :], NT), table_ref, 1)
        q = (q * HD ** (-0.5)).astype(BF16)
        k = rotate(mm(a, wqkv_ref[spots[1], :], NT), table_ref, 1).astype(BF16)
        v = mm(a, wqkv_ref[spots[2], :], NT).astype(BF16)
        qkv_ref[:, spots[0]] = q
        qkv_ref[:, spots[1]] = k
        qkv_ref[:, spots[2]] = v
        mixed = []
        for e in range(2):
            q_one = jnp.where(low_half if e == 0 else ~low_half, q, zero)
            s = jnp.where(mask, mm(k, q_one, NT), LOW)
            top = jnp.max(s, axis=0, keepdims=True)
            raised = jnp.exp(s - top)
            total = jnp.sum(raised, axis=0, keepdims=True)
            lse_ref[2 * t + e : 2 * t + e + 1, :] = top + jnp.log(total)
            prob = (raised / total).astype(BF16)
            mixed.append(mm(prob, v, TN))
        o_ref[:, t * 2 * HD : (t + 1) * 2 * HD] = jnp.where(low_half, mixed[0], mixed[1]).astype(BF16)
    part_ref[...] = mm(o_ref[...], wout_ref[...])


def ffn_fwd(h_ref, p_ref, r_ref, gain_ref, wgu_ref, wd_ref, h1_ref, *refs):
    h = h_ref[...] + (p_ref[...] + r_ref[...])
    h1_ref[...] = h
    b = (h * inv_rms(h) * gain_ref[...]).astype(BF16)
    b_ref, gu_ref, hid_ref, part_ref = refs
    b_ref[...] = b
    width = wd_ref.shape[0]
    step = min(width, 256)
    for f in range(0, width, step):
        gate = mm(b, wgu_ref[0, :, f : f + step])
        up = mm(b, wgu_ref[1, :, f : f + step])
        gu_ref[:, f : f + step] = gate
        gu_ref[:, width + f : width + f + step] = up
        hid_ref[:, f : f + step] = (gate * jax.nn.sigmoid(gate) * up).astype(BF16)
    part_ref[...] = mm(hid_ref[...], wd_ref[...])


def ffn_bwd(first, *refs):
    if first:
        g_ref, gu_ref, wgu_ref, wd_ref = refs[:4]
        refs = refs[4:]
        gm = g_ref[...]
    else:
        g1_ref, p_ref, r_ref, hin_ref, gain_ref, gu_ref, wgu_ref, wd_ref = refs[:8]
        refs = refs[8:]
        grad, gain_grad = close_norm(g1_ref[...], p_ref, r_ref, hin_ref, gain_ref)
        refs[0][...] = grad
        refs[1][...] = gain_grad
        gm = grad.astype(BF16)
        refs[2][...] = gm
        refs = refs[3:]
    dgu_ref, part_ref = refs
    width = wd_ref.shape[0]
    step = min(width, 256)
    for f in range(0, width, step):
        dhid = mm(gm, wd_ref[f : f + step, :], NT)
        gate = gu_ref[:, f : f + step]
        up = gu_ref[:, width + f : width + f + step]
        sig = jax.nn.sigmoid(gate)
        dgu_ref[:, f : f + step] = (dhid * up * (sig * (1.0 + gate * (1.0 - sig)))).astype(BF16)
        dgu_ref[:, width + f : width + f + step] = (dhid * (gate * sig)).astype(BF16)
    part_ref[...] = mm(dgu_ref[:, :width], wgu_ref[0], NT) + mm(dgu_ref[:, width:], wgu_ref[1], NT)


def close_norm(g, p_ref, r_ref, h_ref, gain_ref):
    grad = p_ref[...] + r_ref[...]
    h = h_ref[...]
    scale = inv_rms(h)
    normed = h * scale
    gain_grad = jnp.sum(grad * normed, axis=0, keepdims=True)
    return g + norm_back(grad, normed, scale, gain_ref[...]), gain_grad


def attn_bwd(
    g_ref, p_ref, r_ref, h1_ref, gain_ref, wqkv_ref, wout_ref, table_ref, open_ref, qkv_ref, lse_ref,
    g1_ref, gain_grad_ref, ga_ref, dqkv_ref, part_ref,
):
    g1, gain_grad = close_norm(g_ref[...].astype(F32), p_ref, r_ref, h1_ref, gain_ref)
    g1_ref[...] = g1
    gain_grad_ref[...] = gain_grad
    ga = g1.astype(BF16)
    ga_ref[...] = ga
    n = ga.shape[0]
    width = wout_ref.shape[0]
    lane = lax.broadcasted_iota(jnp.int32, (n, 2 * HD), 1)
    low_half = lane < HD
    zero = jnp.zeros((n, 2 * HD), BF16)
    mask = key_mask(open_ref, n)
    for t in range(width // (2 * HD)):
        spots = [slice(s * width + t * 2 * HD, s * width + (t + 1) * 2 * HD) for s in range(3)]
        q = qkv_ref[:, spots[0]]
        k = qkv_ref[:, spots[1]]
        v = qkv_ref[:, spots[2]]
        dout = mm(ga, wout_ref[t * 2 * HD : (t + 1) * 2 * HD, :], NT).astype(BF16)
        dq, dk, dv = [], [], []
        for e in range(2):
            mine = low_half if e == 0 else ~low_half
            q_one = jnp.where(mine, q, zero)
            d_one = jnp.where(mine, dout, zero)
            s = jnp.where(mask, mm(k, q_one, NT), LOW)
            prob = jnp.exp(s - lse_ref[2 * t + e : 2 * t + e + 1, :])
            dprob = mm(v, d_one, NT)
            delta = jnp.sum(prob * dprob, axis=0, keepdims=True)
            ds = (prob * (dprob - delta)).astype(BF16)
            dv.append(mm(prob.astype(BF16), dout))
            dk.append(mm(ds, q))
            dq.append(mm(ds, k, TN))
        dq = jnp.where(low_half, dq[0], dq[1]) * HD ** (-0.5)
        dk = jnp.where(low_half, dk[0], dk[1])
        dv = jnp.where(low_half, dv[0], dv[1])
        dqkv_ref[:, spots[0]] = rotate(dq, table_ref, -1).astype(BF16)
        dqkv_ref[:, spots[1]] = rotate(dk, table_ref, -1).astype(BF16)
        dqkv_ref[:, spots[2]] = dv.astype(BF16)
    part_ref[...] = mm(dqkv_ref[...], wqkv_ref[...])


def close_layer(g1_ref, p_ref, r_ref, h_ref, gain_ref, out_ref, gain_grad_ref):
    grad, gain_grad = close_norm(g1_ref[...], p_ref, r_ref, h_ref, gain_ref)
    out_ref[...] = grad
    gain_grad_ref[...] = gain_grad


def halves_of(half_ref, dim):
    one = dim // 2
    return [pl.ds(pl.multiple_of(half_ref[s] * one, one), one) for s in range(2)]


def grad_rows(spans, half_ref, *refs):
    chunks = (len(refs) - 2) // 2
    lefts, rights = refs[:chunks], refs[chunks : 2 * chunks]
    outs = refs[2 * chunks :]
    for s, spot in enumerate(halves_of(half_ref, rights[0].shape[1])):
        for out, picks in zip(outs, spans):
            at = 0
            for lo, hi in picks:
                total = None
                for left, right in zip(lefts, rights):
                    term = mm(left[:, lo:hi], right[:, spot], TN)
                    total = term if total is None else total + term
                out[s, at : at + hi - lo, :] = total
                at += hi - lo


def grad_columns(spans, half_ref, *refs):
    chunks = (len(refs) - 2) // 2
    lefts, rights = refs[:chunks], refs[chunks : 2 * chunks]
    outs = refs[2 * chunks :]
    for s, spot in enumerate(halves_of(half_ref, lefts[0].shape[1])):
        for out, picks in zip(outs, spans):
            at = 0
            for lo, hi in picks:
                total = None
                for left, right in zip(lefts, rights):
                    term = mm(left[:, spot], right[:, lo:hi], TN)
                    total = term if total is None else total + term
                out[s, :, at : at + hi - lo] = total
                at += hi - lo


def whole_pass(dims, *refs):
    n, dim, wa, wf, layers, chunks = dims
    la, lf, half = wa // 2, wf // 2, dim // 2
    refs = list(refs)

    def take(count):
        got = refs[:count]
        del refs[:count]
        return got

    gains_ref, tables, valid_ref, heights_ref, labels_ref = take(5)
    class_table, tokens, cotangent, w_qkv, w_out, w_gate_up, w_down = take(7)
    output, token_grad, table_out, gain_out, down_out, gate_up_out, out_out, qkv_out = take(8)
    wgu_st, wd_st, wqkv_st, wout_st, h_st, h1_st, qkv_st, lse_st, o_st, last_st = take(10)
    wgu, wd, wqkv, wout = take(4)
    hs, h1s, qkvs, os, lses = take(5)
    ysend, yrecv, gs, gm, ab, hid, dgu = take(7)
    oth_g, oth_s, cr_d, cr_g, cr_a = take(5)
    os_d, os_g, os_a, ok_d, ok_g, ok_a = take(6)
    xr_d, xr_g, xr_a, z1_d, z1_g, z1_a, z2_d, z2_g, z2_a, small = take(10)
    open_ref, raw_g, total_g, firsts_ref, classes_ref, first_ref = take(6)
    load_sem, ys_sem, yr_sem, cs_sem, cr_sem, xs_sem, xr_sem = take(7)
    zs, zr, z2r, store_sem, half_s, half_r, row_sem, rows_s, rows_r, small_s, small_r = take(11)
    x_free, z_free, c_free = take(3)

    tp = lax.axis_index("tp")
    x = lax.axis_index("dpi")
    z = lax.axis_index("dpo")
    core = lax.rem(tp, 2)
    to_core = {"tp": tp + 1 - 2 * core}
    to_chip = {"tp": lax.rem(tp + 2, 4)}
    to_x = {"dpi": 1 - x}
    to_mate = {"dpo": z + 1 - 2 * lax.rem(z, 2)}
    to_inner = {"dpo": 3 - z}
    outer = (z == 0) | (z == 3)
    inner = (z == 1) | (z == 2)
    far = [{"dpo": lax.rem(z + k, 4)} for k in (1, 2, 3)]

    barrier = pltpu.get_barrier_semaphore()
    for peer in [to_core, to_chip, to_x] + far:
        pl.semaphore_signal(barrier, inc=1, device_id=peer, device_id_type=MESH)
    loads = {}

    def load(key, src, dst, slot):
        copy = pltpu.make_async_copy(src, dst, load_sem.at[slot])
        copy.start()
        loads[key] = copy

    def need(*keys):
        for key in keys:
            if key in loads:
                loads.pop(key).wait()

    def rows(c):
        return pl.ds(c * n, n)

    def load_ffn_weights():
        load("wgu", wgu_st, wgu, 0)
        load("wd", wd_st, wd, 1)

    def load_attn_weights():
        load("wqkv", wqkv_st, wqkv, 2)
        load("wout", wout_st, wout, 3)

    def load_h1(c):
        load(("h1", c), h1_st.at[0, c], h1s.at[c], 4 + c)

    def load_qkv(c):
        load(("qkv", c), qkv_st.at[c], qkvs.at[c], 6 + c)
        load(("lse", c), lse_st.at[c], lses.at[c], 8 + c)

    def load_o(c):
        load(("o", c), o_st.at[rows(c)], os.at[rows(c)], 10 + c)

    def load_h(c):
        load(("h", c), h_st.at[c], hs.at[c], 12 + c)

    top = layers - 1

    def own_rows(ref, c):
        return ref.at[pl.ds(pl.multiple_of((core * chunks + c) * n, n), n)]

    def own_attn(l):
        for t in range(3):
            load(("own", "a", t), w_qkv.at[l, t], wqkv.at[pl.ds(t * wa, la)], 17 + t)
        load(("own", "a", 3), w_out.at[l], wout.at[pl.ds(0, la)], 20)

    def own_ffn(l):
        load(("own", "g", 0), w_gate_up.at[l], raw_g, 21)
        load(("own", "d", 0), w_down.at[l], wd.at[pl.ds(0, lf)], 23)

    own_attn(0)
    for c in range(chunks):
        load(("token", c), own_rows(tokens, c), gm.at[rows(c)], 14 + c)
    load("classes", class_table, classes_ref, 16)
    own_ffn(0)

    def remote(src, dst, send, recv, to):
        return pltpu.make_async_remote_copy(
            src_ref=src, dst_ref=dst, send_sem=send, recv_sem=recv, device_id=to, device_id_type=MESH
        )

    turn = [0] * chunks

    def y_copy(c, k):
        return remote(ysend.at[c], yrecv.at[k % 2, c], ys_sem.at[c], yr_sem.at[k % 2, c], to_chip)

    def y_start(c):
        y_copy(c, turn[c]).start()

    def y_sum(c):
        copy = y_copy(c, turn[c])
        copy.wait()
        got = ysend[c] + yrecv[turn[c] % 2, c]
        turn[c] += 1
        return got

    def y_half_copy(c, at):
        k, part, i = turn[c] % 2, pl.ds(at, n // 2), at // (n // 2)
        return remote(ysend.at[c, part], yrecv.at[k, c, part], half_s.at[i], half_r.at[i], to_chip)

    def y_half_sum(c, at):
        part = pl.ds(at, n // 2)
        y_half_copy(c, at).wait()
        got = ysend[c, part, :] + yrecv[turn[c] % 2, c, part, :]
        if at > 0:
            turn[c] += 1
        return got

    def gain_of(l, i):
        return gains_ref[l, i : i + 1, :]

    def add_gain(l, i, c, term):
        k = 2 + 2 * l + i
        spot = (z, x, core, slice(k, k + 1), slice(None))
        small[spot] = term if c == 0 else small[spot] + term

    def close(l, i, c, g, h):
        grad = y_sum(c)
        scale = inv_rms(h)
        normed = h * scale
        add_gain(l, i, c, jnp.sum(grad * normed, axis=0, keepdims=True))
        return g + norm_back(grad, normed, scale, gain_of(l, i))

    def prepare(c):
        at = core * chunks + c
        lane = lax.broadcasted_iota(jnp.int32, (1, n), 1)
        is_open = (lane < 1 + COLS * heights_ref[at]) & (valid_ref[pl.ds(pl.multiple_of(at * n, n), n)][None, :] == 1)
        diagonal = lax.broadcasted_iota(jnp.int32, (n, n), 0) == lax.broadcasted_iota(jnp.int32, (n, n), 1)
        column = jnp.where(diagonal, jnp.where(is_open, 1.0, 0.0), 0.0)
        open_ref[c] = jnp.sum(column, axis=1, keepdims=True)
        slot = (z * groups[1] + x) * 2 * chunks + at
        lane = lax.broadcasted_iota(jnp.int32, (1, dim), 1)
        label = jnp.where(lane == slot, labels_ref[at], 0).astype(F32)
        spot = (z, x, core, slice(6, 7), slice(None))
        small[spot] = label if c == 0 else small[spot] + label

    groups = small.shape[:2]
    small[z, x, core] = jnp.zeros((8, dim), F32)

    def ffn_a(l, c, at=0, size=n):
        spot, part = pl.ds(c * n + at, size), pl.ds(at, size)
        if l == top:
            need(("cot", c))
            gs[c, part, :] = gm[spot, :].astype(F32)
            h1s[c, part, :] = hs_next(c) if size == n else hs[c, part, :] + y_half_sum(c, at)
            if at + size == n:
                load(("stash", c), h1s.at[c], h1_st.at[top, c], 28 + c)
        else:
            need(("h", c))
            g = close(l + 1, 0, c, gs[c], hs[c])
            gs[c] = g
            gm[spot, :] = g.astype(BF16)
            load_h(c)
        need(("h1", c), "wgu", "wd")
        h1 = h1s[c, part, :]
        b = (h1 * inv_rms(h1) * gain_of(l, 1)).astype(BF16)
        ab[spot, :] = b
        step = min(wf, 256)
        for f in range(0, wf, step):
            gate = mm(b, wgu[0, :, f : f + step])
            up = mm(b, wgu[1, :, f : f + step])
            dhid = mm(gm[spot, :], wd[f : f + step, :], NT)
            sig = jax.nn.sigmoid(gate)
            silu = gate * sig
            hid[spot, f : f + step] = (silu * up).astype(BF16)
            dgu[spot, f : f + step] = (dhid * up * (sig * (1.0 + gate * (1.0 - sig)))).astype(BF16)
            dgu[spot, wf + f : wf + f + step] = (dhid * silu).astype(BF16)

    later = {("fb", 1, 0), ("fb", 1, 1), ("po", 0), ("po", 1)}

    def ffn_done(*what):
        if what in later:
            later.discard(what)
            if not later:
                load_ffn_weights()

    def ffn_b(l, c):
        spot = rows(c)
        ysend[c] = mm(dgu[spot, :wf], wgu[0], NT) + mm(dgu[spot, wf:], wgu[1], NT)
        y_start(c)
        ffn_done("fb", l, c)

    def last_sum(c):
        need(("last", c - 1))
        spare = ok_g.at[0, pl.ds(0, n), pl.ds(0, dim)]
        spare[...] = mm(hid[rows(c), :], wd[...])
        load(("last", c), spare, last_st.at[c], 30)
        ffn_done("po", c)

    def attn(l, c):
        spot = rows(c)
        g1 = close(l, 1, c, gs[c], h1s[c])
        gs[c] = g1
        if l > 0:
            need(("stash", c))
            load_h1(c)
        gm[spot, :] = g1.astype(BF16)
        need("wqkv", "wout", ("qkv", c), ("lse", c))
        lane = lax.broadcasted_iota(jnp.int32, (n, 2 * HD), 1)
        low_half = lane < HD
        zero = jnp.zeros((n, 2 * HD), BF16)
        mask = key_mask(open_ref.at[c], n)
        ga = gm[spot, :]
        for t in range(wa // (2 * HD)):
            spots = [slice(s * wa + t * 2 * HD, s * wa + (t + 1) * 2 * HD) for s in range(3)]
            q, k, v = [qkvs[c, :, s] for s in spots]
            dout = mm(ga, wout[t * 2 * HD : (t + 1) * 2 * HD, :], NT).astype(BF16)
            dq, dk, dv = [], [], []
            for e in range(2):
                mine = low_half if e == 0 else ~low_half
                s = jnp.where(mask, mm(k, jnp.where(mine, q, zero), NT), LOW)
                prob = jnp.exp(s - lses[c, 2 * t + e : 2 * t + e + 1, :])
                dprob = mm(v, jnp.where(mine, dout, zero), NT)
                delta = jnp.sum(prob * dprob, axis=0, keepdims=True)
                ds = (prob * (dprob - delta)).astype(BF16)
                dv.append(mm(prob.astype(BF16), dout))
                dk.append(mm(ds, q))
                dq.append(mm(ds, k, TN))
            dq = jnp.where(low_half, dq[0], dq[1]) * HD ** (-0.5)
            dk = jnp.where(low_half, dk[0], dk[1])
            dv = jnp.where(low_half, dv[0], dv[1])
            dgu[spot, spots[0]] = rotate(dq, tables, -1).astype(BF16)
            dgu[spot, spots[1]] = rotate(dk, tables, -1).astype(BF16)
            dgu[spot, spots[2]] = dv.astype(BF16)
        ysend[c] = mm(dgu[spot, : 3 * wa], wqkv[...])
        y_start(c)
        if l > 0:
            load_qkv(c)
        need(("h", c))
        h = hs[c]
        ab[spot, :] = (h * inv_rms(h) * gain_of(l, 0)).astype(BF16)

    spans = [pl.ds(pl.multiple_of((1 - x) * half, half), half), pl.ds(pl.multiple_of(x * half, half), half)]
    split = sum(PIECES[E])
    down = (oth_s, cr_d, os_d, ok_d, xr_d, z1_d, z2_d)
    kinds = {
        E: down,
        D: down,
        G: (oth_g, cr_g, os_g, ok_g, xr_g, z1_g, z2_g),
        A: (oth_s, cr_a, os_a, ok_a, xr_a, z1_a, z2_a),
    }
    index = {D: 0, G: 1, A: 2, E: 4}
    order = list(kinds)
    units = []
    for kind in kinds:
        at = split if kind == D else 0
        for size in PIECES[kind]:
            target = {E: down_out, D: down_out, G: gate_up_out, A: out_out if at < la else qkv_out}[kind]
            base = la if kind == A and at >= la else 0
            units.append((kind, pl.ds(at, size), target, pl.ds(at - base, size)))
            at += size

    def c_copy(kind, lo=None, size=None):
        at = index[kind]
        source, target = kinds[kind][:2]
        if kind == E:
            lo, size = 0, split
        elif kind == D and lo is None:
            lo, size = split, lf - split
        if kind in (E, D):
            source, target = source.at[:, pl.ds(lo, size)], target.at[:, pl.ds(lo, size)]
        return remote(source, target, cs_sem.at[at], cr_sem.at[at], to_core)

    def weight_copy(kind):
        return c_copy(kind, 0, lf)

    def piece(kind, s, shard, put):
        if kind in (E, D):
            lo, hi = (0, split) if kind == E else (split, lf)
            put(slice(lo, hi), slice(None), mm(hid[:, shard * lf + lo : shard * lf + hi], gm[:, spans[s]], TN))
        elif kind == G:
            for t in range(2):
                cols = slice(t * wf + shard * lf, t * wf + (shard + 1) * lf)
                put(slice(None), slice(t * lf, (t + 1) * lf), mm(ab[:, spans[s]], dgu[:, cols], TN))
        else:
            put(slice(0, la), slice(None), mm(os[:, shard * la : (shard + 1) * la], gm[:, spans[s]], TN))
            for t in range(3):
                cols = slice(t * wa + shard * la, t * wa + (shard + 1) * la)
                put(slice((t + 1) * la, (t + 2) * la), slice(None), mm(dgu[:, cols], ab[:, spans[s]], TN))

    def put_in(ref, *lead):
        def put(r, c, value):
            ref[lead + (r, c)] = value

        return put

    arrived = set()

    def grad_other(l, kind):
        if kind == A:
            need(("o", 0), ("o", 1))
        if "c" not in arrived:
            pl.semaphore_wait(c_free, 1)
            arrived.add("c")
        for s in range(2):
            piece(kind, s, 1, put_in(kinds[kind][0], s))
        c_copy(kind).start()

    def grad_own(l, kind):
        if kind == A:
            need(("o", 0), ("o", 1))
        if l < top and kind == G:
            need(("last", chunks - 1))
        piece(kind, 0, 0, put_in(kinds[kind][2]))
        piece(kind, 1, 0, put_in(kinds[kind][3], l))

    def x_copy(l, u):
        kind, spot = units[u][:2]
        return remote(kinds[kind][2].at[spot], kinds[kind][4].at[spot], xs_sem.at[u], xr_sem.at[u], to_x)

    def core_sum(l, u):
        kind, spot = units[u][:2]
        _, cr, own_s, own_k, *_ = kinds[kind]
        if (l, kind) not in arrived:
            c_copy(kind).wait()
            if l < top:
                pl.semaphore_wait(x_free.at[order.index(kind)], len(PIECES[kind]))
            arrived.add((l, kind))
        own_s[spot, :] = own_s[spot, :] + cr[0, spot, :]
        x_copy(l, u).start()
        own_k[l, spot, :] = own_k[l, spot, :] + cr[1, spot, :]

    def z1_copy(l, u):
        kind, spot = units[u][:2]
        return remote(kinds[kind][3].at[l, spot], kinds[kind][5].at[spot], zs.at[l, u], zr.at[l, u], to_mate)

    def z2_copy(l, u):
        kind, spot = units[u][:2]
        return remote(kinds[kind][3].at[l, spot], kinds[kind][6].at[spot], zs.at[l, u], z2r.at[u], to_inner)

    def total_of(l, u):
        kind, spot, target, place = units[u]
        source = total_g if kind == G else kinds[kind][6]
        return source.at[spot], target.at[l, place]

    def z3_copy(l, u):
        source, target = total_of(l, u)
        return remote(source, target, zs.at[l, u], zr.at[l, u], to_mate)

    def store_copy(l, u):
        source, target = total_of(l, u)
        return pltpu.make_async_copy(source, target, store_sem.at[u])

    def x_sum(l, u):
        kind, spot = units[u][:2]
        keep, got = kinds[kind][3], kinds[kind][4]
        x_copy(l, u).wait()
        keep[l, spot, :] = keep[l, spot, :] + got[spot, :]
        if l > 0:
            pl.semaphore_signal(x_free.at[order.index(kind)], inc=1, device_id=to_x, device_id_type=MESH)

        @pl.when(outer)
        def _():
            if l < top:
                pl.semaphore_wait(z_free.at[u], 1)
            z1_copy(l, u).start()

    def z_one(l, u):
        kind, spot = units[u][:2]
        keep, got = kinds[kind][3], kinds[kind][5]

        @pl.when(inner)
        def _():
            z1_copy(l, u).wait_recv()
            keep[l, spot, :] = keep[l, spot, :] + got[spot, :]
            if l > 0:
                pl.semaphore_signal(z_free.at[u], inc=1, device_id=to_mate, device_id_type=MESH)
            if l < top:
                pl.semaphore_wait(z_free.at[u], 1)
            z2_copy(l, u).start()

    def z_two(l, u):
        kind, spot = units[u][:2]
        keep, got = kinds[kind][3], kinds[kind][6]

        @pl.when(inner)
        def _():
            z2_copy(l, u).wait()
            total = got[spot, :] + keep[l, spot, :]
            if kind == G:
                for t in range(2):
                    total_g[spot, t, :] = total[:, t * lf : (t + 1) * lf]
            else:
                got[spot, :] = total
            z3_copy(l, u).start()
            store_copy(l, u).start()

    def z_end(l, u):
        @pl.when(inner)
        def _():
            z3_copy(l, u).wait_send()
            store_copy(l, u).wait()
            if l > 0:
                pl.semaphore_signal(z_free.at[u], inc=1, device_id=to_inner, device_id_type=MESH)

        @pl.when(outer)
        def _():
            z1_copy(l, u).wait_send()
            z3_copy(l, u).wait_recv()

    def row_copies(src, dst, i, c):
        spot = pl.ds(pl.multiple_of((core * chunks + c) * n, n), n)
        return (
            pltpu.make_async_copy(src, dst.at[spot], row_sem.at[i, c]),
            remote(src, dst.at[spot], rows_s.at[i, c], rows_r.at[i, c], to_core),
        )

    def share_rows(src, dst, i, c):
        for copy in row_copies(src, dst, i, c):
            copy.start()

    def end_rows(src, dst, i, c):
        for copy in row_copies(src, dst, i, c):
            copy.wait()

    def token(c):
        need(("h", c))
        g = close(0, 0, c, gs[c], hs[c])
        small[z, x, core, c : c + 1, :] = g[0:1, :]
        row = lax.broadcasted_iota(jnp.int32, (n, dim), 0)
        gs[c] = jnp.where(row == 0, 0.0, g)
        share_rows(gs.at[c], token_grad, 0, c)

    def pout_copy(c):
        k = turn[c] % 2
        return remote(last_st.at[c], yrecv.at[k, c], ys_sem.at[c], yr_sem.at[k, c], to_chip)

    def start_output(c):
        pout_copy(c).start()
        load(("pout", c), last_st.at[c], ysend.at[c], 4 + c)
        load(("out", c), h1_st.at[top, c], hs.at[c], 12 + c)

    def end_output(c):
        need(("pout", c), ("out", c))
        pout_copy(c).wait()
        hs[c] = hs[c] + (ysend[c] + yrecv[turn[c] % 2, c])
        share_rows(hs.at[c], output, 1, c)

    def small_core():
        return remote(small.at[z, x, core], small.at[z, x, core], small_s.at[0], small_r.at[0], to_core)

    def small_x():
        return remote(small.at[z, x], small.at[z, x], small_s.at[1], small_r.at[1], to_x)

    def small_z(k):
        return remote(small.at[z], small.at[z], small_s.at[2 + k], small_r.at[2 + k], far[k])

    def small_got(k):
        back = lax.rem(z + 3 - k, 4)
        return remote(small.at[back], small.at[back], small_s.at[2 + k], small_r.at[2 + k], far[k])

    def attn_copy(part):
        rows_of = [pl.ds(0, 3 * la), pl.ds(3 * la, la)][part]
        return remote(
            oth_s.at[:, rows_of], cr_a.at[:, rows_of], cs_sem.at[2 + part], cr_sem.at[2 + part], to_core
        )

    def weight_stage(l, kind):
        if kind == A:
            need(*[("own", "a", t) for t in range(4)])
            for s in range(2):
                lanes = slice(s * half, (s + 1) * half)
                for t in range(3):
                    oth_s[s, t * la : (t + 1) * la, :] = wqkv[t * wa : t * wa + la, lanes].astype(F32)
                oth_s[s, 3 * la :, :] = wout[:la, lanes].astype(F32)
        elif kind == G:
            need(("own", "g", 0))
            step = half // 3
            for s in range(2):
                for r in range(0, half, step):
                    for t in range(2):
                        shard = raw_g[s * half + r : s * half + r + step, t, :]
                        wgu[t, s * half + r : s * half + r + step, :lf] = shard
                        oth_g[s, r : r + step, t * lf : (t + 1) * lf] = shard.astype(F32)
        else:
            need(("own", "d", 0))
            for s in range(2):
                oth_s[s, :lf, :] = wd[:lf, s * half : (s + 1) * half].astype(F32)

    def weight_send(l, kind):
        weight_stage(l, kind)
        if kind == A:
            attn_copy(0).start()
            attn_copy(1).start()
        else:
            weight_copy(kind).start()

    def weight_take(l, kind, part=0):
        if kind == A:
            attn_copy(part).wait()
        else:
            weight_copy(kind).wait()
        for s in range(2):
            lanes = slice(s * half, (s + 1) * half)
            if kind == A and part == 0:
                for t in range(3):
                    wqkv[t * wa + la : (t + 1) * wa, lanes] = cr_a[s, t * la : (t + 1) * la, :].astype(BF16)
            elif kind == A:
                wout[la:, lanes] = cr_a[s, 3 * la :, :].astype(BF16)
            elif kind == G:
                for t in range(2):
                    wgu[t, lanes, lf:] = cr_g[s, :, t * lf : (t + 1) * lf].astype(BF16)
            else:
                wd[lf:, lanes] = cr_d[s].astype(BF16)

    def hs_next(c):
        return base_of(c) + y_sum(c)

    def base_of(c):
        return hs[c] if turn[c] % 2 == 0 else h1s[c]

    def attn_up_start(l, c):
        spot = rows(c)
        if l == 0:
            need(("token", c))
            h = gm[spot, :].astype(F32)
            row = lax.broadcasted_iota(jnp.int32, (n, dim), 0)
            h = jnp.where(row == 0, first_ref[c : c + 1, :], h)
        else:
            h = hs_next(c)
            need(("st_h", c), ("st_qkv", c), ("st_lse", c), ("st_o", c))
        hs[c] = h
        ab[spot, :] = (h * inv_rms(h) * gain_of(l, 0)).astype(BF16)

    def attn_up_heads(c, pairs):
        spot = rows(c)
        a = ab[spot, :]
        lane = lax.broadcasted_iota(jnp.int32, (n, 2 * HD), 1)
        low_half = lane < HD
        zero = jnp.zeros((n, 2 * HD), BF16)
        mask = key_mask(open_ref.at[c], n)
        for t in pairs:
            spots = [slice(s * wa + t * 2 * HD, s * wa + (t + 1) * 2 * HD) for s in range(3)]
            q = rotate(mm(a, wqkv[spots[0], :], NT), tables, 1)
            q = (q * HD ** (-0.5)).astype(BF16)
            k = rotate(mm(a, wqkv[spots[1], :], NT), tables, 1).astype(BF16)
            v = mm(a, wqkv[spots[2], :], NT).astype(BF16)
            for part, value in zip(spots, (q, k, v)):
                qkvs[c, :, part] = value
            mixed = []
            for e in range(2):
                q_one = jnp.where(low_half if e == 0 else ~low_half, q, zero)
                s = jnp.where(mask, mm(k, q_one, NT), LOW)
                peak = jnp.max(s, axis=0, keepdims=True)
                raised = jnp.exp(s - peak)
                total = jnp.sum(raised, axis=0, keepdims=True)
                lses[c, 2 * t + e : 2 * t + e + 1, :] = peak + jnp.log(total)
                mixed.append(mm((raised / total).astype(BF16), v, TN))
            os[spot, t * 2 * HD : (t + 1) * 2 * HD] = jnp.where(low_half, mixed[0], mixed[1]).astype(BF16)

    def attn_up_end(l, c):
        if (l, c) == (top, chunks - 1):
            for at in (0, n // 2):
                ysend[c, pl.ds(at, n // 2), :] = mm(os[pl.ds(c * n + at, n // 2), :], wout[...])
                y_half_copy(c, at).start()
            return
        ysend[c] = mm(os[rows(c), :], wout[...])
        y_start(c)
        if l == 0:
            load(("st_h", c), hs.at[c], h_st.at[c], 12 + c)
            load(("st_qkv", c), qkvs.at[c], qkv_st.at[c], 6 + c)
            load(("st_lse", c), lses.at[c], lse_st.at[c], 8 + c)
            load(("st_o", c), os.at[rows(c)], o_st.at[rows(c)], 10 + c)

    def ffn_up(c):
        spot = rows(c)
        h1 = hs_next(c)
        h1s[c] = h1
        b = (h1 * inv_rms(h1) * gain_of(0, 1)).astype(BF16)
        step = min(wf, 256)
        for f in range(0, wf, step):
            gate = mm(b, wgu[0, :, f : f + step])
            up = mm(b, wgu[1, :, f : f + step])
            hid[spot, f : f + step] = (gate * jax.nn.sigmoid(gate) * up).astype(BF16)
        ysend[c] = mm(hid[spot, :], wd[...])
        y_start(c)
        load(("stash", c), h1s.at[c], h1_st.at[0, c], 28 + c)

    pairs = wa // (2 * HD)
    alone = la // (2 * HD)
    weight_stage(0, A)
    pl.semaphore_wait(barrier, 6)
    attn_copy(0).start()
    attn_copy(1).start()
    need("classes")
    row = lax.broadcasted_iota(jnp.int32, (16, classes_ref.shape[0]), 0)
    place = lax.broadcasted_iota(jnp.int32, row.shape, 1)
    chosen = jnp.zeros(row.shape, BF16)
    for c in range(chunks):
        here = (row == c) & (place == labels_ref[core * chunks + c])
        chosen = jnp.where(here, 1.0, chosen.astype(F32)).astype(BF16)
    first_ref[...] = mm(chosen, classes_ref[...])
    for c in range(chunks):
        prepare(c)
        attn_up_start(0, c)
        attn_up_heads(c, range(alone))
    weight_take(0, A, 0)
    attn_up_heads(0, range(alone, pairs))
    weight_take(0, A, 1)
    attn_up_end(0, 0)
    weight_send(0, G)
    attn_up_heads(1, range(alone, pairs))
    attn_up_end(0, 1)
    weight_send(0, D)
    for c in range(chunks):
        load(("cot", c), own_rows(cotangent, c), gm.at[rows(c)], 14 + c)
    load("st_wqkv", wqkv, wqkv_st, 2)
    load("st_wout", wout, wout_st, 3)
    weight_take(0, D)
    weight_take(0, G)
    need("st_wqkv", "st_wout")
    own_attn(1)
    ffn_up(0)
    weight_send(1, A)
    ffn_up(1)
    load("st_wgu", wgu, wgu_st, 0)
    load("st_wd", wd, wd_st, 1)
    weight_take(1, A, 0)
    weight_take(1, A, 1)
    need("st_wgu", "st_wd")
    own_ffn(1)
    for c in range(chunks):
        attn_up_start(1, c)
        attn_up_heads(c, range(pairs))
        attn_up_end(1, c)
        need(("stash", c))
        if c == 0:
            weight_send(1, D)
            weight_send(1, G)
    weight_take(1, D)
    weight_take(1, G)
    pl.semaphore_signal(c_free, inc=1, device_id=to_core, device_id_type=MESH)

    def start_small():
        small_core().start()

    def move_small():
        small_core().wait_send()
        spot = small.at[z, x, 1 - core]
        remote(spot, spot, small_s.at[0], small_r.at[0], to_core).wait_recv()
        small_x().start()

    def spread_small():
        small_x().wait_send()
        spot = small.at[z, 1 - x]
        remote(spot, spot, small_s.at[1], small_r.at[1], to_x).wait_recv()
        for k in range(3):
            small_z(k).start()

    def end_small():
        for k in range(3):
            small_z(k).wait_send()
            small_got(k).wait_recv()
        everyone = [(i, j, k) for i in range(groups[0]) for j in range(groups[1]) for k in range(2)]
        total = None
        for at, place in enumerate(everyone):
            block = small[place]
            total = block if total is None else total + block
            firsts_ref[at * chunks : (at + 1) * chunks, :] = small[place + (slice(0, chunks), spans[1])]
        for l in range(layers):
            gain_out[l] = total[2 + 2 * l : 4 + 2 * l, :]
        slots = firsts_ref.shape[0]
        label = total[6:7, :slots].astype(jnp.int32)
        classes, step = table_out.shape[0], 256
        for at in range(0, classes, step):
            size = min(step, classes - at)
            same = lax.broadcasted_iota(jnp.int32, (size, slots), 0) + at == label
            spare = oth_s.at[at // (4 * la), pl.ds(at % (4 * la), size)]
            spare[...] = lax.dot_general(
                jnp.where(same, 1.0, 0.0), firsts_ref[...], NN,
                precision=lax.Precision.HIGHEST, preferred_element_type=F32,
            )
            load(("table", at), spare, table_out.at[pl.ds(at, size)], 24 + at // step)

    def attn_down(l, c):
        attn(l, c)
        if (l, c) == (1, chunks - 1):
            load_attn_weights()

    def ffn_first(l, c):
        ffn_a(l, c, *((n // 2, n // 2) if (l, c) == (top, chunks - 1) else ()))

    acts = {
        FX: lambda: ffn_a(top, chunks - 1, 0, n // 2),
        FA: ffn_first, FB: ffn_b, PO: last_sum, AT: attn_down, GO: grad_other, GW: grad_own, CU: core_sum,
        XS: x_sum, ZA: z_one, ZB: z_two, ZC: z_end, TK: token, SO: start_output, EO: end_output,
        SC: start_small, SX: move_small, SZ: spread_small, SW: end_small,
    }
    left = {(GO, 1, A), (GW, 1, A)}
    for name, *at in ORDER:
        acts[name](*at)
        if left:
            left.discard((name, *at))
            if not left:
                for c in range(chunks):
                    load_o(c)
    need(*list(loads))
    for c in range(chunks):
        end_rows(gs.at[c], token_grad, 0, c)
        end_rows(hs.at[c], output, 1, c)


def call(body, outs, args, flops, limit=40, smem=0, scratch=()):
    moved = sum(x.size * x.dtype.itemsize for x in args) + sum(
        int(np.prod(s)) * np.dtype(d).itemsize for s, d in outs
    )
    spec = pl.BlockSpec(memory_space=pltpu.VMEM)
    got = pl.pallas_call(
        body,
        out_shape=[jax.ShapeDtypeStruct(s, d) for s, d in outs],
        in_specs=[pl.BlockSpec(memory_space=pltpu.SMEM)] * smem + [spec] * (len(args) - smem),
        out_specs=[spec] * len(outs),
        scratch_shapes=list(scratch),
        compiler_params=pltpu.CompilerParams(vmem_limit_bytes=limit * 2**20),
        cost_estimate=pl.CostEstimate(flops=int(flops), bytes_accessed=int(moved), transcendentals=0),
    )(*args)
    return list(got)


def settle(*refs):
    count = (len(refs) - 2) // 3
    ins, outs, spare = refs[:count], refs[count : 2 * count], refs[2 * count : 3 * count]
    in_sem, out_sem = refs[3 * count :]
    reads = [pltpu.make_async_copy(a, b, in_sem.at[i]) for i, (a, b) in enumerate(zip(ins, spare))]
    writes = [pltpu.make_async_copy(b, a, out_sem.at[i]) for i, (a, b) in enumerate(zip(outs, spare))]
    for read in reads:
        read.start()
    for read, write in zip(reads, writes):
        read.wait()
        write.start()
    for write in writes:
        write.wait()


def call_settle(results):
    anywhere = pl.BlockSpec(memory_space=pl.ANY)
    shapes = [x.shape for x in results]
    return pl.pallas_call(
        settle,
        out_shape=[jax.ShapeDtypeStruct(s, F32) for s in shapes],
        in_specs=[anywhere] * len(shapes),
        out_specs=[anywhere] * len(shapes),
        scratch_shapes=[pltpu.VMEM(s, F32) for s in shapes] + [pltpu.SemaphoreType.DMA((len(shapes),))] * 2,
        compiler_params=pltpu.CompilerParams(vmem_limit_bytes=62 * 2**20),
        name="settle",
    )(*results)


def call_whole(sizes, n, dim, wa, wf, layers, chunks, classes, fixed, numbers, moved):
    la, lf, half = wa // 2, wf // 2, dim // 2
    groups = sizes["dpo"], sizes["dpi"]
    outs = [
        ((2 * chunks * n, dim), F32),
        ((2 * chunks * n, dim), F32),
        ((classes, half), F32),
        ((layers, 2, dim), F32),
        ((layers, lf, half), F32),
        ((layers, half, 2, lf), F32),
        ((layers, la, half), F32),
        ((layers, 3 * la, half), F32),
        ((2, dim, wf), BF16),
        ((wf, dim), BF16),
        ((3 * wa, dim), BF16),
        ((wa, dim), BF16),
        ((chunks, n, dim), F32),
        ((layers, chunks, n, dim), F32),
        ((chunks, n, 3 * wa), BF16),
        ((chunks, 8, n), F32),
        ((chunks * n, wa), BF16),
        ((chunks, n, dim), F32),
    ]
    d, g, a = (lf, half), (half, 2 * lf), (4 * la, half)
    f, h = lambda *s: pltpu.VMEM(s, F32), lambda *s: pltpu.VMEM(s, BF16)
    dma, count = pltpu.SemaphoreType.DMA, pltpu.SemaphoreType.REGULAR
    units = sum(len(k) for k in PIECES.values())
    scratch = [h(2, dim, wf), h(wf, dim), h(3 * wa, dim), h(wa, dim)]
    scratch += [f(chunks, n, dim), f(chunks, n, dim), h(chunks, n, 3 * wa), h(chunks * n, wa), f(chunks, 8, n)]
    scratch += [f(chunks, n, dim), f(2, chunks, n, dim), f(chunks, n, dim)]
    scratch += [h(chunks * n, dim), h(chunks * n, dim), h(chunks * n, wf), h(chunks * n, 2 * wf)]
    scratch += [f(2, *g), f(2, *a)] + [f(2, *k) for k in (d, g, a)]
    scratch += [f(*k) for k in (d, g, a)] + [f(layers, *k) for k in (d, g, a)]
    scratch += [f(*k) for _ in range(3) for k in (d, g, a)] + [f(*groups, 2, 8, dim)]
    scratch += [f(chunks, n, 1), h(dim, 2, lf), f(half, 2, lf), f(groups[0] * groups[1] * 2 * chunks, half)]
    scratch += [h(classes, dim), f(16, dim)]
    scratch += [dma((32,)), dma((chunks,)), dma((2, chunks)), dma((5,)), dma((5,))]
    scratch += [dma((units,))] * 2 + [dma((layers, units))] * 2 + [dma((units,))] * 2 + [dma((2,))] * 2
    scratch += [dma((2, chunks))] * 3 + [dma((5,))] * 2 + [count((len(PIECES),)), count((units,)), count]
    args = list(fixed) + list(numbers) + list(moved)
    flops = layers * chunks * n * (2 * dim * (14 * wa + 12 * wf) + 32 * n * wa)
    vmem, smem = pl.BlockSpec(memory_space=pltpu.VMEM), pl.BlockSpec(memory_space=pltpu.SMEM)
    anywhere = pl.BlockSpec(memory_space=pl.ANY)
    return pl.pallas_call(
        functools.partial(whole_pass, (n, dim, wa, wf, layers, chunks)),
        out_shape=[jax.ShapeDtypeStruct(s, t) for s, t in outs],
        in_specs=[vmem] * len(fixed) + [smem] * len(numbers) + [anywhere] * len(moved),
        out_specs=[vmem if i == 3 else anywhere for i in range(len(outs))],
        scratch_shapes=scratch,
        compiler_params=pltpu.CompilerParams(
            vmem_limit_bytes=63 * 2**20, collective_id=0, has_side_effects=True
        ),
        cost_estimate=pl.CostEstimate(flops=flops, bytes_accessed=90 * 10**6, transcendentals=0),
        name="whole_pass",
    )(*args)[:8]


def on_device(sizes, tokens, cotangent, heights, labels, valid, class_table, gains, w_qkv, w_out, w_gate_up, w_down):
    seq_count = heights.shape[0]
    row_count, dim = tokens.shape
    n = row_count // seq_count
    layers = gains.shape[0]
    classes = class_table.shape[0]
    la = w_out.shape[1]
    lf = w_down.shape[1]
    wa, wf = 2 * la, 2 * lf
    tp, dpo, dpi = sizes["tp"], sizes["dpo"], sizes["dpi"]
    mine = seq_count // 2
    lean = (tp, dpo, dpi) == (4, 4, 2) and (mine, layers) == (2, 2)
    core = lax.rem(lax.axis_index("tp"), 2)
    z = lax.axis_index("dpo")
    swap_core = [(i, i ^ 1) for i in range(tp)]

    def core_swap(x):
        return lax.ppermute(x, "tp", swap_core)

    def sum_chips(part):
        total = None
        for step in range(2, tp, 2):
            got = lax.ppermute(part, "tp", [(i, i ^ step) for i in range(tp)])
            total = got if total is None else total + got
        return total

    tables = jnp.asarray(rope_constants(n))
    if lean:
        fixed = (gains, tables, valid)
        moved = (class_table, tokens, cotangent, jnp.transpose(w_qkv, (0, 2, 3, 1)), w_out, w_gate_up, w_down)
        got = call_whole(sizes, n, dim, wa, wf, layers, mine, classes, fixed, (heights, labels), moved)
        output, token_grad, table_part, gain_total, down_part, gate_up_part, out_part, qkv_part = call_settle(got)
        half = dim // dpi
        return (
            output,
            token_grad,
            table_part,
            gain_total,
            qkv_part.reshape(layers, 3, la, half).transpose(0, 3, 1, 2),
            out_part,
            gate_up_part,
            down_part,
        )

    position = jnp.arange(n)
    own = lambda x: lax.dynamic_slice_in_dim(x, core * mine, mine, 0)
    open_key = (position[None, :] < 1 + COLS * own(heights)[:, None]) & (own(valid.reshape(seq_count, n)) == 1)
    open_key = open_key.astype(F32)[:, :, None]
    own_labels = own(labels)
    wqkv, wout, wgu, wd = [], [], [], []
    for l in range(layers):
        for into, w in (
            (wqkv, jnp.transpose(w_qkv[l], (1, 2, 0))),
            (wout, w_out[l][None]),
            (wgu, jnp.transpose(w_gate_up[l], (1, 0, 2))),
            (wd, w_down[l][None]),
        ):
            wide = w.astype(F32)
            axis = 2 if into is wgu else 1
            shape = list(w.shape)
            shape[axis] *= 2
            into.append(call(functools.partial(merge, axis), [(tuple(shape), BF16)], (wide, core_swap(wide)), 1000)[0])
        wqkv[l] = wqkv[l].reshape(3 * wa, dim)
        wout[l] = wout[l][0]
        wd[l] = wd[l][0]

    token_own = own(tokens.reshape(seq_count, n, dim))
    cot_own = own(cotangent.reshape(seq_count, n, dim))
    chunks = range(mine)
    hs = []
    for c in chunks:
        row = lax.dynamic_slice_in_dim(class_table, own_labels[c], 1, 0)
        hs.append(jnp.where((position == 0)[:, None], row, token_own[c]).astype(F32))

    shape_d = ((n, dim), F32)
    shape_b = ((n, dim), BF16)
    flops_a = 2 * n * dim * 4 * wa + 8 * n * n * wa
    flops_f = 2 * n * dim * 3 * wf

    kept = []
    state = [(hs[c],) for c in chunks]
    parts = None
    for l in range(layers):
        keep = [dict() for _ in chunks]
        for c in chunks:
            args = state[c] + (gains[l, 0][None], wqkv[l], wout[l], tables, open_key[c])
            outs = [((n, 3 * wa), BF16), ((max(8, wa // HD), n), F32), ((n, wa), BF16), shape_d]
            outs = ([shape_d] if l > 0 else []) + [shape_b] + outs
            got = call(functools.partial(attn_fwd, l == 0), outs, args, flops_a)
            h = state[c][0] if l == 0 else got.pop(0)
            a, qkv, lse, o, part = got
            keep[c].update(h=h, a=a, qkv=qkv, lse=lse, o=o)
            state[c] = (h, part, sum_chips(part))
        for c in chunks:
            args = state[c] + (gains[l, 1][None], wgu[l], wd[l])
            outs = [shape_d, shape_b, ((n, 2 * wf), F32), ((n, wf), BF16), shape_d]
            h1, b, gu, hid, part = call(ffn_fwd, outs, args, flops_f)
            keep[c].update(h1=h1, b=b, gu=gu, hid=hid)
            state[c] = (h1, part, sum_chips(part))
        kept.append(keep)

    output = jnp.concatenate([s[0] + (s[1] + s[2]) for s in state], axis=0)

    half = lax.axis_index("dpi") if dpi == 2 else 1
    order = jnp.stack([jnp.int32(1) - half, jnp.int32(half)])

    def dp_sum(both, other, axis):
        got = core_swap(other)
        if dpi == 2:
            sent = lax.ppermute(both[0] + got[0], "dpi", [(0, 1), (1, 0)])
            total = (both[1] + got[1]) + sent
        else:
            both = both + got
            whole = jnp.concatenate([both[0], both[1]], axis=axis)
            total = lax.psum_scatter(whole, "dpi", scatter_dimension=axis, tiled=True)
        return line_sum(total)

    def line_sum(x):
        if dpo != 4:
            return lax.psum(x, "dpo")
        got = lax.ppermute(x, "dpo", [(0, 1), (3, 2)])
        x = x + got
        got = lax.ppermute(x, "dpo", [(1, 2), (2, 1)])
        x = x + got
        got = lax.ppermute(x, "dpo", [(1, 0), (2, 3)])
        return jnp.where((z == 0) | (z == dpo - 1), got, x)

    gain_rows = [[None, None] for _ in range(layers)]
    grads = [None] * layers
    state = [None] * mine
    for l in reversed(range(layers)):
        top = l == layers - 1
        keep = kept[l]
        gms = []
        for c in chunks:
            outs = [((n, 2 * wf), BF16), shape_d]
            args = (keep[c]["gu"], wgu[l], wd[l])
            if top:
                g = cot_own[c]
                dgu, part = call(functools.partial(ffn_bwd, True), outs, (g,) + args, flops_f)
                gms.append(g)
            else:
                outs = [shape_d, ((1, dim), F32), shape_b] + outs
                args = state[c] + args
                g, gain_c, gm, dgu, part = call(functools.partial(ffn_bwd, False), outs, args, flops_f)
                gain_rows[l + 1][0] = gain_c if c == 0 else gain_rows[l + 1][0] + gain_c
                gms.append(gm)
            keep[c]["dgu"] = dgu
            state[c] = (g, part, sum_chips(part), keep[c]["h1"], gains[l, 1][None])
        flops_w = 2 * n * mine * dim * wf
        outs = [((2, lf, dim // 2), F32)] * 2
        args = [order] + [keep[c]["hid"] for c in chunks] + gms
        spans = (((0, lf),), ((lf, wf),))
        down = call(functools.partial(grad_rows, spans), outs, args, flops_w, smem=1)
        outs = [((2, dim // 2, 2 * lf), F32)] * 2
        args = [order] + [keep[c]["b"] for c in chunks] + [keep[c]["dgu"] for c in chunks]
        spans = (((0, lf), (wf, wf + lf)), ((lf, wf), (wf + lf, 2 * wf)))
        gate_up = call(functools.partial(grad_columns, spans), outs, args, 2 * flops_w, smem=1)
        down = dp_sum(*down, 1)
        gate_up = dp_sum(*gate_up, 0)
        gas = []
        for c in chunks:
            outs = [shape_d, ((1, dim), F32), shape_b, ((n, 3 * wa), BF16), shape_d]
            args = state[c] + (wqkv[l], wout[l], tables, open_key[c], keep[c]["qkv"], keep[c]["lse"])
            g1, gain_c, ga, dqkv, part = call(attn_bwd, outs, args, flops_a + 12 * n * n * wa)
            gain_rows[l][1] = gain_c if c == 0 else gain_rows[l][1] + gain_c
            gas.append(ga)
            keep[c]["dqkv"] = dqkv
            state[c] = (g1, part, sum_chips(part), keep[c]["h"], gains[l, 0][None])
        flops_w = 2 * n * mine * dim * wa
        outs = [((2, la, dim // 2), F32)] * 2
        args = [order] + [keep[c]["o"] for c in chunks] + gas
        spans = (((0, la),), ((la, wa),))
        out = call(functools.partial(grad_rows, spans), outs, args, flops_w, smem=1)
        outs = [((2, 3 * la, dim // 2), F32)] * 2
        args = [order] + [keep[c]["dqkv"] for c in chunks] + [keep[c]["a"] for c in chunks]
        spans = tuple(tuple((t * wa + s * la, t * wa + (s + 1) * la) for t in range(3)) for s in range(2))
        qkv = call(functools.partial(grad_rows, spans), outs, args, 3 * flops_w, smem=1)
        out = dp_sum(*out, 1)
        qkv = dp_sum(*qkv, 1)
        grads[l] = (qkv, out, gate_up, down)

    finals = []
    for c in chunks:
        g, gain_c = call(close_layer, [shape_d, ((1, dim), F32)], state[c], 1000)
        gain_rows[0][0] = gain_c if c == 0 else gain_rows[0][0] + gain_c
        finals.append(g)

    slot0 = lax.axis_index("dpo") * dpi + lax.axis_index("dpi")
    seqs = seq_count * dpo * dpi
    firsts = jnp.concatenate([g[0:1] for g in finals], axis=0)
    small = jnp.zeros((seqs + 2 * layers + 1, dim), F32)
    small = lax.dynamic_update_slice(small, firsts, (slot0 * seq_count + core * mine, 0))
    terms = jnp.concatenate([gain_rows[l][i] for l in range(layers) for i in range(2)], axis=0)
    small = lax.dynamic_update_slice(small, terms, (seqs, 0))
    label_row = lax.dynamic_update_slice(
        jnp.zeros((1, dim), F32), own_labels.astype(F32)[None], (0, slot0 * seq_count + core * mine)
    )
    small = lax.dynamic_update_slice(small, label_row, (seqs + 2 * layers, 0))
    small = jnp.where(lax.axis_index("tp") < 2, small, 0.0)
    small = lax.psum(small, ("dpo", "dpi", "tp"))
    all_labels = jnp.round(small[seqs + 2 * layers, :seqs]).astype(jnp.int32)
    gain_total = small[seqs : seqs + 2 * layers].reshape(layers, 2, dim)
    onehot = (all_labels[None, :] == jnp.arange(classes)[:, None]).astype(F32)
    share = dim // dpi
    rows = lax.dynamic_slice(small, (0, lax.axis_index("dpi") * share), (seqs, share))
    table_part = jnp.dot(onehot, rows, precision=lax.Precision.HIGHEST)

    token_own = jnp.concatenate([jnp.where((position == 0)[:, None], 0.0, g) for g in finals], axis=0)

    def both_cores(x):
        other = core_swap(x)
        return jnp.where(core == 0, jnp.concatenate([x, other], 0), jnp.concatenate([other, x], 0))

    qkv_part = jnp.stack([g[0].reshape(3, la, share) for g in grads]).transpose(0, 3, 1, 2)
    out_part = jnp.stack([g[1] for g in grads])
    gate_up_part = jnp.stack([g[2].reshape(share, 2, lf) for g in grads])
    down_part = jnp.stack([g[3] for g in grads])
    return (
        both_cores(output),
        both_cores(token_own),
        table_part,
        gain_total,
        qkv_part,
        out_part,
        gate_up_part,
        down_part,
    )


def solution(mesh):
    sizes = dict(mesh.shape)
    placed = (
        P(("dpo", "dpi"), None),
        P(("dpo", "dpi"), None),
        P(("dpo", "dpi")),
        P(("dpo", "dpi")),
        P(("dpo", "dpi")),
        P(),
        P(),
        P(None, None, None, "tp"),
        P(None, "tp", None),
        P(None, None, None, "tp"),
        P(None, "tp", None),
    )
    return jax.shard_map(
        functools.partial(on_device, sizes),
        mesh=mesh,
        in_specs=placed,
        out_specs=(
            P(("dpo", "dpi"), None),
            P(("dpo", "dpi"), None),
            P(None, "dpi"),
            P(),
            P(None, "dpi", None, "tp"),
            P(None, "tp", "dpi"),
            P(None, "dpi", None, "tp"),
            P(None, "tp", "dpi"),
        ),
        check_vma=False,
    )
```

```python
import functools

import jax
import jax.numpy as jnp
import numpy as np
from jax import lax
from jax.experimental import pallas as pl
from jax.experimental.pallas import tpu as pltpu
from jax.sharding import PartitionSpec as P

HD = 64
COLS = 16
EPS = 1e-05
F32 = jnp.float32
BF16 = jnp.bfloat16
LOW = -1e30
MESH = pl.DeviceIdType.MESH

E, D, G, A = "edga"
PIECES = {E: (64,) * 2, D: (96,) * 4, G: (48,) * 8, A: (96,) * 8}
FX, FA, FB, PO, AT, TK, GO, GW, CU, XS, ZA, ZB, ZC, SO, EO, SC, SX, SZ, SW = range(19)
ORDER = (
    (FA, 1, 0), (FB, 1, 0), (FX,), (FA, 1, 1), (GO, 1, E), (GO, 1, D), (GW, 1, E), (CU, 1, 1), (PO, 0),
    (CU, 1, 0), (GW, 1, D), (CU, 1, 3), (CU, 1, 4), (XS, 1, 1), (GO, 1, G), (XS, 1, 0), (FB, 1, 1), (ZA, 1, 1),
    (XS, 1, 3), (CU, 1, 5), (ZA, 1, 0), (GW, 1, G), (XS, 1, 4), (CU, 1, 12), (CU, 1, 11), (CU, 1, 10),
    (ZB, 1, 1), (CU, 1, 9), (ZA, 1, 3), (XS, 1, 5), (ZA, 1, 4), (AT, 1, 0), (XS, 1, 12), (ZA, 1, 5),
    (CU, 1, 13), (CU, 1, 8), (ZB, 1, 4), (ZB, 1, 0), (PO, 1), (CU, 1, 7), (XS, 1, 11), (ZA, 1, 12), (ZB, 1, 5),
    (ZC, 1, 4), (CU, 1, 6), (ZA, 1, 11), (ZB, 1, 3), (ZB, 1, 12), (XS, 1, 10), (XS, 1, 9), (ZA, 1, 10),
    (ZB, 1, 11), (AT, 1, 1), (ZA, 1, 9), (ZB, 1, 10), (XS, 1, 13), (CU, 1, 2), (GO, 1, A), (XS, 1, 8),
    (ZC, 1, 1), (ZA, 1, 13), (GW, 1, A), (ZB, 1, 9), (XS, 1, 7), (XS, 1, 6), (ZA, 1, 8), (CU, 1, 20),
    (CU, 1, 14), (ZB, 1, 13), (ZA, 1, 7), (FA, 0, 0), (ZB, 1, 8), (ZC, 1, 5), (ZC, 1, 9), (ZA, 1, 6),
    (XS, 1, 2), (CU, 1, 15), (XS, 1, 20), (CU, 1, 19), (ZC, 1, 3), (CU, 1, 18), (CU, 1, 21), (XS, 1, 14),
    (CU, 1, 16), (CU, 1, 17), (ZA, 1, 2), (ZB, 1, 7), (FB, 0, 0), (ZA, 1, 20), (XS, 1, 15), (ZC, 1, 8),
    (ZC, 1, 12), (ZB, 1, 6), (FA, 0, 1), (ZA, 1, 15), (ZB, 1, 2), (XS, 1, 19), (ZA, 1, 14), (XS, 1, 18),
    (GO, 0, D), (ZC, 1, 7), (GO, 0, E), (ZB, 1, 20), (GW, 0, E), (XS, 1, 21), (ZA, 1, 19), (ZB, 1, 15),
    (GW, 0, D), (ZC, 1, 10), (CU, 0, 4), (CU, 0, 3), (ZA, 1, 18), (ZB, 1, 14), (GO, 0, G), (ZC, 1, 0),
    (CU, 0, 5), (XS, 1, 16), (ZA, 1, 21), (XS, 1, 17), (CU, 0, 1), (ZB, 1, 19), (FB, 0, 1), (ZA, 1, 16),
    (XS, 0, 4), (ZB, 1, 18), (ZC, 1, 15), (GW, 0, G), (CU, 0, 12), (ZC, 1, 6), (ZA, 1, 17), (ZB, 1, 21),
    (CU, 0, 8), (ZA, 0, 4), (ZC, 1, 20), (XS, 0, 3), (ZC, 1, 19), (XS, 0, 1), (ZC, 1, 13), (ZC, 1, 11),
    (ZB, 1, 16), (CU, 0, 9), (CU, 0, 10), (XS, 0, 5), (ZA, 0, 3), (ZB, 1, 17), (AT, 0, 0), (ZA, 0, 5),
    (ZB, 0, 4), (ZA, 0, 1), (XS, 0, 12), (CU, 0, 6), (CU, 0, 7), (XS, 0, 8), (ZC, 1, 18), (ZB, 0, 3),
    (CU, 0, 13), (ZA, 0, 12), (ZB, 0, 5), (CU, 0, 0), (AT, 0, 1), (ZB, 0, 1), (ZC, 0, 4), (ZA, 0, 8),
    (XS, 0, 9), (XS, 0, 10), (CU, 0, 11), (ZB, 0, 12), (GW, 0, A), (ZA, 0, 9), (ZC, 0, 1), (ZC, 1, 17),
    (CU, 0, 2), (ZB, 0, 8), (XS, 0, 6), (GO, 0, A), (ZA, 0, 10), (ZB, 0, 9), (ZC, 1, 21), (ZA, 0, 6),
    (ZB, 0, 10), (ZC, 0, 5), (XS, 0, 7), (TK, 0), (ZC, 1, 2), (XS, 0, 13), (ZA, 0, 7), (ZC, 0, 3), (XS, 0, 0),
    (ZB, 0, 6), (ZC, 1, 16), (ZA, 0, 13), (ZC, 0, 9), (ZC, 0, 8), (SO, 0), (CU, 0, 17), (XS, 0, 11), (ZA, 0, 0),
    (CU, 0, 18), (ZC, 0, 10), (XS, 0, 2), (ZB, 0, 7), (CU, 0, 14), (ZA, 0, 11), (ZB, 0, 13), (ZB, 0, 0),
    (CU, 0, 19), (CU, 0, 21), (CU, 0, 15), (TK, 1), (XS, 0, 17), (XS, 0, 18), (SC,), (ZA, 0, 17), (ZB, 0, 11),
    (CU, 0, 20), (ZA, 0, 2), (ZB, 0, 17), (ZA, 0, 18), (SO, 1), (SX,), (XS, 0, 14), (ZB, 0, 2), (CU, 0, 16),
    (ZC, 1, 14), (XS, 0, 19), (ZA, 0, 19), (ZB, 0, 18), (ZC, 0, 0), (ZC, 0, 7), (XS, 0, 21), (ZA, 0, 14),
    (XS, 0, 15), (ZB, 0, 19), (ZC, 0, 2), (ZA, 0, 21), (XS, 0, 16), (ZC, 0, 17), (XS, 0, 20), (ZC, 0, 13),
    (SZ,), (ZA, 0, 15), (ZB, 0, 14), (ZB, 0, 21), (ZA, 0, 20), (ZC, 0, 18), (ZC, 0, 12), (ZA, 0, 16),
    (ZC, 0, 11), (ZB, 0, 15), (ZB, 0, 20), (ZC, 0, 19), (SW,), (ZB, 0, 16), (EO, 0), (ZC, 0, 21), (EO, 1),
    (ZC, 0, 14), (ZC, 0, 6), (ZC, 0, 15), (ZC, 0, 20), (ZC, 0, 16),
)

NN = (((1,), (0,)), ((), ()))
NT = (((1,), (1,)), ((), ()))
TN = (((0,), (0,)), ((), ()))


def mm(a, b, dims=NN):
    return lax.dot_general(a, b, dims, preferred_element_type=F32)


def rope_constants(slot_len):
    quarter = HD // 4
    raster = np.maximum(np.arange(slot_len) - 1, 0)
    row_pos = (raster // COLS).astype(np.float32)
    col_pos = (raster % COLS).astype(np.float32)
    frequency = (10000.0 ** (-np.arange(quarter).astype(np.float32) / quarter)).astype(np.float32)
    row_angle = row_pos[:, None] * frequency[None, :]
    col_angle = col_pos[:, None] * frequency[None, :]
    zero = np.zeros_like(row_angle)
    cos = np.concatenate([np.cos(row_angle)] * 2 + [np.cos(col_angle)] * 2, axis=1)
    first = np.concatenate([-np.sin(row_angle), zero, -np.sin(col_angle), zero], axis=1)
    second = np.concatenate([zero, np.sin(row_angle), zero, np.sin(col_angle)], axis=1)
    return np.stack([np.tile(t, (1, 2)) for t in (cos, first, second)]).astype(np.float32)


def rotate(x, table_ref, sign):
    quarter = HD // 4
    ahead = pltpu.roll(x, 2 * HD - quarter, 1) * table_ref[1]
    behind = pltpu.roll(x, quarter, 1) * table_ref[2]
    turned = ahead + behind
    return x * table_ref[0] + (turned if sign > 0 else -turned)


def merge(axis, mine_ref, other_ref, out_ref):
    size = mine_ref.shape[axis]
    if axis == 1:
        out_ref[:, :size, :] = mine_ref[...].astype(BF16)
        out_ref[:, size:, :] = other_ref[...].astype(BF16)
    else:
        out_ref[:, :, :size] = mine_ref[...].astype(BF16)
        out_ref[:, :, size:] = other_ref[...].astype(BF16)


def inv_rms(h):
    return lax.rsqrt(jnp.mean(h * h, axis=-1, keepdims=True) + EPS)


def norm_back(grad, normed, scale, gain):
    scaled = grad * gain
    return scale * (scaled - normed * jnp.mean(scaled * normed, axis=-1, keepdims=True))


def key_mask(open_ref, lo, hi):
    shape = (hi - lo, open_ref.shape[0] - lo)
    key = lax.broadcasted_iota(jnp.int32, shape, 0)
    query = lax.broadcasted_iota(jnp.int32, shape, 1)
    return ((key < query) & (open_ref[lo:hi, :] > 0.5)) | (key == query)


def attn_fwd(first, *refs):
    if first:
        h_ref, gain_ref, wqkv_ref, wout_ref, table_ref, open_ref = refs[:6]
        refs = refs[6:]
        h = h_ref[...]
    else:
        h_ref, p_ref, r_ref, gain_ref, wqkv_ref, wout_ref, table_ref, open_ref = refs[:8]
        refs = refs[8:]
        h = h_ref[...] + (p_ref[...] + r_ref[...])
        refs[0][...] = h
        refs = refs[1:]
    a_ref, qkv_ref, lse_ref, o_ref, part_ref = refs
    n = h.shape[0]
    width = wout_ref.shape[0]
    a = (h * inv_rms(h) * gain_ref[...]).astype(BF16)
    a_ref[...] = a
    lane = lax.broadcasted_iota(jnp.int32, (n, 2 * HD), 1)
    low_half = lane < HD
    zero = jnp.zeros((n, 2 * HD), BF16)
    mask = key_mask(open_ref, 0, n)
    for t in range(width // (2 * HD)):
        spots = [slice(s * width + t * 2 * HD, s * width + (t + 1) * 2 * HD) for s in range(3)]
        q = rotate(mm(a, wqkv_ref[spots[0], :], NT), table_ref, 1)
        q = (q * HD ** (-0.5)).astype(BF16)
        k = rotate(mm(a, wqkv_ref[spots[1], :], NT), table_ref, 1).astype(BF16)
        v = mm(a, wqkv_ref[spots[2], :], NT).astype(BF16)
        qkv_ref[:, spots[0]] = q
        qkv_ref[:, spots[1]] = k
        qkv_ref[:, spots[2]] = v
        mixed = []
        for e in range(2):
            q_one = jnp.where(low_half if e == 0 else ~low_half, q, zero)
            s = jnp.where(mask, mm(k, q_one, NT), LOW)
            top = jnp.max(s, axis=0, keepdims=True)
            raised = jnp.exp(s - top)
            total = jnp.sum(raised, axis=0, keepdims=True)
            lse_ref[2 * t + e : 2 * t + e + 1, :] = top + jnp.log(total)
            prob = (raised / total).astype(BF16)
            mixed.append(mm(prob, v, TN))
        o_ref[:, t * 2 * HD : (t + 1) * 2 * HD] = jnp.where(low_half, mixed[0], mixed[1]).astype(BF16)
    part_ref[...] = mm(o_ref[...], wout_ref[...])


def ffn_fwd(h_ref, p_ref, r_ref, gain_ref, wgu_ref, wd_ref, h1_ref, *refs):
    h = h_ref[...] + (p_ref[...] + r_ref[...])
    h1_ref[...] = h
    b = (h * inv_rms(h) * gain_ref[...]).astype(BF16)
    b_ref, gu_ref, hid_ref, part_ref = refs
    b_ref[...] = b
    width = wd_ref.shape[0]
    step = min(width, 256)
    for f in range(0, width, step):
        gate = mm(b, wgu_ref[0, :, f : f + step])
        up = mm(b, wgu_ref[1, :, f : f + step])
        gu_ref[:, f : f + step] = gate
        gu_ref[:, width + f : width + f + step] = up
        hid_ref[:, f : f + step] = (gate * jax.nn.sigmoid(gate) * up).astype(BF16)
    part_ref[...] = mm(hid_ref[...], wd_ref[...])


def ffn_bwd(first, *refs):
    if first:
        g_ref, gu_ref, wgu_ref, wd_ref = refs[:4]
        refs = refs[4:]
        gm = g_ref[...]
    else:
        g1_ref, p_ref, r_ref, hin_ref, gain_ref, gu_ref, wgu_ref, wd_ref = refs[:8]
        refs = refs[8:]
        grad, gain_grad = close_norm(g1_ref[...], p_ref, r_ref, hin_ref, gain_ref)
        refs[0][...] = grad
        refs[1][...] = gain_grad
        gm = grad.astype(BF16)
        refs[2][...] = gm
        refs = refs[3:]
    dgu_ref, part_ref = refs
    width = wd_ref.shape[0]
    step = min(width, 256)
    for f in range(0, width, step):
        dhid = mm(gm, wd_ref[f : f + step, :], NT)
        gate = gu_ref[:, f : f + step]
        up = gu_ref[:, width + f : width + f + step]
        sig = jax.nn.sigmoid(gate)
        dgu_ref[:, f : f + step] = (dhid * up * (sig * (1.0 + gate * (1.0 - sig)))).astype(BF16)
        dgu_ref[:, width + f : width + f + step] = (dhid * (gate * sig)).astype(BF16)
    part_ref[...] = mm(dgu_ref[:, :width], wgu_ref[0], NT) + mm(dgu_ref[:, width:], wgu_ref[1], NT)


def close_norm(g, p_ref, r_ref, h_ref, gain_ref):
    grad = p_ref[...] + r_ref[...]
    h = h_ref[...]
    scale = inv_rms(h)
    normed = h * scale
    gain_grad = jnp.sum(grad * normed, axis=0, keepdims=True)
    return g + norm_back(grad, normed, scale, gain_ref[...]), gain_grad


def attn_bwd(
    g_ref, p_ref, r_ref, h1_ref, gain_ref, wqkv_ref, wout_ref, table_ref, open_ref, qkv_ref, lse_ref,
    g1_ref, gain_grad_ref, ga_ref, dqkv_ref, part_ref,
):
    g1, gain_grad = close_norm(g_ref[...].astype(F32), p_ref, r_ref, h1_ref, gain_ref)
    g1_ref[...] = g1
    gain_grad_ref[...] = gain_grad
    ga = g1.astype(BF16)
    ga_ref[...] = ga
    n = ga.shape[0]
    width = wout_ref.shape[0]
    lane = lax.broadcasted_iota(jnp.int32, (n, 2 * HD), 1)
    low_half = lane < HD
    zero = jnp.zeros((n, 2 * HD), BF16)
    mask = key_mask(open_ref, 0, n)
    for t in range(width // (2 * HD)):
        spots = [slice(s * width + t * 2 * HD, s * width + (t + 1) * 2 * HD) for s in range(3)]
        q = qkv_ref[:, spots[0]]
        k = qkv_ref[:, spots[1]]
        v = qkv_ref[:, spots[2]]
        dout = mm(ga, wout_ref[t * 2 * HD : (t + 1) * 2 * HD, :], NT).astype(BF16)
        dq, dk, dv = [], [], []
        for e in range(2):
            mine = low_half if e == 0 else ~low_half
            q_one = jnp.where(mine, q, zero)
            d_one = jnp.where(mine, dout, zero)
            s = jnp.where(mask, mm(k, q_one, NT), LOW)
            prob = jnp.exp(s - lse_ref[2 * t + e : 2 * t + e + 1, :])
            dprob = mm(v, d_one, NT)
            delta = jnp.sum(prob * dprob, axis=0, keepdims=True)
            ds = (prob * (dprob - delta)).astype(BF16)
            dv.append(mm(prob.astype(BF16), dout))
            dk.append(mm(ds, q))
            dq.append(mm(ds, k, TN))
        dq = jnp.where(low_half, dq[0], dq[1]) * HD ** (-0.5)
        dk = jnp.where(low_half, dk[0], dk[1])
        dv = jnp.where(low_half, dv[0], dv[1])
        dqkv_ref[:, spots[0]] = rotate(dq, table_ref, -1).astype(BF16)
        dqkv_ref[:, spots[1]] = rotate(dk, table_ref, -1).astype(BF16)
        dqkv_ref[:, spots[2]] = dv.astype(BF16)
    part_ref[...] = mm(dqkv_ref[...], wqkv_ref[...])


def close_layer(g1_ref, p_ref, r_ref, h_ref, gain_ref, out_ref, gain_grad_ref):
    grad, gain_grad = close_norm(g1_ref[...], p_ref, r_ref, h_ref, gain_ref)
    out_ref[...] = grad
    gain_grad_ref[...] = gain_grad


def halves_of(half_ref, dim):
    one = dim // 2
    return [pl.ds(pl.multiple_of(half_ref[s] * one, one), one) for s in range(2)]


def grad_rows(spans, half_ref, *refs):
    chunks = (len(refs) - 2) // 2
    lefts, rights = refs[:chunks], refs[chunks : 2 * chunks]
    outs = refs[2 * chunks :]
    for s, spot in enumerate(halves_of(half_ref, rights[0].shape[1])):
        for out, picks in zip(outs, spans):
            at = 0
            for lo, hi in picks:
                total = None
                for left, right in zip(lefts, rights):
                    term = mm(left[:, lo:hi], right[:, spot], TN)
                    total = term if total is None else total + term
                out[s, at : at + hi - lo, :] = total
                at += hi - lo


def grad_columns(spans, half_ref, *refs):
    chunks = (len(refs) - 2) // 2
    lefts, rights = refs[:chunks], refs[chunks : 2 * chunks]
    outs = refs[2 * chunks :]
    for s, spot in enumerate(halves_of(half_ref, lefts[0].shape[1])):
        for out, picks in zip(outs, spans):
            at = 0
            for lo, hi in picks:
                total = None
                for left, right in zip(lefts, rights):
                    term = mm(left[:, spot], right[:, lo:hi], TN)
                    total = term if total is None else total + term
                out[s, :, at : at + hi - lo] = total
                at += hi - lo


def whole_pass(dims, *refs):
    n, dim, wa, wf, layers, chunks = dims
    la, lf, half = wa // 2, wf // 2, dim // 2
    refs = list(refs)

    def take(count):
        got = refs[:count]
        del refs[:count]
        return got

    gains_ref, tables, valid_ref, heights_ref, labels_ref = take(5)
    class_table, tokens, cotangent, w_qkv, w_out, w_gate_up, w_down = take(7)
    output, token_grad, table_out, gain_out, down_out, gate_up_out, out_out, qkv_out = take(8)
    wgu_st, wd_st, wqkv_st, wout_st, h_st, h1_st, qkv_st, lse_st, o_st, last_st = take(10)
    wgu, wd, wqkv, wout = take(4)
    hs, h1s, qkvs, os, lses = take(5)
    ysend, yrecv, gs, gm, ab, hid, dgu = take(7)
    oth_g, oth_s, cr_d, cr_g, cr_a = take(5)
    os_d, os_g, os_a, ok_d, ok_g, ok_a = take(6)
    xr_d, xr_g, xr_a, z1_d, z1_g, z1_a, z2_d, z2_g, z2_a, small = take(10)
    open_ref, raw_g, total_g, firsts_ref, classes_ref, first_ref = take(6)
    load_sem, ys_sem, yr_sem, cs_sem, cr_sem, xs_sem, xr_sem = take(7)
    zs, zr, z2r, store_sem, half_s, half_r, row_sem, rows_s, rows_r, small_s, small_r = take(11)
    x_free, z_free, c_free = take(3)

    tp = lax.axis_index("tp")
    x = lax.axis_index("dpi")
    z = lax.axis_index("dpo")
    core = lax.rem(tp, 2)
    to_core = {"tp": tp + 1 - 2 * core}
    to_chip = {"tp": lax.rem(tp + 2, 4)}
    to_x = {"dpi": 1 - x}
    to_mate = {"dpo": z + 1 - 2 * lax.rem(z, 2)}
    to_inner = {"dpo": 3 - z}
    outer = (z == 0) | (z == 3)
    inner = (z == 1) | (z == 2)
    far = [{"dpo": lax.rem(z + k, 4)} for k in (1, 2, 3)]

    barrier = pltpu.get_barrier_semaphore()
    for peer in [to_core, to_chip, to_x] + far:
        pl.semaphore_signal(barrier, inc=1, device_id=peer, device_id_type=MESH)
    loads = {}

    def load(key, src, dst, slot):
        copy = pltpu.make_async_copy(src, dst, load_sem.at[slot])
        copy.start()
        loads[key] = copy

    def need(*keys):
        for key in keys:
            if key in loads:
                loads.pop(key).wait()

    def rows(c):
        return pl.ds(c * n, n)

    def load_ffn_weights():
        load("wgu", wgu_st, wgu, 0)
        load("wd", wd_st, wd, 1)

    def load_attn_weights():
        load("wqkv", wqkv_st, wqkv, 2)
        load("wout", wout_st, wout, 3)

    def load_h1(c):
        load(("h1", c), h1_st.at[0, c], h1s.at[c], 4 + c)

    def load_qkv(c):
        load(("qkv", c), qkv_st.at[c], qkvs.at[c], 6 + c)
        load(("lse", c), lse_st.at[c], lses.at[c], 8 + c)

    def load_o(c):
        load(("o", c), o_st.at[rows(c)], os.at[rows(c)], 10 + c)

    def load_h(c):
        load(("h", c), h_st.at[c], hs.at[c], 12 + c)

    top = layers - 1

    def own_rows(ref, c):
        return ref.at[pl.ds(pl.multiple_of((core * chunks + c) * n, n), n)]

    def own_attn(l):
        for t in range(3):
            load(("own", "a", t), w_qkv.at[l, t], wqkv.at[pl.ds(t * wa, la)], 17 + t)
        load(("own", "a", 3), w_out.at[l], wout.at[pl.ds(0, la)], 20)

    def own_ffn(l):
        load(("own", "g", 0), w_gate_up.at[l], raw_g, 21)
        load(("own", "d", 0), w_down.at[l], wd.at[pl.ds(0, lf)], 23)

    own_attn(0)
    for c in range(chunks):
        load(("token", c), own_rows(tokens, c), gm.at[rows(c)], 14 + c)
    load("classes", class_table, classes_ref, 16)
    own_ffn(0)

    def remote(src, dst, send, recv, to):
        return pltpu.make_async_remote_copy(
            src_ref=src, dst_ref=dst, send_sem=send, recv_sem=recv, device_id=to, device_id_type=MESH
        )

    turn = [0] * chunks

    def y_copy(c, k):
        return remote(ysend.at[c], yrecv.at[k % 2, c], ys_sem.at[c], yr_sem.at[k % 2, c], to_chip)

    def y_start(c):
        y_copy(c, turn[c]).start()

    def y_sum(c):
        copy = y_copy(c, turn[c])
        copy.wait()
        got = ysend[c] + yrecv[turn[c] % 2, c]
        turn[c] += 1
        return got

    def y_half_copy(c, at):
        k, part, i = turn[c] % 2, pl.ds(at, n // 2), at // (n // 2)
        return remote(ysend.at[c, part], yrecv.at[k, c, part], half_s.at[i], half_r.at[i], to_chip)

    def y_half_sum(c, at):
        part = pl.ds(at, n // 2)
        y_half_copy(c, at).wait()
        got = ysend[c, part, :] + yrecv[turn[c] % 2, c, part, :]
        if at > 0:
            turn[c] += 1
        return got

    def gain_of(l, i):
        return gains_ref[l, i : i + 1, :]

    def add_gain(l, i, c, term):
        k = 2 + 2 * l + i
        spot = (z, x, core, slice(k, k + 1), slice(None))
        small[spot] = term if c == 0 else small[spot] + term

    def close(l, i, c, g, h):
        grad = y_sum(c)
        scale = inv_rms(h)
        normed = h * scale
        add_gain(l, i, c, jnp.sum(grad * normed, axis=0, keepdims=True))
        return g + norm_back(grad, normed, scale, gain_of(l, i))

    def prepare(c):
        at = core * chunks + c
        lane = lax.broadcasted_iota(jnp.int32, (1, n), 1)
        is_open = (lane < 1 + COLS * heights_ref[at]) & (valid_ref[pl.ds(pl.multiple_of(at * n, n), n)][None, :] == 1)
        diagonal = lax.broadcasted_iota(jnp.int32, (n, n), 0) == lax.broadcasted_iota(jnp.int32, (n, n), 1)
        column = jnp.where(diagonal, jnp.where(is_open, 1.0, 0.0), 0.0)
        open_ref[c] = jnp.sum(column, axis=1, keepdims=True)
        slot = (z * groups[1] + x) * 2 * chunks + at
        lane = lax.broadcasted_iota(jnp.int32, (1, dim), 1)
        label = jnp.where(lane == slot, labels_ref[at], 0).astype(F32)
        spot = (z, x, core, slice(6, 7), slice(None))
        small[spot] = label if c == 0 else small[spot] + label

    groups = small.shape[:2]
    small[z, x, core] = jnp.zeros((8, dim), F32)

    def ffn_a(l, c, at=0, size=n):
        spot, part = pl.ds(c * n + at, size), pl.ds(at, size)
        if l == top:
            need(("cot", c))
            gs[c, part, :] = gm[spot, :].astype(F32)
            h1s[c, part, :] = hs_next(c) if size == n else hs[c, part, :] + y_half_sum(c, at)
            if at + size == n:
                load(("stash", c), h1s.at[c], h1_st.at[top, c], 28 + c)
        else:
            need(("h", c))
            g = close(l + 1, 0, c, gs[c], hs[c])
            gs[c] = g
            gm[spot, :] = g.astype(BF16)
            load_h(c)
        need(("h1", c), "wgu", "wd")
        h1 = h1s[c, part, :]
        b = (h1 * inv_rms(h1) * gain_of(l, 1)).astype(BF16)
        ab[spot, :] = b
        step = min(wf, 256)
        for f in range(0, wf, step):
            gate = mm(b, wgu[0, :, f : f + step])
            up = mm(b, wgu[1, :, f : f + step])
            dhid = mm(gm[spot, :], wd[f : f + step, :], NT)
            sig = jax.nn.sigmoid(gate)
            silu = gate * sig
            hid[spot, f : f + step] = (silu * up).astype(BF16)
            dgu[spot, f : f + step] = (dhid * up * (sig * (1.0 + gate * (1.0 - sig)))).astype(BF16)
            dgu[spot, wf + f : wf + f + step] = (dhid * silu).astype(BF16)

    later = {("fb", 1, 0), ("fb", 1, 1), ("po", 0), ("po", 1)}

    def ffn_done(*what):
        if what in later:
            later.discard(what)
            if not later:
                load_ffn_weights()

    def ffn_b(l, c):
        spot = rows(c)
        ysend[c] = mm(dgu[spot, :wf], wgu[0], NT) + mm(dgu[spot, wf:], wgu[1], NT)
        y_start(c)
        ffn_done("fb", l, c)

    def last_sum(c):
        need(("last", c - 1))
        spare = ok_g.at[0, pl.ds(0, n), pl.ds(0, dim)]
        spare[...] = mm(hid[rows(c), :], wd[...])
        load(("last", c), spare, last_st.at[c], 30)
        ffn_done("po", c)

    def attn(l, c):
        spot = rows(c)
        g1 = close(l, 1, c, gs[c], h1s[c])
        gs[c] = g1
        if l > 0:
            need(("stash", c))
            load_h1(c)
        gm[spot, :] = g1.astype(BF16)
        need("wqkv", "wout", ("qkv", c), ("lse", c))
        lane = lax.broadcasted_iota(jnp.int32, (n, 2 * HD), 1)
        low_half = lane < HD
        zero = jnp.zeros((n, 2 * HD), BF16)
        m = n // 2
        masks = [key_mask(open_ref.at[c], 0, m), key_mask(open_ref.at[c], m, n)]
        ga = gm[spot, :]
        for t in range(wa // (2 * HD)):
            spots = [slice(s * wa + t * 2 * HD, s * wa + (t + 1) * 2 * HD) for s in range(3)]
            q, k, v = [qkvs[c, :, s] for s in spots]
            dout = mm(ga, wout[t * 2 * HD : (t + 1) * 2 * HD, :], NT).astype(BF16)
            dq, dk, dv = [], [], []
            for e in range(2):
                mine = low_half if e == 0 else ~low_half
                q_one, d_one = jnp.where(mine, q, zero), jnp.where(mine, dout, zero)
                lse = lses[c, 2 * t + e : 2 * t + e + 1, :]
                probs, dprobs, deltas = [], [], []
                for mask, lo in zip(masks, (0, m)):
                    s = jnp.where(mask, mm(k[lo : lo + m], q_one[lo:], NT), LOW)
                    probs.append(jnp.exp(s - lse[:, lo:]))
                    dprobs.append(mm(v[lo : lo + m], d_one[lo:], NT))
                    deltas.append(jnp.sum(probs[-1] * dprobs[-1], axis=0, keepdims=True))
                late = deltas[0][:, m:] + deltas[1]
                deltas = [jnp.concatenate([deltas[0][:, :m], late], axis=1), late]
                ds = [(p * (d - delta)).astype(BF16) for p, d, delta in zip(probs, dprobs, deltas)]
                probs = [p.astype(BF16) for p in probs]
                dv.append(jnp.concatenate([mm(probs[0], dout), mm(probs[1], dout[m:])], axis=0))
                dk.append(jnp.concatenate([mm(ds[0], q), mm(ds[1], q[m:])], axis=0))
                early = mm(ds[0], k[:m], TN)
                dq.append(jnp.concatenate([early[:m], early[m:] + mm(ds[1], k[m:], TN)], axis=0))
            dq = jnp.where(low_half, dq[0], dq[1]) * HD ** (-0.5)
            dk = jnp.where(low_half, dk[0], dk[1])
            dv = jnp.where(low_half, dv[0], dv[1])
            dgu[spot, spots[0]] = rotate(dq, tables, -1).astype(BF16)
            dgu[spot, spots[1]] = rotate(dk, tables, -1).astype(BF16)
            dgu[spot, spots[2]] = dv.astype(BF16)
        ysend[c] = mm(dgu[spot, : 3 * wa], wqkv[...])
        y_start(c)
        if l > 0:
            load_qkv(c)
        need(("h", c))
        h = hs[c]
        ab[spot, :] = (h * inv_rms(h) * gain_of(l, 0)).astype(BF16)

    spans = [pl.ds(pl.multiple_of((1 - x) * half, half), half), pl.ds(pl.multiple_of(x * half, half), half)]
    split = sum(PIECES[E])
    down = (oth_s, cr_d, os_d, ok_d, xr_d, z1_d, z2_d)
    kinds = {
        E: down,
        D: down,
        G: (oth_g, cr_g, os_g, ok_g, xr_g, z1_g, z2_g),
        A: (oth_s, cr_a, os_a, ok_a, xr_a, z1_a, z2_a),
    }
    index = {D: 0, G: 1, A: 2, E: 4}
    order = list(kinds)
    units = []
    for kind in kinds:
        at = split if kind == D else 0
        for size in PIECES[kind]:
            target = {E: down_out, D: down_out, G: gate_up_out, A: out_out if at < la else qkv_out}[kind]
            base = la if kind == A and at >= la else 0
            units.append((kind, pl.ds(at, size), target, pl.ds(at - base, size)))
            at += size

    def c_copy(kind, lo=None, size=None):
        at = index[kind]
        source, target = kinds[kind][:2]
        if kind == E:
            lo, size = 0, split
        elif kind == D and lo is None:
            lo, size = split, lf - split
        if kind in (E, D):
            source, target = source.at[:, pl.ds(lo, size)], target.at[:, pl.ds(lo, size)]
        return remote(source, target, cs_sem.at[at], cr_sem.at[at], to_core)

    def weight_copy(kind):
        return c_copy(kind, 0, lf)

    def piece(kind, s, shard, put):
        if kind in (E, D):
            lo, hi = (0, split) if kind == E else (split, lf)
            put(slice(lo, hi), slice(None), mm(hid[:, shard * lf + lo : shard * lf + hi], gm[:, spans[s]], TN))
        elif kind == G:
            for t in range(2):
                cols = slice(t * wf + shard * lf, t * wf + (shard + 1) * lf)
                put(slice(None), slice(t * lf, (t + 1) * lf), mm(ab[:, spans[s]], dgu[:, cols], TN))
        else:
            put(slice(0, la), slice(None), mm(os[:, shard * la : (shard + 1) * la], gm[:, spans[s]], TN))
            for t in range(3):
                cols = slice(t * wa + shard * la, t * wa + (shard + 1) * la)
                put(slice((t + 1) * la, (t + 2) * la), slice(None), mm(dgu[:, cols], ab[:, spans[s]], TN))

    def put_in(ref, *lead):
        def put(r, c, value):
            ref[lead + (r, c)] = value

        return put

    arrived = set()

    def grad_other(l, kind):
        if kind == A:
            need(("o", 0), ("o", 1))
        if "c" not in arrived:
            pl.semaphore_wait(c_free, 1)
            arrived.add("c")
        for s in range(2):
            piece(kind, s, 1, put_in(kinds[kind][0], s))
        c_copy(kind).start()

    def grad_own(l, kind):
        if kind == A:
            need(("o", 0), ("o", 1))
        if l < top and kind == G:
            need(("last", chunks - 1))
        piece(kind, 0, 0, put_in(kinds[kind][2]))
        piece(kind, 1, 0, put_in(kinds[kind][3], l))

    def x_copy(l, u):
        kind, spot = units[u][:2]
        return remote(kinds[kind][2].at[spot], kinds[kind][4].at[spot], xs_sem.at[u], xr_sem.at[u], to_x)

    def core_sum(l, u):
        kind, spot = units[u][:2]
        _, cr, own_s, own_k, *_ = kinds[kind]
        if (l, kind) not in arrived:
            c_copy(kind).wait()
            if l < top:
                pl.semaphore_wait(x_free.at[order.index(kind)], len(PIECES[kind]))
            arrived.add((l, kind))
        own_s[spot, :] = own_s[spot, :] + cr[0, spot, :]
        x_copy(l, u).start()
        own_k[l, spot, :] = own_k[l, spot, :] + cr[1, spot, :]

    def z1_copy(l, u):
        kind, spot = units[u][:2]
        return remote(kinds[kind][3].at[l, spot], kinds[kind][5].at[spot], zs.at[l, u], zr.at[l, u], to_mate)

    def z2_copy(l, u):
        kind, spot = units[u][:2]
        return remote(kinds[kind][3].at[l, spot], kinds[kind][6].at[spot], zs.at[l, u], z2r.at[u], to_inner)

    def total_of(l, u):
        kind, spot, target, place = units[u]
        source = total_g if kind == G else kinds[kind][6]
        return source.at[spot], target.at[l, place]

    def z3_copy(l, u):
        source, target = total_of(l, u)
        return remote(source, target, zs.at[l, u], zr.at[l, u], to_mate)

    def store_copy(l, u):
        source, target = total_of(l, u)
        return pltpu.make_async_copy(source, target, store_sem.at[u])

    def x_sum(l, u):
        kind, spot = units[u][:2]
        keep, got = kinds[kind][3], kinds[kind][4]
        x_copy(l, u).wait()
        keep[l, spot, :] = keep[l, spot, :] + got[spot, :]
        if l > 0:
            pl.semaphore_signal(x_free.at[order.index(kind)], inc=1, device_id=to_x, device_id_type=MESH)

        @pl.when(outer)
        def _():
            if l < top:
                pl.semaphore_wait(z_free.at[u], 1)
            z1_copy(l, u).start()

    def z_one(l, u):
        kind, spot = units[u][:2]
        keep, got = kinds[kind][3], kinds[kind][5]

        @pl.when(inner)
        def _():
            z1_copy(l, u).wait_recv()
            keep[l, spot, :] = keep[l, spot, :] + got[spot, :]
            if l > 0:
                pl.semaphore_signal(z_free.at[u], inc=1, device_id=to_mate, device_id_type=MESH)
            if l < top:
                pl.semaphore_wait(z_free.at[u], 1)
            z2_copy(l, u).start()

    def z_two(l, u):
        kind, spot = units[u][:2]
        keep, got = kinds[kind][3], kinds[kind][6]

        @pl.when(inner)
        def _():
            z2_copy(l, u).wait()
            total = got[spot, :] + keep[l, spot, :]
            if kind == G:
                for t in range(2):
                    total_g[spot, t, :] = total[:, t * lf : (t + 1) * lf]
            else:
                got[spot, :] = total
            z3_copy(l, u).start()
            store_copy(l, u).start()

    def z_end(l, u):
        @pl.when(inner)
        def _():
            z3_copy(l, u).wait_send()
            store_copy(l, u).wait()
            if l > 0:
                pl.semaphore_signal(z_free.at[u], inc=1, device_id=to_inner, device_id_type=MESH)

        @pl.when(outer)
        def _():
            z1_copy(l, u).wait_send()
            z3_copy(l, u).wait_recv()

    def row_copies(src, dst, i, c):
        spot = pl.ds(pl.multiple_of((core * chunks + c) * n, n), n)
        return (
            pltpu.make_async_copy(src, dst.at[spot], row_sem.at[i, c]),
            remote(src, dst.at[spot], rows_s.at[i, c], rows_r.at[i, c], to_core),
        )

    def share_rows(src, dst, i, c):
        for copy in row_copies(src, dst, i, c):
            copy.start()

    def end_rows(src, dst, i, c):
        for copy in row_copies(src, dst, i, c):
            copy.wait()

    def token(c):
        need(("h", c))
        g = close(0, 0, c, gs[c], hs[c])
        small[z, x, core, c : c + 1, :] = g[0:1, :]
        row = lax.broadcasted_iota(jnp.int32, (n, dim), 0)
        gs[c] = jnp.where(row == 0, 0.0, g)
        share_rows(gs.at[c], token_grad, 0, c)

    def pout_copy(c):
        k = turn[c] % 2
        return remote(last_st.at[c], yrecv.at[k, c], ys_sem.at[c], yr_sem.at[k, c], to_chip)

    def start_output(c):
        pout_copy(c).start()
        load(("pout", c), last_st.at[c], ysend.at[c], 4 + c)
        load(("out", c), h1_st.at[top, c], hs.at[c], 12 + c)

    def end_output(c):
        need(("pout", c), ("out", c))
        pout_copy(c).wait()
        hs[c] = hs[c] + (ysend[c] + yrecv[turn[c] % 2, c])
        share_rows(hs.at[c], output, 1, c)

    def small_core():
        return remote(small.at[z, x, core], small.at[z, x, core], small_s.at[0], small_r.at[0], to_core)

    def small_x():
        return remote(small.at[z, x], small.at[z, x], small_s.at[1], small_r.at[1], to_x)

    def small_z(k):
        return remote(small.at[z], small.at[z], small_s.at[2 + k], small_r.at[2 + k], far[k])

    def small_got(k):
        back = lax.rem(z + 3 - k, 4)
        return remote(small.at[back], small.at[back], small_s.at[2 + k], small_r.at[2 + k], far[k])

    def attn_copy(part):
        rows_of = [pl.ds(0, 3 * la), pl.ds(3 * la, la)][part]
        return remote(
            oth_s.at[:, rows_of], cr_a.at[:, rows_of], cs_sem.at[2 + part], cr_sem.at[2 + part], to_core
        )

    def weight_stage(l, kind):
        if kind == A:
            need(*[("own", "a", t) for t in range(4)])
            for s in range(2):
                lanes = slice(s * half, (s + 1) * half)
                for t in range(3):
                    oth_s[s, t * la : (t + 1) * la, :] = wqkv[t * wa : t * wa + la, lanes].astype(F32)
                oth_s[s, 3 * la :, :] = wout[:la, lanes].astype(F32)
        elif kind == G:
            need(("own", "g", 0))
            step = half // 3
            for s in range(2):
                for r in range(0, half, step):
                    for t in range(2):
                        shard = raw_g[s * half + r : s * half + r + step, t, :]
                        wgu[t, s * half + r : s * half + r + step, :lf] = shard
                        oth_g[s, r : r + step, t * lf : (t + 1) * lf] = shard.astype(F32)
        else:
            need(("own", "d", 0))
            for s in range(2):
                oth_s[s, :lf, :] = wd[:lf, s * half : (s + 1) * half].astype(F32)

    def weight_send(l, kind):
        weight_stage(l, kind)
        if kind == A:
            attn_copy(0).start()
            attn_copy(1).start()
        else:
            weight_copy(kind).start()

    def weight_take(l, kind, part=0):
        if kind == A:
            attn_copy(part).wait()
        else:
            weight_copy(kind).wait()
        for s in range(2):
            lanes = slice(s * half, (s + 1) * half)
            if kind == A and part == 0:
                for t in range(3):
                    wqkv[t * wa + la : (t + 1) * wa, lanes] = cr_a[s, t * la : (t + 1) * la, :].astype(BF16)
            elif kind == A:
                wout[la:, lanes] = cr_a[s, 3 * la :, :].astype(BF16)
            elif kind == G:
                for t in range(2):
                    wgu[t, lanes, lf:] = cr_g[s, :, t * lf : (t + 1) * lf].astype(BF16)
            else:
                wd[lf:, lanes] = cr_d[s].astype(BF16)

    def hs_next(c):
        return base_of(c) + y_sum(c)

    def base_of(c):
        return hs[c] if turn[c] % 2 == 0 else h1s[c]

    def attn_up_start(l, c):
        spot = rows(c)
        if l == 0:
            need(("token", c))
            h = gm[spot, :].astype(F32)
            row = lax.broadcasted_iota(jnp.int32, (n, dim), 0)
            h = jnp.where(row == 0, first_ref[c : c + 1, :], h)
        else:
            h = hs_next(c)
            need(("st_h", c), ("st_qkv", c), ("st_lse", c), ("st_o", c))
        hs[c] = h
        ab[spot, :] = (h * inv_rms(h) * gain_of(l, 0)).astype(BF16)

    def attn_up_heads(c, pairs):
        spot = rows(c)
        a = ab[spot, :]
        lane = lax.broadcasted_iota(jnp.int32, (n, 2 * HD), 1)
        low_half = lane < HD
        zero = jnp.zeros((n, 2 * HD), BF16)
        m = n // 2
        masks = [key_mask(open_ref.at[c], 0, m), key_mask(open_ref.at[c], m, n)]
        for t in pairs:
            spots = [slice(s * wa + t * 2 * HD, s * wa + (t + 1) * 2 * HD) for s in range(3)]
            q = rotate(mm(a, wqkv[spots[0], :], NT), tables, 1)
            q = (q * HD ** (-0.5)).astype(BF16)
            k = rotate(mm(a, wqkv[spots[1], :], NT), tables, 1).astype(BF16)
            v = mm(a, wqkv[spots[2], :], NT).astype(BF16)
            for part, value in zip(spots, (q, k, v)):
                qkvs[c, :, part] = value
            mixed = []
            for e in range(2):
                q_one = jnp.where(low_half if e == 0 else ~low_half, q, zero)
                s = [jnp.where(mask, mm(k[lo : lo + m], q_one[lo:], NT), LOW) for mask, lo in zip(masks, (0, m))]
                peaks = [jnp.max(x, axis=0, keepdims=True) for x in s]
                late = jnp.maximum(peaks[0][:, m:], peaks[1])
                peak = jnp.concatenate([peaks[0][:, :m], late], axis=1)
                raised = [jnp.exp(s[0] - peak), jnp.exp(s[1] - late)]
                totals = [jnp.sum(x, axis=0, keepdims=True) for x in raised]
                total = jnp.concatenate([totals[0][:, :m], totals[0][:, m:] + totals[1]], axis=1)
                lses[c, 2 * t + e : 2 * t + e + 1, :] = peak + jnp.log(total)
                share = 1.0 / total
                prob = [(raised[0] * share).astype(BF16), (raised[1] * share[:, m:]).astype(BF16)]
                early = mm(prob[0], v[:m], TN)
                mixed.append(jnp.concatenate([early[:m], early[m:] + mm(prob[1], v[m:], TN)], axis=0))
            os[spot, t * 2 * HD : (t + 1) * 2 * HD] = jnp.where(low_half, mixed[0], mixed[1]).astype(BF16)

    def attn_up_end(l, c):
        if (l, c) == (top, chunks - 1):
            for at in (0, n // 2):
                ysend[c, pl.ds(at, n // 2), :] = mm(os[pl.ds(c * n + at, n // 2), :], wout[...])
                y_half_copy(c, at).start()
            return
        ysend[c] = mm(os[rows(c), :], wout[...])
        y_start(c)
        if l == 0:
            load(("st_h", c), hs.at[c], h_st.at[c], 12 + c)
            load(("st_qkv", c), qkvs.at[c], qkv_st.at[c], 6 + c)
            load(("st_lse", c), lses.at[c], lse_st.at[c], 8 + c)
            load(("st_o", c), os.at[rows(c)], o_st.at[rows(c)], 10 + c)

    def ffn_up(c):
        spot = rows(c)
        h1 = hs_next(c)
        h1s[c] = h1
        b = (h1 * inv_rms(h1) * gain_of(0, 1)).astype(BF16)
        step = min(wf, 256)
        for f in range(0, wf, step):
            gate = mm(b, wgu[0, :, f : f + step])
            up = mm(b, wgu[1, :, f : f + step])
            hid[spot, f : f + step] = (gate * jax.nn.sigmoid(gate) * up).astype(BF16)
        ysend[c] = mm(hid[spot, :], wd[...])
        y_start(c)
        load(("stash", c), h1s.at[c], h1_st.at[0, c], 28 + c)

    pairs = wa // (2 * HD)
    alone = la // (2 * HD)
    weight_stage(0, A)
    pl.semaphore_wait(barrier, 6)
    attn_copy(0).start()
    attn_copy(1).start()
    need("classes")
    row = lax.broadcasted_iota(jnp.int32, (16, classes_ref.shape[0]), 0)
    place = lax.broadcasted_iota(jnp.int32, row.shape, 1)
    chosen = jnp.zeros(row.shape, BF16)
    for c in range(chunks):
        here = (row == c) & (place == labels_ref[core * chunks + c])
        chosen = jnp.where(here, 1.0, chosen.astype(F32)).astype(BF16)
    first_ref[...] = mm(chosen, classes_ref[...])
    for c in range(chunks):
        prepare(c)
        attn_up_start(0, c)
        attn_up_heads(c, range(alone))
    weight_take(0, A, 0)
    attn_up_heads(0, range(alone, pairs))
    weight_take(0, A, 1)
    attn_up_end(0, 0)
    weight_send(0, G)
    attn_up_heads(1, range(alone, pairs))
    attn_up_end(0, 1)
    weight_send(0, D)
    for c in range(chunks):
        load(("cot", c), own_rows(cotangent, c), gm.at[rows(c)], 14 + c)
    load("st_wqkv", wqkv, wqkv_st, 2)
    load("st_wout", wout, wout_st, 3)
    weight_take(0, D)
    weight_take(0, G)
    need("st_wqkv", "st_wout")
    own_attn(1)
    ffn_up(0)
    weight_send(1, A)
    ffn_up(1)
    load("st_wgu", wgu, wgu_st, 0)
    load("st_wd", wd, wd_st, 1)
    weight_take(1, A, 0)
    weight_take(1, A, 1)
    need("st_wgu", "st_wd")
    own_ffn(1)
    for c in range(chunks):
        attn_up_start(1, c)
        attn_up_heads(c, range(pairs))
        attn_up_end(1, c)
        need(("stash", c))
        if c == 0:
            weight_send(1, D)
            weight_send(1, G)
    weight_take(1, D)
    weight_take(1, G)
    pl.semaphore_signal(c_free, inc=1, device_id=to_core, device_id_type=MESH)

    def start_small():
        small_core().start()

    def move_small():
        small_core().wait_send()
        spot = small.at[z, x, 1 - core]
        remote(spot, spot, small_s.at[0], small_r.at[0], to_core).wait_recv()
        small_x().start()

    def spread_small():
        small_x().wait_send()
        spot = small.at[z, 1 - x]
        remote(spot, spot, small_s.at[1], small_r.at[1], to_x).wait_recv()
        for k in range(3):
            small_z(k).start()

    def end_small():
        for k in range(3):
            small_z(k).wait_send()
            small_got(k).wait_recv()
        everyone = [(i, j, k) for i in range(groups[0]) for j in range(groups[1]) for k in range(2)]
        total = None
        for at, place in enumerate(everyone):
            block = small[place]
            total = block if total is None else total + block
            firsts_ref[at * chunks : (at + 1) * chunks, :] = small[place + (slice(0, chunks), spans[1])]
        for l in range(layers):
            gain_out[l] = total[2 + 2 * l : 4 + 2 * l, :]
        slots = firsts_ref.shape[0]
        label = total[6:7, :slots].astype(jnp.int32)
        classes, step = table_out.shape[0], 256
        for at in range(0, classes, step):
            size = min(step, classes - at)
            same = lax.broadcasted_iota(jnp.int32, (size, slots), 0) + at == label
            spare = oth_s.at[at // (4 * la), pl.ds(at % (4 * la), size)]
            spare[...] = lax.dot_general(
                jnp.where(same, 1.0, 0.0), firsts_ref[...], NN,
                precision=lax.Precision.HIGHEST, preferred_element_type=F32,
            )
            load(("table", at), spare, table_out.at[pl.ds(at, size)], 24 + at // step)

    def attn_down(l, c):
        attn(l, c)
        if (l, c) == (1, chunks - 1):
            load_attn_weights()

    def ffn_first(l, c):
        ffn_a(l, c, *((n // 2, n // 2) if (l, c) == (top, chunks - 1) else ()))

    acts = {
        FX: lambda: ffn_a(top, chunks - 1, 0, n // 2),
        FA: ffn_first, FB: ffn_b, PO: last_sum, AT: attn_down, GO: grad_other, GW: grad_own, CU: core_sum,
        XS: x_sum, ZA: z_one, ZB: z_two, ZC: z_end, TK: token, SO: start_output, EO: end_output,
        SC: start_small, SX: move_small, SZ: spread_small, SW: end_small,
    }
    left = {(GO, 1, A), (GW, 1, A)}
    for name, *at in ORDER:
        acts[name](*at)
        if left:
            left.discard((name, *at))
            if not left:
                for c in range(chunks):
                    load_o(c)
    need(*list(loads))
    for c in range(chunks):
        end_rows(gs.at[c], token_grad, 0, c)
        end_rows(hs.at[c], output, 1, c)


def call(body, outs, args, flops, limit=40, smem=0, scratch=()):
    moved = sum(x.size * x.dtype.itemsize for x in args) + sum(
        int(np.prod(s)) * np.dtype(d).itemsize for s, d in outs
    )
    spec = pl.BlockSpec(memory_space=pltpu.VMEM)
    got = pl.pallas_call(
        body,
        out_shape=[jax.ShapeDtypeStruct(s, d) for s, d in outs],
        in_specs=[pl.BlockSpec(memory_space=pltpu.SMEM)] * smem + [spec] * (len(args) - smem),
        out_specs=[spec] * len(outs),
        scratch_shapes=list(scratch),
        compiler_params=pltpu.CompilerParams(vmem_limit_bytes=limit * 2**20),
        cost_estimate=pl.CostEstimate(flops=int(flops), bytes_accessed=int(moved), transcendentals=0),
    )(*args)
    return list(got)


def settle(*refs):
    count = (len(refs) - 2) // 3
    ins, outs, spare = refs[:count], refs[count : 2 * count], refs[2 * count : 3 * count]
    in_sem, out_sem = refs[3 * count :]
    reads = [pltpu.make_async_copy(a, b, in_sem.at[i]) for i, (a, b) in enumerate(zip(ins, spare))]
    writes = [pltpu.make_async_copy(b, a, out_sem.at[i]) for i, (a, b) in enumerate(zip(outs, spare))]
    for read in reads:
        read.start()
    for read, write in zip(reads, writes):
        read.wait()
        write.start()
    for write in writes:
        write.wait()


def call_settle(results):
    anywhere = pl.BlockSpec(memory_space=pl.ANY)
    shapes = [x.shape for x in results]
    return pl.pallas_call(
        settle,
        out_shape=[jax.ShapeDtypeStruct(s, F32) for s in shapes],
        in_specs=[anywhere] * len(shapes),
        out_specs=[anywhere] * len(shapes),
        scratch_shapes=[pltpu.VMEM(s, F32) for s in shapes] + [pltpu.SemaphoreType.DMA((len(shapes),))] * 2,
        compiler_params=pltpu.CompilerParams(vmem_limit_bytes=62 * 2**20),
        name="settle",
    )(*results)


def call_whole(sizes, n, dim, wa, wf, layers, chunks, classes, fixed, numbers, moved):
    la, lf, half = wa // 2, wf // 2, dim // 2
    groups = sizes["dpo"], sizes["dpi"]
    outs = [
        ((2 * chunks * n, dim), F32),
        ((2 * chunks * n, dim), F32),
        ((classes, half), F32),
        ((layers, 2, dim), F32),
        ((layers, lf, half), F32),
        ((layers, half, 2, lf), F32),
        ((layers, la, half), F32),
        ((layers, 3 * la, half), F32),
        ((2, dim, wf), BF16),
        ((wf, dim), BF16),
        ((3 * wa, dim), BF16),
        ((wa, dim), BF16),
        ((chunks, n, dim), F32),
        ((layers, chunks, n, dim), F32),
        ((chunks, n, 3 * wa), BF16),
        ((chunks, 8, n), F32),
        ((chunks * n, wa), BF16),
        ((chunks, n, dim), F32),
    ]
    d, g, a = (lf, half), (half, 2 * lf), (4 * la, half)
    f, h = lambda *s: pltpu.VMEM(s, F32), lambda *s: pltpu.VMEM(s, BF16)
    dma, count = pltpu.SemaphoreType.DMA, pltpu.SemaphoreType.REGULAR
    units = sum(len(k) for k in PIECES.values())
    scratch = [h(2, dim, wf), h(wf, dim), h(3 * wa, dim), h(wa, dim)]
    scratch += [f(chunks, n, dim), f(chunks, n, dim), h(chunks, n, 3 * wa), h(chunks * n, wa), f(chunks, 8, n)]
    scratch += [f(chunks, n, dim), f(2, chunks, n, dim), f(chunks, n, dim)]
    scratch += [h(chunks * n, dim), h(chunks * n, dim), h(chunks * n, wf), h(chunks * n, 2 * wf)]
    scratch += [f(2, *g), f(2, *a)] + [f(2, *k) for k in (d, g, a)]
    scratch += [f(*k) for k in (d, g, a)] + [f(layers, *k) for k in (d, g, a)]
    scratch += [f(*k) for _ in range(3) for k in (d, g, a)] + [f(*groups, 2, 8, dim)]
    scratch += [f(chunks, n, 1), h(dim, 2, lf), f(half, 2, lf), f(groups[0] * groups[1] * 2 * chunks, half)]
    scratch += [h(classes, dim), f(16, dim)]
    scratch += [dma((32,)), dma((chunks,)), dma((2, chunks)), dma((5,)), dma((5,))]
    scratch += [dma((units,))] * 2 + [dma((layers, units))] * 2 + [dma((units,))] * 2 + [dma((2,))] * 2
    scratch += [dma((2, chunks))] * 3 + [dma((5,))] * 2 + [count((len(PIECES),)), count((units,)), count]
    args = list(fixed) + list(numbers) + list(moved)
    flops = layers * chunks * n * (2 * dim * (14 * wa + 12 * wf) + 32 * n * wa)
    vmem, smem = pl.BlockSpec(memory_space=pltpu.VMEM), pl.BlockSpec(memory_space=pltpu.SMEM)
    anywhere = pl.BlockSpec(memory_space=pl.ANY)
    return pl.pallas_call(
        functools.partial(whole_pass, (n, dim, wa, wf, layers, chunks)),
        out_shape=[jax.ShapeDtypeStruct(s, t) for s, t in outs],
        in_specs=[vmem] * len(fixed) + [smem] * len(numbers) + [anywhere] * len(moved),
        out_specs=[vmem if i == 3 else anywhere for i in range(len(outs))],
        scratch_shapes=scratch,
        compiler_params=pltpu.CompilerParams(
            vmem_limit_bytes=63 * 2**20, collective_id=0, has_side_effects=True
        ),
        cost_estimate=pl.CostEstimate(flops=flops, bytes_accessed=90 * 10**6, transcendentals=0),
        name="whole_pass",
    )(*args)[:8]


def on_device(sizes, tokens, cotangent, heights, labels, valid, class_table, gains, w_qkv, w_out, w_gate_up, w_down):
    seq_count = heights.shape[0]
    row_count, dim = tokens.shape
    n = row_count // seq_count
    layers = gains.shape[0]
    classes = class_table.shape[0]
    la = w_out.shape[1]
    lf = w_down.shape[1]
    wa, wf = 2 * la, 2 * lf
    tp, dpo, dpi = sizes["tp"], sizes["dpo"], sizes["dpi"]
    mine = seq_count // 2
    lean = (tp, dpo, dpi) == (4, 4, 2) and (mine, layers) == (2, 2)
    core = lax.rem(lax.axis_index("tp"), 2)
    z = lax.axis_index("dpo")
    swap_core = [(i, i ^ 1) for i in range(tp)]

    def core_swap(x):
        return lax.ppermute(x, "tp", swap_core)

    def sum_chips(part):
        total = None
        for step in range(2, tp, 2):
            got = lax.ppermute(part, "tp", [(i, i ^ step) for i in range(tp)])
            total = got if total is None else total + got
        return total

    tables = jnp.asarray(rope_constants(n))
    if lean:
        fixed = (gains, tables, valid)
        moved = (class_table, tokens, cotangent, jnp.transpose(w_qkv, (0, 2, 3, 1)), w_out, w_gate_up, w_down)
        got = call_whole(sizes, n, dim, wa, wf, layers, mine, classes, fixed, (heights, labels), moved)
        output, token_grad, table_part, gain_total, down_part, gate_up_part, out_part, qkv_part = call_settle(got)
        half = dim // dpi
        return (
            output,
            token_grad,
            table_part,
            gain_total,
            qkv_part.reshape(layers, 3, la, half).transpose(0, 3, 1, 2),
            out_part,
            gate_up_part,
            down_part,
        )

    position = jnp.arange(n)
    own = lambda x: lax.dynamic_slice_in_dim(x, core * mine, mine, 0)
    open_key = (position[None, :] < 1 + COLS * own(heights)[:, None]) & (own(valid.reshape(seq_count, n)) == 1)
    open_key = open_key.astype(F32)[:, :, None]
    own_labels = own(labels)
    wqkv, wout, wgu, wd = [], [], [], []
    for l in range(layers):
        for into, w in (
            (wqkv, jnp.transpose(w_qkv[l], (1, 2, 0))),
            (wout, w_out[l][None]),
            (wgu, jnp.transpose(w_gate_up[l], (1, 0, 2))),
            (wd, w_down[l][None]),
        ):
            wide = w.astype(F32)
            axis = 2 if into is wgu else 1
            shape = list(w.shape)
            shape[axis] *= 2
            into.append(call(functools.partial(merge, axis), [(tuple(shape), BF16)], (wide, core_swap(wide)), 1000)[0])
        wqkv[l] = wqkv[l].reshape(3 * wa, dim)
        wout[l] = wout[l][0]
        wd[l] = wd[l][0]

    token_own = own(tokens.reshape(seq_count, n, dim))
    cot_own = own(cotangent.reshape(seq_count, n, dim))
    chunks = range(mine)
    hs = []
    for c in chunks:
        row = lax.dynamic_slice_in_dim(class_table, own_labels[c], 1, 0)
        hs.append(jnp.where((position == 0)[:, None], row, token_own[c]).astype(F32))

    shape_d = ((n, dim), F32)
    shape_b = ((n, dim), BF16)
    flops_a = 2 * n * dim * 4 * wa + 8 * n * n * wa
    flops_f = 2 * n * dim * 3 * wf

    kept = []
    state = [(hs[c],) for c in chunks]
    parts = None
    for l in range(layers):
        keep = [dict() for _ in chunks]
        for c in chunks:
            args = state[c] + (gains[l, 0][None], wqkv[l], wout[l], tables, open_key[c])
            outs = [((n, 3 * wa), BF16), ((max(8, wa // HD), n), F32), ((n, wa), BF16), shape_d]
            outs = ([shape_d] if l > 0 else []) + [shape_b] + outs
            got = call(functools.partial(attn_fwd, l == 0), outs, args, flops_a)
            h = state[c][0] if l == 0 else got.pop(0)
            a, qkv, lse, o, part = got
            keep[c].update(h=h, a=a, qkv=qkv, lse=lse, o=o)
            state[c] = (h, part, sum_chips(part))
        for c in chunks:
            args = state[c] + (gains[l, 1][None], wgu[l], wd[l])
            outs = [shape_d, shape_b, ((n, 2 * wf), F32), ((n, wf), BF16), shape_d]
            h1, b, gu, hid, part = call(ffn_fwd, outs, args, flops_f)
            keep[c].update(h1=h1, b=b, gu=gu, hid=hid)
            state[c] = (h1, part, sum_chips(part))
        kept.append(keep)

    output = jnp.concatenate([s[0] + (s[1] + s[2]) for s in state], axis=0)

    half = lax.axis_index("dpi") if dpi == 2 else 1
    order = jnp.stack([jnp.int32(1) - half, jnp.int32(half)])

    def dp_sum(both, other, axis):
        got = core_swap(other)
        if dpi == 2:
            sent = lax.ppermute(both[0] + got[0], "dpi", [(0, 1), (1, 0)])
            total = (both[1] + got[1]) + sent
        else:
            both = both + got
            whole = jnp.concatenate([both[0], both[1]], axis=axis)
            total = lax.psum_scatter(whole, "dpi", scatter_dimension=axis, tiled=True)
        return line_sum(total)

    def line_sum(x):
        if dpo != 4:
            return lax.psum(x, "dpo")
        got = lax.ppermute(x, "dpo", [(0, 1), (3, 2)])
        x = x + got
        got = lax.ppermute(x, "dpo", [(1, 2), (2, 1)])
        x = x + got
        got = lax.ppermute(x, "dpo", [(1, 0), (2, 3)])
        return jnp.where((z == 0) | (z == dpo - 1), got, x)

    gain_rows = [[None, None] for _ in range(layers)]
    grads = [None] * layers
    state = [None] * mine
    for l in reversed(range(layers)):
        top = l == layers - 1
        keep = kept[l]
        gms = []
        for c in chunks:
            outs = [((n, 2 * wf), BF16), shape_d]
            args = (keep[c]["gu"], wgu[l], wd[l])
            if top:
                g = cot_own[c]
                dgu, part = call(functools.partial(ffn_bwd, True), outs, (g,) + args, flops_f)
                gms.append(g)
            else:
                outs = [shape_d, ((1, dim), F32), shape_b] + outs
                args = state[c] + args
                g, gain_c, gm, dgu, part = call(functools.partial(ffn_bwd, False), outs, args, flops_f)
                gain_rows[l + 1][0] = gain_c if c == 0 else gain_rows[l + 1][0] + gain_c
                gms.append(gm)
            keep[c]["dgu"] = dgu
            state[c] = (g, part, sum_chips(part), keep[c]["h1"], gains[l, 1][None])
        flops_w = 2 * n * mine * dim * wf
        outs = [((2, lf, dim // 2), F32)] * 2
        args = [order] + [keep[c]["hid"] for c in chunks] + gms
        spans = (((0, lf),), ((lf, wf),))
        down = call(functools.partial(grad_rows, spans), outs, args, flops_w, smem=1)
        outs = [((2, dim // 2, 2 * lf), F32)] * 2
        args = [order] + [keep[c]["b"] for c in chunks] + [keep[c]["dgu"] for c in chunks]
        spans = (((0, lf), (wf, wf + lf)), ((lf, wf), (wf + lf, 2 * wf)))
        gate_up = call(functools.partial(grad_columns, spans), outs, args, 2 * flops_w, smem=1)
        down = dp_sum(*down, 1)
        gate_up = dp_sum(*gate_up, 0)
        gas = []
        for c in chunks:
            outs = [shape_d, ((1, dim), F32), shape_b, ((n, 3 * wa), BF16), shape_d]
            args = state[c] + (wqkv[l], wout[l], tables, open_key[c], keep[c]["qkv"], keep[c]["lse"])
            g1, gain_c, ga, dqkv, part = call(attn_bwd, outs, args, flops_a + 12 * n * n * wa)
            gain_rows[l][1] = gain_c if c == 0 else gain_rows[l][1] + gain_c
            gas.append(ga)
            keep[c]["dqkv"] = dqkv
            state[c] = (g1, part, sum_chips(part), keep[c]["h"], gains[l, 0][None])
        flops_w = 2 * n * mine * dim * wa
        outs = [((2, la, dim // 2), F32)] * 2
        args = [order] + [keep[c]["o"] for c in chunks] + gas
        spans = (((0, la),), ((la, wa),))
        out = call(functools.partial(grad_rows, spans), outs, args, flops_w, smem=1)
        outs = [((2, 3 * la, dim // 2), F32)] * 2
        args = [order] + [keep[c]["dqkv"] for c in chunks] + [keep[c]["a"] for c in chunks]
        spans = tuple(tuple((t * wa + s * la, t * wa + (s + 1) * la) for t in range(3)) for s in range(2))
        qkv = call(functools.partial(grad_rows, spans), outs, args, 3 * flops_w, smem=1)
        out = dp_sum(*out, 1)
        qkv = dp_sum(*qkv, 1)
        grads[l] = (qkv, out, gate_up, down)

    finals = []
    for c in chunks:
        g, gain_c = call(close_layer, [shape_d, ((1, dim), F32)], state[c], 1000)
        gain_rows[0][0] = gain_c if c == 0 else gain_rows[0][0] + gain_c
        finals.append(g)

    slot0 = lax.axis_index("dpo") * dpi + lax.axis_index("dpi")
    seqs = seq_count * dpo * dpi
    firsts = jnp.concatenate([g[0:1] for g in finals], axis=0)
    small = jnp.zeros((seqs + 2 * layers + 1, dim), F32)
    small = lax.dynamic_update_slice(small, firsts, (slot0 * seq_count + core * mine, 0))
    terms = jnp.concatenate([gain_rows[l][i] for l in range(layers) for i in range(2)], axis=0)
    small = lax.dynamic_update_slice(small, terms, (seqs, 0))
    label_row = lax.dynamic_update_slice(
        jnp.zeros((1, dim), F32), own_labels.astype(F32)[None], (0, slot0 * seq_count + core * mine)
    )
    small = lax.dynamic_update_slice(small, label_row, (seqs + 2 * layers, 0))
    small = jnp.where(lax.axis_index("tp") < 2, small, 0.0)
    small = lax.psum(small, ("dpo", "dpi", "tp"))
    all_labels = jnp.round(small[seqs + 2 * layers, :seqs]).astype(jnp.int32)
    gain_total = small[seqs : seqs + 2 * layers].reshape(layers, 2, dim)
    onehot = (all_labels[None, :] == jnp.arange(classes)[:, None]).astype(F32)
    share = dim // dpi
    rows = lax.dynamic_slice(small, (0, lax.axis_index("dpi") * share), (seqs, share))
    table_part = jnp.dot(onehot, rows, precision=lax.Precision.HIGHEST)

    token_own = jnp.concatenate([jnp.where((position == 0)[:, None], 0.0, g) for g in finals], axis=0)

    def both_cores(x):
        other = core_swap(x)
        return jnp.where(core == 0, jnp.concatenate([x, other], 0), jnp.concatenate([other, x], 0))

    qkv_part = jnp.stack([g[0].reshape(3, la, share) for g in grads]).transpose(0, 3, 1, 2)
    out_part = jnp.stack([g[1] for g in grads])
    gate_up_part = jnp.stack([g[2].reshape(share, 2, lf) for g in grads])
    down_part = jnp.stack([g[3] for g in grads])
    return (
        both_cores(output),
        both_cores(token_own),
        table_part,
        gain_total,
        qkv_part,
        out_part,
        gate_up_part,
        down_part,
    )


def solution(mesh):
    sizes = dict(mesh.shape)
    placed = (
        P(("dpo", "dpi"), None),
        P(("dpo", "dpi"), None),
        P(("dpo", "dpi")),
        P(("dpo", "dpi")),
        P(("dpo", "dpi")),
        P(),
        P(),
        P(None, None, None, "tp"),
        P(None, "tp", None),
        P(None, None, None, "tp"),
        P(None, "tp", None),
    )
    return jax.shard_map(
        functools.partial(on_device, sizes),
        mesh=mesh,
        in_specs=placed,
        out_specs=(
            P(("dpo", "dpi"), None),
            P(("dpo", "dpi"), None),
            P(None, "dpi"),
            P(),
            P(None, "dpi", None, "tp"),
            P(None, "tp", "dpi"),
            P(None, "dpi", None, "tp"),
            P(None, "tp", "dpi"),
        ),
        check_vma=False,
    )
```
